32 devices in a mesh: ctx: 8 (over y, x, core), fsdp: 4 (over z).
Axes of the slice: x: 2, y: 2, z: 4, core: 2. Of those that a mesh axis runs over, the one named last changes fastest.
Arguments:
- tokens: bfloat16 [16, 1024, 768], P('fsdp', 'ctx'), may hold values from -6 to 6
- cotangent: bfloat16 [16, 1024, 768], P('fsdp', 'ctx'), may hold values from -6 to 6
- lengths: int32 [16], P('fsdp'), may hold values from 256 to 1024, as said below
- bucket_table: int32 [2047], replicated, may hold values from 0 to 31, as said below
- gain_attn: bfloat16 [768], P('fsdp'), may hold values from 0.5 to 1.5
- w_query: bfloat16 [768, 768], P('fsdp'), may hold values from -0.109375 to 0.109375
- w_key: bfloat16 [768, 768], P('fsdp'), may hold values from -0.109375 to 0.109375
- w_value: bfloat16 [768, 768], P('fsdp'), may hold values from -0.21875 to 0.21875
- w_out: bfloat16 [768, 768], P('fsdp'), may hold values from -6 to 6
- bias_table: bfloat16 [32, 12], P('fsdp'), may hold values from -4 to 4
- gain_ffn: bfloat16 [768], P('fsdp'), may hold values from 0.5 to 1.5
- w_gate: bfloat16 [768, 3072], P('fsdp'), may hold values from -0.21875 to 0.21875
- w_up: bfloat16 [768, 3072], P('fsdp'), may hold values from -0.21875 to 0.21875
- w_ffn_out: bfloat16 [3072, 768], P('fsdp'), may hold values from -0.109375 to 0.109375
Outputs:
- out: bfloat16 [16, 1024, 768], P('fsdp', 'ctx')
- grad_tokens: float32 [16, 1024, 768], P('fsdp', 'ctx')
- grad_gain_attn: float32 [768], P('fsdp')
- grad_w_query: float32 [768, 768], P('fsdp')
- grad_w_key: float32 [768, 768], P('fsdp')
- grad_w_value: float32 [768, 768], P('fsdp')
- grad_w_out: float32 [768, 768], P('fsdp')
- grad_bias_table: float32 [32, 12], P('fsdp')
- grad_gain_ffn: float32 [768], P('fsdp')
- grad_w_gate: float32 [768, 3072], P('fsdp')
- grad_w_up: float32 [768, 3072], P('fsdp')
- grad_w_ffn_out: float32 [3072, 768], P('fsdp')
The draws below stay inside these ranges and needn't reach their ends.
Inputs may be any that keep to these rules, and one draw needn't show every extreme that they name: `lengths`: of the 4 sequences of each index of fsdp (consecutive sequences), one has 1024 used slots and one a quarter of 1024. `bucket_table`: entry r + 1023 is the bucket of a key r slots after its query; it depends on |r| and the sign of r only, equals |r| for |r| < 32 // 4 (plus 32 // 2 where r > 0) and never falls as |r| grows.
All inputs are finite; a program needn't handle non-finite values.
Results may differ from the reference program's by a relative error of at most 0.02.
Values may be sent and summed in bfloat16 or wider, within the bound.
No kernel may reach another device: no remote copies, remote signals or barrier semaphores. Data moves between devices by JAX's collectives and lax.ppermute only.
A program may use at most 256 MiB of HBM per device.

```python
import math
import jax
import jax.numpy as jnp
from jax import lax

D = 768
HEADS = 12
HEAD_DIM = 64
FF = 3072
BUCKETS = 32
MB = 4
SEQ = 1024
SEQS = 16


def draw_lengths(key, part):
    groups = SEQS // MB
    drawn = jax.random.randint(jax.random.fold_in(key, 11), (groups, MB), SEQ // 4, SEQ + 1)
    subkeys = jax.random.split(jax.random.fold_in(key, 12), groups)
    orders = jax.vmap(lambda subkey: jax.random.permutation(subkey, MB))(subkeys)
    column = jnp.arange(MB, dtype=jnp.int32)[None, :]
    longest = column == orders[:, 0:1]
    shortest = column == orders[:, 1:2]
    chosen = jnp.where(longest, SEQ, jnp.where(shortest, SEQ // 4, drawn))
    return chosen.reshape(SEQS).astype(jnp.int32)


def draw_bucket_table(key, part):
    exact_span = BUCKETS // 4
    bound_count = BUCKETS // 2 - exact_span - 1
    widths = jax.random.randint(jax.random.fold_in(key, 21), (bound_count,), 1, max(2, SEQ // 8))
    bounds = exact_span + jnp.cumsum(widths)
    offsets = jnp.arange(2 * SEQ - 1, dtype=jnp.int32) - (SEQ - 1)
    distance = jnp.abs(offsets)
    far_bucket = exact_span + jnp.sum((distance[:, None] >= bounds[None, :]).astype(jnp.int32), axis=1)
    bucket = jnp.where(distance < exact_span, distance, far_bucket)
    return (bucket + BUCKETS // 2 * (offsets > 0).astype(jnp.int32)).astype(jnp.int32)


def shard_levels(stream_key, dims, cuts, low, high):
    loudness = 1.0
    for dim, parts in cuts:
        heights = jax.random.uniform(jax.random.fold_in(jax.random.fold_in(stream_key, 6), dim), (parts,), jnp.float32, low / len(cuts), high / len(cuts))
        loudness = loudness * jnp.repeat(jnp.exp(heights), dims[dim] // parts).reshape((-1,) + (1,) * (len(dims) - 1 - dim))
    return loudness


def noise(rng, shape, spread, bound, cuts=(), kind=jnp.bfloat16):
    array = jax.random.normal(rng, shape, jnp.float32) * spread
    if len(cuts) > 0:
        array = shard_levels(rng, shape, cuts, -0.22, 0.18) * array
    return jnp.clip(array, min=-bound, max=bound).astype(kind)


def setup_inputs(seed: int = 0) -> dict:
    seeds = jax.random.split(jax.random.key(seed), 15)
    return {
        "tokens": noise(seeds[0], (SEQS, SEQ, D), 1.0, 6.0, ((0, 4), (1, 8))),
        "cotangent": noise(seeds[1], (SEQS, SEQ, D), 1.0, 6.0, ((0, 4), (1, 8))),
        "lengths": draw_lengths(jax.random.fold_in(seeds[14], 71), 0),
        "bucket_table": draw_bucket_table(jax.random.fold_in(seeds[14], 71), 0),
        "gain_attn": jnp.clip(1.0 + 0.1 * jax.random.normal(seeds[4], (D,), jnp.float32), 0.5, 1.5).astype(jnp.bfloat16),
        "w_query": noise(seeds[5], (D, D), (4 * D) ** -0.5, 0.109375, ((0, 4),)),
        "w_key": noise(seeds[6], (D, D), (4 * D) ** -0.5, 0.109375, ((0, 4),)),
        "w_value": noise(seeds[7], (D, D), D ** -0.5, 0.21875, ((0, 4),)),
        "w_out": noise(seeds[8], (D, D), 1.0, 6.0, ((0, 4),)),
        "bias_table": noise(seeds[9], (BUCKETS, HEADS), 1.0, 4.0, ((0, 4),)),
        "gain_ffn": jnp.clip(1.0 + 0.1 * jax.random.normal(seeds[10], (D,), jnp.float32), 0.5, 1.5).astype(jnp.bfloat16),
        "w_gate": noise(seeds[11], (D, FF), D ** -0.5, 0.21875, ((0, 4),)),
        "w_up": noise(seeds[12], (D, FF), D ** -0.5, 0.21875, ((0, 4),)),
        "w_ffn_out": noise(seeds[13], (FF, D), FF ** -0.5, 0.109375, ((0, 4),)),
    }


norm_eps = 1e-06
highest = lax.Precision.HIGHEST

@jax.custom_vjp
def low(v):
    return lax.optimization_barrier(v.astype(jnp.bfloat16)).astype(jnp.float32)

@jax.custom_vjp
def low_back(v):
    return v

def low_keep(v):
    return (low(v), None)

def low_pass(kept, grad):
    return (grad,)

def back_keep(v):
    return (v, None)

def back_low(kept, grad):
    return (low(grad),)
low.defvjp(low_keep, low_pass)
low_back.defvjp(back_keep, back_low)

def gelu_tanh(values):
    return 0.5 * values * (1.0 + jnp.tanh(0.7978845608028654 * (values + 0.044715 * values * values * values)))

def normalize(values, gain_vec):
    return values * lax.rsqrt(lax.optimization_barrier(jnp.mean(values * values, axis=-1, keepdims=True)) + norm_eps) * gain_vec

def project(values, matrix):
    return jnp.einsum('gsd,de->gse', values, matrix, precision=highest)

def layer_block(params, tokens_f, valid_rows, buckets):
    gain_attn, w_query, w_key, w_value, w_out, bias_table, gain_ffn, w_gate, w_up, w_ffn_out = params
    groups, length, model_width = tokens_f.shape
    normed = low(normalize(tokens_f, gain_attn))
    queries = low(low_back(project(normed, w_query))).reshape(groups, length, HEADS, HEAD_DIM)
    keys_all = low(low_back(project(normed, w_key))).reshape(groups, length, HEADS, HEAD_DIM)
    values_all = low(low_back(project(normed, w_value))).reshape(groups, length, HEADS, HEAD_DIM)
    pair_bias = jnp.transpose(bias_table[buckets], (2, 0, 1))
    scores = jnp.einsum('gihe,gjhe->ghij', queries, keys_all, precision=highest) + pair_bias[None]
    scores = low_back(scores)
    scores = jnp.where(valid_rows[:, None, None, :] > 0, scores, -1e+30)
    shifted = jnp.exp(scores - lax.optimization_barrier(jnp.max(scores, axis=-1, keepdims=True)))
    probabilities = low(shifted / lax.optimization_barrier(jnp.sum(shifted, axis=-1, keepdims=True)))
    attended = jnp.einsum('ghij,gjhe->gihe', probabilities, values_all, precision=highest)
    attended = low(low_back(attended.reshape(groups, length, model_width)))
    residual = tokens_f + low_back(project(attended, w_out))
    normed_ffn = low(normalize(residual, gain_ffn))
    gate_proj = low_back(project(normed_ffn, w_gate))
    up_proj = low_back(project(normed_ffn, w_up))
    hidden = low(gelu_tanh(gate_proj) * up_proj)
    return valid_rows[:, :, None] * (residual + project(hidden, w_ffn_out))

def reference(tokens, cotangent, lengths, bucket_table, gain_attn, w_query, w_key, w_value, w_out, bias_table, gain_ffn, w_gate, w_up, w_ffn_out):
    params = tuple((weight.astype(jnp.float32) for weight in (gain_attn, w_query, w_key, w_value, w_out, bias_table, gain_ffn, w_gate, w_up, w_ffn_out)))
    tokens_f = tokens.astype(jnp.float32)
    positions = jnp.arange(SEQ, dtype=jnp.int32)
    valid_rows = (positions[None, :] < lengths[:, None]).astype(jnp.float32)
    offsets = (positions[None, :] - positions[:, None] + (SEQ - 1)).astype(jnp.int32)
    buckets = bucket_table[offsets]
    group_size = math.gcd(SEQS, max(1, 4096 // SEQ))
    group_count = SEQS // group_size
    checked_block = jax.checkpoint(layer_block)

    def forward(params, tokens_f):
        outputs = []
        for group in range(group_count):
            first = group * group_size
            members = tokens_f[first:first + group_size]
            member_valid = valid_rows[first:first + group_size]
            outputs.append(checked_block(params, members, member_valid, buckets))
        return jnp.concatenate(outputs, axis=0)
    result, pullback = jax.vjp(forward, params, tokens_f)
    grad_params, grad_tokens = pullback(cotangent.astype(jnp.float32))
    return (result.astype(jnp.bfloat16), grad_tokens, grad_params[0], grad_params[1], grad_params[2], grad_params[3], grad_params[4], grad_params[5], grad_params[6], grad_params[7], grad_params[8], grad_params[9])
```

```python
import functools
import math

import jax
import jax.numpy as jnp
from jax import lax
from jax.experimental import pallas as pl
from jax.experimental.pallas import tpu as pltpu
from jax.sharding import PartitionSpec as P

HEADS = 12
HEAD_DIM = 64
BUCKETS = 32
BLOCK = 256
VMEM_BYTES = 56 * 1024 * 1024
TILE = 256

norm_eps = 1e-06
F32 = jnp.float32
LOW = jnp.bfloat16
NT = (((1,), (1,)), ((), ()))
NN = (((1,), (0,)), ((), ()))
TN = (((0,), (0,)), ((), ()))


def dot(left, right, dims=NN):
    return lax.dot_general(left, right, dims, preferred_element_type=F32)


def block_rows(index, rows=BLOCK):
    return pl.ds(pl.multiple_of(index * rows, rows), rows)


def build_bias(offsets_ref, bias_ref):
    heads, _, width = bias_ref.shape
    span = offsets_ref.shape[1]
    for head in range(heads):
        line = jnp.broadcast_to(offsets_ref[head : head + 1, :], (8, span))
        for group in range(BLOCK // 8):
            turned = pltpu.roll(
                line, (group * 8 - (BLOCK - 1)) % span, 1, stride=1, stride_axis=0
            )
            bias_ref[head, group * 8 : group * 8 + 8, :] = turned[:, :width]


def fold_diagonals(bias_grad_ref, offsets_grad_ref):
    heads, _, width = bias_grad_ref.shape
    span = offsets_grad_ref.shape[1]
    for head in range(heads):
        total = jnp.zeros((8, span), F32)
        for group in range(BLOCK // 8):
            rows = bias_grad_ref[head, group * 8 : group * 8 + 8, :]
            wide = jnp.concatenate([rows, jnp.zeros((8, span - width), F32)], axis=1)
            total = total + pltpu.roll(wide, (BLOCK - 8 - group * 8) % span, 1)
        line = jnp.zeros((1, span), F32)
        for row in range(8):
            line = line + pltpu.roll(total, (7 - row) % span, 1)[row : row + 1, :]
        offsets_grad_ref[head : head + 1, :] = line


def rms_rows(rows_f):
    return lax.rsqrt(jnp.mean(rows_f * rows_f, axis=-1, keepdims=True) + norm_eps)


def attn_forward_kernel(
    lens_ref, tok_ref, gain_ref, w_ref, off_ref,
    o_ref, of_ref, lse_ref, q_ref, k_ref, v_ref,
    bias_ref, vm_ref,
):
    slot = pl.program_id(0)
    blocks = tok_ref.shape[1] // BLOCK
    per_chip, width = w_ref.shape[2] // HEAD_DIM, w_ref.shape[2]
    length = lens_ref[slot]
    used = (length + BLOCK - 1) // BLOCK

    @pl.when(slot == 0)
    def _():
        build_bias(off_ref, bias_ref)

    owner = lax.broadcasted_iota(jnp.int32, (BLOCK, width), 1) // HEAD_DIM
    column = lax.broadcasted_iota(jnp.int32, (BLOCK, BLOCK), 1)
    nothing = jnp.zeros((BLOCK, width), LOW)
    parts = BLOCK // o_ref.shape[2]

    def project(index, carry):
        rows = block_rows(index)
        rows_f = tok_ref[0, rows, :].astype(F32)
        normed = (rows_f * rms_rows(rows_f) * gain_ref[...]).astype(LOW)
        q_ref[0, rows, :] = dot(normed, w_ref[0]).astype(LOW)
        k_ref[0, rows, :] = dot(normed, w_ref[1]).astype(LOW)
        val = dot(normed, w_ref[2]).astype(LOW)
        v_ref[0, rows, :] = val
        for head in range(per_chip):
            vm_ref[head, rows, :] = jnp.where(owner == head, val, nothing)
        return carry

    lax.fori_loop(0, used, project, 0)

    def attend(index, carry):
        rows = block_rows(index)
        query = q_ref[0, rows, :]
        start = pl.multiple_of((blocks - 1 - index) * BLOCK, BLOCK)
        for count in range(1, blocks + 1):

            @pl.when(used == count)
            def _(count=count):
                wide = count * BLOCK
                total = jnp.zeros((BLOCK, width), F32)
                for head in range(per_chip):
                    mine = jnp.where(owner == head, query, nothing)
                    scores = dot(mine, k_ref[0, :wide, :], NT)
                    scores = scores + bias_ref[head, :, pl.ds(start, wide)]
                    tail = jnp.where(
                        column < length - (count - 1) * BLOCK, scores[:, wide - BLOCK :], -1e30
                    )
                    if count > 1:
                        scores = jnp.concatenate([scores[:, : wide - BLOCK], tail], axis=1)
                    else:
                        scores = tail
                    top = jnp.max(scores, axis=-1, keepdims=True)
                    weights = jnp.exp(scores - top)
                    row_total = jnp.sum(weights, axis=-1, keepdims=True)
                    probs = (weights * (1.0 / row_total)).astype(LOW)
                    total = total + dot(probs, vm_ref[head, :wide, :])
                    lse_ref[0, head, rows, :] = jnp.broadcast_to(
                        top + jnp.log(row_total), (BLOCK, 128)
                    )
                of_ref[0, rows, :] = total
                o_ref[pl.ds(index * parts, parts), 0] = total.astype(LOW).reshape(
                    parts, BLOCK // parts, width
                )

        return carry

    lax.fori_loop(0, used, attend, 0)

    def clear(index, carry):
        o_ref[pl.ds(index * parts, parts), 0] = jnp.zeros((parts, BLOCK // parts, width), LOW)
        return carry

    lax.fori_loop(used, blocks, clear, 0)


def attn_forward(lens, tokens, gain, w_qkv, offsets, pieces):
    slots, seq, model = tokens.shape
    width = w_qkv.shape[2]
    per_chip = width // HEAD_DIM
    rows = seq // pieces
    lane_rows = pl.BlockSpec((1, seq, width), lambda s: (s, 0, 0))
    return pl.pallas_call(
        attn_forward_kernel,
        grid=(slots,),
        in_specs=[
            pl.BlockSpec(memory_space=pltpu.SMEM),
            pl.BlockSpec((1, seq, model), lambda s: (s, 0, 0)),
            pl.BlockSpec((1, model), lambda s: (0, 0)),
            pl.BlockSpec((3, model, width), lambda s: (0, 0, 0)),
            pl.BlockSpec(offsets.shape, lambda s: (0, 0)),
        ],
        out_specs=[
            pl.BlockSpec((pieces, 1, rows, width), lambda s: (0, s, 0, 0)),
            lane_rows,
            pl.BlockSpec((1, per_chip, seq, 128), lambda s: (s, 0, 0, 0)),
            lane_rows,
            lane_rows,
            lane_rows,
        ],
        out_shape=[
            jax.ShapeDtypeStruct((pieces, slots, rows, width), LOW),
            jax.ShapeDtypeStruct((slots, seq, width), F32),
            jax.ShapeDtypeStruct((slots, per_chip, seq, 128), F32),
            jax.ShapeDtypeStruct((slots, seq, width), LOW),
            jax.ShapeDtypeStruct((slots, seq, width), LOW),
            jax.ShapeDtypeStruct((slots, seq, width), LOW),
        ],
        scratch_shapes=[
            pltpu.VMEM((per_chip, BLOCK, 2 * seq - BLOCK), F32),
            pltpu.VMEM((per_chip, seq, width), LOW),
        ],
        compiler_params=pltpu.CompilerParams(vmem_limit_bytes=VMEM_BYTES),
        cost_estimate=pl.CostEstimate(
            flops=2 * slots * seq * (model * 3 * width + 2 * seq * 256 * per_chip),
            bytes_accessed=slots * seq * 2 * (model + 8 * width),
            transcendentals=slots * seq * seq * per_chip,
        ),
        name="attn_forward",
    )(lens, tokens, gain, w_qkv, offsets)


def attn_backward_kernel(
    lens_ref, tok_ref, gain_ref, w_ref, off_ref, q_ref, k_ref, v_ref, of_ref, lse_ref, do_ref,
    dn_ref, dw_ref, dgain_ref, doff_ref,
    bias_ref, dbias_ref, km_ref, dq_ref, dqt_ref, dkt_ref, dvt_ref,
):
    slot = pl.program_id(0)
    blocks = tok_ref.shape[1] // BLOCK
    per_chip, width = w_ref.shape[2] // HEAD_DIM, w_ref.shape[2]
    length = lens_ref[slot]
    used = (length + BLOCK - 1) // BLOCK
    parts = BLOCK // do_ref.shape[2]

    @pl.when(slot == 0)
    def _():
        build_bias(off_ref, bias_ref)
        dbias_ref[...] = jnp.zeros_like(dbias_ref)
        dw_ref[...] = jnp.zeros_like(dw_ref)
        dgain_ref[...] = jnp.zeros_like(dgain_ref)

    dkt_ref[...] = jnp.zeros_like(dkt_ref)
    dvt_ref[...] = jnp.zeros_like(dvt_ref)
    owner = lax.broadcasted_iota(jnp.int32, (BLOCK, width), 1) // HEAD_DIM
    column = lax.broadcasted_iota(jnp.int32, (BLOCK, BLOCK), 1)
    nothing = jnp.zeros((BLOCK, width), LOW)

    def split_keys(index, carry):
        rows = block_rows(index)
        key = k_ref[0, rows, :]
        for head in range(per_chip):
            km_ref[head, rows, :] = jnp.where(owner == head, key, nothing)
        return carry

    lax.fori_loop(0, used, split_keys, 0)

    def attend(index, carry):
        rows = block_rows(index)
        query = q_ref[0, rows, :]
        grad = do_ref[pl.ds(index * parts, parts), 0].reshape(BLOCK, width)
        query_t = jnp.transpose(query)
        grad_t = jnp.transpose(grad)
        product = grad.astype(F32) * of_ref[0, rows, :]
        start = pl.multiple_of((blocks - 1 - index) * BLOCK, BLOCK)
        for count in range(1, blocks + 1):

            @pl.when(used == count)
            def _(count=count):
                wide = count * BLOCK
                grad_query = jnp.zeros((BLOCK, width), F32)
                for head in range(per_chip):
                    lanes = slice(head * HEAD_DIM, (head + 1) * HEAD_DIM)
                    mine = jnp.where(owner == head, query, nothing)
                    scores = dot(mine, k_ref[0, :wide, :], NT)
                    scores = scores + bias_ref[head, :, pl.ds(start, wide)]
                    tail = jnp.where(
                        column < length - (count - 1) * BLOCK, scores[:, wide - BLOCK :], -1e30
                    )
                    if count > 1:
                        scores = jnp.concatenate([scores[:, : wide - BLOCK], tail], axis=1)
                    else:
                        scores = tail
                    probs = jnp.exp(scores - lse_ref[0, head, rows, :][:, :1])
                    delta = jnp.sum(
                        jnp.where(owner == head, product, 0.0), axis=-1, keepdims=True
                    )
                    grad_mine = jnp.where(owner == head, grad, nothing)
                    grad_probs = dot(grad_mine, v_ref[0, :wide, :], NT)
                    grad_scores = (probs * (grad_probs - delta)).astype(LOW)
                    grad_query = grad_query + dot(grad_scores, km_ref[head, :wide, :])
                    dkt_ref[lanes, :wide] += dot(query_t[lanes, :], grad_scores)
                    dvt_ref[lanes, :wide] += dot(grad_t[lanes, :], probs.astype(LOW))
                    dbias_ref[head, :, pl.ds(start, wide)] += grad_scores.astype(F32)
                dq_ref[rows, :] = grad_query.astype(LOW)

        return carry

    lax.fori_loop(0, used, attend, 0)

    def finish(index, carry):
        rows = block_rows(index)
        grad_query = dq_ref[rows, :]
        key_t = dkt_ref[:, rows].astype(LOW)
        value_t = dvt_ref[:, rows].astype(LOW)
        rows_f = tok_ref[0, rows, :].astype(F32)
        unit = rows_f * rms_rows(rows_f)
        normed = (unit * gain_ref[...]).astype(LOW)
        grad_normed = (
            dot(grad_query, w_ref[0], NT)
            + dot(jnp.transpose(key_t), w_ref[1], NT)
            + dot(jnp.transpose(value_t), w_ref[2], NT)
        )
        dgain_ref[...] += jnp.sum(grad_normed * unit, axis=0, keepdims=True)
        dn_ref[index, 0] = grad_normed.astype(LOW)
        dw_ref[0:width, :] += dot(jnp.transpose(grad_query), normed)
        dw_ref[width : 2 * width, :] += dot(key_t, normed)
        dw_ref[2 * width :, :] += dot(value_t, normed)
        return carry

    lax.fori_loop(0, used, finish, 0)

    def clear(index, carry):
        dn_ref[index, 0] = jnp.zeros(dn_ref.shape[2:], LOW)
        return carry

    lax.fori_loop(used, blocks, clear, 0)

    @pl.when(slot == pl.num_programs(0) - 1)
    def _():
        fold_diagonals(dbias_ref, doff_ref)


def attn_backward(lens, tokens, gain, w_qkv, offsets, query, key, value, attn_full, lse, grad):
    slots, seq, model = tokens.shape
    width = w_qkv.shape[2]
    per_chip = width // HEAD_DIM
    pieces, _, rows, _ = grad.shape
    blocks = seq // BLOCK
    lane_rows = pl.BlockSpec((1, seq, width), lambda s: (s, 0, 0))
    return pl.pallas_call(
        attn_backward_kernel,
        grid=(slots,),
        in_specs=[
            pl.BlockSpec(memory_space=pltpu.SMEM),
            pl.BlockSpec((1, seq, model), lambda s: (s, 0, 0)),
            pl.BlockSpec((1, model), lambda s: (0, 0)),
            pl.BlockSpec((3, model, width), lambda s: (0, 0, 0)),
            pl.BlockSpec(offsets.shape, lambda s: (0, 0)),
            lane_rows,
            lane_rows,
            lane_rows,
            lane_rows,
            pl.BlockSpec((1, per_chip, seq, 128), lambda s: (s, 0, 0, 0)),
            pl.BlockSpec((pieces, 1, rows, width), lambda s: (0, s, 0, 0)),
        ],
        out_specs=[
            pl.BlockSpec((blocks, 1, BLOCK, model), lambda s: (0, s, 0, 0)),
            pl.BlockSpec((3 * width, model), lambda s: (0, 0)),
            pl.BlockSpec((1, model), lambda s: (0, 0)),
            pl.BlockSpec(offsets.shape, lambda s: (0, 0)),
        ],
        out_shape=[
            jax.ShapeDtypeStruct((blocks, slots, BLOCK, model), LOW),
            jax.ShapeDtypeStruct((3 * width, model), F32),
            jax.ShapeDtypeStruct((1, model), F32),
            jax.ShapeDtypeStruct(offsets.shape, F32),
        ],
        scratch_shapes=[
            pltpu.VMEM((per_chip, BLOCK, 2 * seq - BLOCK), F32),
            pltpu.VMEM((per_chip, BLOCK, 2 * seq - BLOCK), F32),
            pltpu.VMEM((per_chip, seq, width), LOW),
            pltpu.VMEM((seq, width), LOW),
            pltpu.VMEM((width, BLOCK), LOW),
            pltpu.VMEM((width, seq), F32),
            pltpu.VMEM((width, seq), F32),
        ],
        compiler_params=pltpu.CompilerParams(vmem_limit_bytes=VMEM_BYTES),
        cost_estimate=pl.CostEstimate(
            flops=2 * slots * seq * (model * 6 * width + 5 * seq * 256 * per_chip),
            bytes_accessed=slots * seq * 2 * (2 * model + 12 * width),
            transcendentals=slots * seq * seq * per_chip,
        ),
        name="attn_backward",
    )(lens, tokens, gain, w_qkv, offsets, query, key, value, attn_full, lse, grad)


def out_project_kernel(tok_ref, attn_ref, w_ref, gain_ref, res_ref, nf_ref):
    chips = attn_ref.shape[0] // 2
    width = attn_ref.shape[3]
    rows = tok_ref.shape[0]
    total = tok_ref[...].astype(F32)
    for chip in range(chips):
        part = attn_ref[2 * chip : 2 * chip + 2].reshape(rows, width)
        total = total + dot(part, w_ref[chip * width : (chip + 1) * width, :])
    res_ref[...] = total
    nf_ref[...] = (total * rms_rows(total) * gain_ref[...]).astype(LOW)


def out_project(tokens, attn, w_out, gain):
    rows, model = tokens.shape
    return pl.pallas_call(
        out_project_kernel,
        out_shape=[
            jax.ShapeDtypeStruct((rows, model), F32),
            jax.ShapeDtypeStruct((rows, model), LOW),
        ],
        compiler_params=pltpu.CompilerParams(vmem_limit_bytes=VMEM_BYTES),
        cost_estimate=pl.CostEstimate(
            flops=2 * rows * model * model, bytes_accessed=rows * model * 10, transcendentals=0
        ),
        name="out_project",
    )(tokens, attn, w_out, gain)


def gate_and_slope(gate):
    inner = 0.7978845608028654 * (gate + 0.044715 * gate * gate * gate)
    bent = jnp.tanh(inner)
    half = 0.5 * (1.0 + bent)
    slope = half + 0.5 * gate * (1.0 - bent * bent) * (
        0.7978845608028654 * (1.0 + 3.0 * 0.044715 * gate * gate)
    )
    return gate * half, slope


def ffn_first_kernel(
    nf_own_ref, nf_other_ref, dy_own_ref, dy_other_ref, gate_ref, up_ref, down_ref,
    hidden_ref, dgate_ref, dup_ref, own_ref, other_ref,
    nf_ref, dy_ref, total_ref,
):
    step = pl.program_id(0)
    half = nf_own_ref.shape[0]

    @pl.when(step == 0)
    def _():
        nf_ref[:half, :] = nf_own_ref[...]
        nf_ref[half:, :] = nf_other_ref[...]
        dy_ref[:half, :] = dy_own_ref[...]
        dy_ref[half:, :] = dy_other_ref[...]
        total_ref[...] = jnp.zeros_like(total_ref)

    for part in range(4):
        rows = slice(part * half // 2, (part + 1) * half // 2)
        nf = nf_ref[rows, :]
        gate = dot(nf, gate_ref[...])
        up = dot(nf, up_ref[...])
        dhidden = dot(dy_ref[rows, :], down_ref[...], NT)
        bent, slope = gate_and_slope(gate)
        hidden_ref[rows, :] = (bent * up).astype(LOW)
        dgate = (dhidden * up * slope).astype(LOW)
        dup = (dhidden * bent).astype(LOW)
        dgate_ref[rows, :] = dgate
        dup_ref[rows, :] = dup
        total_ref[rows, :] += dot(dgate, gate_ref[...], NT) + dot(dup, up_ref[...], NT)

    @pl.when(step == pl.num_programs(0) - 1)
    def _():
        own_ref[...] = total_ref[:half, :]
        other_ref[...] = total_ref[half:, :].astype(LOW)


def ffn_first(nf_own, nf_other, dy_own, dy_other, w_gate, w_up, w_down, tile):
    half, model = nf_own.shape
    units = w_down.shape[0]
    per = model // tile
    whole = pl.BlockSpec((half, model), lambda t: (0, 0))
    lane_tile = pl.BlockSpec((2 * half, tile), lambda t: (0, t))
    return pl.pallas_call(
        ffn_first_kernel,
        grid=(units // tile,),
        in_specs=[
            whole,
            whole,
            whole,
            whole,
            pl.BlockSpec((None, model, tile), lambda t: (t // per, 0, t % per)),
            pl.BlockSpec((None, model, tile), lambda t: (t // per, 0, t % per)),
            pl.BlockSpec((tile, model), lambda t: (t, 0)),
        ],
        out_specs=[lane_tile, lane_tile, lane_tile, whole, whole],
        out_shape=[
            jax.ShapeDtypeStruct((2 * half, units), LOW),
            jax.ShapeDtypeStruct((2 * half, units), LOW),
            jax.ShapeDtypeStruct((2 * half, units), LOW),
            jax.ShapeDtypeStruct((half, model), F32),
            jax.ShapeDtypeStruct((half, model), LOW),
        ],
        scratch_shapes=[
            pltpu.VMEM((2 * half, model), LOW),
            pltpu.VMEM((2 * half, model), LOW),
            pltpu.VMEM((2 * half, model), F32),
        ],
        compiler_params=pltpu.CompilerParams(vmem_limit_bytes=VMEM_BYTES),
        cost_estimate=pl.CostEstimate(
            flops=2 * 5 * 2 * half * model * units,
            bytes_accessed=6 * model * units + 12 * half * units + 20 * half * model,
            transcendentals=2 * half * units,
        ),
        name="ffn_first",
    )(nf_own, nf_other, dy_own, dy_other, w_gate, w_up, w_down)


def out_back_kernel(
    own_ref, recv_ref, res_ref, dy_ref, gain_ref, w_ref, dattn_ref, dres_ref, branch_ref, dgain_ref
):
    chips = dattn_ref.shape[0] // 2
    width = dattn_ref.shape[3]
    grad = own_ref[...] + recv_ref[...].astype(F32)
    residual = res_ref[...]
    scale = rms_rows(residual)
    unit = residual * scale
    dgain_ref[...] = jnp.sum(grad * unit, axis=0, keepdims=True)
    inner = grad * gain_ref[...]
    dres = dy_ref[...].astype(F32) + scale * (
        inner - unit * jnp.mean(inner * unit, axis=-1, keepdims=True)
    )
    dres_ref[...] = dres
    branch = dres.astype(LOW)
    branch_ref[...] = branch
    for chip in range(chips):
        part = dot(branch, w_ref[chip * width : (chip + 1) * width, :], NT).astype(LOW)
        dattn_ref[2 * chip : 2 * chip + 2] = part.reshape(2, *dattn_ref.shape[1:])


def out_back(own, recv, residual, dy, gain, w_out, attn_shape):
    rows, model = own.shape
    return pl.pallas_call(
        out_back_kernel,
        out_shape=[
            jax.ShapeDtypeStruct(attn_shape, LOW),
            jax.ShapeDtypeStruct((rows, model), F32),
            jax.ShapeDtypeStruct((rows, model), LOW),
            jax.ShapeDtypeStruct((1, model), F32),
        ],
        compiler_params=pltpu.CompilerParams(vmem_limit_bytes=VMEM_BYTES),
        cost_estimate=pl.CostEstimate(
            flops=2 * rows * model * model, bytes_accessed=rows * model * 20, transcendentals=0
        ),
        name="out_back",
    )(own, recv, residual, dy, gain, w_out)


def ffn_second_kernel(
    nf_own_ref, nf_other_ref, dy_own_ref, dy_other_ref, hidden_ref, dgate_ref, dup_ref, down_ref,
    attn_ref, branch_ref,
    own_ref, other_ref, gdown_ref, ggate_ref, gup_ref, gout_ref,
    nft_ref, dy_ref, total_ref,
):
    step = pl.program_id(0)
    half = nf_own_ref.shape[0]

    @pl.when(step == 0)
    def _():
        nft_ref[:, :half] = jnp.transpose(nf_own_ref[...])
        nft_ref[:, half:] = jnp.transpose(nf_other_ref[...])
        dy_ref[:half, :] = dy_own_ref[...]
        dy_ref[half:, :] = dy_other_ref[...]
        total_ref[...] = jnp.zeros_like(total_ref)
        chips, width = attn_ref.shape[0] // 2, attn_ref.shape[3]
        for chip in range(chips):
            part = attn_ref[2 * chip : 2 * chip + 2].reshape(half, width)
            gout_ref[chip * width : (chip + 1) * width, :] = dot(
                jnp.transpose(part), branch_ref[...]
            ).astype(LOW)

    hidden = hidden_ref[...]
    ggate_ref[...] = dot(nft_ref[...], dgate_ref[...]).astype(LOW)
    gup_ref[...] = dot(nft_ref[...], dup_ref[...]).astype(LOW)
    gdown_ref[...] = dot(jnp.transpose(hidden), dy_ref[...]).astype(LOW)
    total_ref[...] += dot(hidden, down_ref[...])

    @pl.when(step == pl.num_programs(0) - 1)
    def _():
        own_ref[...] = total_ref[:half, :]
        other_ref[...] = total_ref[half:, :].astype(LOW)


def ffn_second(nf_own, nf_other, dy_own, dy_other, hidden, dgate, dup, w_down, attn, branch, tile):
    half, model = nf_own.shape
    units = hidden.shape[1]
    whole = pl.BlockSpec((half, model), lambda t: (0, 0))
    lane_tile = pl.BlockSpec((2 * half, tile), lambda t: (0, t))
    row_tile = pl.BlockSpec((tile, model), lambda t: (t, 0))
    per = model // tile
    out_tile = pl.BlockSpec((None, model, tile), lambda t: (t // per, 0, t % per))
    return pl.pallas_call(
        ffn_second_kernel,
        grid=(units // tile,),
        in_specs=[
            whole, whole, whole, whole, lane_tile, lane_tile, lane_tile, row_tile,
            pl.BlockSpec(attn.shape, lambda t: (0, 0, 0, 0)),
            whole,
        ],
        out_specs=[
            whole, whole, row_tile, out_tile, out_tile,
            pl.BlockSpec((model, model), lambda t: (0, 0)),
        ],
        out_shape=[
            jax.ShapeDtypeStruct((half, model), F32),
            jax.ShapeDtypeStruct((half, model), LOW),
            jax.ShapeDtypeStruct((units, model), LOW),
            jax.ShapeDtypeStruct((units // model, model, model), LOW),
            jax.ShapeDtypeStruct((units // model, model, model), LOW),
            jax.ShapeDtypeStruct((model, model), LOW),
        ],
        scratch_shapes=[
            pltpu.VMEM((model, 2 * half), LOW),
            pltpu.VMEM((2 * half, model), LOW),
            pltpu.VMEM((2 * half, model), F32),
        ],
        compiler_params=pltpu.CompilerParams(vmem_limit_bytes=VMEM_BYTES),
        cost_estimate=pl.CostEstimate(
            flops=2 * 4 * 2 * half * model * units,
            bytes_accessed=8 * model * units + 12 * half * units + 20 * half * model,
            transcendentals=0,
        ),
        name="ffn_second",
    )(nf_own, nf_other, dy_own, dy_other, hidden, dgate, dup, w_down, attn, branch)


CORE, X, Y = 1, 2, 4


def swap(values, bit):
    count = lax.axis_size("ctx")
    return lax.ppermute(values, "ctx", [(i, i ^ bit) for i in range(count)])


def ring_step(values):
    count = lax.axis_size("fsdp")
    return lax.ppermute(values, "fsdp", [(i, (i + 1) % count) for i in range(count)])


def bit_of(bit):
    return (lax.axis_index("ctx") // bit) % 2


def pick(values, index, axis):
    return lax.dynamic_index_in_dim(values, index, axis, keepdims=False)


def put_in_order(mine, other, bit, axis=0):
    first = bit_of(bit) == 0
    return jnp.stack([jnp.where(first, mine, other), jnp.where(first, other, mine)], axis)


def halve_sum(values, bit, axis):
    side = bit_of(bit)
    kept = pick(values, side, axis)
    came = swap(pick(values, 1 - side, axis), bit)
    return (kept.astype(F32) + came.astype(F32)).astype(LOW)


def ring_sum(values, axis):
    count = lax.axis_size("fsdp")
    me = lax.axis_index("fsdp")
    running = pick(values, (me + count - 1) % count, axis)
    for step in range(count - 1):
        came = ring_step(running)
        mine = pick(values, (me + 2 * count - 2 - step) % count, axis)
        running = (came.astype(F32) + mine.astype(F32)).astype(LOW)
    return running


def ring_pieces(piece):
    count = lax.axis_size("fsdp")
    me = lax.axis_index("fsdp")
    found = []
    for step in range(count - 1):
        piece = ring_step(piece)
        found.append(((me + 2 * count - 1 - step) % count, piece))
    return found


def place(whole, piece, owner):
    return lax.dynamic_update_slice_in_dim(whole, piece[None], owner, 0)


def per_device_plane(
    tokens, cotangent, lengths, bucket_table, gain_attn, w_query, w_key, w_value, w_out,
    bias_table, gain_ffn, w_gate, w_up, w_ffn_out,
):
    batch, rows, model = tokens.shape
    planes = lax.axis_size("fsdp")
    chips = lax.axis_size("ctx") // 2
    seq = rows * chips * 2
    me = lax.axis_index("ctx")
    plane = lax.axis_index("fsdp")
    core, chip = me % 2, me // 2
    depth = model // planes
    units = w_gate.shape[1]
    chip_heads = HEADS // chips
    width = chip_heads * HEAD_DIM
    half_rows = batch * rows

    order = jnp.argsort(-lengths)
    order = jnp.stack([order[0], order[3], order[1], order[2]])
    lens = lengths[order]
    local = jnp.concatenate([pick(tokens, order[i], 0)[None] for i in range(batch)])
    grads_in = jnp.concatenate([pick(cotangent, order[i], 0)[None] for i in range(batch)])
    positions = me * rows + jnp.arange(rows, dtype=jnp.int32)
    valid = positions[None, :] < lens[:, None]
    dy = jnp.where(valid[..., None], grads_in, jnp.zeros_like(grads_in)).reshape(half_rows, model)
    flat = local.reshape(half_rows, model)
    lens_mine = lax.dynamic_slice_in_dim(lens, 2 * core, 2)

    by_core = local.reshape(2, 2, rows, model)
    came = swap(pick(by_core, 1 - core, 0), CORE)
    block = put_in_order(pick(by_core, core, 0), came, CORE, 1).reshape(2, 2 * rows, model)
    from_x = swap(block, X)
    from_y = swap(block, Y)
    from_xy = jnp.stack([swap(from_x[0], Y), swap(from_y[1], X)])
    by_distance = jnp.stack([block, from_x, from_y, from_xy])
    gathered = jnp.concatenate(
        [pick(by_distance, chip ^ i, 0) for i in range(chips)], axis=1
    )

    small = jnp.concatenate([gain_attn, gain_ffn, bias_table.reshape(-1)])[None]
    all_small = jnp.zeros((planes, 1, small.shape[1]), LOW)
    all_small = place(all_small, small, plane)
    for owner, piece in ring_pieces(small):
        all_small = place(all_small, piece, owner)
    all_small = all_small[:, 0]
    full_gain_attn = all_small[:, :depth].reshape(1, model).astype(F32)
    full_gain_ffn = all_small[:, depth : 2 * depth].reshape(1, model).astype(F32)
    full_table = all_small[:, 2 * depth :].reshape(BUCKETS, HEADS)

    qkv_piece = jnp.stack(
        [
            lax.dynamic_slice_in_dim(w, chip * width, width, 1)
            for w in (w_query, w_key, w_value)
        ]
    )
    w_qkv = jnp.zeros((planes, 3, depth, width), LOW)
    w_qkv = place(w_qkv, qkv_piece, plane)
    for owner, piece in ring_pieces(qkv_piece):
        w_qkv = place(w_qkv, piece, owner)
    w_qkv = jnp.transpose(w_qkv, (1, 0, 2, 3)).reshape(3, model, width)

    out_halves = w_out.reshape(2, depth // 2, model)
    half_out = jnp.zeros((planes, depth // 2, model), LOW)
    mine = pick(out_halves, core, 0)
    half_out = place(half_out, mine, plane)
    for owner, piece in ring_pieces(mine):
        half_out = place(half_out, piece, owner)
    full_out = put_in_order(half_out, swap(half_out, CORE), CORE, 1).reshape(model, model)

    part = units // planes // 2
    wide = units // 2 // model

    def my_columns(w):
        mine = pick(w.reshape(depth, planes, 2, part), core, 2).reshape(depth, wide, model)
        return jnp.transpose(mine, (1, 0, 2))

    gate_mine, up_mine = my_columns(w_gate), my_columns(w_up)
    down_mine = pick(w_ffn_out.reshape(2, part, model), core, 0)
    down_two = down_mine.reshape(2, part // 2, model)
    slab = depth // 2
    x_piece = jnp.concatenate(
        [
            pick(gate_mine.reshape(wide, 2, slab, model), bit_of(X), 1).reshape(-1, model),
            pick(down_two[0].reshape(2, part // 4, model), bit_of(X), 0),
        ]
    )
    y_piece = jnp.concatenate(
        [
            pick(up_mine.reshape(wide, 2, slab, model), bit_of(Y), 1).reshape(-1, model),
            pick(down_two[1].reshape(2, part // 4, model), bit_of(Y), 0),
        ]
    )
    full_gate = place(jnp.zeros((planes, wide, depth, model), LOW), gate_mine, plane)
    full_up = place(jnp.zeros((planes, wide, depth, model), LOW), up_mine, plane)
    full_down = place(jnp.zeros((planes, 2, part // 2, model), LOW), down_two, plane)
    x_found, y_found = ring_pieces(x_piece), ring_pieces(y_piece)
    for (owner, from_ring), (_, from_ring_y) in zip(x_found, y_found):
        both_x = put_in_order(from_ring, swap(from_ring, X), X)
        both_y = put_in_order(from_ring_y, swap(from_ring_y, Y), Y)
        cut = wide * slab

        def columns(both):
            return jnp.transpose(both[:, :cut].reshape(2, wide, slab, model), (1, 0, 2, 3)).reshape(
                wide, depth, model
            )

        full_gate = place(full_gate, columns(both_x), owner)
        full_up = place(full_up, columns(both_y), owner)
        full_down = place(
            full_down,
            jnp.stack(
                [
                    both_x[:, cut:].reshape(part // 2, model),
                    both_y[:, cut:].reshape(part // 2, model),
                ]
            ),
            owner,
        )
    full_gate = jnp.transpose(full_gate, (1, 0, 2, 3)).reshape(wide, model, model)
    full_up = jnp.transpose(full_up, (1, 0, 2, 3)).reshape(wide, model, model)
    full_down = full_down.reshape(units // 2, model)

    hot = (bucket_table[:, None] == jnp.arange(BUCKETS, dtype=jnp.int32)[None, :])
    hot = jnp.concatenate([hot, jnp.zeros((1, BUCKETS), bool)])
    my_table = lax.dynamic_slice_in_dim(full_table, chip * chip_heads, chip_heads, 1)
    offsets = jnp.einsum("tb,bh->ht", hot.astype(LOW), my_table, preferred_element_type=F32)

    attn_out, attn_full, lse, query, key, value = attn_forward(
        lens_mine, gathered, full_gain_attn, w_qkv, offsets, 2 * chips
    )
    attn = lax.all_to_all(attn_out, "ctx", 0, 0)
    residual, nf_own = out_project(flat, attn, full_out, full_gain_ffn)
    dy_other = swap(dy, CORE)
    nf_other = swap(nf_own, CORE)
    hidden, dgate, dup, dnf_own, dnf_send = ffn_first(
        nf_own, nf_other, dy, dy_other, full_gate, full_up, full_down, TILE
    )
    dattn, dres, branch, dgain_ffn = out_back(
        dnf_own, swap(dnf_send, CORE), residual, dy, full_gain_ffn, full_out, attn.shape
    )
    dattn_all = lax.all_to_all(dattn, "ctx", 0, 0)
    out_own, out_send, gdown, ggate, gup, gout = ffn_second(
        nf_own, nf_other, dy, dy_other, hidden, dgate, dup, full_down, attn, branch, TILE
    )
    out_rows = residual + out_own + swap(out_send, CORE).astype(F32)
    out_rows = jnp.where(valid[..., None], out_rows.reshape(batch, rows, model), 0.0).astype(LOW)

    quarter = depth // 4
    g_sum = ring_sum(ggate.reshape(wide, planes, depth, model), 1)
    g_sum = halve_sum(g_sum.reshape(wide, 2, 2, quarter, model), X, 1)
    g_sum = halve_sum(g_sum, Y, 1)
    u_sum = halve_sum(gup.reshape(wide, planes, 2, 2, quarter, model), X, 2)
    u_sum = ring_sum(halve_sum(u_sum, Y, 2), 1)
    f_sum = halve_sum(gdown.reshape(planes, 2, 2, part // 4, model), Y, 1)
    f_sum = ring_sum(halve_sum(f_sum, X, 1), 0)
    o_sum = halve_sum(gout.reshape(planes, 2, 2, 2, depth // 8, model), CORE, 1)
    o_sum = ring_sum(halve_sum(halve_sum(o_sum, X, 1), Y, 1), 0)

    dn_all, dw_qkv, dgain_attn, doffsets = attn_backward(
        lens_mine, gathered, full_gain_attn, w_qkv, offsets,
        query, key, value, attn_full, lse, dattn_all,
    )

    dn = dn_all.reshape(2, 2, 2, 2 * rows, model)
    dn_x = halve_sum(halve_sum(dn[:, :, 0], X, 1), Y, 0)
    dn_y = halve_sum(halve_sum(dn[:, :, 1], Y, 0), X, 0)
    dn = jnp.stack([dn_x, dn_y]).reshape(2, 2, rows, model)
    dn_came = swap(pick(dn, 1 - core, 1), CORE)
    dn_rows = put_in_order(pick(dn, core, 1), dn_came, CORE).reshape(half_rows, model)
    dn_rows = dn_rows.astype(F32)
    rows_f = flat.astype(F32)
    scale = rms_rows(rows_f)
    unit = rows_f * scale
    inner = dn_rows * full_gain_attn
    dtok = dres + scale * (inner - unit * jnp.mean(inner * unit, axis=-1, keepdims=True))
    dtok = dtok.reshape(batch, rows, model)

    dw = jnp.transpose(dw_qkv.astype(LOW)).reshape(planes, 2, depth // 2, 3 * width)
    dw = ring_sum(halve_sum(dw, CORE, 1), 0)
    dw = put_in_order(dw, swap(dw, X), X)
    dw = put_in_order(dw, swap(dw, Y), Y)
    dw = put_in_order(dw, swap(dw, CORE), CORE).reshape(2, chips, depth // 2, 3, width)
    dw = jnp.transpose(dw, (3, 0, 2, 1, 4)).reshape(3, depth, model).astype(F32)

    pack_x = jnp.concatenate([g_sum.reshape(-1, model), u_sum[0].reshape(-1, model)])
    pack_y = jnp.concatenate(
        [u_sum[1:].reshape(-1, model), f_sum.reshape(-1, model), o_sum.reshape(-1, model)]
    )
    pack_x = put_in_order(pack_x, swap(pack_x, X), X)
    pack_x = put_in_order(pack_x, swap(pack_x, Y), Y)
    pack_y = put_in_order(pack_y, swap(pack_y, Y), Y)
    pack_y = put_in_order(pack_y, swap(pack_y, X), X, 1)
    pack = jnp.concatenate([pack_x, pack_y], axis=2)
    gate_rows = wide * quarter
    down_at = 2 * gate_rows
    out_at = down_at + part // 4
    pack = put_in_order(pack, swap(pack, CORE), CORE)

    def columns_of(gathered_rows):
        cut = gathered_rows.reshape(2, 2, 2, wide, quarter, planes // wide, part)
        cut = jnp.transpose(cut, (2, 1, 4, 3, 5, 0, 6))
        return cut.reshape(depth, units).astype(F32)

    grad_gate = columns_of(pack[:, :, :, :gate_rows])
    grad_up = columns_of(pack[:, :, :, gate_rows:down_at])
    grad_down = jnp.transpose(pack[:, :, :, down_at:out_at], (0, 1, 2, 3, 4))
    grad_down = grad_down.reshape(units // planes, model).astype(F32)
    grad_out = jnp.transpose(pack[:, :, :, out_at:], (0, 2, 1, 3, 4))
    grad_out = grad_out.reshape(depth, model).astype(F32)

    mine_buckets = jnp.einsum(
        "ht,tb->bh", doffsets, hot.astype(F32), precision=lax.Precision.HIGHEST
    )
    buckets = lax.dynamic_update_slice_in_dim(
        jnp.zeros((BUCKETS, HEADS), F32), mine_buckets, chip * chip_heads, 1
    )
    sums = jnp.concatenate([dgain_attn[0], dgain_ffn[0], buckets.reshape(-1)])
    sums = lax.psum(sums, ("ctx", "fsdp"))
    grad_gain_attn = lax.dynamic_slice_in_dim(sums, plane * depth, depth)
    grad_gain_ffn = lax.dynamic_slice_in_dim(sums, model + plane * depth, depth)
    grad_buckets = lax.dynamic_slice_in_dim(
        sums[2 * model :].reshape(BUCKETS, HEADS), plane * (BUCKETS // planes), BUCKETS // planes
    )

    back = jnp.argsort(order)
    out_rows = jnp.concatenate([pick(out_rows, back[i], 0)[None] for i in range(batch)])
    dtok = jnp.concatenate([pick(dtok, back[i], 0)[None] for i in range(batch)])
    return (
        out_rows, dtok, grad_gain_attn, dw[0], dw[1], dw[2], grad_out, grad_buckets,
        grad_gain_ffn, grad_gate, grad_up, grad_down,
    )


def gelu_tanh(values):
    return (
        0.5
        * values
        * (1.0 + jnp.tanh(0.7978845608028654 * (values + 0.044715 * values * values * values)))
    )


def normalize(values, gain_vec):
    return (
        values * lax.rsqrt(jnp.mean(values * values, axis=-1, keepdims=True) + norm_eps) * gain_vec
    )


def project(values, matrix):
    return jnp.einsum("msd,de->mse", values, matrix, preferred_element_type=jnp.float32)


def back_project(values, matrix):
    return jnp.einsum("mse,de->msd", values, matrix, preferred_element_type=jnp.float32)


def outer_sum(left_rows, right_rows):
    return jnp.einsum("msd,mse->de", left_rows, right_rows, preferred_element_type=jnp.float32)


def split_heads(values):
    return values.reshape(values.shape[0], values.shape[1], HEADS, HEAD_DIM)


def toeplitz_bias(offset_bias, start, query_rows, key_rows):
    span = query_rows + key_rows - 1
    window = lax.dynamic_slice_in_dim(offset_bias, start, span, 1)
    wrapped = jnp.concatenate(
        [
            window[:, query_rows - 1 :],
            jnp.zeros((window.shape[0], 1), jnp.float32),
            window[:, : query_rows - 1],
        ],
        axis=1,
    )
    tiled = jnp.tile(wrapped, (1, query_rows))
    shaped = tiled[:, : query_rows * span].reshape(window.shape[0], query_rows, span)
    return shaped[:, :, :key_rows]


def diagonal_sums(grad_bias, query_rows, key_rows):
    span = query_rows + key_rows - 1
    heads = grad_bias.shape[0]
    padded = jnp.pad(grad_bias, ((0, 0), (0, 0), (0, span - key_rows)))
    flat = jnp.pad(padded.reshape(heads, query_rows * span), ((0, 0), (0, query_rows)))
    slots = jnp.sum(flat.reshape(heads, query_rows, span + 1), axis=1)
    return jnp.concatenate([slots[:, key_rows + 1 :], slots[:, :key_rows]], axis=1)


def block_scores(query_heads, key_heads, pair_bias, key_ok):
    scores = jnp.einsum(
        "mihe,mjhe->mhij", query_heads, key_heads, preferred_element_type=jnp.float32
    )
    scores = scores + pair_bias[None]
    return jnp.where(key_ok[:, None, None, :], scores, -1e30)


def over_blocks(update, make_bias, carried, pieces):
    piece_rows = pieces[0].shape[1]
    block_rows = math.gcd(piece_rows, 256)
    block_count = piece_rows // block_rows

    def advance(block_index, running):
        block_start = block_index * block_rows
        sub_pieces = tuple(
            (
                lax.dynamic_slice_in_dim(member, block_index * block_rows, block_rows, 1)
                for member in pieces
            )
        )
        bias_info = make_bias(block_start, block_rows)
        return update(running, sub_pieces, block_start, slice(None), bias_info)

    return lax.fori_loop(0, block_count, advance, carried)


def per_device_general(
    tokens,
    cotangent,
    lengths,
    bucket_table,
    gain_attn,
    w_query,
    w_key,
    w_value,
    w_out,
    bias_table,
    gain_ffn,
    w_gate,
    w_up,
    w_ffn_out,
):
    shards = (
        gain_attn,
        w_query,
        w_key,
        w_value,
        w_out,
        bias_table,
        gain_ffn,
        w_gate,
        w_up,
        w_ffn_out,
    )
    gathered = (
        lax.all_gather(shards[0], "fsdp", axis=0, tiled=True),
        lax.all_gather(shards[1], "fsdp", axis=0, tiled=True),
        lax.all_gather(shards[2], "fsdp", axis=0, tiled=True),
        lax.all_gather(shards[3], "fsdp", axis=0, tiled=True),
        lax.all_gather(shards[4], "fsdp", axis=0, tiled=True),
        lax.all_gather(shards[5], "fsdp", axis=0, tiled=True),
        lax.all_gather(shards[6], "fsdp", axis=0, tiled=True),
        lax.all_gather(shards[7], "fsdp", axis=0, tiled=True),
        lax.all_gather(shards[8], "fsdp", axis=0, tiled=True),
        lax.all_gather(shards[9], "fsdp", axis=0, tiled=True),
    )
    (
        full_gain_attn,
        full_query,
        full_key,
        full_value,
        full_out,
        full_bias,
        full_gain_ffn,
        full_gate,
        full_up,
        full_ffn_out,
    ) = gathered
    batch_rows, local_rows, model_width = tokens.shape
    seq_len = local_rows * lax.axis_size("ctx")
    table_len = bucket_table.shape[0]
    first_pos = lax.axis_index("ctx") * local_rows
    positions = first_pos + jnp.arange(local_rows, dtype=jnp.int32)
    valid_mask = positions[None, :] < lengths[:, None]
    valid_rows = valid_mask.astype(jnp.float32)
    bucket_hot = bucket_table[:, None] == jnp.arange(BUCKETS, dtype=jnp.int32)[None, :]

    def offset_bias_of(bias_weights):
        return jnp.einsum(
            "tb,bh->ht",
            bucket_hot.astype(jnp.bfloat16),
            bias_weights,
            preferred_element_type=jnp.float32,
        )

    forward_offsets = offset_bias_of(full_bias)

    def keys_bias(offset_bias):

        def keys_make(block_start, block_rows):
            start = block_start - first_pos - (local_rows - 1) + (seq_len - 1)
            return (toeplitz_bias(offset_bias, start, local_rows, block_rows), start)

        return keys_make

    def queries_bias(offset_bias):

        def queries_make(block_start, block_rows):
            start = first_pos - block_start - (block_rows - 1) + (seq_len - 1)
            return (toeplitz_bias(offset_bias, start, block_rows, local_rows), start)

        return queries_make

    tokens_f = tokens.astype(jnp.float32)
    attn_gain = full_gain_attn.astype(jnp.float32)
    normed = normalize(tokens_f, attn_gain).astype(jnp.bfloat16)
    queries = project(normed, full_query).astype(jnp.bfloat16)
    keys_local = project(normed, full_key).astype(jnp.bfloat16)
    values_local = project(normed, full_value).astype(jnp.bfloat16)
    query_heads = split_heads(queries)

    def forward_block(running, sub_pieces, block_start, member_pick, bias_info):
        max_score, row_total, weighted = running
        key_part, value_part = sub_pieces
        key_pos = block_start + jnp.arange(key_part.shape[1], dtype=jnp.int32)
        key_ok = key_pos[None, :] < lengths[:, None]
        scores = block_scores(query_heads, split_heads(key_part), bias_info[0], key_ok)
        new_max = jnp.maximum(max_score, jnp.max(scores, axis=-1))
        shrink = jnp.exp(max_score - new_max)
        weights = jnp.exp(scores - new_max[..., None])
        row_total = row_total * shrink + jnp.sum(weights, axis=-1)
        weighted = weighted * jnp.transpose(shrink, (0, 2, 1))[..., None] + jnp.einsum(
            "mhij,mjhe->mihe",
            weights.astype(jnp.bfloat16),
            split_heads(value_part),
            preferred_element_type=jnp.float32,
        )
        return (new_max, row_total, weighted)

    start_state = (
        jnp.full((batch_rows, HEADS, local_rows), -1e30, jnp.float32),
        jnp.zeros((batch_rows, HEADS, local_rows), jnp.float32),
        jnp.zeros((batch_rows, local_rows, HEADS, HEAD_DIM), jnp.float32),
    )
    max_score, row_total, weighted = over_blocks(
        forward_block,
        keys_bias(forward_offsets),
        start_state,
        (
            lax.all_gather(keys_local, "ctx", axis=1, tiled=True),
            lax.all_gather(values_local, "ctx", axis=1, tiled=True),
        ),
    )
    log_total = max_score + jnp.log(row_total)
    attn_full = weighted / jnp.transpose(row_total, (0, 2, 1))[..., None]
    attn_low = attn_full.reshape(batch_rows, local_rows, model_width).astype(jnp.bfloat16)
    residual = tokens_f + project(attn_low, full_out)
    ffn_gain = full_gain_ffn.astype(jnp.float32)
    normed_ffn = normalize(residual, ffn_gain).astype(jnp.bfloat16)
    gate_proj = project(normed_ffn, full_gate)
    up_proj = project(normed_ffn, full_up)
    hidden = (gelu_tanh(gate_proj) * up_proj).astype(jnp.bfloat16)
    result = valid_rows[..., None] * (residual + project(hidden, full_ffn_out))
    output = result.astype(jnp.bfloat16)
    back_weights = (
        lax.all_gather(shards[0], "fsdp", axis=0, tiled=True),
        lax.all_gather(shards[1], "fsdp", axis=0, tiled=True),
        lax.all_gather(shards[2], "fsdp", axis=0, tiled=True),
        lax.all_gather(shards[3], "fsdp", axis=0, tiled=True),
        lax.all_gather(shards[4], "fsdp", axis=0, tiled=True),
        lax.all_gather(shards[5], "fsdp", axis=0, tiled=True),
        lax.all_gather(shards[6], "fsdp", axis=0, tiled=True),
        lax.all_gather(shards[7], "fsdp", axis=0, tiled=True),
        lax.all_gather(shards[8], "fsdp", axis=0, tiled=True),
        lax.all_gather(shards[9], "fsdp", axis=0, tiled=True),
    )
    (
        back_gain_attn,
        back_query,
        back_key,
        back_value,
        back_out,
        back_bias,
        back_gain_ffn,
        back_gate,
        back_up,
        back_ffn_out,
    ) = back_weights
    back_offsets = offset_bias_of(back_bias)
    grad_out = cotangent.astype(jnp.float32) * valid_rows[..., None]
    grad_low = grad_out.astype(jnp.bfloat16)
    grad_w_ffn_out = outer_sum(hidden, grad_low)
    grad_hidden = back_project(grad_low, back_ffn_out)

    def gated_product(gate_in, up_in):
        return gelu_tanh(gate_in) * up_in

    gated_value, gated_back = jax.vjp(gated_product, gate_proj, up_proj)
    grad_gate, grad_up = gated_back(grad_hidden)
    grad_gate = grad_gate.astype(jnp.bfloat16)
    grad_up = grad_up.astype(jnp.bfloat16)
    grad_w_gate = outer_sum(normed_ffn, grad_gate)
    grad_w_up = outer_sum(normed_ffn, grad_up)
    grad_normed_ffn = back_project(grad_gate, back_gate) + back_project(grad_up, back_up)
    norm_value, norm_back = jax.vjp(normalize, residual, back_gain_ffn.astype(jnp.float32))
    grad_resid_part, grad_gain_ffn = norm_back(grad_normed_ffn)
    grad_resid = grad_out + grad_resid_part
    grad_branch = grad_resid.astype(jnp.bfloat16)
    grad_w_out = outer_sum(attn_low, grad_branch)
    grad_attn = back_project(grad_branch, back_out).astype(jnp.bfloat16)
    grad_heads = split_heads(grad_attn)
    delta_row = jnp.einsum(
        "mihe,mihe->mhi", grad_heads, attn_full, preferred_element_type=jnp.float32
    )

    def query_grad_block(running, sub_pieces, block_start, member_pick, bias_info):
        grad_query, grad_offsets = running
        pair_bias, table_start = bias_info
        key_part, value_part = sub_pieces
        key_heads = split_heads(key_part)
        key_pos = block_start + jnp.arange(key_part.shape[1], dtype=jnp.int32)
        key_ok = key_pos[None, :] < lengths[:, None]
        scores = block_scores(query_heads, key_heads, pair_bias, key_ok)
        probabilities = jnp.exp(scores - log_total[..., None])
        grad_probs = jnp.einsum(
            "mihe,mjhe->mhij",
            grad_heads,
            split_heads(value_part),
            preferred_element_type=jnp.float32,
        )
        grad_scores = (probabilities * (grad_probs - delta_row[..., None])).astype(jnp.bfloat16)
        grad_query = grad_query + jnp.einsum(
            "mhij,mjhe->mihe", grad_scores, key_heads, preferred_element_type=jnp.float32
        )
        pair_grad = jnp.sum(grad_scores.astype(jnp.float32), axis=0)
        diag = diagonal_sums(pair_grad, pair_grad.shape[1], pair_grad.shape[2])
        current = lax.dynamic_slice_in_dim(grad_offsets, table_start, diag.shape[1], 1)
        grad_offsets = lax.dynamic_update_slice_in_dim(grad_offsets, current + diag, table_start, 1)
        return (grad_query, grad_offsets)

    query_state = (
        jnp.zeros((batch_rows, local_rows, HEADS, HEAD_DIM), jnp.float32),
        jnp.zeros((HEADS, table_len), jnp.float32),
    )
    grad_query, grad_offsets = over_blocks(
        query_grad_block,
        keys_bias(back_offsets),
        query_state,
        (
            lax.all_gather(keys_local, "ctx", axis=1, tiled=True),
            lax.all_gather(values_local, "ctx", axis=1, tiled=True),
        ),
    )
    grad_buckets = jnp.einsum(
        "ht,tb->bh", grad_offsets, bucket_hot.astype(jnp.float32), precision=lax.Precision.HIGHEST
    )
    stats_lse, stats_delta = (
        lax.all_gather(log_total, "ctx", axis=2, tiled=True),
        lax.all_gather(delta_row, "ctx", axis=2, tiled=True),
    )
    key_heads_local = split_heads(keys_local)
    value_heads_local = split_heads(values_local)

    def key_grad_block(running, sub_pieces, block_start, member_pick, bias_info):
        grad_key, grad_value = running
        query_part, grad_part = sub_pieces
        rows_here = query_part.shape[1]
        query_part_heads = split_heads(query_part)
        grad_part_heads = split_heads(grad_part)
        scores = block_scores(query_part_heads, key_heads_local, bias_info[0], valid_mask)
        lse_part = lax.dynamic_slice_in_dim(stats_lse, block_start, rows_here, 2)
        delta_part = lax.dynamic_slice_in_dim(stats_delta, block_start, rows_here, 2)
        probabilities = jnp.exp(scores - lse_part[..., None])
        grad_value = grad_value + jnp.einsum(
            "mhij,mihe->mjhe",
            probabilities.astype(jnp.bfloat16),
            grad_part_heads,
            preferred_element_type=jnp.float32,
        )
        grad_probs = jnp.einsum(
            "mihe,mjhe->mhij",
            grad_part_heads,
            value_heads_local,
            preferred_element_type=jnp.float32,
        )
        grad_scores = (probabilities * (grad_probs - delta_part[..., None])).astype(jnp.bfloat16)
        grad_key = grad_key + jnp.einsum(
            "mhij,mihe->mjhe", grad_scores, query_part_heads, preferred_element_type=jnp.float32
        )
        return (grad_key, grad_value)

    key_state = (
        jnp.zeros((batch_rows, local_rows, HEADS, HEAD_DIM), jnp.float32),
        jnp.zeros((batch_rows, local_rows, HEADS, HEAD_DIM), jnp.float32),
    )
    grad_key, grad_value = over_blocks(
        key_grad_block,
        queries_bias(back_offsets),
        key_state,
        (
            lax.all_gather(queries, "ctx", axis=1, tiled=True),
            lax.all_gather(grad_attn, "ctx", axis=1, tiled=True),
        ),
    )
    grad_q = grad_query.reshape(batch_rows, local_rows, model_width).astype(jnp.bfloat16)
    grad_k = grad_key.reshape(batch_rows, local_rows, model_width).astype(jnp.bfloat16)
    grad_v = grad_value.reshape(batch_rows, local_rows, model_width).astype(jnp.bfloat16)
    grad_w_query = outer_sum(normed, grad_q)
    grad_w_key = outer_sum(normed, grad_k)
    grad_w_value = outer_sum(normed, grad_v)
    grad_normed = (
        back_project(grad_q, back_query)
        + back_project(grad_k, back_key)
        + back_project(grad_v, back_value)
    )
    attn_norm_value, attn_norm_back = jax.vjp(
        normalize, tokens_f, back_gain_attn.astype(jnp.float32)
    )
    grad_tokens_part, grad_gain_attn = attn_norm_back(grad_normed)
    grad_tokens = grad_resid + grad_tokens_part
    grads = (
        grad_gain_attn,
        grad_w_query,
        grad_w_key,
        grad_w_value,
        grad_w_out,
        grad_buckets,
        grad_gain_ffn,
        grad_w_gate,
        grad_w_up,
        grad_w_ffn_out,
    )
    shard_sums = (
        lax.psum_scatter(grads[0], "fsdp", scatter_dimension=0, tiled=True),
        lax.psum_scatter(grads[1], "fsdp", scatter_dimension=0, tiled=True),
        lax.psum_scatter(grads[2], "fsdp", scatter_dimension=0, tiled=True),
        lax.psum_scatter(grads[3], "fsdp", scatter_dimension=0, tiled=True),
        lax.psum_scatter(grads[4], "fsdp", scatter_dimension=0, tiled=True),
        lax.psum_scatter(grads[5], "fsdp", scatter_dimension=0, tiled=True),
        lax.psum_scatter(grads[6], "fsdp", scatter_dimension=0, tiled=True),
        lax.psum_scatter(grads[7], "fsdp", scatter_dimension=0, tiled=True),
        lax.psum_scatter(grads[8], "fsdp", scatter_dimension=0, tiled=True),
        lax.psum_scatter(grads[9], "fsdp", scatter_dimension=0, tiled=True),
    )
    totals = lax.psum(
        (
            shard_sums[0],
            shard_sums[1],
            shard_sums[2],
            shard_sums[3],
            shard_sums[4],
            shard_sums[5],
            shard_sums[6],
            shard_sums[7],
            shard_sums[8],
            shard_sums[9],
        ),
        "ctx",
    )
    return (output, grad_tokens) + tuple(totals)


def solution(mesh):
    placed = (
        P("fsdp", "ctx", None),
        P("fsdp", "ctx", None),
        P("fsdp"),
        P(),
        P("fsdp"),
        P("fsdp", None),
        P("fsdp", None),
        P("fsdp", None),
        P("fsdp", None),
        P("fsdp", None),
        P("fsdp"),
        P("fsdp", None),
        P("fsdp", None),
        P("fsdp", None),
    )
    plane = mesh.shape["ctx"] == 8 and mesh.shape["fsdp"] == 4
    return jax.shard_map(
        per_device_plane if plane else per_device_general,
        mesh=mesh,
        in_specs=placed,
        out_specs=(
            P("fsdp", "ctx", None),
            P("fsdp", "ctx", None),
            P("fsdp"),
            P("fsdp", None),
            P("fsdp", None),
            P("fsdp", None),
            P("fsdp", None),
            P("fsdp", None),
            P("fsdp"),
            P("fsdp", None),
            P("fsdp", None),
            P("fsdp", None),
        ),
        check_vma=False,
    )
```

```python
import jax
import jax.numpy as jnp
import math
from jax import lax
from jax.experimental import pallas as pl
from jax.experimental.pallas import tpu as pltpu
from jax.sharding import PartitionSpec as P

HEADS = 12
HEAD_DIM = 64
BUCKETS = 32
BLOCK = 256
TILE = 256
VMEM_BYTES = 56 * 1024 * 1024

norm_eps = 1e-06
F32 = jnp.float32
LOW = jnp.bfloat16
NN = (((1,), (0,)), ((), ()))
NT = (((1,), (1,)), ((), ()))
TN = (((0,), (0,)), ((), ()))
SMEM = pl.BlockSpec(memory_space=pltpu.SMEM)
ANY = pl.BlockSpec(memory_space=pl.ANY)


def dot(left, right, dims=NN):
    return lax.dot_general(left, right, dims, preferred_element_type=F32)


def shape_of(dims, kind):
    return jax.ShapeDtypeStruct(dims, kind)


def params(limit=VMEM_BYTES):
    return pltpu.CompilerParams(vmem_limit_bytes=limit)


def cost(flops, moved, exps=0):
    return pl.CostEstimate(flops=int(flops), bytes_accessed=int(moved), transcendentals=int(exps))


def block_rows(index, rows=BLOCK):
    return pl.ds(pl.multiple_of(index * rows, rows), rows)


def rms_rows(rows_f):
    return lax.rsqrt(jnp.mean(rows_f * rows_f, axis=-1, keepdims=True) + norm_eps)


def pack_kernel(
    where_ref, gate_ref, up_ref, down_ref, out_ref, q_ref, k_ref, v_ref, small_ref,
    gate_mine_ref, up_mine_ref, x_ref, y_ref, qkv_ref, out_piece_ref,
):
    chip, core = where_ref[0], where_ref[1]
    x_side, y_side = chip % 2, chip // 2
    wide, depth, model = gate_mine_ref.shape
    planes = gate_ref.shape[1] // model
    part = gate_ref.shape[1] // planes // 2
    slab = depth // 2
    for plane in range(planes):
        columns = pl.ds(pl.multiple_of(plane * 2 * part + core * part, 128), part)
        half, at = divmod(plane * part, model)
        gate_mine_ref[half, :, at : at + part] = gate_ref[:, columns]
        up_mine_ref[half, :, at : at + part] = up_ref[:, columns]
    x_rows, y_rows = block_rows(x_side, slab), block_rows(y_side, slab)
    for half in range(wide):
        x_ref[half * slab : (half + 1) * slab, :] = gate_mine_ref[half, x_rows, :]
        y_ref[half * slab : (half + 1) * slab, :] = up_mine_ref[half, y_rows, :]
    quarter = part // 4
    x_down = pl.ds(pl.multiple_of(core * part + x_side * quarter, quarter), quarter)
    y_down = pl.ds(pl.multiple_of(core * part + 2 * quarter + y_side * quarter, quarter), quarter)
    x_ref[wide * slab :, :] = down_ref[x_down, :]
    y_ref[wide * slab :, :] = down_ref[y_down, :]
    out_piece_ref[:slab, :] = out_ref[block_rows(core, slab), :]
    out_piece_ref[slab:, :] = small_ref[...]
    width = qkv_ref.shape[2]
    for owner in range(model // width):

        @pl.when(chip == owner)
        def _(owner=owner):
            lanes = slice(owner * width, (owner + 1) * width)
            qkv_ref[0] = q_ref[:, lanes]
            qkv_ref[1] = k_ref[:, lanes]
            qkv_ref[2] = v_ref[:, lanes]


def pack_weights(where, gate, up, down, out, query, key, value, small, width):
    depth, units = gate.shape
    model = query.shape[1]
    planes = model // depth
    wide = units // 2 // model
    part = units // planes // 2
    vmem = pl.BlockSpec(memory_space=pltpu.VMEM)
    return pl.pallas_call(
        pack_kernel,
        in_specs=[SMEM] + [vmem] * 8,
        out_specs=[vmem] * 6,
        out_shape=[
            shape_of((wide, depth, model), LOW),
            shape_of((wide, depth, model), LOW),
            shape_of((wide * depth // 2 + part // 4, model), LOW),
            shape_of((wide * depth // 2 + part // 4, model), LOW),
            shape_of((3, depth, width), LOW),
            shape_of((depth // 2 + small.shape[0], model), LOW),
        ],
        compiler_params=params(),
        cost_estimate=cost(0, 16e6),
        name="pack_weights",
    )(where, gate, up, down, out, query, key, value, small)


def prepare_kernel(order_ref, lens_ref, tok_ref, cot_ref, send_ref, local_ref, dy_ref):
    slot = pl.program_id(0)
    rows = tok_ref[0]
    for chip in range(send_ref.shape[0]):
        send_ref[chip, 0] = rows
    local_ref[...] = rows
    place_in = lax.broadcasted_iota(jnp.int32, rows.shape, 0) + lens_ref[lens_ref.shape[0] - 1]
    grads = cot_ref[0].astype(F32)
    dy_ref[...] = jnp.where(place_in < lens_ref[slot], grads, 0.0).astype(LOW)


def prepare(order, lens_and_start, tokens, cotangent, chips):
    batch, rows, model = tokens.shape
    by_order = pl.BlockSpec((1, rows, model), lambda s, order, lens: (order[s], 0, 0))
    in_order = pl.BlockSpec((rows, model), lambda s, order, lens: (s, 0))
    return pl.pallas_call(
        prepare_kernel,
        grid_spec=pltpu.PrefetchScalarGridSpec(
            num_scalar_prefetch=2,
            grid=(batch,),
            in_specs=[by_order, by_order],
            out_specs=[
                pl.BlockSpec((chips, 1, rows, model), lambda s, order, lens: (0, s, 0, 0)),
                in_order,
                in_order,
            ],
        ),
        out_shape=[
            shape_of((chips, batch, rows, model), LOW),
            shape_of((batch * rows, model), LOW),
            shape_of((batch * rows, model), LOW),
        ],
        compiler_params=params(),
        cost_estimate=cost(0, 8e6),
        name="prepare",
    )(order, lens_and_start, tokens, cotangent)


def build_bias(offsets_ref, bias_ref):
    heads, _, width = bias_ref.shape
    span = offsets_ref.shape[1]
    for head in range(heads):
        line = jnp.broadcast_to(offsets_ref[head : head + 1, :], (8, span))
        for group in range(BLOCK // 8):
            turned = pltpu.roll(
                line, (group * 8 - (BLOCK - 1)) % span, 1, stride=1, stride_axis=0
            )
            bias_ref[head, group * 8 : group * 8 + 8, :] = turned[:, :width]


def fold_diagonals(bias_grad_ref, offsets_grad_ref):
    heads, _, width = bias_grad_ref.shape
    span = offsets_grad_ref.shape[1]
    for head in range(heads):
        total = jnp.zeros((8, span), F32)
        for group in range(BLOCK // 8):
            rows = bias_grad_ref[head, group * 8 : group * 8 + 8, :]
            wide = jnp.concatenate([rows, jnp.zeros((8, span - width), F32)], axis=1)
            total = total + pltpu.roll(wide, (BLOCK - 8 - group * 8) % span, 1)
        line = jnp.zeros((1, span), F32)
        for row in range(8):
            line = line + pltpu.roll(total, (7 - row) % span, 1)[row : row + 1, :]
        offsets_grad_ref[head : head + 1, :] = line


def kept_scores(scores, column, length, count):
    wide = count * BLOCK
    tail = jnp.where(column < length - (wide - BLOCK), scores[:, wide - BLOCK :], -1e30)
    if count == 1:
        return tail
    return jnp.concatenate([scores[:, : wide - BLOCK], tail], axis=1)


def token_block(tok_ref, index):
    pieces, _, rows, model = tok_ref.shape
    parts = BLOCK // rows
    return tok_ref[pl.ds(index * parts, parts), 0].reshape(BLOCK, model)


def attn_forward_kernel(
    meta_ref, tok_ref, gain_ref, w0_ref, w1_ref, w2_ref, w3_ref, off_ref,
    ot_ref, of_ref, lse_ref, q_ref, k_ref, v_ref, w_ref,
    bias_ref, vm_ref,
):
    slot = pl.program_id(0)
    pieces, _, piece_rows, model = tok_ref.shape
    blocks = pieces * piece_rows // BLOCK
    width = w_ref.shape[2]
    per_chip = width // HEAD_DIM
    length = meta_ref[slot]
    used = (length + BLOCK - 1) // BLOCK
    parts = BLOCK // piece_rows

    @pl.when(slot == 0)
    def _():
        build_bias(off_ref, bias_ref)
        depth = w0_ref.shape[1]
        planes = model // depth
        for back, piece_ref in enumerate((w0_ref, w1_ref, w2_ref, w3_ref)):
            owner = lax.rem(meta_ref[2] + planes - back, planes)
            for kind in range(3):
                w_ref[kind, block_rows(owner, depth), :] = piece_ref[kind]

    owner = lax.broadcasted_iota(jnp.int32, (BLOCK, width), 1) // HEAD_DIM
    column = lax.broadcasted_iota(jnp.int32, (BLOCK, BLOCK), 1)
    nothing = jnp.zeros((BLOCK, width), LOW)

    def project(index, carry):
        rows = block_rows(index)
        rows_f = token_block(tok_ref, index).astype(F32)
        normed = (rows_f * rms_rows(rows_f) * gain_ref[...]).astype(LOW)
        q_ref[0, rows, :] = dot(normed, w_ref[0]).astype(LOW)
        k_ref[0, rows, :] = dot(normed, w_ref[1]).astype(LOW)
        val = dot(normed, w_ref[2]).astype(LOW)
        v_ref[0, rows, :] = val
        for head in range(per_chip):
            vm_ref[head, rows, :] = jnp.where(owner == head, val, nothing)
        return carry

    lax.fori_loop(0, used, project, 0)

    def attend(index, carry):
        rows = block_rows(index)
        query = q_ref[0, rows, :]
        start = pl.multiple_of((blocks - 1 - index) * BLOCK, BLOCK)
        for count in range(1, blocks + 1):

            @pl.when(used == count)
            def _(count=count):
                wide = count * BLOCK
                total = jnp.zeros((BLOCK, width), F32)
                for head in range(per_chip):
                    mine = jnp.where(owner == head, query, nothing)
                    scores = dot(mine, k_ref[0, :wide, :], NT)
                    scores = scores + bias_ref[head, :, pl.ds(start, wide)]
                    scores = kept_scores(scores, column, length, count)
                    top = jnp.max(scores, axis=-1, keepdims=True)
                    weights = jnp.exp(scores - top)
                    row_total = jnp.sum(weights, axis=-1, keepdims=True)
                    probs = (weights * (1.0 / row_total)).astype(LOW)
                    total = total + dot(probs, vm_ref[head, :wide, :])
                    lse_ref[0, head, rows, :] = jnp.broadcast_to(
                        top + jnp.log(row_total), (BLOCK, 128)
                    )
                of_ref[0, rows, :] = total
                turned = jnp.transpose(total.astype(LOW))
                for piece in range(parts):
                    lanes = slice(piece * piece_rows, (piece + 1) * piece_rows)
                    ot_ref[index * parts + piece, 0] = turned[:, lanes]

        return carry

    lax.fori_loop(0, used, attend, 0)

    def clear(index, carry):
        ot_ref[pl.ds(index * parts, parts), 0] = jnp.zeros((parts, width, piece_rows), LOW)
        return carry

    lax.fori_loop(used, blocks, clear, 0)


def attn_forward(meta, tokens, gain, w_pieces, offsets):
    pieces, slots, rows, model = tokens.shape
    _, depth, width = w_pieces[0].shape
    per_chip = width // HEAD_DIM
    seq = pieces * rows
    lane_rows = pl.BlockSpec((1, seq, width), lambda s: (s, 0, 0))
    by_slot = lambda s: (0, s, 0, 0)
    once = lambda s: (0, 0, 0)
    return pl.pallas_call(
        attn_forward_kernel,
        grid=(slots,),
        in_specs=[
            SMEM,
            pl.BlockSpec((pieces, 1, rows, model), by_slot),
            pl.BlockSpec((1, model), lambda s: (0, 0)),
        ]
        + [pl.BlockSpec((3, depth, width), once)] * 4
        + [pl.BlockSpec(offsets.shape, lambda s: (0, 0))],
        out_specs=[
            pl.BlockSpec((pieces, 1, width, rows), by_slot),
            lane_rows,
            pl.BlockSpec((1, per_chip, seq, 128), lambda s: (s, 0, 0, 0)),
            lane_rows,
            lane_rows,
            lane_rows,
            pl.BlockSpec((3, model, width), once),
        ],
        out_shape=[
            shape_of((pieces, slots, width, rows), LOW),
            shape_of((slots, seq, width), F32),
            shape_of((slots, per_chip, seq, 128), F32),
            shape_of((slots, seq, width), LOW),
            shape_of((slots, seq, width), LOW),
            shape_of((slots, seq, width), LOW),
            shape_of((3, model, width), LOW),
        ],
        scratch_shapes=[
            pltpu.VMEM((per_chip, BLOCK, 2 * seq - BLOCK), F32),
            pltpu.VMEM((per_chip, seq, width), LOW),
        ],
        compiler_params=params(),
        cost_estimate=cost(
            4 * slots * seq * (model * 3 * width + 2 * seq * 256 * per_chip),
            slots * seq * 2 * (model + 8 * width),
        ),
        name="attn_forward",
    )(meta, tokens, gain, *w_pieces, offsets)


def attn_backward_kernel(
    meta_ref, tok_ref, gain_ref, w_ref, off_ref, q_ref, k_ref, v_ref, of_ref, lse_ref, dot_ref,
    dn_ref, dw_ref, dgain_ref, doff_ref,
    bias_ref, dbias_ref, km_ref, dq_ref, dkt_ref, dvt_ref, dwt_ref,
):
    slot = pl.program_id(0)
    pieces, _, piece_rows, model = tok_ref.shape
    blocks = pieces * piece_rows // BLOCK
    width = w_ref.shape[2]
    per_chip = width // HEAD_DIM
    length = meta_ref[slot]
    used = (length + BLOCK - 1) // BLOCK
    parts = BLOCK // piece_rows

    @pl.when(slot == 0)
    def _():
        build_bias(off_ref, bias_ref)
        dbias_ref[...] = jnp.zeros_like(dbias_ref)
        dwt_ref[...] = jnp.zeros_like(dwt_ref)
        dgain_ref[...] = jnp.zeros_like(dgain_ref)

    dkt_ref[...] = jnp.zeros_like(dkt_ref)
    dvt_ref[...] = jnp.zeros_like(dvt_ref)
    owner = lax.broadcasted_iota(jnp.int32, (BLOCK, width), 1) // HEAD_DIM
    column = lax.broadcasted_iota(jnp.int32, (BLOCK, BLOCK), 1)
    nothing = jnp.zeros((BLOCK, width), LOW)

    def split_keys(index, carry):
        rows = block_rows(index)
        key = k_ref[0, rows, :]
        for head in range(per_chip):
            km_ref[head, rows, :] = jnp.where(owner == head, key, nothing)
        return carry

    lax.fori_loop(0, used, split_keys, 0)

    def attend(index, carry):
        rows = block_rows(index)
        query = q_ref[0, rows, :]
        query_t = jnp.transpose(query)
        grad_t = jnp.concatenate(
            [dot_ref[index * parts + piece, 0] for piece in range(parts)], axis=1
        )
        grad = jnp.transpose(grad_t)
        product = grad.astype(F32) * of_ref[0, rows, :]
        start = pl.multiple_of((blocks - 1 - index) * BLOCK, BLOCK)
        for count in range(1, blocks + 1):

            @pl.when(used == count)
            def _(count=count):
                wide = count * BLOCK
                grad_query = jnp.zeros((BLOCK, width), F32)
                for head in range(per_chip):
                    lanes = slice(head * HEAD_DIM, (head + 1) * HEAD_DIM)
                    mine = jnp.where(owner == head, query, nothing)
                    scores = dot(mine, k_ref[0, :wide, :], NT)
                    scores = scores + bias_ref[head, :, pl.ds(start, wide)]
                    scores = kept_scores(scores, column, length, count)
                    probs = jnp.exp(scores - lse_ref[0, head, rows, :][:, :1])
                    delta = jnp.sum(
                        jnp.where(owner == head, product, 0.0), axis=-1, keepdims=True
                    )
                    grad_mine = jnp.where(owner == head, grad, nothing)
                    grad_probs = dot(grad_mine, v_ref[0, :wide, :], NT)
                    grad_scores = (probs * (grad_probs - delta)).astype(LOW)
                    grad_query = grad_query + dot(grad_scores, km_ref[head, :wide, :])
                    dkt_ref[lanes, :wide] += dot(query_t[lanes, :], grad_scores)
                    dvt_ref[lanes, :wide] += dot(grad_t[lanes, :], probs.astype(LOW))
                    dbias_ref[head, :, pl.ds(start, wide)] += grad_scores.astype(F32)
                dq_ref[rows, :] = grad_query.astype(LOW)

        return carry

    lax.fori_loop(0, used, attend, 0)

    def finish(index, carry):
        rows = block_rows(index)
        grad_query = dq_ref[rows, :]
        key_t = dkt_ref[:, rows].astype(LOW)
        value_t = dvt_ref[:, rows].astype(LOW)
        rows_f = token_block(tok_ref, index).astype(F32)
        unit = rows_f * rms_rows(rows_f)
        normed = (unit * gain_ref[...]).astype(LOW)
        grad_normed = (
            dot(grad_query, w_ref[0], NT)
            + dot(jnp.transpose(key_t), w_ref[1], NT)
            + dot(jnp.transpose(value_t), w_ref[2], NT)
        )
        dgain_ref[...] += jnp.sum(grad_normed * unit, axis=0, keepdims=True)
        dn_ref[pl.ds(index * parts, parts), 0] = grad_normed.astype(LOW).reshape(
            parts, piece_rows, model
        )
        dwt_ref[0:width, :] += dot(jnp.transpose(grad_query), normed)
        dwt_ref[width : 2 * width, :] += dot(key_t, normed)
        dwt_ref[2 * width :, :] += dot(value_t, normed)
        return carry

    lax.fori_loop(0, used, finish, 0)

    def clear(index, carry):
        dn_ref[pl.ds(index * parts, parts), 0] = jnp.zeros((parts, piece_rows, model), LOW)
        return carry

    lax.fori_loop(used, blocks, clear, 0)

    @pl.when(slot == pl.num_programs(0) - 1)
    def _():
        fold_diagonals(dbias_ref, doff_ref)
        dw_ref[...] = jnp.transpose(dwt_ref[...].astype(LOW))


def attn_backward(meta, tokens, gain, w_qkv, offsets, query, key, value, attn_full, lse, grad):
    pieces, slots, rows, model = tokens.shape
    width = w_qkv.shape[2]
    per_chip = width // HEAD_DIM
    seq = pieces * rows
    lane_rows = pl.BlockSpec((1, seq, width), lambda s: (s, 0, 0))
    by_slot = lambda s: (0, s, 0, 0)
    once = lambda s: (0, 0)
    return pl.pallas_call(
        attn_backward_kernel,
        grid=(slots,),
        in_specs=[
            SMEM,
            pl.BlockSpec((pieces, 1, rows, model), by_slot),
            pl.BlockSpec((1, model), once),
            pl.BlockSpec((3, model, width), lambda s: (0, 0, 0)),
            pl.BlockSpec(offsets.shape, once),
            lane_rows,
            lane_rows,
            lane_rows,
            lane_rows,
            pl.BlockSpec((1, per_chip, seq, 128), lambda s: (s, 0, 0, 0)),
            pl.BlockSpec((pieces, 1, width, rows), by_slot),
        ],
        out_specs=[
            pl.BlockSpec((pieces, 1, rows, model), by_slot),
            pl.BlockSpec((model, 3 * width), once),
            pl.BlockSpec((1, model), once),
            pl.BlockSpec(offsets.shape, once),
        ],
        out_shape=[
            shape_of((pieces, slots, rows, model), LOW),
            shape_of((model, 3 * width), LOW),
            shape_of((1, model), F32),
            shape_of(offsets.shape, F32),
        ],
        scratch_shapes=[
            pltpu.VMEM((per_chip, BLOCK, 2 * seq - BLOCK), F32),
            pltpu.VMEM((per_chip, BLOCK, 2 * seq - BLOCK), F32),
            pltpu.VMEM((per_chip, seq, width), LOW),
            pltpu.VMEM((seq, width), LOW),
            pltpu.VMEM((width, seq), F32),
            pltpu.VMEM((width, seq), F32),
            pltpu.VMEM((3 * width, model), F32),
        ],
        compiler_params=params(),
        cost_estimate=cost(
            4 * slots * seq * (model * 6 * width + 5 * seq * 256 * per_chip),
            slots * seq * 2 * (2 * model + 12 * width),
        ),
        name="attn_backward",
    )(meta, tokens, gain, w_qkv, offsets, query, key, value, attn_full, lse, grad)


def side_by_side(attn_ref, chip):
    return jnp.concatenate(
        [attn_ref[2 * chip + core, slot] for core in range(2) for slot in range(2)], axis=1
    )


def out_project_kernel(
    where_ref, tok_ref, attn_ref, own_ref, a1_ref, a2_ref, a3_ref, others_ref, gain_ref,
    res_ref, nf_ref, w_ref,
):
    core, plane = where_ref[1], where_ref[2]
    depth = own_ref.shape[0]
    slab = depth // 2
    planes = w_ref.shape[0] // depth
    w_ref[block_rows(plane, depth), :] = own_ref[...]
    for back, piece_ref in enumerate((a1_ref, a2_ref, a3_ref)):
        owner = lax.rem(plane + planes - 1 - back, planes)
        w_ref[block_rows(owner * 2 + core, slab), :] = piece_ref[:slab, :]
        w_ref[block_rows(owner * 2 + 1 - core, slab), :] = others_ref[back, :slab, :]
    chips, width = attn_ref.shape[0] // 2, attn_ref.shape[2]
    total = tok_ref[...].astype(F32)
    for chip in range(chips):
        total = total + dot(
            side_by_side(attn_ref, chip), w_ref[chip * width : (chip + 1) * width, :], TN
        )
    res_ref[...] = total
    nf_ref[...] = (total * rms_rows(total) * gain_ref[...]).astype(LOW)


def out_project(where, tokens, attn, own, pieces, others, gain):
    rows, model = tokens.shape
    vmem = pl.BlockSpec(memory_space=pltpu.VMEM)
    return pl.pallas_call(
        out_project_kernel,
        in_specs=[SMEM] + [vmem] * 8,
        out_specs=[vmem] * 3,
        out_shape=[
            shape_of((rows, model), F32),
            shape_of((rows, model), LOW),
            shape_of((model, model), LOW),
        ],
        compiler_params=params(),
        cost_estimate=cost(4 * rows * model * model, rows * model * 12),
        name="out_project",
    )(where, tokens, attn, own, *pieces, others, gain)


def out_back_kernel(
    own_ref, recv_ref, res_ref, dy_ref, gain_ref, w_ref, dattn_ref, dres_ref, branch_ref, dgain_ref
):
    chips, width, rows = dattn_ref.shape[0] // 2, dattn_ref.shape[2], dattn_ref.shape[3]
    grad = own_ref[...] + recv_ref[...].astype(F32)
    residual = res_ref[...]
    scale = rms_rows(residual)
    unit = residual * scale
    dgain_ref[...] = jnp.sum(grad * unit, axis=0, keepdims=True)
    inner = grad * gain_ref[...]
    dres = dy_ref[...].astype(F32) + scale * (
        inner - unit * jnp.mean(inner * unit, axis=-1, keepdims=True)
    )
    dres_ref[...] = dres
    branch = dres.astype(LOW)
    branch_ref[...] = branch
    for chip in range(chips):
        part = dot(w_ref[chip * width : (chip + 1) * width, :], branch, NT).astype(LOW)
        for slot in range(4):
            dattn_ref[2 * chip + slot // 2, slot % 2] = part[:, slot * rows : (slot + 1) * rows]


def out_back(own, recv, residual, dy, gain, w_out, attn_shape):
    rows, model = own.shape
    return pl.pallas_call(
        out_back_kernel,
        out_shape=[
            shape_of(attn_shape, LOW),
            shape_of((rows, model), F32),
            shape_of((rows, model), LOW),
            shape_of((1, model), F32),
        ],
        compiler_params=params(),
        cost_estimate=cost(4 * rows * model * model, rows * model * 20),
        name="out_back",
    )(own, recv, residual, dy, gain, w_out)


def gate_and_slope(gate):
    inner = 0.7978845608028654 * (gate + 0.044715 * gate * gate * gate)
    bent = jnp.tanh(inner)
    half = 0.5 * (1.0 + bent)
    slope = half + 0.5 * gate * (1.0 - bent * bent) * (
        0.7978845608028654 * (1.0 + 3.0 * 0.044715 * gate * gate)
    )
    return gate * half, slope


def ffn_first_kernel(
    where_ref, nf_own_ref, nf_other_ref, dy_own_ref, dy_other_ref,
    gate_own, up_own, down_own, x1, x2, x3, sx1, sx2, sx3, y1, y2, y3, sy1, sy2, sy3,
    hidden_ref, dgate_ref, dup_ref, own_ref, other_ref, down_ref,
    gate_ref, up_ref, nf_ref, dy_ref, total_ref, sems,
):
    step = pl.program_id(0)
    half = nf_own_ref.shape[0]
    chip, core, plane = where_ref[0], where_ref[1], where_ref[2]
    wide, model, _ = gate_ref.shape
    units = down_ref.shape[0]
    tile = hidden_ref.shape[1]
    depth = gate_own.shape[1]
    planes = model // depth
    slab = depth // 2
    part = units // planes
    quarter = part // 4

    @pl.when(step == 0)
    def _():
        copies = []

        def copy(source, target):
            started = pltpu.make_async_copy(source, target, sems.at[len(copies)])
            started.start()
            copies.append(started)

        own_rows = pl.ds(pl.multiple_of(plane * depth, depth), depth)
        for index in range(wide):
            copy(gate_own.at[index], gate_ref.at[index, own_rows, :])
            copy(up_own.at[index], up_ref.at[index, own_rows, :])
        copy(
            down_own.at[pl.ds(pl.multiple_of(core * part, part), part), :],
            down_ref.at[pl.ds(pl.multiple_of(plane * part, part), part), :],
        )
        for back in range(planes - 1):
            owner = lax.rem(plane + planes - 1 - back, planes)
            for along, (straight, swapped), weight_ref, side in (
                (0, ((x1, x2, x3)[back], (sx1, sx2, sx3)[back]), gate_ref, lax.rem(chip, 2)),
                (1, ((y1, y2, y3)[back], (sy1, sy2, sy3)[back]), up_ref, chip // 2),
            ):
                for piece, here in ((straight, side), (swapped, 1 - side)):
                    at = pl.ds(pl.multiple_of(owner * depth + here * slab, slab), slab)
                    for index in range(wide):
                        copy(
                            piece.at[pl.ds(index * slab, slab), :],
                            weight_ref.at[index, at, :],
                        )
                    copy(
                        piece.at[pl.ds(wide * slab, quarter), :],
                        down_ref.at[
                            pl.ds(
                                pl.multiple_of(
                                    owner * part + (2 * along + here) * quarter, quarter
                                ),
                                quarter,
                            ),
                            :,
                        ],
                    )
        nf_ref[:half, :] = nf_own_ref[...]
        nf_ref[half:, :] = nf_other_ref[...]
        dy_ref[:half, :] = dy_own_ref[...]
        dy_ref[half:, :] = dy_other_ref[...]
        total_ref[...] = jnp.zeros_like(total_ref)
        for started in copies:
            started.wait()

    per = model // tile
    index = step // per
    lanes = pl.ds(pl.multiple_of(lax.rem(step, per) * tile, tile), tile)
    gate_w = gate_ref[index, :, lanes]
    up_w = up_ref[index, :, lanes]
    down_w = down_ref[block_rows(step, tile), :]
    for quarter_rows in range(4):
        rows = slice(quarter_rows * half // 2, (quarter_rows + 1) * half // 2)
        nf = nf_ref[rows, :]
        gate = dot(nf, gate_w)
        up = dot(nf, up_w)
        dhidden = dot(dy_ref[rows, :], down_w, NT)
        bent, slope = gate_and_slope(gate)
        hidden_ref[rows, :] = (bent * up).astype(LOW)
        dgate = (dhidden * up * slope).astype(LOW)
        dup = (dhidden * bent).astype(LOW)
        dgate_ref[rows, :] = dgate
        dup_ref[rows, :] = dup
        total_ref[rows, :] += dot(dgate, gate_w, NT) + dot(dup, up_w, NT)

    @pl.when(step == pl.num_programs(0) - 1)
    def _():
        own_ref[...] = total_ref[:half, :]
        other_ref[...] = total_ref[half:, :].astype(LOW)


def ffn_first(where, nf_own, nf_other, dy_own, dy_other, own_weights, pieces, tile=TILE):
    half, model = nf_own.shape
    wide, depth, _ = own_weights[0].shape
    units = wide * model
    whole = pl.BlockSpec((half, model), lambda t: (0, 0))
    lane_tile = pl.BlockSpec((2 * half, tile), lambda t: (0, t))
    copies = 2 * wide + 1 + 3 * 4 * (wide + 1)
    return pl.pallas_call(
        ffn_first_kernel,
        grid=(units // tile,),
        in_specs=[SMEM, whole, whole, whole, whole] + [ANY] * 15,
        out_specs=[
            lane_tile, lane_tile, lane_tile, whole, whole,
            pl.BlockSpec((units, model), lambda t: (0, 0)),
        ],
        out_shape=[
            shape_of((2 * half, units), LOW),
            shape_of((2 * half, units), LOW),
            shape_of((2 * half, units), LOW),
            shape_of((half, model), F32),
            shape_of((half, model), LOW),
            shape_of((units, model), LOW),
        ],
        scratch_shapes=[
            pltpu.VMEM((wide, model, model), LOW),
            pltpu.VMEM((wide, model, model), LOW),
            pltpu.VMEM((2 * half, model), LOW),
            pltpu.VMEM((2 * half, model), LOW),
            pltpu.VMEM((2 * half, model), F32),
            pltpu.SemaphoreType.DMA((copies,)),
        ],
        compiler_params=params(),
        cost_estimate=cost(
            2 * 2 * 5 * 2 * half * model * units,
            6 * model * units + 12 * half * units + 20 * half * model,
        ),
        name="ffn_first",
    )(where, nf_own, nf_other, dy_own, dy_other, *own_weights, *pieces)


def ffn_second_kernel(
    nf_own_ref, nf_other_ref, dy_own_ref, dy_other_ref, hidden_ref, dgate_ref, dup_ref, down_ref,
    attn_ref, branch_ref,
    own_ref, other_ref, gdown_ref, ggate_ref, gup_ref, gout_ref,
    nft_ref, dy_ref, total_ref,
):
    step = pl.program_id(0)
    half = nf_own_ref.shape[0]
    planes, _, depth, tile = ggate_ref.shape

    @pl.when(step == 0)
    def _():
        nft_ref[:, :half] = jnp.transpose(nf_own_ref[...])
        nft_ref[:, half:] = jnp.transpose(nf_other_ref[...])
        dy_ref[:half, :] = dy_own_ref[...]
        dy_ref[half:, :] = dy_other_ref[...]
        total_ref[...] = jnp.zeros_like(total_ref)
        chips, width = attn_ref.shape[0] // 2, attn_ref.shape[2]
        for chip in range(chips):
            gout_ref[chip * width : (chip + 1) * width, :] = dot(
                side_by_side(attn_ref, chip), branch_ref[...]
            ).astype(LOW)

    hidden = hidden_ref[...]
    ggate_ref[...] = dot(nft_ref[...], dgate_ref[...]).astype(LOW).reshape(planes, 1, depth, tile)
    gup_ref[...] = dot(nft_ref[...], dup_ref[...]).astype(LOW).reshape(planes, 1, depth, tile)
    gdown_ref[...] = dot(jnp.transpose(hidden), dy_ref[...]).astype(LOW)
    total_ref[...] += dot(hidden, down_ref[...])

    @pl.when(step == pl.num_programs(0) - 1)
    def _():
        own_ref[...] = total_ref[:half, :]
        other_ref[...] = total_ref[half:, :].astype(LOW)


def ffn_second(
    nf_own, nf_other, dy_own, dy_other, hidden, dgate, dup, w_down, attn, branch, planes, tile=TILE
):
    half, model = nf_own.shape
    units = hidden.shape[1]
    depth = model // planes
    per = model // tile
    whole = pl.BlockSpec((half, model), lambda t: (0, 0))
    lane_tile = pl.BlockSpec((2 * half, tile), lambda t: (0, t))
    row_tile = pl.BlockSpec((tile, model), lambda t: (t, 0))
    out_tile = pl.BlockSpec((planes, 1, depth, tile), lambda t: (0, t // per, 0, t % per))
    return pl.pallas_call(
        ffn_second_kernel,
        grid=(units // tile,),
        in_specs=[
            whole, whole, whole, whole, lane_tile, lane_tile, lane_tile, row_tile,
            pl.BlockSpec(attn.shape, lambda t: (0, 0, 0, 0)),
            whole,
        ],
        out_specs=[
            whole, whole, row_tile, out_tile, out_tile,
            pl.BlockSpec((model, model), lambda t: (0, 0)),
        ],
        out_shape=[
            shape_of((half, model), F32),
            shape_of((half, model), LOW),
            shape_of((units, model), LOW),
            shape_of((planes, units // model, depth, model), LOW),
            shape_of((planes, units // model, depth, model), LOW),
            shape_of((model, model), LOW),
        ],
        scratch_shapes=[
            pltpu.VMEM((model, 2 * half), LOW),
            pltpu.VMEM((2 * half, model), LOW),
            pltpu.VMEM((2 * half, model), F32),
        ],
        compiler_params=params(),
        cost_estimate=cost(
            2 * 2 * 4 * 2 * half * model * units,
            8 * model * units + 12 * half * units + 20 * half * model,
        ),
        name="ffn_second",
    )(nf_own, nf_other, dy_own, dy_other, hidden, dgate, dup, w_down, attn, branch)


def finish_out_kernel(order_ref, lens_ref, res_ref, own_ref, recv_ref, out_ref):
    slot = pl.program_id(0)
    total = res_ref[...] + own_ref[...] + recv_ref[...].astype(F32)
    place_in = lax.broadcasted_iota(jnp.int32, total.shape, 0) + lens_ref[lens_ref.shape[0] - 1]
    out_ref[0] = jnp.where(place_in < lens_ref[slot], total, 0.0).astype(LOW)


def finish_out(order, lens_and_start, residual, own, recv, batch):
    rows, model = residual.shape[0] // batch, residual.shape[1]
    in_order = pl.BlockSpec((rows, model), lambda s, order, lens: (s, 0))
    return pl.pallas_call(
        finish_out_kernel,
        grid_spec=pltpu.PrefetchScalarGridSpec(
            num_scalar_prefetch=2,
            grid=(batch,),
            in_specs=[in_order, in_order, in_order],
            out_specs=pl.BlockSpec((1, rows, model), lambda s, order, lens: (order[s], 0, 0)),
        ),
        out_shape=shape_of((batch, rows, model), LOW),
        compiler_params=params(),
        cost_estimate=cost(0, 6e6),
        name="finish_out",
    )(order, lens_and_start, residual, own, recv)


def finish_tokens_kernel(order_ref, dn_ref, tok_ref, dres_ref, gain_ref, out_ref):
    grad = dn_ref[0, 0].astype(F32)
    for chip in range(1, dn_ref.shape[0]):
        grad = grad + dn_ref[chip, 0].astype(F32)
    rows_f = tok_ref[...].astype(F32)
    scale = rms_rows(rows_f)
    unit = rows_f * scale
    inner = grad * gain_ref[...]
    out_ref[0] = dres_ref[...] + scale * (
        inner - unit * jnp.mean(inner * unit, axis=-1, keepdims=True)
    )


def finish_tokens(order, dn, tokens, dres, gain):
    chips, batch, rows, model = dn.shape
    in_order = pl.BlockSpec((rows, model), lambda s, order: (s, 0))
    return pl.pallas_call(
        finish_tokens_kernel,
        grid_spec=pltpu.PrefetchScalarGridSpec(
            num_scalar_prefetch=1,
            grid=(batch,),
            in_specs=[
                pl.BlockSpec((chips, 1, rows, model), lambda s, order: (0, s, 0, 0)),
                in_order,
                in_order,
                pl.BlockSpec((1, model), lambda s, order: (0, 0)),
            ],
            out_specs=pl.BlockSpec((1, rows, model), lambda s, order: (order[s], 0, 0)),
        ),
        out_shape=shape_of((batch, rows, model), F32),
        compiler_params=params(),
        cost_estimate=cost(0, 10e6),
        name="finish_tokens",
    )(order, dn, tokens, dres, gain)


def unpack_kernel(where_ref, *refs):
    piece_refs, (gate_ref, up_ref, down_ref, out_ref) = refs[:8], refs[8:]
    chip, core = where_ref[0], where_ref[1]
    depth, units = gate_ref.shape
    model = down_ref.shape[1]
    part = down_ref.shape[0] // 2
    quarter, tail = depth // 4, depth // 8
    wide = units // 2 // model
    planes = units // 2 // part
    for far in range(8):
        away, other = far % 4, far // 4
        from_core = core if other == 0 else 1 - core
        from_chip = jnp.bitwise_xor(chip, away)
        from_x, from_y = lax.rem(from_chip, 2), from_chip // 2
        piece_ref = piece_refs[far]
        gate_rows = block_rows(from_x * 2 + from_y, quarter)
        for plane in range(planes):
            index, at = divmod(plane * part, model)
            lanes = pl.ds(pl.multiple_of(plane * 2 * part + from_core * part, 128), part)
            rows = slice(index * quarter, (index + 1) * quarter)
            gate_ref[gate_rows, lanes] = piece_ref[rows, at : at + part].astype(F32)
            rows = slice((wide + index) * quarter, (wide + index + 1) * quarter)
            up_ref[gate_rows, lanes] = piece_ref[rows, at : at + part].astype(F32)
        down_at = 2 * wide * quarter
        rows = part // 4
        down_ref[block_rows(from_core * 4 + from_y * 2 + from_x, rows), :] = piece_ref[
            down_at : down_at + rows, :
        ].astype(F32)
        out_ref[block_rows(from_core * 4 + from_x * 2 + from_y, tail), :] = piece_ref[
            down_at + rows :, :
        ].astype(F32)[:tail, :]


def unpack(where, pieces, depth, units):
    model = pieces[0].shape[1]
    planes = model // depth
    vmem = pl.BlockSpec(memory_space=pltpu.VMEM)
    return pl.pallas_call(
        unpack_kernel,
        in_specs=[SMEM] + [vmem] * 8,
        out_specs=[vmem] * 4,
        out_shape=[
            shape_of((depth, units), F32),
            shape_of((depth, units), F32),
            shape_of((units // planes, model), F32),
            shape_of((depth, model), F32),
        ],
        compiler_params=params(),
        cost_estimate=cost(0, 24e6),
        name="unpack",
    )(where, *pieces)


def unpack_qkv_kernel(where_ref, *refs):
    mine_refs, others_ref = refs[:4], refs[4]
    out_refs, small_ref = refs[5:8], refs[8]
    chip, core = where_ref[0], where_ref[1]
    width = mine_refs[0].shape[1] // 3
    slab = out_refs[0].shape[0] // 2
    for home in range(4):

        @pl.when(chip == home)
        def _(home=home):
            for away in range(4):
                lanes = slice((home ^ away) * width, ((home ^ away) + 1) * width)
                for kind in range(3):
                    from_lanes = slice(kind * width, (kind + 1) * width)
                    out_refs[kind][block_rows(core, slab), lanes] = mine_refs[away][
                        :slab, from_lanes
                    ].astype(F32)
                    out_refs[kind][block_rows(1 - core, slab), lanes] = others_ref[
                        away, :slab, from_lanes
                    ].astype(F32)

    mine = mine_refs[0][slab:, :].astype(F32)
    other = others_ref[0, slab:, :].astype(F32)
    for away in range(1, 4):
        mine = mine + mine_refs[away][slab:, :].astype(F32)
        other = other + others_ref[away, slab:, :].astype(F32)
    small_ref[...] = mine + other


def unpack_qkv(where, mine, others, depth, model):
    vmem = pl.BlockSpec(memory_space=pltpu.VMEM)
    rows, lanes = mine[0].shape
    return pl.pallas_call(
        unpack_qkv_kernel,
        in_specs=[SMEM] + [vmem] * 5,
        out_specs=[vmem] * 4,
        out_shape=[shape_of((depth, model), F32)] * 3 + [shape_of((rows - depth // 2, lanes), F32)],
        compiler_params=params(),
        cost_estimate=cost(0, 4e6),
        name="unpack_qkv",
    )(where, *mine, others)


CORE, X, Y, XY = 1, 2, 4, 6


def swap(values, bits):
    count = lax.axis_size("ctx")
    return lax.ppermute(values, "ctx", [(i, i ^ bits) for i in range(count)])


def ring_step(values):
    count = lax.axis_size("fsdp")
    return lax.ppermute(values, "fsdp", [(i, (i + 1) % count) for i in range(count)])


def ring_pieces(piece):
    found = []
    for _ in range(lax.axis_size("fsdp") - 1):
        piece = ring_step(piece)
        found.append(piece)
    return found


def pick(values, index, axis):
    return lax.dynamic_index_in_dim(values, index, axis, keepdims=False)


def halve_sum(values, bit, axis):
    side = (lax.axis_index("ctx") // bit) % 2
    came = swap(pick(values, 1 - side, axis), bit)
    return (pick(values, side, axis).astype(F32) + came.astype(F32)).astype(LOW)


def plane_sum(values):
    chip = lax.axis_index("ctx") // 2
    total = pick(values, chip, 0).astype(F32)
    for away, bits in ((1, X), (2, Y), (3, XY)):
        total = total + swap(pick(values, chip ^ away, 0), bits).astype(F32)
    return total.astype(LOW)


def ring_sum(values):
    came = lax.all_to_all(values, "fsdp", 0, 0)
    return jnp.sum(came.astype(F32), axis=0).astype(LOW)


def per_device_plane(
    tokens, cotangent, lengths, bucket_table, gain_attn, w_query, w_key, w_value, w_out,
    bias_table, gain_ffn, w_gate, w_up, w_ffn_out,
):
    batch, rows, model = tokens.shape
    planes = lax.axis_size("fsdp")
    chips = lax.axis_size("ctx") // 2
    me = lax.axis_index("ctx")
    plane = lax.axis_index("fsdp")
    core, chip = me % 2, me // 2
    depth, units = w_gate.shape
    chip_heads = HEADS // chips
    width = chip_heads * HEAD_DIM
    quarter = depth // 4
    where = jnp.stack([chip, core, plane]).astype(jnp.int32)

    entry = jnp.arange(batch, dtype=jnp.int32)
    ahead = (lengths[None, :] > lengths[:, None]) | (
        (lengths[None, :] == lengths[:, None]) & (entry[None, :] < entry[:, None])
    )
    rank = jnp.sum(ahead.astype(jnp.int32), axis=1)
    slot = jnp.where(rank == 0, 0, jnp.where(rank == batch - 1, 1, rank + 1))
    chosen = (slot[None, :] == entry[:, None]).astype(jnp.int32)
    order = jnp.sum(chosen * entry[None, :], axis=1)
    lens = jnp.sum(chosen * lengths[None, :], axis=1)
    lens_and_start = jnp.concatenate([lens, (me * rows)[None].astype(jnp.int32)])
    meta = jnp.concatenate([lax.dynamic_slice_in_dim(lens, 2 * core, 2), plane[None]])

    send, flat, dy = prepare(order, lens_and_start, tokens, cotangent, chips)
    gathered = lax.all_to_all(send.reshape(2 * chips, 2, rows, model), "ctx", 0, 0)

    small = jnp.concatenate([gain_attn, gain_ffn, bias_table.reshape(-1)])
    small = jnp.pad(small[None], ((0, 15), (0, model - small.shape[0])))
    gate_mine, up_mine, x_piece, y_piece, qkv_piece, out_piece = pack_weights(
        where, w_gate, w_up, w_ffn_out, w_out, w_query, w_key, w_value, small, width
    )
    qkv_found = ring_pieces(qkv_piece)
    out_found = ring_pieces(out_piece)
    out_others = swap(jnp.stack(out_found), CORE)
    x_found, y_found = ring_pieces(x_piece), ring_pieces(y_piece)
    x_swapped = [swap(piece, X) for piece in x_found]
    y_swapped = [swap(piece, Y) for piece in y_found]

    by_distance = jnp.stack([piece[depth // 2] for piece in [out_piece] + out_found])
    all_small = jnp.stack([pick(by_distance, (plane + planes - i) % planes, 0) for i in range(planes)])
    full_gain_attn = all_small[:, :depth].reshape(1, model).astype(F32)
    full_gain_ffn = all_small[:, depth : 2 * depth].reshape(1, model).astype(F32)
    small_end = 2 * depth + bias_table.size
    full_table = all_small[:, 2 * depth : small_end].reshape(BUCKETS, HEADS)

    hot = bucket_table[:, None] == jnp.arange(BUCKETS, dtype=jnp.int32)[None, :]
    hot = jnp.concatenate([hot, jnp.zeros((1, BUCKETS), bool)])
    my_table = lax.dynamic_slice_in_dim(full_table, chip * chip_heads, chip_heads, 1)
    offsets = jnp.einsum("tb,bh->ht", hot.astype(LOW), my_table, preferred_element_type=F32)

    attn_out, attn_full, lse, query, key, value, w_qkv = attn_forward(
        meta, gathered, full_gain_attn, [qkv_piece] + qkv_found, offsets
    )
    attn = lax.all_to_all(attn_out, "ctx", 0, 0)
    residual, nf_own, full_out = out_project(
        where, flat, attn, w_out, out_found, out_others, full_gain_ffn
    )
    dy_other = swap(dy, CORE)
    nf_other = swap(nf_own, CORE)
    hidden, dgate, dup, dnf_own, dnf_send, full_down = ffn_first(
        where, nf_own, nf_other, dy, dy_other, (gate_mine, up_mine, w_ffn_out),
        x_found + x_swapped + y_found + y_swapped,
    )

    dattn, dres, branch, dgain_ffn = out_back(
        dnf_own, swap(dnf_send, CORE), residual, dy, full_gain_ffn, full_out, attn.shape
    )
    dattn_all = lax.all_to_all(dattn, "ctx", 0, 0)
    out_own, out_send, gdown, ggate, gup, gout = ffn_second(
        nf_own, nf_other, dy, dy_other, hidden, dgate, dup, full_down, attn, branch, planes
    )
    out_rows = finish_out(order, lens_and_start, residual, out_own, swap(out_send, CORE), batch)

    wide = units // 2 // model
    part = units // planes // 2
    g_sum = ring_sum(ggate).reshape(wide, 2, 2, quarter, model)
    g_sum = plane_sum(jnp.transpose(g_sum, (2, 1, 0, 3, 4)).reshape(4, wide * quarter, model))
    u_sum = halve_sum(gup.reshape(planes, wide, 2, 2, quarter, model), X, 2)
    u_sum = halve_sum(u_sum, Y, 2).reshape(planes, wide * quarter, model)
    f_sum = halve_sum(gdown.reshape(planes, 2, 2, part // 4, model), Y, 1)
    f_sum = halve_sum(f_sum, X, 1)
    o_sum = halve_sum(gout.reshape(planes, 2, 2, 2, depth // 8, model), CORE, 1)
    o_sum = halve_sum(halve_sum(o_sum, X, 1), Y, 1)
    ufo_sum = ring_sum(jnp.concatenate([u_sum, f_sum, o_sum], axis=1))

    dn, dw, dgain_attn, doffsets = attn_backward(
        meta, gathered, full_gain_attn, w_qkv, offsets,
        query, key, value, attn_full, lse, dattn_all,
    )
    dn = lax.all_to_all(dn, "ctx", 0, 0).reshape(chips, batch, rows, model)
    dtok = finish_tokens(order, dn, flat, dres, full_gain_attn)

    mine_buckets = jnp.einsum(
        "ht,tb->bh", doffsets, hot.astype(F32), precision=lax.Precision.HIGHEST
    )
    buckets = lax.dynamic_update_slice_in_dim(
        jnp.zeros((BUCKETS, HEADS), F32), mine_buckets, chip * chip_heads, 1
    )
    line = jnp.concatenate(
        [
            dgain_attn.reshape(planes, depth),
            dgain_ffn.reshape(planes, depth),
            buckets.reshape(planes, -1),
        ],
        axis=1,
    ).astype(LOW)
    line = jnp.pad(line[:, None, None, :], ((0, 0), (0, 1), (0, 15), (0, 3 * width - line.shape[1])))
    dw = jnp.concatenate([dw.reshape(planes, 2, depth // 2, 3 * width), line], axis=2)
    dw = ring_sum(halve_sum(dw, CORE, 1))
    dw_all = [dw, swap(dw, X), swap(dw, Y), swap(dw, XY)]
    dw_others = swap(jnp.stack(dw_all), CORE)
    grad_query, grad_key, grad_value, sums = unpack_qkv(where, dw_all, dw_others, depth, model)
    grad_gain_attn = sums[0, :depth]
    grad_gain_ffn = sums[0, depth : 2 * depth]
    grad_buckets = sums[0, 2 * depth : small_end].reshape(BUCKETS // planes, HEADS)

    pack = jnp.pad(jnp.concatenate([g_sum, ufo_sum]), ((0, depth // 24), (0, 0)))
    packs = [pack, swap(pack, X), swap(pack, Y), swap(pack, XY)]
    packs = packs + [swap(piece, CORE) for piece in packs]
    grad_gate, grad_up, grad_down, grad_out = unpack(where, packs, depth, units)

    return (
        out_rows, dtok, grad_gain_attn, grad_query, grad_key, grad_value, grad_out, grad_buckets,
        grad_gain_ffn, grad_gate, grad_up, grad_down,
    )


def gelu_tanh(values):
    return (
        0.5
        * values
        * (1.0 + jnp.tanh(0.7978845608028654 * (values + 0.044715 * values * values * values)))
    )


def normalize(values, gain_vec):
    return (
        values * lax.rsqrt(jnp.mean(values * values, axis=-1, keepdims=True) + norm_eps) * gain_vec
    )


def project(values, matrix):
    return jnp.einsum("msd,de->mse", values, matrix, preferred_element_type=jnp.float32)


def back_project(values, matrix):
    return jnp.einsum("mse,de->msd", values, matrix, preferred_element_type=jnp.float32)


def outer_sum(left_rows, right_rows):
    return jnp.einsum("msd,mse->de", left_rows, right_rows, preferred_element_type=jnp.float32)


def split_heads(values):
    return values.reshape(values.shape[0], values.shape[1], HEADS, HEAD_DIM)


def toeplitz_bias(offset_bias, start, query_rows, key_rows):
    span = query_rows + key_rows - 1
    window = lax.dynamic_slice_in_dim(offset_bias, start, span, 1)
    wrapped = jnp.concatenate(
        [
            window[:, query_rows - 1 :],
            jnp.zeros((window.shape[0], 1), jnp.float32),
            window[:, : query_rows - 1],
        ],
        axis=1,
    )
    tiled = jnp.tile(wrapped, (1, query_rows))
    shaped = tiled[:, : query_rows * span].reshape(window.shape[0], query_rows, span)
    return shaped[:, :, :key_rows]


def diagonal_sums(grad_bias, query_rows, key_rows):
    span = query_rows + key_rows - 1
    heads = grad_bias.shape[0]
    padded = jnp.pad(grad_bias, ((0, 0), (0, 0), (0, span - key_rows)))
    flat = jnp.pad(padded.reshape(heads, query_rows * span), ((0, 0), (0, query_rows)))
    slots = jnp.sum(flat.reshape(heads, query_rows, span + 1), axis=1)
    return jnp.concatenate([slots[:, key_rows + 1 :], slots[:, :key_rows]], axis=1)


def block_scores(query_heads, key_heads, pair_bias, key_ok):
    scores = jnp.einsum(
        "mihe,mjhe->mhij", query_heads, key_heads, preferred_element_type=jnp.float32
    )
    scores = scores + pair_bias[None]
    return jnp.where(key_ok[:, None, None, :], scores, -1e30)


def over_blocks(update, make_bias, carried, pieces):
    piece_rows = pieces[0].shape[1]
    block_rows = math.gcd(piece_rows, 256)
    block_count = piece_rows // block_rows

    def advance(block_index, running):
        block_start = block_index * block_rows
        sub_pieces = tuple(
            (
                lax.dynamic_slice_in_dim(member, block_index * block_rows, block_rows, 1)
                for member in pieces
            )
        )
        bias_info = make_bias(block_start, block_rows)
        return update(running, sub_pieces, block_start, slice(None), bias_info)

    return lax.fori_loop(0, block_count, advance, carried)


def per_device_general(
    tokens,
    cotangent,
    lengths,
    bucket_table,
    gain_attn,
    w_query,
    w_key,
    w_value,
    w_out,
    bias_table,
    gain_ffn,
    w_gate,
    w_up,
    w_ffn_out,
):
    shards = (
        gain_attn,
        w_query,
        w_key,
        w_value,
        w_out,
        bias_table,
        gain_ffn,
        w_gate,
        w_up,
        w_ffn_out,
    )
    gathered = (
        lax.all_gather(shards[0], "fsdp", axis=0, tiled=True),
        lax.all_gather(shards[1], "fsdp", axis=0, tiled=True),
        lax.all_gather(shards[2], "fsdp", axis=0, tiled=True),
        lax.all_gather(shards[3], "fsdp", axis=0, tiled=True),
        lax.all_gather(shards[4], "fsdp", axis=0, tiled=True),
        lax.all_gather(shards[5], "fsdp", axis=0, tiled=True),
        lax.all_gather(shards[6], "fsdp", axis=0, tiled=True),
        lax.all_gather(shards[7], "fsdp", axis=0, tiled=True),
        lax.all_gather(shards[8], "fsdp", axis=0, tiled=True),
        lax.all_gather(shards[9], "fsdp", axis=0, tiled=True),
    )
    (
        full_gain_attn,
        full_query,
        full_key,
        full_value,
        full_out,
        full_bias,
        full_gain_ffn,
        full_gate,
        full_up,
        full_ffn_out,
    ) = gathered
    batch_rows, local_rows, model_width = tokens.shape
    seq_len = local_rows * lax.axis_size("ctx")
    table_len = bucket_table.shape[0]
    first_pos = lax.axis_index("ctx") * local_rows
    positions = first_pos + jnp.arange(local_rows, dtype=jnp.int32)
    valid_mask = positions[None, :] < lengths[:, None]
    valid_rows = valid_mask.astype(jnp.float32)
    bucket_hot = bucket_table[:, None] == jnp.arange(BUCKETS, dtype=jnp.int32)[None, :]

    def offset_bias_of(bias_weights):
        return jnp.einsum(
            "tb,bh->ht",
            bucket_hot.astype(jnp.bfloat16),
            bias_weights,
            preferred_element_type=jnp.float32,
        )

    forward_offsets = offset_bias_of(full_bias)

    def keys_bias(offset_bias):

        def keys_make(block_start, block_rows):
            start = block_start - first_pos - (local_rows - 1) + (seq_len - 1)
            return (toeplitz_bias(offset_bias, start, local_rows, block_rows), start)

        return keys_make

    def queries_bias(offset_bias):

        def queries_make(block_start, block_rows):
            start = first_pos - block_start - (block_rows - 1) + (seq_len - 1)
            return (toeplitz_bias(offset_bias, start, block_rows, local_rows), start)

        return queries_make

    tokens_f = tokens.astype(jnp.float32)
    attn_gain = full_gain_attn.astype(jnp.float32)
    normed = normalize(tokens_f, attn_gain).astype(jnp.bfloat16)
    queries = project(normed, full_query).astype(jnp.bfloat16)
    keys_local = project(normed, full_key).astype(jnp.bfloat16)
    values_local = project(normed, full_value).astype(jnp.bfloat16)
    query_heads = split_heads(queries)

    def forward_block(running, sub_pieces, block_start, member_pick, bias_info):
        max_score, row_total, weighted = running
        key_part, value_part = sub_pieces
        key_pos = block_start + jnp.arange(key_part.shape[1], dtype=jnp.int32)
        key_ok = key_pos[None, :] < lengths[:, None]
        scores = block_scores(query_heads, split_heads(key_part), bias_info[0], key_ok)
        new_max = jnp.maximum(max_score, jnp.max(scores, axis=-1))
        shrink = jnp.exp(max_score - new_max)
        weights = jnp.exp(scores - new_max[..., None])
        row_total = row_total * shrink + jnp.sum(weights, axis=-1)
        weighted = weighted * jnp.transpose(shrink, (0, 2, 1))[..., None] + jnp.einsum(
            "mhij,mjhe->mihe",
            weights.astype(jnp.bfloat16),
            split_heads(value_part),
            preferred_element_type=jnp.float32,
        )
        return (new_max, row_total, weighted)

    start_state = (
        jnp.full((batch_rows, HEADS, local_rows), -1e30, jnp.float32),
        jnp.zeros((batch_rows, HEADS, local_rows), jnp.float32),
        jnp.zeros((batch_rows, local_rows, HEADS, HEAD_DIM), jnp.float32),
    )
    max_score, row_total, weighted = over_blocks(
        forward_block,
        keys_bias(forward_offsets),
        start_state,
        (
            lax.all_gather(keys_local, "ctx", axis=1, tiled=True),
            lax.all_gather(values_local, "ctx", axis=1, tiled=True),
        ),
    )
    log_total = max_score + jnp.log(row_total)
    attn_full = weighted / jnp.transpose(row_total, (0, 2, 1))[..., None]
    attn_low = attn_full.reshape(batch_rows, local_rows, model_width).astype(jnp.bfloat16)
    residual = tokens_f + project(attn_low, full_out)
    ffn_gain = full_gain_ffn.astype(jnp.float32)
    normed_ffn = normalize(residual, ffn_gain).astype(jnp.bfloat16)
    gate_proj = project(normed_ffn, full_gate)
    up_proj = project(normed_ffn, full_up)
    hidden = (gelu_tanh(gate_proj) * up_proj).astype(jnp.bfloat16)
    result = valid_rows[..., None] * (residual + project(hidden, full_ffn_out))
    output = result.astype(jnp.bfloat16)
    back_weights = (
        lax.all_gather(shards[0], "fsdp", axis=0, tiled=True),
        lax.all_gather(shards[1], "fsdp", axis=0, tiled=True),
        lax.all_gather(shards[2], "fsdp", axis=0, tiled=True),
        lax.all_gather(shards[3], "fsdp", axis=0, tiled=True),
        lax.all_gather(shards[4], "fsdp", axis=0, tiled=True),
        lax.all_gather(shards[5], "fsdp", axis=0, tiled=True),
        lax.all_gather(shards[6], "fsdp", axis=0, tiled=True),
        lax.all_gather(shards[7], "fsdp", axis=0, tiled=True),
        lax.all_gather(shards[8], "fsdp", axis=0, tiled=True),
        lax.all_gather(shards[9], "fsdp", axis=0, tiled=True),
    )
    (
        back_gain_attn,
        back_query,
        back_key,
        back_value,
        back_out,
        back_bias,
        back_gain_ffn,
        back_gate,
        back_up,
        back_ffn_out,
    ) = back_weights
    back_offsets = offset_bias_of(back_bias)
    grad_out = cotangent.astype(jnp.float32) * valid_rows[..., None]
    grad_low = grad_out.astype(jnp.bfloat16)
    grad_w_ffn_out = outer_sum(hidden, grad_low)
    grad_hidden = back_project(grad_low, back_ffn_out)

    def gated_product(gate_in, up_in):
        return gelu_tanh(gate_in) * up_in

    gated_value, gated_back = jax.vjp(gated_product, gate_proj, up_proj)
    grad_gate, grad_up = gated_back(grad_hidden)
    grad_gate = grad_gate.astype(jnp.bfloat16)
    grad_up = grad_up.astype(jnp.bfloat16)
    grad_w_gate = outer_sum(normed_ffn, grad_gate)
    grad_w_up = outer_sum(normed_ffn, grad_up)
    grad_normed_ffn = back_project(grad_gate, back_gate) + back_project(grad_up, back_up)
    norm_value, norm_back = jax.vjp(normalize, residual, back_gain_ffn.astype(jnp.float32))
    grad_resid_part, grad_gain_ffn = norm_back(grad_normed_ffn)
    grad_resid = grad_out + grad_resid_part
    grad_branch = grad_resid.astype(jnp.bfloat16)
    grad_w_out = outer_sum(attn_low, grad_branch)
    grad_attn = back_project(grad_branch, back_out).astype(jnp.bfloat16)
    grad_heads = split_heads(grad_attn)
    delta_row = jnp.einsum(
        "mihe,mihe->mhi", grad_heads, attn_full, preferred_element_type=jnp.float32
    )

    def query_grad_block(running, sub_pieces, block_start, member_pick, bias_info):
        grad_query, grad_offsets = running
        pair_bias, table_start = bias_info
        key_part, value_part = sub_pieces
        key_heads = split_heads(key_part)
        key_pos = block_start + jnp.arange(key_part.shape[1], dtype=jnp.int32)
        key_ok = key_pos[None, :] < lengths[:, None]
        scores = block_scores(query_heads, key_heads, pair_bias, key_ok)
        probabilities = jnp.exp(scores - log_total[..., None])
        grad_probs = jnp.einsum(
            "mihe,mjhe->mhij",
            grad_heads,
            split_heads(value_part),
            preferred_element_type=jnp.float32,
        )
        grad_scores = (probabilities * (grad_probs - delta_row[..., None])).astype(jnp.bfloat16)
        grad_query = grad_query + jnp.einsum(
            "mhij,mjhe->mihe", grad_scores, key_heads, preferred_element_type=jnp.float32
        )
        pair_grad = jnp.sum(grad_scores.astype(jnp.float32), axis=0)
        diag = diagonal_sums(pair_grad, pair_grad.shape[1], pair_grad.shape[2])
        current = lax.dynamic_slice_in_dim(grad_offsets, table_start, diag.shape[1], 1)
        grad_offsets = lax.dynamic_update_slice_in_dim(grad_offsets, current + diag, table_start, 1)
        return (grad_query, grad_offsets)

    query_state = (
        jnp.zeros((batch_rows, local_rows, HEADS, HEAD_DIM), jnp.float32),
        jnp.zeros((HEADS, table_len), jnp.float32),
    )
    grad_query, grad_offsets = over_blocks(
        query_grad_block,
        keys_bias(back_offsets),
        query_state,
        (
            lax.all_gather(keys_local, "ctx", axis=1, tiled=True),
            lax.all_gather(values_local, "ctx", axis=1, tiled=True),
        ),
    )
    grad_buckets = jnp.einsum(
        "ht,tb->bh", grad_offsets, bucket_hot.astype(jnp.float32), precision=lax.Precision.HIGHEST
    )
    stats_lse, stats_delta = (
        lax.all_gather(log_total, "ctx", axis=2, tiled=True),
        lax.all_gather(delta_row, "ctx", axis=2, tiled=True),
    )
    key_heads_local = split_heads(keys_local)
    value_heads_local = split_heads(values_local)

    def key_grad_block(running, sub_pieces, block_start, member_pick, bias_info):
        grad_key, grad_value = running
        query_part, grad_part = sub_pieces
        rows_here = query_part.shape[1]
        query_part_heads = split_heads(query_part)
        grad_part_heads = split_heads(grad_part)
        scores = block_scores(query_part_heads, key_heads_local, bias_info[0], valid_mask)
        lse_part = lax.dynamic_slice_in_dim(stats_lse, block_start, rows_here, 2)
        delta_part = lax.dynamic_slice_in_dim(stats_delta, block_start, rows_here, 2)
        probabilities = jnp.exp(scores - lse_part[..., None])
        grad_value = grad_value + jnp.einsum(
            "mhij,mihe->mjhe",
            probabilities.astype(jnp.bfloat16),
            grad_part_heads,
            preferred_element_type=jnp.float32,
        )
        grad_probs = jnp.einsum(
            "mihe,mjhe->mhij",
            grad_part_heads,
            value_heads_local,
            preferred_element_type=jnp.float32,
        )
        grad_scores = (probabilities * (grad_probs - delta_part[..., None])).astype(jnp.bfloat16)
        grad_key = grad_key + jnp.einsum(
            "mhij,mihe->mjhe", grad_scores, query_part_heads, preferred_element_type=jnp.float32
        )
        return (grad_key, grad_value)

    key_state = (
        jnp.zeros((batch_rows, local_rows, HEADS, HEAD_DIM), jnp.float32),
        jnp.zeros((batch_rows, local_rows, HEADS, HEAD_DIM), jnp.float32),
    )
    grad_key, grad_value = over_blocks(
        key_grad_block,
        queries_bias(back_offsets),
        key_state,
        (
            lax.all_gather(queries, "ctx", axis=1, tiled=True),
            lax.all_gather(grad_attn, "ctx", axis=1, tiled=True),
        ),
    )
    grad_q = grad_query.reshape(batch_rows, local_rows, model_width).astype(jnp.bfloat16)
    grad_k = grad_key.reshape(batch_rows, local_rows, model_width).astype(jnp.bfloat16)
    grad_v = grad_value.reshape(batch_rows, local_rows, model_width).astype(jnp.bfloat16)
    grad_w_query = outer_sum(normed, grad_q)
    grad_w_key = outer_sum(normed, grad_k)
    grad_w_value = outer_sum(normed, grad_v)
    grad_normed = (
        back_project(grad_q, back_query)
        + back_project(grad_k, back_key)
        + back_project(grad_v, back_value)
    )
    attn_norm_value, attn_norm_back = jax.vjp(
        normalize, tokens_f, back_gain_attn.astype(jnp.float32)
    )
    grad_tokens_part, grad_gain_attn = attn_norm_back(grad_normed)
    grad_tokens = grad_resid + grad_tokens_part
    grads = (
        grad_gain_attn,
        grad_w_query,
        grad_w_key,
        grad_w_value,
        grad_w_out,
        grad_buckets,
        grad_gain_ffn,
        grad_w_gate,
        grad_w_up,
        grad_w_ffn_out,
    )
    shard_sums = (
        lax.psum_scatter(grads[0], "fsdp", scatter_dimension=0, tiled=True),
        lax.psum_scatter(grads[1], "fsdp", scatter_dimension=0, tiled=True),
        lax.psum_scatter(grads[2], "fsdp", scatter_dimension=0, tiled=True),
        lax.psum_scatter(grads[3], "fsdp", scatter_dimension=0, tiled=True),
        lax.psum_scatter(grads[4], "fsdp", scatter_dimension=0, tiled=True),
        lax.psum_scatter(grads[5], "fsdp", scatter_dimension=0, tiled=True),
        lax.psum_scatter(grads[6], "fsdp", scatter_dimension=0, tiled=True),
        lax.psum_scatter(grads[7], "fsdp", scatter_dimension=0, tiled=True),
        lax.psum_scatter(grads[8], "fsdp", scatter_dimension=0, tiled=True),
        lax.psum_scatter(grads[9], "fsdp", scatter_dimension=0, tiled=True),
    )
    totals = lax.psum(
        (
            shard_sums[0],
            shard_sums[1],
            shard_sums[2],
            shard_sums[3],
            shard_sums[4],
            shard_sums[5],
            shard_sums[6],
            shard_sums[7],
            shard_sums[8],
            shard_sums[9],
        ),
        "ctx",
    )
    return (output, grad_tokens) + tuple(totals)


def solution(mesh):
    placed = (
        P("fsdp", "ctx", None),
        P("fsdp", "ctx", None),
        P("fsdp"),
        P(),
        P("fsdp"),
        P("fsdp", None),
        P("fsdp", None),
        P("fsdp", None),
        P("fsdp", None),
        P("fsdp", None),
        P("fsdp"),
        P("fsdp", None),
        P("fsdp", None),
        P("fsdp", None),
    )
    plane = mesh.shape["ctx"] == 8 and mesh.shape["fsdp"] == 4
    return jax.shard_map(
        per_device_plane if plane else per_device_general,
        mesh=mesh,
        in_specs=placed,
        out_specs=(
            P("fsdp", "ctx", None),
            P("fsdp", "ctx", None),
            P("fsdp"),
            P("fsdp", None),
            P("fsdp", None),
            P("fsdp", None),
            P("fsdp", None),
            P("fsdp", None),
            P("fsdp"),
            P("fsdp", None),
            P("fsdp", None),
            P("fsdp", None),
        ),
        check_vma=False,
    )
```

```python
import jax
import jax.numpy as jnp
import math
from jax import lax
from jax.experimental import pallas as pl
from jax.experimental.pallas import tpu as pltpu
from jax.sharding import PartitionSpec as P

HEADS = 12
HEAD_DIM = 64
BUCKETS = 32
BLOCK = 256
TILE = 256
VMEM_BYTES = 56 * 1024 * 1024
COST = 0.5

norm_eps = 1e-06
F32 = jnp.float32
LOW = jnp.bfloat16
NN = (((1,), (0,)), ((), ()))
NT = (((1,), (1,)), ((), ()))
TN = (((0,), (0,)), ((), ()))
SMEM = pl.BlockSpec(memory_space=pltpu.SMEM)
ANY = pl.BlockSpec(memory_space=pl.ANY)


def dot(left, right, dims=NN):
    return lax.dot_general(left, right, dims, preferred_element_type=F32)


def shape_of(dims, kind):
    return jax.ShapeDtypeStruct(dims, kind)


def params(limit=VMEM_BYTES):
    return pltpu.CompilerParams(vmem_limit_bytes=limit)


def cost(flops, moved, exps=0):
    return pl.CostEstimate(
        flops=int(flops * COST), bytes_accessed=int(moved * COST), transcendentals=int(exps)
    )


def block_rows(index, rows=BLOCK):
    return pl.ds(pl.multiple_of(index * rows, rows), rows)


def rms_rows(rows_f):
    return lax.rsqrt(jnp.mean(rows_f * rows_f, axis=-1, keepdims=True) + norm_eps)


def pack_kernel(
    where_ref, gate_ref, up_ref, down_ref, out_ref, q_ref, k_ref, v_ref, small_ref,
    gate_mine_ref, up_mine_ref, ffn_ref, qkv_ref, early_ref,
):
    chip, core = where_ref[0], where_ref[1]
    x_side, y_side = chip % 2, chip // 2
    wide, depth, model = gate_mine_ref.shape
    planes = gate_ref.shape[1] // model
    part = gate_ref.shape[1] // planes // 2
    slab = depth // 2
    for plane in range(planes):
        columns = pl.ds(pl.multiple_of(plane * 2 * part + core * part, 128), part)
        half, at = divmod(plane * part, model)
        gate_mine_ref[half, :, at : at + part] = gate_ref[:, columns]
        up_mine_ref[half, :, at : at + part] = up_ref[:, columns]
    quarter = part // 4
    x_rows, y_rows = block_rows(x_side, slab), block_rows(y_side, slab)
    y_start = wide * slab + quarter
    for half in range(wide):
        ffn_ref[half * slab : (half + 1) * slab, :] = gate_mine_ref[half, x_rows, :]
        at = y_start + half * slab
        ffn_ref[at : at + slab, :] = up_mine_ref[half, y_rows, :]
    x_down = pl.ds(pl.multiple_of(core * part + x_side * quarter, quarter), quarter)
    y_down = pl.ds(pl.multiple_of(core * part + 2 * quarter + y_side * quarter, quarter), quarter)
    ffn_ref[wide * slab : y_start, :] = down_ref[x_down, :]
    ffn_ref[y_start + wide * slab :, :] = down_ref[y_down, :]
    early_ref[slab : 2 * slab, :] = out_ref[block_rows(core, slab), :]
    early_ref[2 * slab :, :] = small_ref[...]
    width = model // 4
    for owner in range(4):

        @pl.when(chip == owner)
        def _(owner=owner):
            lanes = slice(owner * width, (owner + 1) * width)
            qkv_ref[:, :width] = q_ref[:, lanes]
            qkv_ref[:, width : 2 * width] = k_ref[:, lanes]
            qkv_ref[:, 2 * width : 3 * width] = v_ref[:, lanes]
            qkv_ref[:, 3 * width :] = jnp.zeros((depth, width), LOW)

    early_ref[:slab, :] = qkv_ref[block_rows(core, slab), :]


def pack_weights(where, gate, up, down, out, query, key, value, small):
    depth, units = gate.shape
    model = query.shape[1]
    planes = model // depth
    wide = units // 2 // model
    part = units // planes // 2
    vmem = pl.BlockSpec(memory_space=pltpu.VMEM)
    return pl.pallas_call(
        pack_kernel,
        in_specs=[SMEM] + [vmem] * 8,
        out_specs=[vmem] * 5,
        out_shape=[
            shape_of((wide, depth, model), LOW),
            shape_of((wide, depth, model), LOW),
            shape_of((wide * depth + part // 2, model), LOW),
            shape_of((depth, model), LOW),
            shape_of((depth + small.shape[0], model), LOW),
        ],
        compiler_params=params(),
        cost_estimate=cost(0, 16e6),
        name="pack_weights",
    )(where, gate, up, down, out, query, key, value, small)


def prepare_kernel(order_ref, lens_ref, tok_ref, cot_ref, send_ref, local_ref, dy_ref):
    slot = pl.program_id(0)
    rows = tok_ref[0]
    for chip in range(send_ref.shape[0]):
        send_ref[chip, 0] = rows
    local_ref[...] = rows
    place_in = lax.broadcasted_iota(jnp.int32, rows.shape, 0) + lens_ref[lens_ref.shape[0] - 1]
    grads = cot_ref[0].astype(F32)
    dy_ref[...] = jnp.where(place_in < lens_ref[slot], grads, 0.0).astype(LOW)


def prepare(order, lens_and_start, tokens, cotangent, chips):
    batch, rows, model = tokens.shape
    by_order = pl.BlockSpec((1, rows, model), lambda s, order, lens: (order[s], 0, 0))
    in_order = pl.BlockSpec((rows, model), lambda s, order, lens: (s, 0))
    return pl.pallas_call(
        prepare_kernel,
        grid_spec=pltpu.PrefetchScalarGridSpec(
            num_scalar_prefetch=2,
            grid=(batch,),
            in_specs=[by_order, by_order],
            out_specs=[
                pl.BlockSpec((chips, 1, rows, model), lambda s, order, lens: (0, s, 0, 0)),
                in_order,
                in_order,
            ],
        ),
        out_shape=[
            shape_of((chips, batch, rows, model), LOW),
            shape_of((batch * rows, model), LOW),
            shape_of((batch * rows, model), LOW),
        ],
        compiler_params=params(),
        cost_estimate=cost(0, 8e6),
        name="prepare",
    )(order, lens_and_start, tokens, cotangent)


def build_bias(offsets_ref, bias_ref):
    heads, _, width = bias_ref.shape
    span = offsets_ref.shape[1]
    for head in range(heads):
        line = jnp.broadcast_to(offsets_ref[head : head + 1, :], (8, span))
        for group in range(BLOCK // 8):
            turned = pltpu.roll(
                line, (group * 8 - (BLOCK - 1)) % span, 1, stride=1, stride_axis=0
            )
            bias_ref[head, group * 8 : group * 8 + 8, :] = turned[:, :width]


def fold_diagonals(bias_grad_ref, offsets_grad_ref):
    heads, _, width = bias_grad_ref.shape
    span = offsets_grad_ref.shape[1]
    for head in range(heads):
        total = jnp.zeros((8, span), F32)
        for group in range(BLOCK // 8):
            rows = bias_grad_ref[head, group * 8 : group * 8 + 8, :]
            wide = jnp.concatenate([rows, jnp.zeros((8, span - width), F32)], axis=1)
            total = total + pltpu.roll(wide, (BLOCK - 8 - group * 8) % span, 1)
        line = jnp.zeros((1, span), F32)
        for row in range(8):
            line = line + pltpu.roll(total, (7 - row) % span, 1)[row : row + 1, :]
        offsets_grad_ref[head : head + 1, :] = line


def kept_scores(scores, column, length, count):
    wide = count * BLOCK
    tail = jnp.where(column < length - (wide - BLOCK), scores[:, wide - BLOCK :], -1e30)
    if count == 1:
        return tail
    return jnp.concatenate([scores[:, : wide - BLOCK], tail], axis=1)


def token_block(tok_ref, index):
    pieces, _, rows, model = tok_ref.shape
    parts = BLOCK // rows
    return tok_ref[pl.ds(index * parts, parts), 0].reshape(BLOCK, model)


def attn_forward_kernel(
    meta_ref, tok_ref, gain_ref, w0_ref, w1_ref, w2_ref, w3_ref, others_ref, off_ref,
    ot_ref, of_ref, lse_ref, q_ref, k_ref, v_ref, w_ref,
    bias_ref, vm_ref,
):
    slot = pl.program_id(0)
    pieces, _, piece_rows, model = tok_ref.shape
    blocks = pieces * piece_rows // BLOCK
    width = w_ref.shape[2]
    per_chip = width // HEAD_DIM
    length = meta_ref[slot]
    used = (length + BLOCK - 1) // BLOCK
    parts = BLOCK // piece_rows

    @pl.when(slot == 0)
    def _():
        build_bias(off_ref, bias_ref)
        depth = w0_ref.shape[0]
        planes, slab = model // depth, depth // 2
        plane, core = meta_ref[2], meta_ref[3]
        for kind in range(3):
            lanes = slice(kind * width, (kind + 1) * width)
            w_ref[kind, block_rows(plane, depth), :] = w0_ref[:, lanes]
            for back, piece_ref in enumerate((w1_ref, w2_ref, w3_ref)):
                owner = lax.rem(plane + planes - 1 - back, planes)
                w_ref[kind, block_rows(owner * 2 + core, slab), :] = piece_ref[:slab, lanes]
                w_ref[kind, block_rows(owner * 2 + 1 - core, slab), :] = others_ref[
                    back, :slab, lanes
                ]

    owner = lax.broadcasted_iota(jnp.int32, (BLOCK, width), 1) // HEAD_DIM
    column = lax.broadcasted_iota(jnp.int32, (BLOCK, BLOCK), 1)
    nothing = jnp.zeros((BLOCK, width), LOW)

    def project(index, carry):
        rows = block_rows(index)
        rows_f = token_block(tok_ref, index).astype(F32)
        normed = (rows_f * rms_rows(rows_f) * gain_ref[...]).astype(LOW)
        q_ref[0, rows, :] = dot(normed, w_ref[0]).astype(LOW)
        k_ref[0, rows, :] = dot(normed, w_ref[1]).astype(LOW)
        val = dot(normed, w_ref[2]).astype(LOW)
        v_ref[0, rows, :] = val
        for head in range(per_chip):
            vm_ref[head, rows, :] = jnp.where(owner == head, val, nothing)
        return carry

    lax.fori_loop(0, used, project, 0)

    def attend(index, carry):
        rows = block_rows(index)
        query = q_ref[0, rows, :]
        start = pl.multiple_of((blocks - 1 - index) * BLOCK, BLOCK)
        for count in range(1, blocks + 1):

            @pl.when(used == count)
            def _(count=count):
                wide = count * BLOCK
                total = jnp.zeros((BLOCK, width), F32)
                for head in range(per_chip):
                    mine = jnp.where(owner == head, query, nothing)
                    scores = dot(mine, k_ref[0, :wide, :], NT)
                    scores = scores + bias_ref[head, :, pl.ds(start, wide)]
                    scores = kept_scores(scores, column, length, count)
                    top = jnp.max(scores, axis=-1, keepdims=True)
                    weights = jnp.exp(scores - top)
                    row_total = jnp.sum(weights, axis=-1, keepdims=True)
                    probs = (weights * (1.0 / row_total)).astype(LOW)
                    total = total + dot(probs, vm_ref[head, :wide, :])
                    lse_ref[0, head, rows, :] = jnp.broadcast_to(
                        top + jnp.log(row_total), (BLOCK, 128)
                    )
                of_ref[0, rows, :] = total
                turned = jnp.transpose(total.astype(LOW))
                for piece in range(parts):
                    lanes = slice(piece * piece_rows, (piece + 1) * piece_rows)
                    ot_ref[index * parts + piece, 0] = turned[:, lanes]

        return carry

    lax.fori_loop(0, used, attend, 0)

    def clear(index, carry):
        ot_ref[pl.ds(index * parts, parts), 0] = jnp.zeros((parts, width, piece_rows), LOW)
        return carry

    lax.fori_loop(used, blocks, clear, 0)


def attn_forward(meta, tokens, gain, own, early, others, offsets):
    pieces, slots, rows, model = tokens.shape
    width = model // 4
    per_chip = width // HEAD_DIM
    seq = pieces * rows
    lane_rows = pl.BlockSpec((1, seq, width), lambda s: (s, 0, 0))
    by_slot = lambda s: (0, s, 0, 0)
    once = lambda s: (0, 0, 0)
    flat = lambda s: (0, 0)
    return pl.pallas_call(
        attn_forward_kernel,
        grid=(slots,),
        in_specs=[
            SMEM,
            pl.BlockSpec((pieces, 1, rows, model), by_slot),
            pl.BlockSpec((1, model), lambda s: (0, 0)),
        ]
        + [pl.BlockSpec(own.shape, flat)]
        + [pl.BlockSpec(early[0].shape, flat)] * 3
        + [pl.BlockSpec(others.shape, once), pl.BlockSpec(offsets.shape, flat)],
        out_specs=[
            pl.BlockSpec((pieces, 1, width, rows), by_slot),
            lane_rows,
            pl.BlockSpec((1, per_chip, seq, 128), lambda s: (s, 0, 0, 0)),
            lane_rows,
            lane_rows,
            lane_rows,
            pl.BlockSpec((3, model, width), once),
        ],
        out_shape=[
            shape_of((pieces, slots, width, rows), LOW),
            shape_of((slots, seq, width), F32),
            shape_of((slots, per_chip, seq, 128), F32),
            shape_of((slots, seq, width), LOW),
            shape_of((slots, seq, width), LOW),
            shape_of((slots, seq, width), LOW),
            shape_of((3, model, width), LOW),
        ],
        scratch_shapes=[
            pltpu.VMEM((per_chip, BLOCK, 2 * seq - BLOCK), F32),
            pltpu.VMEM((per_chip, seq, width), LOW),
        ],
        compiler_params=params(),
        cost_estimate=cost(
            4 * slots * seq * (model * 3 * width + 2 * seq * 256 * per_chip),
            slots * seq * 2 * (model + 8 * width),
        ),
        name="attn_forward",
    )(meta, tokens, gain, own, *early, others, offsets)


def attn_backward_kernel(
    meta_ref, tok_ref, gain_ref, w_ref, off_ref, q_ref, k_ref, v_ref, of_ref, lse_ref, dot_ref,
    dn_ref, dw_keep_ref, dw_send_ref, dgain_ref, doff_ref,
    bias_ref, dbias_ref, km_ref, dq_ref, dkt_ref, dvt_ref, dwt_ref, dw_ref,
):
    slot = pl.program_id(0)
    pieces, _, piece_rows, model = tok_ref.shape
    blocks = pieces * piece_rows // BLOCK
    width = w_ref.shape[2]
    per_chip = width // HEAD_DIM
    length = meta_ref[slot]
    used = (length + BLOCK - 1) // BLOCK
    parts = BLOCK // piece_rows

    @pl.when(slot == 0)
    def _():
        build_bias(off_ref, bias_ref)
        dbias_ref[...] = jnp.zeros_like(dbias_ref)
        dwt_ref[...] = jnp.zeros_like(dwt_ref)
        dgain_ref[...] = jnp.zeros_like(dgain_ref)

    dkt_ref[...] = jnp.zeros_like(dkt_ref)
    dvt_ref[...] = jnp.zeros_like(dvt_ref)
    owner = lax.broadcasted_iota(jnp.int32, (BLOCK, width), 1) // HEAD_DIM
    column = lax.broadcasted_iota(jnp.int32, (BLOCK, BLOCK), 1)
    nothing = jnp.zeros((BLOCK, width), LOW)

    def split_keys(index, carry):
        rows = block_rows(index)
        key = k_ref[0, rows, :]
        for head in range(per_chip):
            km_ref[head, rows, :] = jnp.where(owner == head, key, nothing)
        return carry

    lax.fori_loop(0, used, split_keys, 0)

    def attend(index, carry):
        rows = block_rows(index)
        query = q_ref[0, rows, :]
        query_t = jnp.transpose(query)
        grad_t = jnp.concatenate(
            [dot_ref[index * parts + piece, 0] for piece in range(parts)], axis=1
        )
        grad = jnp.transpose(grad_t)
        product = grad.astype(F32) * of_ref[0, rows, :]
        start = pl.multiple_of((blocks - 1 - index) * BLOCK, BLOCK)
        for count in range(1, blocks + 1):

            @pl.when(used == count)
            def _(count=count):
                wide = count * BLOCK
                grad_query = jnp.zeros((BLOCK, width), F32)
                for head in range(per_chip):
                    lanes = slice(head * HEAD_DIM, (head + 1) * HEAD_DIM)
                    mine = jnp.where(owner == head, query, nothing)
                    scores = dot(mine, k_ref[0, :wide, :], NT)
                    scores = scores + bias_ref[head, :, pl.ds(start, wide)]
                    scores = kept_scores(scores, column, length, count)
                    probs = jnp.exp(scores - lse_ref[0, head, rows, :][:, :1])
                    delta = jnp.sum(
                        jnp.where(owner == head, product, 0.0), axis=-1, keepdims=True
                    )
                    grad_mine = jnp.where(owner == head, grad, nothing)
                    grad_probs = dot(grad_mine, v_ref[0, :wide, :], NT)
                    grad_scores = (probs * (grad_probs - delta)).astype(LOW)
                    grad_query = grad_query + dot(grad_scores, km_ref[head, :wide, :])
                    dkt_ref[lanes, :wide] += dot(query_t[lanes, :], grad_scores)
                    dvt_ref[lanes, :wide] += dot(grad_t[lanes, :], probs.astype(LOW))
                    dbias_ref[head, :, pl.ds(start, wide)] += grad_scores.astype(F32)
                dq_ref[rows, :] = grad_query.astype(LOW)

        return carry

    lax.fori_loop(0, used, attend, 0)

    def finish(index, carry):
        rows = block_rows(index)
        grad_query = dq_ref[rows, :]
        key_t = dkt_ref[:, rows].astype(LOW)
        value_t = dvt_ref[:, rows].astype(LOW)
        rows_f = token_block(tok_ref, index).astype(F32)
        unit = rows_f * rms_rows(rows_f)
        normed = (unit * gain_ref[...]).astype(LOW)
        grad_normed = (
            dot(grad_query, w_ref[0], NT)
            + dot(jnp.transpose(key_t), w_ref[1], NT)
            + dot(jnp.transpose(value_t), w_ref[2], NT)
        )
        dgain_ref[...] += jnp.sum(grad_normed * unit, axis=0, keepdims=True)
        dn_ref[pl.ds(index * parts, parts), 0] = grad_normed.astype(LOW).reshape(
            parts, piece_rows, model
        )
        dwt_ref[0:width, :] += dot(jnp.transpose(grad_query), normed)
        dwt_ref[width : 2 * width, :] += dot(key_t, normed)
        dwt_ref[2 * width :, :] += dot(value_t, normed)
        return carry

    lax.fori_loop(0, used, finish, 0)

    def clear(index, carry):
        dn_ref[pl.ds(index * parts, parts), 0] = jnp.zeros((parts, piece_rows, model), LOW)
        return carry

    lax.fori_loop(used, blocks, clear, 0)

    @pl.when(slot == pl.num_programs(0) - 1)
    def _():
        fold_diagonals(dbias_ref, doff_ref)
        dw_ref[...] = jnp.transpose(dwt_ref[...].astype(LOW))
        core = meta_ref[3]
        planes, slab, _ = dw_keep_ref.shape
        for plane in range(planes):
            dw_keep_ref[plane] = dw_ref[block_rows(2 * plane + core, slab), :]
            dw_send_ref[plane] = dw_ref[block_rows(2 * plane + 1 - core, slab), :]


def attn_backward(
    meta, tokens, gain, w_qkv, offsets, query, key, value, attn_full, lse, grad, planes
):
    pieces, slots, rows, model = tokens.shape
    width = w_qkv.shape[2]
    per_chip = width // HEAD_DIM
    seq = pieces * rows
    lane_rows = pl.BlockSpec((1, seq, width), lambda s: (s, 0, 0))
    by_slot = lambda s: (0, s, 0, 0)
    once = lambda s: (0, 0)
    return pl.pallas_call(
        attn_backward_kernel,
        grid=(slots,),
        in_specs=[
            SMEM,
            pl.BlockSpec((pieces, 1, rows, model), by_slot),
            pl.BlockSpec((1, model), once),
            pl.BlockSpec((3, model, width), lambda s: (0, 0, 0)),
            pl.BlockSpec(offsets.shape, once),
            lane_rows,
            lane_rows,
            lane_rows,
            lane_rows,
            pl.BlockSpec((1, per_chip, seq, 128), lambda s: (s, 0, 0, 0)),
            pl.BlockSpec((pieces, 1, width, rows), by_slot),
        ],
        out_specs=[
            pl.BlockSpec((pieces, 1, rows, model), by_slot),
            pl.BlockSpec((planes, model // planes // 2, 3 * width), lambda s: (0, 0, 0)),
            pl.BlockSpec((planes, model // planes // 2, 3 * width), lambda s: (0, 0, 0)),
            pl.BlockSpec((1, model), once),
            pl.BlockSpec(offsets.shape, once),
        ],
        out_shape=[
            shape_of((pieces, slots, rows, model), LOW),
            shape_of((planes, model // planes // 2, 3 * width), LOW),
            shape_of((planes, model // planes // 2, 3 * width), LOW),
            shape_of((1, model), F32),
            shape_of(offsets.shape, F32),
        ],
        scratch_shapes=[
            pltpu.VMEM((per_chip, BLOCK, 2 * seq - BLOCK), F32),
            pltpu.VMEM((per_chip, BLOCK, 2 * seq - BLOCK), F32),
            pltpu.VMEM((per_chip, seq, width), LOW),
            pltpu.VMEM((seq, width), LOW),
            pltpu.VMEM((width, seq), F32),
            pltpu.VMEM((width, seq), F32),
            pltpu.VMEM((3 * width, model), F32),
            pltpu.VMEM((model, 3 * width), LOW),
        ],
        compiler_params=params(),
        cost_estimate=cost(
            4 * slots * seq * (model * 6 * width + 5 * seq * 256 * per_chip),
            slots * seq * 2 * (2 * model + 12 * width),
        ),
        name="attn_backward",
    )(meta, tokens, gain, w_qkv, offsets, query, key, value, attn_full, lse, grad)


def side_by_side(attn_ref, chip):
    return jnp.concatenate(
        [attn_ref[2 * chip + core, slot] for core in range(2) for slot in range(2)], axis=1
    )


def out_project_kernel(
    where_ref, tok_ref, attn_ref, own_ref, a1_ref, a2_ref, a3_ref, others_ref, gain_ref,
    res_ref, nf_ref, w_ref,
):
    core, plane = where_ref[1], where_ref[2]
    depth = own_ref.shape[0]
    slab = depth // 2
    planes = w_ref.shape[0] // depth
    w_ref[block_rows(plane, depth), :] = own_ref[...]
    for back, piece_ref in enumerate((a1_ref, a2_ref, a3_ref)):
        owner = lax.rem(plane + planes - 1 - back, planes)
        w_ref[block_rows(owner * 2 + core, slab), :] = piece_ref[slab : 2 * slab, :]
        w_ref[block_rows(owner * 2 + 1 - core, slab), :] = others_ref[back, slab : 2 * slab, :]
    chips, width = attn_ref.shape[0] // 2, attn_ref.shape[2]
    total = tok_ref[...].astype(F32)
    for chip in range(chips):
        total = total + dot(
            side_by_side(attn_ref, chip), w_ref[chip * width : (chip + 1) * width, :], TN
        )
    res_ref[...] = total
    nf_ref[...] = (total * rms_rows(total) * gain_ref[...]).astype(LOW)


def out_project(where, tokens, attn, own, pieces, others, gain):
    rows, model = tokens.shape
    vmem = pl.BlockSpec(memory_space=pltpu.VMEM)
    return pl.pallas_call(
        out_project_kernel,
        in_specs=[SMEM] + [vmem] * 8,
        out_specs=[vmem] * 3,
        out_shape=[
            shape_of((rows, model), F32),
            shape_of((rows, model), LOW),
            shape_of((model, model), LOW),
        ],
        compiler_params=params(),
        cost_estimate=cost(4 * rows * model * model, rows * model * 12),
        name="out_project",
    )(where, tokens, attn, own, *pieces, others, gain)


def out_back_kernel(
    where_ref, own_ref, recv_ref, res_ref, dy_ref, gain_ref, w_ref, attn_ref,
    dattn_ref, dres_ref, dgain_ref, keep_ref, send_ref,
    gout_ref,
):
    chips, width, rows = dattn_ref.shape[0] // 2, dattn_ref.shape[2], dattn_ref.shape[3]
    grad = own_ref[...] + recv_ref[...].astype(F32)
    residual = res_ref[...]
    scale = rms_rows(residual)
    unit = residual * scale
    dgain_ref[...] = jnp.sum(grad * unit, axis=0, keepdims=True)
    inner = grad * gain_ref[...]
    dres = dy_ref[...].astype(F32) + scale * (
        inner - unit * jnp.mean(inner * unit, axis=-1, keepdims=True)
    )
    dres_ref[...] = dres
    branch = dres.astype(LOW)
    for chip in range(chips):
        heads = slice(chip * width, (chip + 1) * width)
        part = dot(w_ref[heads, :], branch, NT).astype(LOW)
        for slot in range(4):
            dattn_ref[2 * chip + slot // 2, slot % 2] = part[:, slot * rows : (slot + 1) * rows]
        gout_ref[heads, :] = dot(side_by_side(attn_ref, chip), branch).astype(LOW)
    core = where_ref[1]
    planes, slab, _ = keep_ref.shape
    for plane in range(planes):
        keep_ref[plane] = gout_ref[block_rows(2 * plane + core, slab), :]
        send_ref[plane] = gout_ref[block_rows(2 * plane + 1 - core, slab), :]


def out_back(where, own, recv, residual, dy, gain, w_out, attn, planes):
    rows, model = own.shape
    vmem = pl.BlockSpec(memory_space=pltpu.VMEM)
    half = shape_of((planes, model // planes // 2, model), LOW)
    return pl.pallas_call(
        out_back_kernel,
        in_specs=[SMEM] + [vmem] * 7,
        out_specs=[vmem] * 5,
        out_shape=[
            shape_of(attn.shape, LOW),
            shape_of((rows, model), F32),
            shape_of((1, model), F32),
            half,
            half,
        ],
        scratch_shapes=[pltpu.VMEM((model, model), LOW)],
        compiler_params=params(),
        cost_estimate=cost(8 * rows * model * model, rows * model * 20),
        name="out_back",
    )(where, own, recv, residual, dy, gain, w_out, attn)


def gate_and_slope(gate):
    inner = 0.7978845608028654 * (gate + 0.044715 * gate * gate * gate)
    bent = jnp.tanh(inner)
    half = 0.5 * (1.0 + bent)
    slope = half + 0.5 * gate * (1.0 - bent * bent) * (
        0.7978845608028654 * (1.0 + 3.0 * 0.044715 * gate * gate)
    )
    return gate * half, slope


def ffn_first_kernel(
    where_ref, nf_own_ref, nf_other_ref, dy_own_ref, dy_other_ref,
    gate_own, up_own, down_own, f1, f2, f3, sx1, sx2, sx3, sy1, sy2, sy3,
    hidden_ref, dup_ref, own_ref, other_ref, down_ref, g0_ref, g1_ref, g2_ref, g3_ref,
    gate_ref, up_ref, nf_ref, nft_ref, dy_ref, total_ref, dgate_ref, grad_ref, sems,
):
    step = pl.program_id(0)
    half = nf_own_ref.shape[0]
    chip, core, plane = where_ref[0], where_ref[1], where_ref[2]
    wide, model, _ = gate_ref.shape
    units = down_ref.shape[0]
    tile = hidden_ref.shape[1]
    depth = gate_own.shape[1]
    planes = model // depth
    slab = depth // 2
    part = units // planes
    quarter = part // 4

    @pl.when(step == 0)
    def _():
        copies = []

        def copy(source, target):
            started = pltpu.make_async_copy(source, target, sems.at[len(copies)])
            started.start()
            copies.append(started)

        own_rows = pl.ds(pl.multiple_of(plane * depth, depth), depth)
        for index in range(wide):
            copy(gate_own.at[index], gate_ref.at[index, own_rows, :])
            copy(up_own.at[index], up_ref.at[index, own_rows, :])
        copy(
            down_own.at[pl.ds(pl.multiple_of(core * part, part), part), :],
            down_ref.at[pl.ds(pl.multiple_of(plane * part, part), part), :],
        )
        for back in range(planes - 1):
            owner = lax.rem(plane + planes - 1 - back, planes)
            straight = (f1, f2, f3)[back]
            for along, swapped, weight_ref, side in (
                (0, (sx1, sx2, sx3)[back], gate_ref, lax.rem(chip, 2)),
                (1, (sy1, sy2, sy3)[back], up_ref, chip // 2),
            ):
                skip = along * (wide * slab + quarter)
                for piece, here, first in ((straight, side, skip), (swapped, 1 - side, 0)):
                    at = pl.ds(pl.multiple_of(owner * depth + here * slab, slab), slab)
                    for index in range(wide):
                        copy(
                            piece.at[pl.ds(first + index * slab, slab), :],
                            weight_ref.at[index, at, :],
                        )
                    copy(
                        piece.at[pl.ds(first + wide * slab, quarter), :],
                        down_ref.at[
                            pl.ds(
                                pl.multiple_of(
                                    owner * part + (2 * along + here) * quarter, quarter
                                ),
                                quarter,
                            ),
                            :,
                        ],
                    )
        nf_ref[:half, :] = nf_own_ref[...]
        nf_ref[half:, :] = nf_other_ref[...]
        nft_ref[:, :half] = jnp.transpose(nf_own_ref[...])
        nft_ref[:, half:] = jnp.transpose(nf_other_ref[...])
        dy_ref[:half, :] = dy_own_ref[...]
        dy_ref[half:, :] = dy_other_ref[...]
        total_ref[...] = jnp.zeros_like(total_ref)
        for started in copies:
            started.wait()

    per = model // tile
    index = step // per
    lanes = pl.ds(pl.multiple_of(lax.rem(step, per) * tile, tile), tile)
    gate_w = gate_ref[index, :, lanes]
    up_w = up_ref[index, :, lanes]
    down_w = down_ref[block_rows(step, tile), :]
    for quarter_rows in range(4):
        rows = slice(quarter_rows * half // 2, (quarter_rows + 1) * half // 2)
        nf = nf_ref[rows, :]
        gate = dot(nf, gate_w)
        up = dot(nf, up_w)
        dhidden = dot(dy_ref[rows, :], down_w, NT)
        bent, slope = gate_and_slope(gate)
        hidden_ref[rows, :] = (bent * up).astype(LOW)
        dgate = (dhidden * up * slope).astype(LOW)
        dup = (dhidden * bent).astype(LOW)
        dgate_ref[rows, :] = dgate
        dup_ref[rows, :] = dup
        total_ref[rows, :] += dot(dgate, gate_w, NT) + dot(dup, up_w, NT)

    grad_ref[...] = dot(nft_ref[...], dgate_ref[...]).astype(LOW)
    for away, out_ref in enumerate((g0_ref, g1_ref, g2_ref, g3_ref)):
        out_ref[0] = grad_ref[block_rows(lax.rem(plane + away, planes), depth), :]

    @pl.when(step == pl.num_programs(0) - 1)
    def _():
        own_ref[...] = total_ref[:half, :]
        other_ref[...] = total_ref[half:, :].astype(LOW)


def ffn_first(where, nf_own, nf_other, dy_own, dy_other, own_weights, pieces, tile=TILE):
    half, model = nf_own.shape
    wide, depth, _ = own_weights[0].shape
    units = wide * model
    per = model // tile
    whole = pl.BlockSpec((half, model), lambda t: (0, 0))
    lane_tile = pl.BlockSpec((2 * half, tile), lambda t: (0, t))
    grad_tile = pl.BlockSpec((1, depth, tile), lambda t: (t // per, 0, t % per))
    copies = 2 * wide + 1 + 3 * 4 * (wide + 1)
    return pl.pallas_call(
        ffn_first_kernel,
        grid=(units // tile,),
        in_specs=[SMEM, whole, whole, whole, whole] + [ANY] * 12,
        out_specs=[
            lane_tile, lane_tile, whole, whole,
            pl.BlockSpec((units, model), lambda t: (0, 0)),
        ]
        + [grad_tile] * 4,
        out_shape=[
            shape_of((2 * half, units), LOW),
            shape_of((2 * half, units), LOW),
            shape_of((half, model), F32),
            shape_of((half, model), LOW),
            shape_of((units, model), LOW),
        ]
        + [shape_of((wide, depth, model), LOW)] * 4,
        scratch_shapes=[
            pltpu.VMEM((wide, model, model), LOW),
            pltpu.VMEM((wide, model, model), LOW),
            pltpu.VMEM((2 * half, model), LOW),
            pltpu.VMEM((model, 2 * half), LOW),
            pltpu.VMEM((2 * half, model), LOW),
            pltpu.VMEM((2 * half, model), F32),
            pltpu.VMEM((2 * half, tile), LOW),
            pltpu.VMEM((model, tile), LOW),
            pltpu.SemaphoreType.DMA((copies,)),
        ],
        compiler_params=params(),
        cost_estimate=cost(
            2 * 2 * 6 * 2 * half * model * units,
            6 * model * units + 12 * half * units + 20 * half * model,
        ),
        name="ffn_first",
    )(where, nf_own, nf_other, dy_own, dy_other, *own_weights, *pieces)


def ffn_second_kernel(
    where_ref, nf_own_ref, nf_other_ref, dy_own_ref, dy_other_ref, hidden_ref, dup_ref, down_ref,
    own_ref, other_ref, u_keep_ref, u_send_ref, f_keep_ref, f_send_ref,
    nft_ref, dy_ref, total_ref, grad_ref, gdown_ref,
):
    step = pl.program_id(0)
    half = nf_own_ref.shape[0]
    chip = where_ref[0]
    x_side, y_side = lax.rem(chip, 2), chip // 2
    planes, _, slab, tile = u_keep_ref.shape

    @pl.when(step == 0)
    def _():
        nft_ref[:, :half] = jnp.transpose(nf_own_ref[...])
        nft_ref[:, half:] = jnp.transpose(nf_other_ref[...])
        dy_ref[:half, :] = dy_own_ref[...]
        dy_ref[half:, :] = dy_other_ref[...]
        total_ref[...] = jnp.zeros_like(total_ref)

    hidden = hidden_ref[...]
    grad_ref[...] = dot(nft_ref[...], dup_ref[...]).astype(LOW)
    for plane in range(planes):
        u_keep_ref[plane, 0] = grad_ref[block_rows(2 * plane + x_side, slab), :]
        u_send_ref[plane, 0] = grad_ref[block_rows(2 * plane + 1 - x_side, slab), :]
    gdown_ref[block_rows(step, tile), :] = dot(jnp.transpose(hidden), dy_ref[...]).astype(LOW)
    total_ref[...] += dot(hidden, down_ref[...])

    @pl.when(step == pl.num_programs(0) - 1)
    def _():
        own_ref[...] = total_ref[:half, :]
        other_ref[...] = total_ref[half:, :].astype(LOW)
        rows = f_keep_ref.shape[1]
        for plane in range(planes):
            f_keep_ref[plane] = gdown_ref[block_rows(2 * plane + y_side, rows), :]
            f_send_ref[plane] = gdown_ref[block_rows(2 * plane + 1 - y_side, rows), :]


def ffn_second(
    where, nf_own, nf_other, dy_own, dy_other, hidden, dup, w_down, planes, tile=TILE
):
    half, model = nf_own.shape
    units = hidden.shape[1]
    wide, slab, rows = units // model, model // planes // 2, units // planes // 2
    per = model // tile
    whole = pl.BlockSpec((half, model), lambda t: (0, 0))
    lane_tile = pl.BlockSpec((2 * half, tile), lambda t: (0, t))
    row_tile = pl.BlockSpec((tile, model), lambda t: (t, 0))
    up_tile = pl.BlockSpec((planes, 1, slab, tile), lambda t: (0, t // per, 0, t % per))
    down_whole = pl.BlockSpec((planes, rows, model), lambda t: (0, 0, 0))
    return pl.pallas_call(
        ffn_second_kernel,
        grid=(units // tile,),
        in_specs=[SMEM, whole, whole, whole, whole, lane_tile, lane_tile, row_tile],
        out_specs=[whole, whole, up_tile, up_tile, down_whole, down_whole],
        out_shape=[
            shape_of((half, model), F32),
            shape_of((half, model), LOW),
            shape_of((planes, wide, slab, model), LOW),
            shape_of((planes, wide, slab, model), LOW),
            shape_of((planes, rows, model), LOW),
            shape_of((planes, rows, model), LOW),
        ],
        scratch_shapes=[
            pltpu.VMEM((model, 2 * half), LOW),
            pltpu.VMEM((2 * half, model), LOW),
            pltpu.VMEM((2 * half, model), F32),
            pltpu.VMEM((model, tile), LOW),
            pltpu.VMEM((units, model), LOW),
        ],
        compiler_params=params(),
        cost_estimate=cost(
            2 * 2 * 3 * 2 * half * model * units,
            8 * model * units + 12 * half * units + 20 * half * model,
        ),
        name="ffn_second",
    )(where, nf_own, nf_other, dy_own, dy_other, hidden, dup, w_down)


def finish_out_kernel(order_ref, lens_ref, res_ref, own_ref, recv_ref, out_ref):
    slot = pl.program_id(0)
    total = res_ref[...] + own_ref[...] + recv_ref[...].astype(F32)
    place_in = lax.broadcasted_iota(jnp.int32, total.shape, 0) + lens_ref[lens_ref.shape[0] - 1]
    out_ref[0] = jnp.where(place_in < lens_ref[slot], total, 0.0).astype(LOW)


def finish_out(order, lens_and_start, residual, own, recv, batch):
    rows, model = residual.shape[0] // batch, residual.shape[1]
    in_order = pl.BlockSpec((rows, model), lambda s, order, lens: (s, 0))
    return pl.pallas_call(
        finish_out_kernel,
        grid_spec=pltpu.PrefetchScalarGridSpec(
            num_scalar_prefetch=2,
            grid=(batch,),
            in_specs=[in_order, in_order, in_order],
            out_specs=pl.BlockSpec((1, rows, model), lambda s, order, lens: (order[s], 0, 0)),
        ),
        out_shape=shape_of((batch, rows, model), LOW),
        compiler_params=params(),
        cost_estimate=cost(0, 6e6),
        name="finish_out",
    )(order, lens_and_start, residual, own, recv)


def finish_tokens_kernel(order_ref, dn_ref, tok_ref, dres_ref, gain_ref, out_ref):
    grad = dn_ref[0, 0].astype(F32)
    for chip in range(1, dn_ref.shape[0]):
        grad = grad + dn_ref[chip, 0].astype(F32)
    rows_f = tok_ref[...].astype(F32)
    scale = rms_rows(rows_f)
    unit = rows_f * scale
    inner = grad * gain_ref[...]
    out_ref[0] = dres_ref[...] + scale * (
        inner - unit * jnp.mean(inner * unit, axis=-1, keepdims=True)
    )


def finish_tokens(order, dn, tokens, dres, gain):
    chips, batch, rows, model = dn.shape
    in_order = pl.BlockSpec((rows, model), lambda s, order: (s, 0))
    return pl.pallas_call(
        finish_tokens_kernel,
        grid_spec=pltpu.PrefetchScalarGridSpec(
            num_scalar_prefetch=1,
            grid=(batch,),
            in_specs=[
                pl.BlockSpec((chips, 1, rows, model), lambda s, order: (0, s, 0, 0)),
                in_order,
                in_order,
                pl.BlockSpec((1, model), lambda s, order: (0, 0)),
            ],
            out_specs=pl.BlockSpec((1, rows, model), lambda s, order: (order[s], 0, 0)),
        ),
        out_shape=shape_of((batch, rows, model), F32),
        compiler_params=params(),
        cost_estimate=cost(0, 10e6),
        name="finish_tokens",
    )(order, dn, tokens, dres, gain)


def unpack_kernel(where_ref, *refs):
    piece_refs, (gate_ref, up_ref, down_ref, out_ref) = refs[:8], refs[8:]
    chip, core = where_ref[0], where_ref[1]
    depth, units = gate_ref.shape
    model = down_ref.shape[1]
    part = down_ref.shape[0] // 2
    quarter, tail = depth // 4, depth // 8
    wide = units // 2 // model
    planes = units // 2 // part
    for far in range(8):
        away, other = far % 4, far // 4
        from_core = core if other == 0 else 1 - core
        from_chip = jnp.bitwise_xor(chip, away)
        from_x, from_y = lax.rem(from_chip, 2), from_chip // 2
        piece_ref = piece_refs[far]
        gate_rows = block_rows(from_x * 2 + from_y, quarter)
        for plane in range(planes):
            index, at = divmod(plane * part, model)
            lanes = pl.ds(pl.multiple_of(plane * 2 * part + from_core * part, 128), part)
            rows = slice(index * quarter, (index + 1) * quarter)
            gate_ref[gate_rows, lanes] = piece_ref[rows, at : at + part].astype(F32)
            rows = slice((wide + index) * quarter, (wide + index + 1) * quarter)
            up_ref[gate_rows, lanes] = piece_ref[rows, at : at + part].astype(F32)
        down_at = 2 * wide * quarter
        rows = part // 4
        down_ref[block_rows(from_core * 4 + from_y * 2 + from_x, rows), :] = piece_ref[
            down_at : down_at + rows, :
        ].astype(F32)
        out_ref[block_rows(from_core * 4 + from_x * 2 + from_y, tail), :] = piece_ref[
            down_at + rows :, :
        ].astype(F32)[:tail, :]


def unpack(where, pieces, depth, units):
    model = pieces[0].shape[1]
    planes = model // depth
    vmem = pl.BlockSpec(memory_space=pltpu.VMEM)
    return pl.pallas_call(
        unpack_kernel,
        in_specs=[SMEM] + [vmem] * 8,
        out_specs=[vmem] * 4,
        out_shape=[
            shape_of((depth, units), F32),
            shape_of((depth, units), F32),
            shape_of((units // planes, model), F32),
            shape_of((depth, model), F32),
        ],
        compiler_params=params(),
        cost_estimate=cost(0, 24e6),
        name="unpack",
    )(where, *pieces)


def unpack_qkv_kernel(where_ref, *refs):
    mine_refs, others_ref = refs[:4], refs[4]
    out_refs, small_ref = refs[5:8], refs[8]
    chip, core = where_ref[0], where_ref[1]
    width = mine_refs[0].shape[1] // 3
    slab = out_refs[0].shape[0] // 2
    for home in range(4):

        @pl.when(chip == home)
        def _(home=home):
            for away in range(4):
                lanes = slice((home ^ away) * width, ((home ^ away) + 1) * width)
                for kind in range(3):
                    from_lanes = slice(kind * width, (kind + 1) * width)
                    out_refs[kind][block_rows(core, slab), lanes] = mine_refs[away][
                        :slab, from_lanes
                    ].astype(F32)
                    out_refs[kind][block_rows(1 - core, slab), lanes] = others_ref[
                        away, :slab, from_lanes
                    ].astype(F32)

    mine = mine_refs[0][slab:, :].astype(F32)
    other = others_ref[0, slab:, :].astype(F32)
    for away in range(1, 4):
        mine = mine + mine_refs[away][slab:, :].astype(F32)
        other = other + others_ref[away, slab:, :].astype(F32)
    small_ref[...] = mine + other


def unpack_qkv(where, mine, others, depth, model):
    vmem = pl.BlockSpec(memory_space=pltpu.VMEM)
    rows, lanes = mine[0].shape
    return pl.pallas_call(
        unpack_qkv_kernel,
        in_specs=[SMEM] + [vmem] * 5,
        out_specs=[vmem] * 4,
        out_shape=[shape_of((depth, model), F32)] * 3 + [shape_of((rows - depth // 2, lanes), F32)],
        compiler_params=params(),
        cost_estimate=cost(0, 4e6),
        name="unpack_qkv",
    )(where, *mine, others)


CORE, X, Y, XY = 1, 2, 4, 6


def swap(values, bits):
    count = lax.axis_size("ctx")
    return lax.ppermute(values, "ctx", [(i, i ^ bits) for i in range(count)])


def shift(values, places):
    count = lax.axis_size("fsdp")
    return lax.ppermute(values, "fsdp", [(i, (i + places) % count) for i in range(count)])


def column_pieces(piece):
    one, three = shift(piece, 1), shift(piece, 3)
    return [one, shift(one, 1), three]


def after(values, *others):
    return lax.optimization_barrier((values, *others))[0]


def pick(values, index, axis):
    return lax.dynamic_index_in_dim(values, index, axis, keepdims=False)


def add(*parts):
    total = parts[0].astype(F32)
    for part in parts[1:]:
        total = total + part.astype(F32)
    return total.astype(LOW)


def plane_sum(parts):
    chip = lax.axis_index("ctx") // 2
    found = [pick(part, chip, 0) for part in parts]
    for away, bits in ((1, X), (2, Y), (3, XY)):
        found.append(swap(add(*(pick(part, chip ^ away, 0) for part in parts)), bits))
    return add(*found)


def column_sum(picks):
    return [picks[0]] + [shift(picks[away], away) for away in range(1, len(picks))]


def plane_picks(values):
    count = lax.axis_size("fsdp")
    me = lax.axis_index("fsdp")
    return [pick(values, (me + away) % count, 0) for away in range(count)]


def per_device_plane(
    tokens, cotangent, lengths, bucket_table, gain_attn, w_query, w_key, w_value, w_out,
    bias_table, gain_ffn, w_gate, w_up, w_ffn_out,
):
    batch, rows, model = tokens.shape
    planes = lax.axis_size("fsdp")
    chips = lax.axis_size("ctx") // 2
    me = lax.axis_index("ctx")
    plane = lax.axis_index("fsdp")
    core, chip = me % 2, me // 2
    depth, units = w_gate.shape
    chip_heads = HEADS // chips
    width = chip_heads * HEAD_DIM
    quarter = depth // 4
    where = jnp.stack([chip, core, plane]).astype(jnp.int32)

    entry = jnp.arange(batch, dtype=jnp.int32)
    ahead = (lengths[None, :] > lengths[:, None]) | (
        (lengths[None, :] == lengths[:, None]) & (entry[None, :] < entry[:, None])
    )
    rank = jnp.sum(ahead.astype(jnp.int32), axis=1)
    slot = jnp.where(rank == 0, 0, jnp.where(rank == batch - 1, 1, rank + 1))
    chosen = (slot[None, :] == entry[:, None]).astype(jnp.int32)
    order = jnp.sum(chosen * entry[None, :], axis=1)
    lens = jnp.sum(chosen * lengths[None, :], axis=1)
    lens_and_start = jnp.concatenate([lens, (me * rows)[None].astype(jnp.int32)])
    meta = jnp.concatenate([lax.dynamic_slice_in_dim(lens, 2 * core, 2), plane[None], core[None]])

    send, flat, dy = prepare(order, lens_and_start, tokens, cotangent, chips)
    gathered = lax.all_to_all(send.reshape(2 * chips, 2, rows, model), "ctx", 0, 0)

    small = jnp.concatenate([gain_attn, gain_ffn, bias_table.reshape(-1)])
    small = jnp.pad(small[None], ((0, 15), (0, model - small.shape[0])))
    gate_mine, up_mine, ffn_piece, qkv_mine, early_piece = pack_weights(
        where, w_gate, w_up, w_ffn_out, w_out, w_query, w_key, w_value, small
    )
    early = column_pieces(early_piece)
    early_others = swap(jnp.stack(early), CORE)
    found = column_pieces(ffn_piece)
    x_rows = ffn_piece.shape[0] // 2
    x_swapped = [swap(after(piece, gathered)[:x_rows], X) for piece in found]
    y_swapped = [swap(after(piece, gathered)[x_rows:], Y) for piece in found]

    by_distance = jnp.stack([piece[depth] for piece in [early_piece] + early])
    all_small = jnp.stack([pick(by_distance, (plane + planes - i) % planes, 0) for i in range(planes)])
    full_gain_attn = all_small[:, :depth].reshape(1, model).astype(F32)
    full_gain_ffn = all_small[:, depth : 2 * depth].reshape(1, model).astype(F32)
    small_end = 2 * depth + bias_table.size
    full_table = all_small[:, 2 * depth : small_end].reshape(BUCKETS, HEADS)

    hot = bucket_table[:, None] == jnp.arange(BUCKETS, dtype=jnp.int32)[None, :]
    hot = jnp.concatenate([hot, jnp.zeros((1, BUCKETS), bool)])
    my_table = lax.dynamic_slice_in_dim(full_table, chip * chip_heads, chip_heads, 1)
    offsets = jnp.einsum("tb,bh->ht", hot.astype(LOW), my_table, preferred_element_type=F32)

    attn_out, attn_full, lse, query, key, value, w_qkv = attn_forward(
        meta, gathered, full_gain_attn, qkv_mine, early, early_others, offsets
    )
    attn_out = after(attn_out, x_swapped[0], y_swapped[0])
    attn = lax.all_to_all(attn_out, "ctx", 0, 0)
    residual, nf_own, full_out = out_project(
        where, flat, attn, w_out, early, early_others, full_gain_ffn
    )
    dy_other = swap(dy, CORE)
    nf_other = swap(nf_own, CORE)
    hidden, dup, dnf_own, dnf_send, full_down, *g_picks = ffn_first(
        where, nf_own, nf_other, dy, dy_other, (gate_mine, up_mine, w_ffn_out),
        found + x_swapped + y_swapped,
    )
    g_parts = column_sum(g_picks)

    dattn, dres, dgain_ffn, o_keep, o_send = out_back(
        where, dnf_own, swap(dnf_send, CORE), residual, dy, full_gain_ffn, full_out, attn, planes
    )
    dattn_all = lax.all_to_all(dattn, "ctx", 0, 0)
    o_came = swap(o_send, CORE)
    out_own, out_send, u_keep, u_send, f_keep, f_send = ffn_second(
        where, nf_own, nf_other, dy, dy_other, hidden, dup, full_down, planes
    )

    x_side, y_side = chip % 2, chip // 2
    wide, part, tail = units // 2 // model, units // planes // 2, depth // 8
    o_half = [t.reshape(planes, 2, 2 * tail, model) for t in (o_keep, o_came)]
    u_send, f_send, dattn_all = lax.optimization_barrier((u_send, f_send, dattn_all))
    uo_send = jnp.concatenate(
        [
            u_send.reshape(planes, wide * depth // 2, model),
            add(*(pick(t, 1 - x_side, 1) for t in o_half)),
        ],
        axis=1,
    )
    dattn_all = after(dattn_all, uo_send)
    uo_came, f_came = swap(uo_send, X), swap(f_send, Y)

    dn, dw_keep, dw_send, dgain_attn, doffsets = attn_backward(
        meta, gathered, full_gain_attn, w_qkv, offsets,
        query, key, value, attn_full, lse, dattn_all, planes,
    )

    uo_came, f_came, dn = lax.optimization_barrier((uo_came, f_came, dn))
    u_two = [u_keep, uo_came[:, : wide * depth // 2]]
    u_two = [t.reshape(planes, wide, 2, quarter, model) for t in u_two]
    o_two = [pick(t, x_side, 1).reshape(planes, 2, tail, model) for t in o_half]
    o_two = o_two + [uo_came[:, wide * depth // 2 :].reshape(planes, 2, tail, model)]
    f_two = [t.reshape(planes, 2, part // 4, model) for t in (f_keep, f_came)]
    uo_send = jnp.concatenate(
        [
            add(*(pick(t, 1 - y_side, 2) for t in u_two)).reshape(planes, wide * quarter, model),
            add(*(pick(t, 1 - y_side, 1) for t in o_two)),
        ],
        axis=1,
    )
    f_send = add(*(pick(t, 1 - x_side, 1) for t in f_two))
    dn = after(dn, uo_send, f_send)
    uo_came, f_came = swap(uo_send, Y), swap(f_send, X)
    u_three = [pick(t, y_side, 2).reshape(planes, wide * quarter, model) for t in u_two]
    u_three = add(*u_three, uo_came[:, : wide * quarter])
    f_three = add(*(pick(t, x_side, 1) for t in f_two), f_came)
    o_three = add(*(pick(t, y_side, 1) for t in o_two), uo_came[:, wide * quarter :])
    ufo_sum = add(
        *column_sum(plane_picks(jnp.concatenate([u_three, f_three, o_three], axis=1)))
    )
    g_parts = [
        jnp.transpose(t.reshape(wide, 2, 2, quarter, model), (2, 1, 0, 3, 4)).reshape(
            4, wide * quarter, model
        )
        for t in g_parts
    ]
    g_sum = plane_sum(g_parts)

    out_rows = finish_out(order, lens_and_start, residual, out_own, swap(out_send, CORE), batch)
    dn = lax.all_to_all(dn, "ctx", 0, 0).reshape(chips, batch, rows, model)
    dtok = finish_tokens(order, dn, flat, dres, full_gain_attn)

    mine_buckets = jnp.einsum(
        "ht,tb->bh", doffsets, hot.astype(F32), precision=lax.Precision.HIGHEST
    )
    buckets = lax.dynamic_update_slice_in_dim(
        jnp.zeros((BUCKETS, HEADS), F32), mine_buckets, chip * chip_heads, 1
    )
    line = jnp.concatenate(
        [
            dgain_attn.reshape(planes, depth),
            dgain_ffn.reshape(planes, depth),
            buckets.reshape(planes, -1),
        ],
        axis=1,
    ).astype(LOW)
    line = jnp.pad(line[:, None, :], ((0, 0), (0, 15), (0, 3 * width - line.shape[1])))
    nothing = jnp.zeros_like(line)
    dw_send = jnp.concatenate([dw_send, jnp.where(core == 1, line, nothing)], axis=1)
    dw_keep = jnp.concatenate([dw_keep, jnp.where(core == 0, line, nothing)], axis=1)
    dw = add(*column_sum(plane_picks(add(dw_keep, swap(dw_send, CORE)))))
    dw_all = [dw, swap(dw, X), swap(dw, Y), swap(dw, XY)]
    dw_others = swap(jnp.stack(dw_all), CORE)
    grad_query, grad_key, grad_value, sums = unpack_qkv(where, dw_all, dw_others, depth, model)
    grad_gain_attn = sums[0, :depth]
    grad_gain_ffn = sums[0, depth : 2 * depth]
    grad_buckets = sums[0, 2 * depth : small_end].reshape(BUCKETS // planes, HEADS)

    pack = jnp.pad(jnp.concatenate([g_sum, ufo_sum]), ((0, depth // 24), (0, 0)))
    packs = [pack, swap(pack, X), swap(pack, Y), swap(pack, XY)]
    packs = packs + [swap(piece, CORE) for piece in packs]
    grad_gate, grad_up, grad_down, grad_out = unpack(where, packs, depth, units)

    return (
        out_rows, dtok, grad_gain_attn, grad_query, grad_key, grad_value, grad_out, grad_buckets,
        grad_gain_ffn, grad_gate, grad_up, grad_down,
    )


def gelu_tanh(values):
    return (
        0.5
        * values
        * (1.0 + jnp.tanh(0.7978845608028654 * (values + 0.044715 * values * values * values)))
    )


def normalize(values, gain_vec):
    return (
        values * lax.rsqrt(jnp.mean(values * values, axis=-1, keepdims=True) + norm_eps) * gain_vec
    )


def project(values, matrix):
    return jnp.einsum("msd,de->mse", values, matrix, preferred_element_type=jnp.float32)


def back_project(values, matrix):
    return jnp.einsum("mse,de->msd", values, matrix, preferred_element_type=jnp.float32)


def outer_sum(left_rows, right_rows):
    return jnp.einsum("msd,mse->de", left_rows, right_rows, preferred_element_type=jnp.float32)


def split_heads(values):
    return values.reshape(values.shape[0], values.shape[1], HEADS, HEAD_DIM)


def toeplitz_bias(offset_bias, start, query_rows, key_rows):
    span = query_rows + key_rows - 1
    window = lax.dynamic_slice_in_dim(offset_bias, start, span, 1)
    wrapped = jnp.concatenate(
        [
            window[:, query_rows - 1 :],
            jnp.zeros((window.shape[0], 1), jnp.float32),
            window[:, : query_rows - 1],
        ],
        axis=1,
    )
    tiled = jnp.tile(wrapped, (1, query_rows))
    shaped = tiled[:, : query_rows * span].reshape(window.shape[0], query_rows, span)
    return shaped[:, :, :key_rows]


def diagonal_sums(grad_bias, query_rows, key_rows):
    span = query_rows + key_rows - 1
    heads = grad_bias.shape[0]
    padded = jnp.pad(grad_bias, ((0, 0), (0, 0), (0, span - key_rows)))
    flat = jnp.pad(padded.reshape(heads, query_rows * span), ((0, 0), (0, query_rows)))
    slots = jnp.sum(flat.reshape(heads, query_rows, span + 1), axis=1)
    return jnp.concatenate([slots[:, key_rows + 1 :], slots[:, :key_rows]], axis=1)


def block_scores(query_heads, key_heads, pair_bias, key_ok):
    scores = jnp.einsum(
        "mihe,mjhe->mhij", query_heads, key_heads, preferred_element_type=jnp.float32
    )
    scores = scores + pair_bias[None]
    return jnp.where(key_ok[:, None, None, :], scores, -1e30)


def over_blocks(update, make_bias, carried, pieces):
    piece_rows = pieces[0].shape[1]
    block_rows = math.gcd(piece_rows, 256)
    block_count = piece_rows // block_rows

    def advance(block_index, running):
        block_start = block_index * block_rows
        sub_pieces = tuple(
            (
                lax.dynamic_slice_in_dim(member, block_index * block_rows, block_rows, 1)
                for member in pieces
            )
        )
        bias_info = make_bias(block_start, block_rows)
        return update(running, sub_pieces, block_start, slice(None), bias_info)

    return lax.fori_loop(0, block_count, advance, carried)


def per_device_general(
    tokens,
    cotangent,
    lengths,
    bucket_table,
    gain_attn,
    w_query,
    w_key,
    w_value,
    w_out,
    bias_table,
    gain_ffn,
    w_gate,
    w_up,
    w_ffn_out,
):
    shards = (
        gain_attn,
        w_query,
        w_key,
        w_value,
        w_out,
        bias_table,
        gain_ffn,
        w_gate,
        w_up,
        w_ffn_out,
    )
    gathered = (
        lax.all_gather(shards[0], "fsdp", axis=0, tiled=True),
        lax.all_gather(shards[1], "fsdp", axis=0, tiled=True),
        lax.all_gather(shards[2], "fsdp", axis=0, tiled=True),
        lax.all_gather(shards[3], "fsdp", axis=0, tiled=True),
        lax.all_gather(shards[4], "fsdp", axis=0, tiled=True),
        lax.all_gather(shards[5], "fsdp", axis=0, tiled=True),
        lax.all_gather(shards[6], "fsdp", axis=0, tiled=True),
        lax.all_gather(shards[7], "fsdp", axis=0, tiled=True),
        lax.all_gather(shards[8], "fsdp", axis=0, tiled=True),
        lax.all_gather(shards[9], "fsdp", axis=0, tiled=True),
    )
    (
        full_gain_attn,
        full_query,
        full_key,
        full_value,
        full_out,
        full_bias,
        full_gain_ffn,
        full_gate,
        full_up,
        full_ffn_out,
    ) = gathered
    batch_rows, local_rows, model_width = tokens.shape
    seq_len = local_rows * lax.axis_size("ctx")
    table_len = bucket_table.shape[0]
    first_pos = lax.axis_index("ctx") * local_rows
    positions = first_pos + jnp.arange(local_rows, dtype=jnp.int32)
    valid_mask = positions[None, :] < lengths[:, None]
    valid_rows = valid_mask.astype(jnp.float32)
    bucket_hot = bucket_table[:, None] == jnp.arange(BUCKETS, dtype=jnp.int32)[None, :]

    def offset_bias_of(bias_weights):
        return jnp.einsum(
            "tb,bh->ht",
            bucket_hot.astype(jnp.bfloat16),
            bias_weights,
            preferred_element_type=jnp.float32,
        )

    forward_offsets = offset_bias_of(full_bias)

    def keys_bias(offset_bias):

        def keys_make(block_start, block_rows):
            start = block_start - first_pos - (local_rows - 1) + (seq_len - 1)
            return (toeplitz_bias(offset_bias, start, local_rows, block_rows), start)

        return keys_make

    def queries_bias(offset_bias):

        def queries_make(block_start, block_rows):
            start = first_pos - block_start - (block_rows - 1) + (seq_len - 1)
            return (toeplitz_bias(offset_bias, start, block_rows, local_rows), start)

        return queries_make

    tokens_f = tokens.astype(jnp.float32)
    attn_gain = full_gain_attn.astype(jnp.float32)
    normed = normalize(tokens_f, attn_gain).astype(jnp.bfloat16)
    queries = project(normed, full_query).astype(jnp.bfloat16)
    keys_local = project(normed, full_key).astype(jnp.bfloat16)
    values_local = project(normed, full_value).astype(jnp.bfloat16)
    query_heads = split_heads(queries)

    def forward_block(running, sub_pieces, block_start, member_pick, bias_info):
        max_score, row_total, weighted = running
        key_part, value_part = sub_pieces
        key_pos = block_start + jnp.arange(key_part.shape[1], dtype=jnp.int32)
        key_ok = key_pos[None, :] < lengths[:, None]
        scores = block_scores(query_heads, split_heads(key_part), bias_info[0], key_ok)
        new_max = jnp.maximum(max_score, jnp.max(scores, axis=-1))
        shrink = jnp.exp(max_score - new_max)
        weights = jnp.exp(scores - new_max[..., None])
        row_total = row_total * shrink + jnp.sum(weights, axis=-1)
        weighted = weighted * jnp.transpose(shrink, (0, 2, 1))[..., None] + jnp.einsum(
            "mhij,mjhe->mihe",
            weights.astype(jnp.bfloat16),
            split_heads(value_part),
            preferred_element_type=jnp.float32,
        )
        return (new_max, row_total, weighted)

    start_state = (
        jnp.full((batch_rows, HEADS, local_rows), -1e30, jnp.float32),
        jnp.zeros((batch_rows, HEADS, local_rows), jnp.float32),
        jnp.zeros((batch_rows, local_rows, HEADS, HEAD_DIM), jnp.float32),
    )
    max_score, row_total, weighted = over_blocks(
        forward_block,
        keys_bias(forward_offsets),
        start_state,
        (
            lax.all_gather(keys_local, "ctx", axis=1, tiled=True),
            lax.all_gather(values_local, "ctx", axis=1, tiled=True),
        ),
    )
    log_total = max_score + jnp.log(row_total)
    attn_full = weighted / jnp.transpose(row_total, (0, 2, 1))[..., None]
    attn_low = attn_full.reshape(batch_rows, local_rows, model_width).astype(jnp.bfloat16)
    residual = tokens_f + project(attn_low, full_out)
    ffn_gain = full_gain_ffn.astype(jnp.float32)
    normed_ffn = normalize(residual, ffn_gain).astype(jnp.bfloat16)
    gate_proj = project(normed_ffn, full_gate)
    up_proj = project(normed_ffn, full_up)
    hidden = (gelu_tanh(gate_proj) * up_proj).astype(jnp.bfloat16)
    result = valid_rows[..., None] * (residual + project(hidden, full_ffn_out))
    output = result.astype(jnp.bfloat16)
    back_weights = (
        lax.all_gather(shards[0], "fsdp", axis=0, tiled=True),
        lax.all_gather(shards[1], "fsdp", axis=0, tiled=True),
        lax.all_gather(shards[2], "fsdp", axis=0, tiled=True),
        lax.all_gather(shards[3], "fsdp", axis=0, tiled=True),
        lax.all_gather(shards[4], "fsdp", axis=0, tiled=True),
        lax.all_gather(shards[5], "fsdp", axis=0, tiled=True),
        lax.all_gather(shards[6], "fsdp", axis=0, tiled=True),
        lax.all_gather(shards[7], "fsdp", axis=0, tiled=True),
        lax.all_gather(shards[8], "fsdp", axis=0, tiled=True),
        lax.all_gather(shards[9], "fsdp", axis=0, tiled=True),
    )
    (
        back_gain_attn,
        back_query,
        back_key,
        back_value,
        back_out,
        back_bias,
        back_gain_ffn,
        back_gate,
        back_up,
        back_ffn_out,
    ) = back_weights
    back_offsets = offset_bias_of(back_bias)
    grad_out = cotangent.astype(jnp.float32) * valid_rows[..., None]
    grad_low = grad_out.astype(jnp.bfloat16)
    grad_w_ffn_out = outer_sum(hidden, grad_low)
    grad_hidden = back_project(grad_low, back_ffn_out)

    def gated_product(gate_in, up_in):
        return gelu_tanh(gate_in) * up_in

    gated_value, gated_back = jax.vjp(gated_product, gate_proj, up_proj)
    grad_gate, grad_up = gated_back(grad_hidden)
    grad_gate = grad_gate.astype(jnp.bfloat16)
    grad_up = grad_up.astype(jnp.bfloat16)
    grad_w_gate = outer_sum(normed_ffn, grad_gate)
    grad_w_up = outer_sum(normed_ffn, grad_up)
    grad_normed_ffn = back_project(grad_gate, back_gate) + back_project(grad_up, back_up)
    norm_value, norm_back = jax.vjp(normalize, residual, back_gain_ffn.astype(jnp.float32))
    grad_resid_part, grad_gain_ffn = norm_back(grad_normed_ffn)
    grad_resid = grad_out + grad_resid_part
    grad_branch = grad_resid.astype(jnp.bfloat16)
    grad_w_out = outer_sum(attn_low, grad_branch)
    grad_attn = back_project(grad_branch, back_out).astype(jnp.bfloat16)
    grad_heads = split_heads(grad_attn)
    delta_row = jnp.einsum(
        "mihe,mihe->mhi", grad_heads, attn_full, preferred_element_type=jnp.float32
    )

    def query_grad_block(running, sub_pieces, block_start, member_pick, bias_info):
        grad_query, grad_offsets = running
        pair_bias, table_start = bias_info
        key_part, value_part = sub_pieces
        key_heads = split_heads(key_part)
        key_pos = block_start + jnp.arange(key_part.shape[1], dtype=jnp.int32)
        key_ok = key_pos[None, :] < lengths[:, None]
        scores = block_scores(query_heads, key_heads, pair_bias, key_ok)
        probabilities = jnp.exp(scores - log_total[..., None])
        grad_probs = jnp.einsum(
            "mihe,mjhe->mhij",
            grad_heads,
            split_heads(value_part),
            preferred_element_type=jnp.float32,
        )
        grad_scores = (probabilities * (grad_probs - delta_row[..., None])).astype(jnp.bfloat16)
        grad_query = grad_query + jnp.einsum(
            "mhij,mjhe->mihe", grad_scores, key_heads, preferred_element_type=jnp.float32
        )
        pair_grad = jnp.sum(grad_scores.astype(jnp.float32), axis=0)
        diag = diagonal_sums(pair_grad, pair_grad.shape[1], pair_grad.shape[2])
        current = lax.dynamic_slice_in_dim(grad_offsets, table_start, diag.shape[1], 1)
        grad_offsets = lax.dynamic_update_slice_in_dim(grad_offsets, current + diag, table_start, 1)
        return (grad_query, grad_offsets)

    query_state = (
        jnp.zeros((batch_rows, local_rows, HEADS, HEAD_DIM), jnp.float32),
        jnp.zeros((HEADS, table_len), jnp.float32),
    )
    grad_query, grad_offsets = over_blocks(
        query_grad_block,
        keys_bias(back_offsets),
        query_state,
        (
            lax.all_gather(keys_local, "ctx", axis=1, tiled=True),
            lax.all_gather(values_local, "ctx", axis=1, tiled=True),
        ),
    )
    grad_buckets = jnp.einsum(
        "ht,tb->bh", grad_offsets, bucket_hot.astype(jnp.float32), precision=lax.Precision.HIGHEST
    )
    stats_lse, stats_delta = (
        lax.all_gather(log_total, "ctx", axis=2, tiled=True),
        lax.all_gather(delta_row, "ctx", axis=2, tiled=True),
    )
    key_heads_local = split_heads(keys_local)
    value_heads_local = split_heads(values_local)

    def key_grad_block(running, sub_pieces, block_start, member_pick, bias_info):
        grad_key, grad_value = running
        query_part, grad_part = sub_pieces
        rows_here = query_part.shape[1]
        query_part_heads = split_heads(query_part)
        grad_part_heads = split_heads(grad_part)
        scores = block_scores(query_part_heads, key_heads_local, bias_info[0], valid_mask)
        lse_part = lax.dynamic_slice_in_dim(stats_lse, block_start, rows_here, 2)
        delta_part = lax.dynamic_slice_in_dim(stats_delta, block_start, rows_here, 2)
        probabilities = jnp.exp(scores - lse_part[..., None])
        grad_value = grad_value + jnp.einsum(
            "mhij,mihe->mjhe",
            probabilities.astype(jnp.bfloat16),
            grad_part_heads,
            preferred_element_type=jnp.float32,
        )
        grad_probs = jnp.einsum(
            "mihe,mjhe->mhij",
            grad_part_heads,
            value_heads_local,
            preferred_element_type=jnp.float32,
        )
        grad_scores = (probabilities * (grad_probs - delta_part[..., None])).astype(jnp.bfloat16)
        grad_key = grad_key + jnp.einsum(
            "mhij,mihe->mjhe", grad_scores, query_part_heads, preferred_element_type=jnp.float32
        )
        return (grad_key, grad_value)

    key_state = (
        jnp.zeros((batch_rows, local_rows, HEADS, HEAD_DIM), jnp.float32),
        jnp.zeros((batch_rows, local_rows, HEADS, HEAD_DIM), jnp.float32),
    )
    grad_key, grad_value = over_blocks(
        key_grad_block,
        queries_bias(back_offsets),
        key_state,
        (
            lax.all_gather(queries, "ctx", axis=1, tiled=True),
            lax.all_gather(grad_attn, "ctx", axis=1, tiled=True),
        ),
    )
    grad_q = grad_query.reshape(batch_rows, local_rows, model_width).astype(jnp.bfloat16)
    grad_k = grad_key.reshape(batch_rows, local_rows, model_width).astype(jnp.bfloat16)
    grad_v = grad_value.reshape(batch_rows, local_rows, model_width).astype(jnp.bfloat16)
    grad_w_query = outer_sum(normed, grad_q)
    grad_w_key = outer_sum(normed, grad_k)
    grad_w_value = outer_sum(normed, grad_v)
    grad_normed = (
        back_project(grad_q, back_query)
        + back_project(grad_k, back_key)
        + back_project(grad_v, back_value)
    )
    attn_norm_value, attn_norm_back = jax.vjp(
        normalize, tokens_f, back_gain_attn.astype(jnp.float32)
    )
    grad_tokens_part, grad_gain_attn = attn_norm_back(grad_normed)
    grad_tokens = grad_resid + grad_tokens_part
    grads = (
        grad_gain_attn,
        grad_w_query,
        grad_w_key,
        grad_w_value,
        grad_w_out,
        grad_buckets,
        grad_gain_ffn,
        grad_w_gate,
        grad_w_up,
        grad_w_ffn_out,
    )
    shard_sums = (
        lax.psum_scatter(grads[0], "fsdp", scatter_dimension=0, tiled=True),
        lax.psum_scatter(grads[1], "fsdp", scatter_dimension=0, tiled=True),
        lax.psum_scatter(grads[2], "fsdp", scatter_dimension=0, tiled=True),
        lax.psum_scatter(grads[3], "fsdp", scatter_dimension=0, tiled=True),
        lax.psum_scatter(grads[4], "fsdp", scatter_dimension=0, tiled=True),
        lax.psum_scatter(grads[5], "fsdp", scatter_dimension=0, tiled=True),
        lax.psum_scatter(grads[6], "fsdp", scatter_dimension=0, tiled=True),
        lax.psum_scatter(grads[7], "fsdp", scatter_dimension=0, tiled=True),
        lax.psum_scatter(grads[8], "fsdp", scatter_dimension=0, tiled=True),
        lax.psum_scatter(grads[9], "fsdp", scatter_dimension=0, tiled=True),
    )
    totals = lax.psum(
        (
            shard_sums[0],
            shard_sums[1],
            shard_sums[2],
            shard_sums[3],
            shard_sums[4],
            shard_sums[5],
            shard_sums[6],
            shard_sums[7],
            shard_sums[8],
            shard_sums[9],
        ),
        "ctx",
    )
    return (output, grad_tokens) + tuple(totals)


def solution(mesh):
    placed = (
        P("fsdp", "ctx", None),
        P("fsdp", "ctx", None),
        P("fsdp"),
        P(),
        P("fsdp"),
        P("fsdp", None),
        P("fsdp", None),
        P("fsdp", None),
        P("fsdp", None),
        P("fsdp", None),
        P("fsdp"),
        P("fsdp", None),
        P("fsdp", None),
        P("fsdp", None),
    )
    plane = mesh.shape["ctx"] == 8 and mesh.shape["fsdp"] == 4
    return jax.shard_map(
        per_device_plane if plane else per_device_general,
        mesh=mesh,
        in_specs=placed,
        out_specs=(
            P("fsdp", "ctx", None),
            P("fsdp", "ctx", None),
            P("fsdp"),
            P("fsdp", None),
            P("fsdp", None),
            P("fsdp", None),
            P("fsdp", None),
            P("fsdp", None),
            P("fsdp"),
            P("fsdp", None),
            P("fsdp", None),
            P("fsdp", None),
        ),
        check_vma=False,
    )
```

```python
import math

import jax
import jax.numpy as jnp
from jax import lax
from jax.experimental import pallas as pl
from jax.experimental.pallas import tpu as pltpu
from jax.sharding import PartitionSpec as P

HEADS = 12
HEAD_DIM = 64
BUCKETS = 32
BLOCK = 256
TILE = 256
VMEM_BYTES = 56 * 1024 * 1024
COST = 0.5

norm_eps = 1e-06
F32 = jnp.float32
LOW = jnp.bfloat16
NN = (((1,), (0,)), ((), ()))
NT = (((1,), (1,)), ((), ()))
TN = (((0,), (0,)), ((), ()))
SMEM = pl.BlockSpec(memory_space=pltpu.SMEM)
ANY = pl.BlockSpec(memory_space=pl.ANY)


def dot(left, right, dims=NN):
    return lax.dot_general(left, right, dims, preferred_element_type=F32)


def shape_of(dims, kind):
    return jax.ShapeDtypeStruct(dims, kind)


def params(limit=VMEM_BYTES):
    return pltpu.CompilerParams(vmem_limit_bytes=limit)


def cost(flops, moved, exps=0):
    return pl.CostEstimate(
        flops=int(flops * COST), bytes_accessed=int(moved * COST), transcendentals=int(exps)
    )


def block_rows(index, rows=BLOCK):
    return pl.ds(pl.multiple_of(index * rows, rows), rows)


def rms_rows(rows_f):
    return lax.rsqrt(jnp.mean(rows_f * rows_f, axis=-1, keepdims=True) + norm_eps)


def pack_kernel(
    where_ref, gate_ref, up_ref, down_ref, out_ref, q_ref, k_ref, v_ref, small_ref,
    gate_mine_ref, up_mine_ref, x_ref, y_ref, qkv_ref, early_ref,
):
    chip, core = where_ref[0], where_ref[1]
    x_side, y_side = chip % 2, chip // 2
    wide, depth, model = gate_mine_ref.shape
    planes = gate_ref.shape[1] // model
    part = gate_ref.shape[1] // planes // 2
    slab = depth // 2
    for plane in range(planes):
        columns = pl.ds(pl.multiple_of(plane * 2 * part + core * part, 128), part)
        half, at = divmod(plane * part, model)
        gate_mine_ref[half, :, at : at + part] = gate_ref[:, columns]
        up_mine_ref[half, :, at : at + part] = up_ref[:, columns]
    quarter = part // 4
    x_rows, y_rows = block_rows(x_side, slab), block_rows(y_side, slab)
    for half in range(wide):
        at = slice(half * slab, (half + 1) * slab)
        x_ref[at, :] = gate_mine_ref[half, x_rows, :]
        y_ref[at, :] = up_mine_ref[half, y_rows, :]
    x_down = pl.ds(pl.multiple_of(core * part + x_side * quarter, quarter), quarter)
    y_down = pl.ds(pl.multiple_of(core * part + 2 * quarter + y_side * quarter, quarter), quarter)
    x_ref[wide * slab :, :] = down_ref[x_down, :]
    y_ref[wide * slab :, :] = down_ref[y_down, :]
    early_ref[slab : 2 * slab, :] = out_ref[block_rows(core, slab), :]
    early_ref[2 * slab :, :] = small_ref[...]
    width = model // 4
    for owner in range(4):

        @pl.when(chip == owner)
        def _(owner=owner):
            lanes = slice(owner * width, (owner + 1) * width)
            qkv_ref[:, :width] = q_ref[:, lanes]
            qkv_ref[:, width : 2 * width] = k_ref[:, lanes]
            qkv_ref[:, 2 * width : 3 * width] = v_ref[:, lanes]
            qkv_ref[:, 3 * width :] = jnp.zeros((depth, width), LOW)

    early_ref[:slab, :] = qkv_ref[block_rows(core, slab), :]


def pack_weights(where, gate, up, down, out, query, key, value, small):
    depth, units = gate.shape
    model = query.shape[1]
    planes = model // depth
    wide = units // 2 // model
    part = units // planes // 2
    vmem = pl.BlockSpec(memory_space=pltpu.VMEM)
    return pl.pallas_call(
        pack_kernel,
        in_specs=[SMEM] + [vmem] * 8,
        out_specs=[vmem] * 6,
        out_shape=[
            shape_of((wide, depth, model), LOW),
            shape_of((wide, depth, model), LOW),
            shape_of((wide * depth // 2 + part // 4, model), LOW),
            shape_of((wide * depth // 2 + part // 4, model), LOW),
            shape_of((depth, model), LOW),
            shape_of((depth + small.shape[0], model), LOW),
        ],
        compiler_params=params(),
        cost_estimate=cost(0, 16e6),
        name="pack_weights",
    )(where, gate, up, down, out, query, key, value, small)


def prepare_kernel(lens_ref, tok_ref, send_ref, order_ref, sorted_ref):
    batch = tok_ref.shape[0]
    lens = [lens_ref[i] for i in range(batch)]
    for mine in range(batch):
        rank = 0
        for other in range(batch):
            if other != mine:
                ahead = lens[other] > lens[mine] if other > mine else lens[other] >= lens[mine]
                rank = rank + ahead.astype(jnp.int32)
        slot = jnp.where(rank == 0, 0, jnp.where(rank == batch - 1, 1, rank + 1))
        order_ref[slot] = mine
        sorted_ref[slot] = lens[mine]
    for slot in range(batch):
        rows = tok_ref[order_ref[slot]]
        for chip in range(send_ref.shape[0]):
            send_ref[chip, slot] = rows


def prepare(lengths, tokens, chips):
    batch, rows, model = tokens.shape
    vmem = pl.BlockSpec(memory_space=pltpu.VMEM)
    return pl.pallas_call(
        prepare_kernel,
        in_specs=[SMEM, vmem],
        out_specs=[vmem, SMEM, SMEM],
        out_shape=[
            shape_of((chips, batch, rows, model), LOW),
            shape_of((batch,), jnp.int32),
            shape_of((batch,), jnp.int32),
        ],
        compiler_params=params(),
        cost_estimate=cost(0, 4e6),
        name="prepare",
    )(lengths, tokens)


def sort_rows_kernel(order_ref, lens_ref, start_ref, tok_ref, cot_ref, local_ref, dy_ref):
    slot = pl.program_id(0)
    local_ref[...] = tok_ref[0]
    grads = cot_ref[0].astype(F32)
    place_in = lax.broadcasted_iota(jnp.int32, grads.shape, 0) + start_ref[0]
    dy_ref[...] = jnp.where(place_in < lens_ref[slot], grads, 0.0).astype(LOW)


def sort_rows(order, lens, start, tokens, cotangent):
    batch, rows, model = tokens.shape
    by_order = pl.BlockSpec((1, rows, model), lambda s, order, lens, start: (order[s], 0, 0))
    in_order = pl.BlockSpec((rows, model), lambda s, order, lens, start: (s, 0))
    return pl.pallas_call(
        sort_rows_kernel,
        grid_spec=pltpu.PrefetchScalarGridSpec(
            num_scalar_prefetch=3,
            grid=(batch,),
            in_specs=[by_order, by_order],
            out_specs=[in_order, in_order],
        ),
        out_shape=[
            shape_of((batch * rows, model), LOW),
            shape_of((batch * rows, model), LOW),
        ],
        compiler_params=params(),
        cost_estimate=cost(0, 3e6),
        name="sort_rows",
    )(order, lens, start, tokens, cotangent)


def build_bias(offsets_ref, bias_ref):
    heads, _, width = bias_ref.shape
    span = offsets_ref.shape[1]
    for head in range(heads):
        line = jnp.broadcast_to(offsets_ref[head : head + 1, :], (8, span))
        for group in range(BLOCK // 8):
            turned = pltpu.roll(
                line, (group * 8 - (BLOCK - 1)) % span, 1, stride=1, stride_axis=0
            )
            bias_ref[head, group * 8 : group * 8 + 8, :] = turned[:, :width]


def fold_diagonals(bias_grad_ref, offsets_grad_ref):
    heads, _, width = bias_grad_ref.shape
    span = offsets_grad_ref.shape[1]
    for head in range(heads):
        total = jnp.zeros((8, span), F32)
        for group in range(BLOCK // 8):
            rows = bias_grad_ref[head, group * 8 : group * 8 + 8, :]
            wide = jnp.concatenate([rows, jnp.zeros((8, span - width), F32)], axis=1)
            total = total + pltpu.roll(wide, (BLOCK - 8 - group * 8) % span, 1)
        line = jnp.zeros((1, span), F32)
        for row in range(8):
            line = line + pltpu.roll(total, (7 - row) % span, 1)[row : row + 1, :]
        offsets_grad_ref[head : head + 1, :] = line


def kept_scores(scores, column, length, count):
    wide = count * BLOCK
    tail = jnp.where(column < length - (wide - BLOCK), scores[:, wide - BLOCK :], -1e30)
    if count == 1:
        return tail
    return jnp.concatenate([scores[:, : wide - BLOCK], tail], axis=1)


def token_block(tok_ref, index):
    pieces, _, rows, model = tok_ref.shape
    parts = BLOCK // rows
    return tok_ref[pl.ds(index * parts, parts), 0].reshape(BLOCK, model)


def attn_forward_first_kernel(
    lens_ref, where_ref, tok_ref, gain_ref, w0_ref, w1_ref, w2_ref, w3_ref, v1_ref, v2_ref, v3_ref, off_ref,
    ot_ref, of_ref, q_ref, k_ref, v_ref, w_ref,
    bias_ref, vm_ref,
):
    depth, model = w0_ref.shape
    width = w_ref.shape[2]
    planes, slab = model // depth, depth // 2
    core, plane = where_ref[1], where_ref[2]
    for kind in range(3):
        lanes = slice(kind * width, (kind + 1) * width)
        w_ref[kind, block_rows(plane, depth), :] = w0_ref[:, lanes]
        for back, (piece_ref, other_ref) in enumerate(
            ((w1_ref, v1_ref), (w2_ref, v2_ref), (w3_ref, v3_ref))
        ):
            owner = lax.rem(plane + planes - 1 - back, planes)
            w_ref[kind, block_rows(owner * 2 + core, slab), :] = piece_ref[:slab, lanes]
            w_ref[kind, block_rows(owner * 2 + 1 - core, slab), :] = other_ref[:slab, lanes]
    attend_slot(
        lens_ref[2 * core], tok_ref, gain_ref, w_ref, off_ref,
        ot_ref, of_ref, q_ref, k_ref, v_ref, bias_ref, vm_ref,
    )


def attn_forward_second_kernel(
    lens_ref, where_ref, tok_ref, gain_ref, w_ref, off_ref, of_in, q_in, k_in, v_in,
    ot_ref, of_ref, q_ref, k_ref, v_ref,
    bias_ref, vm_ref,
):
    attend_slot(
        lens_ref[2 * where_ref[1] + 1], tok_ref, gain_ref, w_ref, off_ref,
        ot_ref, of_ref, q_ref, k_ref, v_ref, bias_ref, vm_ref,
    )


def attend_slot(
    length, tok_ref, gain_ref, w_ref, off_ref,
    ot_ref, of_ref, q_ref, k_ref, v_ref, bias_ref, vm_ref,
):
    pieces, _, piece_rows, model = tok_ref.shape
    blocks = pieces * piece_rows // BLOCK
    width = w_ref.shape[2]
    per_chip = width // HEAD_DIM
    used = (length + BLOCK - 1) // BLOCK
    parts = BLOCK // piece_rows
    build_bias(off_ref, bias_ref)
    owner = lax.broadcasted_iota(jnp.int32, (BLOCK, width), 1) // HEAD_DIM
    column = lax.broadcasted_iota(jnp.int32, (BLOCK, BLOCK), 1)
    spare = lax.broadcasted_iota(jnp.int32, (BLOCK, HEAD_DIM), 1)
    nothing = jnp.zeros((BLOCK, width), LOW)

    def project(index, carry):
        rows = block_rows(index)
        rows_f = token_block(tok_ref, index).astype(F32)
        normed = (rows_f * rms_rows(rows_f) * gain_ref[...]).astype(LOW)
        q_ref[0, rows, :] = dot(normed, w_ref[0]).astype(LOW)
        k_ref[0, rows, :] = dot(normed, w_ref[1]).astype(LOW)
        val = dot(normed, w_ref[2]).astype(LOW)
        v_ref[0, rows, :] = val
        for head in range(per_chip):
            vm_ref[head, rows, :] = jnp.where(owner == head, val, nothing)
        return carry

    lax.fori_loop(0, used, project, 0)

    def attend(index, carry):
        rows = block_rows(index)
        query = q_ref[0, rows, :]
        start = pl.multiple_of((blocks - 1 - index) * BLOCK, BLOCK)
        for count in range(1, blocks + 1):

            @pl.when(used == count)
            def _(count=count):
                wide = count * BLOCK
                total = jnp.zeros((BLOCK, width), F32)
                sums = jnp.zeros((BLOCK, HEAD_DIM), F32)
                for head in range(per_chip):
                    mine = jnp.where(owner == head, query, nothing)
                    scores = dot(mine, k_ref[0, :wide, :], NT)
                    scores = scores + bias_ref[head, :, pl.ds(start, wide)]
                    scores = kept_scores(scores, column, length, count)
                    top = jnp.max(scores, axis=-1, keepdims=True)
                    weights = jnp.exp(scores - top)
                    row_total = jnp.sum(weights, axis=-1, keepdims=True)
                    part = dot(weights.astype(LOW), vm_ref[head, :wide, :])
                    total = total + part * (1.0 / row_total)
                    sums = jnp.where(spare == head, top + jnp.log(row_total), sums)
                of_ref[0, rows, :width] = total
                of_ref[0, rows, width:] = sums
                turned = jnp.transpose(total.astype(LOW))
                for piece in range(parts):
                    lanes = slice(piece * piece_rows, (piece + 1) * piece_rows)
                    ot_ref[index * parts + piece, 0] = turned[:, lanes]

        return carry

    lax.fori_loop(0, used, attend, 0)

    def clear(index, carry):
        ot_ref[pl.ds(index * parts, parts), 0] = jnp.zeros((parts, width, piece_rows), LOW)
        return carry

    lax.fori_loop(used, blocks, clear, 0)


def attn_forward(slot, lens, where, tokens, gain, weights, offsets, kept=()):
    pieces, slots, rows, model = tokens.shape
    width = model // 4
    per_chip = width // HEAD_DIM
    seq = pieces * rows
    by_slot = lambda i: (slot, 0, 0)
    whole = lambda array: pl.BlockSpec(array.shape, lambda i: (0,) * array.ndim)
    lane_rows = pl.BlockSpec((1, seq, width), by_slot)
    results = [
        shape_of((slots, seq, width + HEAD_DIM), F32),
        shape_of((slots, seq, width), LOW),
        shape_of((slots, seq, width), LOW),
        shape_of((slots, seq, width), LOW),
    ]
    last = [shape_of((3, model, width), LOW)] if slot == 0 else []
    return pl.pallas_call(
        attn_forward_first_kernel if slot == 0 else attn_forward_second_kernel,
        grid=(1,),
        in_specs=[
            SMEM,
            SMEM,
            pl.BlockSpec((pieces, 1, rows, model), lambda i: (0, slot, 0, 0)),
            whole(gain),
        ]
        + [whole(array) for array in weights]
        + [whole(offsets)]
        + [ANY] * len(kept),
        out_specs=[
            pl.BlockSpec((pieces, 1, width, rows), lambda i: (0, 0, 0, 0)),
            pl.BlockSpec((1, seq, width + HEAD_DIM), by_slot),
            lane_rows,
            lane_rows,
            lane_rows,
        ]
        + [whole(array) for array in last],
        out_shape=[shape_of((pieces, 1, width, rows), LOW)] + results + last,
        scratch_shapes=[
            pltpu.VMEM((per_chip, BLOCK, 2 * seq - BLOCK), F32),
            pltpu.VMEM((per_chip, seq, width), LOW),
        ],
        input_output_aliases={5 + len(weights) + i: 1 + i for i in range(len(kept))},
        compiler_params=params(),
        cost_estimate=cost(
            2 * seq * (model * 3 * width + 2 * seq * 256 * per_chip),
            seq * 2 * (model + 8 * width),
        ),
        name="attn_forward",
    )(lens, where, tokens, gain, *weights, offsets, *kept)


def attn_backward_kernel(
    lens_ref, where_ref, tok_ref, gain_ref, w_ref, off_ref, q_ref, k_ref, v_ref, of_ref, dot_ref,
    dn_ref, dw_keep_ref, dw_send_ref, dgain_ref, doff_ref,
    bias_ref, dbias_ref, km_ref, dq_ref, dkt_ref, dvt_ref, dwt_ref, dw_ref,
):
    slot = pl.program_id(0)
    pieces, _, piece_rows, model = tok_ref.shape
    blocks = pieces * piece_rows // BLOCK
    width = w_ref.shape[2]
    per_chip = width // HEAD_DIM
    core = where_ref[1]
    length = lens_ref[2 * core + slot]
    used = (length + BLOCK - 1) // BLOCK
    parts = BLOCK // piece_rows

    @pl.when(slot == 0)
    def _():
        build_bias(off_ref, bias_ref)
        dbias_ref[...] = jnp.zeros_like(dbias_ref)
        dwt_ref[...] = jnp.zeros_like(dwt_ref)
        dgain_ref[...] = jnp.zeros_like(dgain_ref)

    dkt_ref[...] = jnp.zeros_like(dkt_ref)
    dvt_ref[...] = jnp.zeros_like(dvt_ref)
    owner = lax.broadcasted_iota(jnp.int32, (BLOCK, width), 1) // HEAD_DIM
    column = lax.broadcasted_iota(jnp.int32, (BLOCK, BLOCK), 1)
    nothing = jnp.zeros((BLOCK, width), LOW)

    def split_keys(index, carry):
        rows = block_rows(index)
        key = k_ref[0, rows, :]
        for head in range(per_chip):
            km_ref[head, rows, :] = jnp.where(owner == head, key, nothing)
        return carry

    lax.fori_loop(0, used, split_keys, 0)

    def attend(index, carry):
        rows = block_rows(index)
        query = q_ref[0, rows, :]
        query_t = jnp.transpose(query)
        grad_t = jnp.concatenate(
            [dot_ref[index * parts + piece, 0] for piece in range(parts)], axis=1
        )
        grad = jnp.transpose(grad_t)
        product = grad.astype(F32) * of_ref[0, rows, :width]
        start = pl.multiple_of((blocks - 1 - index) * BLOCK, BLOCK)
        for count in range(1, blocks + 1):

            @pl.when(used == count)
            def _(count=count):
                wide = count * BLOCK
                grad_query = jnp.zeros((BLOCK, width), F32)
                for head in range(per_chip):
                    lanes = slice(head * HEAD_DIM, (head + 1) * HEAD_DIM)
                    mine = jnp.where(owner == head, query, nothing)
                    scores = dot(mine, k_ref[0, :wide, :], NT)
                    scores = scores + bias_ref[head, :, pl.ds(start, wide)]
                    scores = kept_scores(scores, column, length, count)
                    lse = of_ref[0, rows, width + head : width + head + 1]
                    probs = jnp.exp(scores - lse)
                    delta = jnp.sum(
                        jnp.where(owner == head, product, 0.0), axis=-1, keepdims=True
                    )
                    grad_mine = jnp.where(owner == head, grad, nothing)
                    grad_probs = dot(grad_mine, v_ref[0, :wide, :], NT)
                    grad_scores = probs * (grad_probs - delta)
                    dbias_ref[head, :, pl.ds(start, wide)] += grad_scores
                    grad_scores = grad_scores.astype(LOW)
                    grad_query = grad_query + dot(grad_scores, km_ref[head, :wide, :])
                    dkt_ref[lanes, :wide] += dot(query_t[lanes, :], grad_scores)
                    dvt_ref[lanes, :wide] += dot(grad_t[lanes, :], probs.astype(LOW))
                dq_ref[rows, :] = grad_query.astype(LOW)

        return carry

    lax.fori_loop(0, used, attend, 0)

    def finish(index, carry):
        rows = block_rows(index)
        grad_query = dq_ref[rows, :]
        key_t = dkt_ref[:, rows].astype(LOW)
        value_t = dvt_ref[:, rows].astype(LOW)
        rows_f = token_block(tok_ref, index).astype(F32)
        unit = rows_f * rms_rows(rows_f)
        normed = (unit * gain_ref[...]).astype(LOW)
        grad_normed = (
            dot(grad_query, w_ref[0], NT)
            + dot(jnp.transpose(key_t), w_ref[1], NT)
            + dot(jnp.transpose(value_t), w_ref[2], NT)
        )
        dgain_ref[...] += jnp.sum(grad_normed * unit, axis=0, keepdims=True)
        dn_ref[pl.ds(index * parts, parts), 0] = grad_normed.astype(LOW).reshape(
            parts, piece_rows, model
        )
        dwt_ref[0:width, :] += dot(jnp.transpose(grad_query), normed)
        dwt_ref[width : 2 * width, :] += dot(key_t, normed)
        dwt_ref[2 * width :, :] += dot(value_t, normed)
        return carry

    lax.fori_loop(0, used, finish, 0)

    def clear(index, carry):
        dn_ref[pl.ds(index * parts, parts), 0] = jnp.zeros((parts, piece_rows, model), LOW)
        return carry

    lax.fori_loop(used, blocks, clear, 0)

    @pl.when(slot == pl.num_programs(0) - 1)
    def _():
        fold_diagonals(dbias_ref, doff_ref)
        dw_ref[...] = jnp.transpose(dwt_ref[...].astype(LOW))
        planes, slab, _ = dw_keep_ref.shape
        for plane in range(planes):
            lanes = slice(0, 3 * width)
            dw_keep_ref[plane, :, lanes] = dw_ref[block_rows(2 * plane + core, slab), :]
            dw_send_ref[plane, :, lanes] = dw_ref[block_rows(2 * plane + 1 - core, slab), :]
            rest = jnp.zeros((slab, model - 3 * width), LOW)
            dw_keep_ref[plane, :, 3 * width :] = rest
            dw_send_ref[plane, :, 3 * width :] = rest


def attn_backward(
    lens, where, tokens, gain, w_qkv, offsets, query, key, value, attn_full, grad, planes
):
    pieces, slots, rows, model = tokens.shape
    width = w_qkv.shape[2]
    per_chip = width // HEAD_DIM
    seq = pieces * rows
    lane_rows = pl.BlockSpec((1, seq, width), lambda s: (s, 0, 0))
    by_slot = lambda s: (0, s, 0, 0)
    once = lambda s: (0, 0)
    return pl.pallas_call(
        attn_backward_kernel,
        grid=(slots,),
        in_specs=[
            SMEM,
            SMEM,
            pl.BlockSpec((pieces, 1, rows, model), by_slot),
            pl.BlockSpec((1, model), once),
            pl.BlockSpec((3, model, width), lambda s: (0, 0, 0)),
            pl.BlockSpec(offsets.shape, once),
            lane_rows,
            lane_rows,
            lane_rows,
            pl.BlockSpec((1, seq, width + HEAD_DIM), lambda s: (s, 0, 0)),
            pl.BlockSpec((pieces, 1, width, rows), by_slot),
        ],
        out_specs=[
            pl.BlockSpec((pieces, 1, rows, model), by_slot),
            pl.BlockSpec((planes, model // planes // 2, model), lambda s: (0, 0, 0)),
            pl.BlockSpec((planes, model // planes // 2, model), lambda s: (0, 0, 0)),
            pl.BlockSpec((1, model), once),
            pl.BlockSpec((per_chip, 2 * seq), once),
        ],
        out_shape=[
            shape_of((pieces, slots, rows, model), LOW),
            shape_of((planes, model // planes // 2, model), LOW),
            shape_of((planes, model // planes // 2, model), LOW),
            shape_of((1, model), F32),
            shape_of((per_chip, 2 * seq), F32),
        ],
        scratch_shapes=[
            pltpu.VMEM((per_chip, BLOCK, 2 * seq - BLOCK), F32),
            pltpu.VMEM((per_chip, BLOCK, 2 * seq - BLOCK), F32),
            pltpu.VMEM((per_chip, seq, width), LOW),
            pltpu.VMEM((seq, width), LOW),
            pltpu.VMEM((width, seq), F32),
            pltpu.VMEM((width, seq), F32),
            pltpu.VMEM((3 * width, model), F32),
            pltpu.VMEM((model, 3 * width), LOW),
        ],
        compiler_params=params(),
        cost_estimate=cost(
            4 * slots * seq * (model * 6 * width + 5 * seq * 256 * per_chip),
            slots * seq * 2 * (2 * model + 12 * width),
        ),
        name="attn_backward",
    )(lens, where, tokens, gain, w_qkv, offsets, query, key, value, attn_full, grad)


def side_by_side(attn_refs, chip):
    return jnp.concatenate(
        [ref[2 * chip + core, 0] for core in range(2) for ref in attn_refs], axis=1
    )


def out_project_kernel(
    where_ref, tok_ref, attn0_ref, attn1_ref, own_ref, a1_ref, a2_ref, a3_ref, b1_ref, b2_ref, b3_ref, gain_ref,
    res_ref, nf_ref, w_ref,
):
    core, plane = where_ref[1], where_ref[2]
    depth = own_ref.shape[0]
    slab = depth // 2
    planes = w_ref.shape[0] // depth
    w_ref[block_rows(plane, depth), :] = own_ref[...]
    for back, (piece_ref, other_ref) in enumerate(
        ((a1_ref, b1_ref), (a2_ref, b2_ref), (a3_ref, b3_ref))
    ):
        owner = lax.rem(plane + planes - 1 - back, planes)
        w_ref[block_rows(owner * 2 + core, slab), :] = piece_ref[slab : 2 * slab, :]
        w_ref[block_rows(owner * 2 + 1 - core, slab), :] = other_ref[slab : 2 * slab, :]
    chips, width = attn0_ref.shape[0] // 2, attn0_ref.shape[2]
    total = tok_ref[...].astype(F32)
    for chip in range(chips):
        total = total + dot(
            side_by_side((attn0_ref, attn1_ref), chip), w_ref[chip * width : (chip + 1) * width, :], TN
        )
    res_ref[...] = total
    nf_ref[...] = (total * rms_rows(total) * gain_ref[...]).astype(LOW)


def out_project(where, tokens, attn, own, pieces, others, gain):
    rows, model = tokens.shape
    vmem = pl.BlockSpec(memory_space=pltpu.VMEM)
    return pl.pallas_call(
        out_project_kernel,
        in_specs=[SMEM] + [vmem] * 11,
        out_specs=[vmem] * 3,
        out_shape=[
            shape_of((rows, model), F32),
            shape_of((rows, model), LOW),
            shape_of((model, model), LOW),
        ],
        compiler_params=params(),
        cost_estimate=cost(4 * rows * model * model, rows * model * 12),
        name="out_project",
    )(where, tokens, *attn, own, *pieces, *others, gain)


def out_back_kernel(
    where_ref, own_ref, recv_ref, res_ref, dy_ref, gain_ref, w_ref, attn0_ref, attn1_ref,
    dattn_ref, dres_ref, dgain_ref, keep_ref, send_ref,
    gout_ref,
):
    chips, width, rows = dattn_ref.shape[0] // 2, dattn_ref.shape[2], dattn_ref.shape[3]
    grad = own_ref[...] + recv_ref[...].astype(F32)
    residual = res_ref[...]
    scale = rms_rows(residual)
    unit = residual * scale
    dgain_ref[...] = jnp.sum(grad * unit, axis=0, keepdims=True)
    inner = grad * gain_ref[...]
    dres = dy_ref[...].astype(F32) + scale * (
        inner - unit * jnp.mean(inner * unit, axis=-1, keepdims=True)
    )
    dres_ref[...] = dres
    branch = dres.astype(LOW)
    for chip in range(chips):
        heads = slice(chip * width, (chip + 1) * width)
        part = dot(w_ref[heads, :], branch, NT).astype(LOW)
        for slot in range(4):
            dattn_ref[2 * chip + slot // 2, slot % 2] = part[:, slot * rows : (slot + 1) * rows]
        gout_ref[heads, :] = dot(side_by_side((attn0_ref, attn1_ref), chip), branch).astype(LOW)
    core = where_ref[1]
    planes, slab, _ = keep_ref.shape
    for plane in range(planes):
        keep_ref[plane] = gout_ref[block_rows(2 * plane + core, slab), :]
        send_ref[plane] = gout_ref[block_rows(2 * plane + 1 - core, slab), :]


def out_back(where, own, recv, residual, dy, gain, w_out, attn, planes):
    rows, model = own.shape
    vmem = pl.BlockSpec(memory_space=pltpu.VMEM)
    half = shape_of((planes, model // planes // 2, model), LOW)
    return pl.pallas_call(
        out_back_kernel,
        in_specs=[SMEM] + [vmem] * 8,
        out_specs=[vmem] * 5,
        out_shape=[
            shape_of((attn[0].shape[0], 2, *attn[0].shape[2:]), LOW),
            shape_of((rows, model), F32),
            shape_of((1, model), F32),
            half,
            half,
        ],
        scratch_shapes=[pltpu.VMEM((model, model), LOW)],
        compiler_params=params(),
        cost_estimate=cost(8 * rows * model * model, rows * model * 20),
        name="out_back",
    )(where, own, recv, residual, dy, gain, w_out, *attn)


def gate_and_slope(gate):
    inner = 0.7978845608028654 * (gate + 0.044715 * gate * gate * gate)
    bent = jnp.tanh(inner)
    half = 0.5 * (1.0 + bent)
    slope = half + 0.5 * gate * (1.0 - bent * bent) * (
        0.7978845608028654 * (1.0 + 3.0 * 0.044715 * gate * gate)
    )
    return gate * half, slope


def ffn_first_kernel(
    where_ref, nf_own_ref, nf_other_ref, dy_own_ref, dy_other_ref,
    gate_own, up_own, down_own, x1, x2, x3, y1, y2, y3, sx1, sx2, sx3, sy1, sy2, sy3,
    hidden_ref, dup_ref, own_ref, other_ref, down_ref, g0_ref, g1_ref, g2_ref, g3_ref,
    gate_ref, up_ref, nf_ref, nft_ref, dy_ref, total_ref, dgate_ref, grad_ref, sems,
):
    step = pl.program_id(0)
    half = nf_own_ref.shape[0]
    chip, core, plane = where_ref[0], where_ref[1], where_ref[2]
    wide, model, _ = gate_ref.shape
    units = down_ref.shape[0]
    tile = hidden_ref.shape[1]
    depth = gate_own.shape[1]
    planes = model // depth
    slab = depth // 2
    part = units // planes
    quarter = part // 4

    @pl.when(step == 0)
    def _():
        copies = []

        def copy(source, target):
            started = pltpu.make_async_copy(source, target, sems.at[len(copies)])
            started.start()
            copies.append(started)

        own_rows = pl.ds(pl.multiple_of(plane * depth, depth), depth)
        for index in range(wide):
            copy(gate_own.at[index], gate_ref.at[index, own_rows, :])
            copy(up_own.at[index], up_ref.at[index, own_rows, :])
        copy(
            down_own.at[pl.ds(pl.multiple_of(core * part, part), part), :],
            down_ref.at[pl.ds(pl.multiple_of(plane * part, part), part), :],
        )
        for back in range(planes - 1):
            owner = lax.rem(plane + planes - 1 - back, planes)
            for along, straight, swapped, weight_ref, side in (
                (0, (x1, x2, x3)[back], (sx1, sx2, sx3)[back], gate_ref, lax.rem(chip, 2)),
                (1, (y1, y2, y3)[back], (sy1, sy2, sy3)[back], up_ref, chip // 2),
            ):
                for piece, here in ((straight, side), (swapped, 1 - side)):
                    at = pl.ds(pl.multiple_of(owner * depth + here * slab, slab), slab)
                    for index in range(wide):
                        copy(
                            piece.at[pl.ds(index * slab, slab), :],
                            weight_ref.at[index, at, :],
                        )
                    copy(
                        piece.at[pl.ds(wide * slab, quarter), :],
                        down_ref.at[
                            pl.ds(
                                pl.multiple_of(
                                    owner * part + (2 * along + here) * quarter, quarter
                                ),
                                quarter,
                            ),
                            :,
                        ],
                    )
        nf_ref[:half, :] = nf_own_ref[...]
        nf_ref[half:, :] = nf_other_ref[...]
        nft_ref[:, :half] = jnp.transpose(nf_own_ref[...])
        nft_ref[:, half:] = jnp.transpose(nf_other_ref[...])
        dy_ref[:half, :] = dy_own_ref[...]
        dy_ref[half:, :] = dy_other_ref[...]
        total_ref[...] = jnp.zeros_like(total_ref)
        for started in copies:
            started.wait()

    per = model // tile
    index = step // per
    lanes = pl.ds(pl.multiple_of(lax.rem(step, per) * tile, tile), tile)
    gate_w = gate_ref[index, :, lanes]
    up_w = up_ref[index, :, lanes]
    down_w = down_ref[block_rows(step, tile), :]
    for quarter_rows in range(4):
        rows = slice(quarter_rows * half // 2, (quarter_rows + 1) * half // 2)
        nf = nf_ref[rows, :]
        gate = dot(nf, gate_w)
        up = dot(nf, up_w)
        dhidden = dot(dy_ref[rows, :], down_w, NT)
        bent, slope = gate_and_slope(gate)
        hidden_ref[rows, :] = (bent * up).astype(LOW)
        dgate = (dhidden * up * slope).astype(LOW)
        dup = (dhidden * bent).astype(LOW)
        dgate_ref[rows, :] = dgate
        dup_ref[rows, :] = dup
        total_ref[rows, :] += dot(dgate, gate_w, NT) + dot(dup, up_w, NT)

    grad_ref[...] = dot(nft_ref[...], dgate_ref[...]).astype(LOW)
    for away, out_ref in enumerate((g0_ref, g1_ref, g2_ref, g3_ref)):
        out_ref[0] = grad_ref[block_rows(lax.rem(plane + away, planes), depth), :]

    @pl.when(step == pl.num_programs(0) - 1)
    def _():
        own_ref[...] = total_ref[:half, :]
        other_ref[...] = total_ref[half:, :].astype(LOW)


def ffn_first(where, nf_own, nf_other, dy_own, dy_other, own_weights, pieces, tile=TILE):
    half, model = nf_own.shape
    wide, depth, _ = own_weights[0].shape
    units = wide * model
    per = model // tile
    whole = pl.BlockSpec((half, model), lambda t: (0, 0))
    lane_tile = pl.BlockSpec((2 * half, tile), lambda t: (0, t))
    grad_tile = pl.BlockSpec((1, depth, tile), lambda t: (t // per, 0, t % per))
    copies = 2 * wide + 1 + 3 * 4 * (wide + 1)
    return pl.pallas_call(
        ffn_first_kernel,
        grid=(units // tile,),
        in_specs=[SMEM, whole, whole, whole, whole] + [ANY] * 15,
        out_specs=[
            lane_tile, lane_tile, whole, whole,
            pl.BlockSpec((units, model), lambda t: (0, 0)),
        ]
        + [grad_tile] * 4,
        out_shape=[
            shape_of((2 * half, units), LOW),
            shape_of((2 * half, units), LOW),
            shape_of((half, model), F32),
            shape_of((half, model), LOW),
            shape_of((units, model), LOW),
        ]
        + [shape_of((wide, depth, model), LOW)] * 4,
        scratch_shapes=[
            pltpu.VMEM((wide, model, model), LOW),
            pltpu.VMEM((wide, model, model), LOW),
            pltpu.VMEM((2 * half, model), LOW),
            pltpu.VMEM((model, 2 * half), LOW),
            pltpu.VMEM((2 * half, model), LOW),
            pltpu.VMEM((2 * half, model), F32),
            pltpu.VMEM((2 * half, tile), LOW),
            pltpu.VMEM((model, tile), LOW),
            pltpu.SemaphoreType.DMA((copies,)),
        ],
        compiler_params=params(),
        cost_estimate=cost(
            2 * 2 * 6 * 2 * half * model * units,
            6 * model * units + 12 * half * units + 20 * half * model,
        ),
        name="ffn_first",
    )(where, nf_own, nf_other, dy_own, dy_other, *own_weights, *pieces)


def ffn_second_kernel(
    where_ref, nf_own_ref, nf_other_ref, dy_own_ref, dy_other_ref, hidden_ref, dup_ref, down_ref,
    own_ref, other_ref, u_keep_ref, u_send_ref, f_keep_ref, f_send_ref,
    nft_ref, dy_ref, total_ref, grad_ref, gdown_ref,
):
    step = pl.program_id(0)
    half = nf_own_ref.shape[0]
    chip = where_ref[0]
    x_side, y_side = lax.rem(chip, 2), chip // 2
    planes, _, slab, tile = u_keep_ref.shape

    @pl.when(step == 0)
    def _():
        nft_ref[:, :half] = jnp.transpose(nf_own_ref[...])
        nft_ref[:, half:] = jnp.transpose(nf_other_ref[...])
        dy_ref[:half, :] = dy_own_ref[...]
        dy_ref[half:, :] = dy_other_ref[...]
        total_ref[...] = jnp.zeros_like(total_ref)

    hidden = hidden_ref[...]
    grad_ref[...] = dot(nft_ref[...], dup_ref[...]).astype(LOW)
    for plane in range(planes):
        u_keep_ref[plane, 0] = grad_ref[block_rows(2 * plane + x_side, slab), :]
        u_send_ref[plane, 0] = grad_ref[block_rows(2 * plane + 1 - x_side, slab), :]
    gdown_ref[block_rows(step, tile), :] = dot(jnp.transpose(hidden), dy_ref[...]).astype(LOW)
    total_ref[...] += dot(hidden, down_ref[...])

    @pl.when(step == pl.num_programs(0) - 1)
    def _():
        own_ref[...] = total_ref[:half, :]
        other_ref[...] = total_ref[half:, :].astype(LOW)
        rows = f_keep_ref.shape[1]
        for plane in range(planes):
            f_keep_ref[plane] = gdown_ref[block_rows(2 * plane + y_side, rows), :]
            f_send_ref[plane] = gdown_ref[block_rows(2 * plane + 1 - y_side, rows), :]


def ffn_second(
    where, nf_own, nf_other, dy_own, dy_other, hidden, dup, w_down, planes, tile=TILE
):
    half, model = nf_own.shape
    units = hidden.shape[1]
    wide, slab, rows = units // model, model // planes // 2, units // planes // 2
    per = model // tile
    whole = pl.BlockSpec((half, model), lambda t: (0, 0))
    lane_tile = pl.BlockSpec((2 * half, tile), lambda t: (0, t))
    row_tile = pl.BlockSpec((tile, model), lambda t: (t, 0))
    up_tile = pl.BlockSpec((planes, 1, slab, tile), lambda t: (0, t // per, 0, t % per))
    down_whole = pl.BlockSpec((planes, rows, model), lambda t: (0, 0, 0))
    return pl.pallas_call(
        ffn_second_kernel,
        grid=(units // tile,),
        in_specs=[SMEM, whole, whole, whole, whole, lane_tile, lane_tile, row_tile],
        out_specs=[whole, whole, up_tile, up_tile, down_whole, down_whole],
        out_shape=[
            shape_of((half, model), F32),
            shape_of((half, model), LOW),
            shape_of((planes, wide, slab, model), LOW),
            shape_of((planes, wide, slab, model), LOW),
            shape_of((planes, rows, model), LOW),
            shape_of((planes, rows, model), LOW),
        ],
        scratch_shapes=[
            pltpu.VMEM((model, 2 * half), LOW),
            pltpu.VMEM((2 * half, model), LOW),
            pltpu.VMEM((2 * half, model), F32),
            pltpu.VMEM((model, tile), LOW),
            pltpu.VMEM((units, model), LOW),
        ],
        compiler_params=params(),
        cost_estimate=cost(
            2 * 2 * 3 * 2 * half * model * units,
            8 * model * units + 12 * half * units + 20 * half * model,
        ),
        name="ffn_second",
    )(where, nf_own, nf_other, dy_own, dy_other, hidden, dup, w_down)


def second_halves_kernel(
    where_ref, u_keep_ref, u_came_ref, f_keep_ref, f_came_ref,
    u_mine_ref, u_send_ref, f_mine_ref, f_send_ref,
):
    chip = where_ref[0]
    x_side, y_side = lax.rem(chip, 2), chip // 2
    for wanted, u_ref, f_ref in ((0, u_mine_ref, f_mine_ref), (1, u_send_ref, f_send_ref)):
        u_side = jnp.bitwise_xor(y_side, wanted)
        rows = block_rows(u_side, u_ref.shape[2])
        u_ref[...] = (
            u_keep_ref[:, :, rows, :].astype(F32) + u_came_ref[:, :, rows, :].astype(F32)
        ).astype(LOW)
        f_side = jnp.bitwise_xor(x_side, wanted)
        rows = block_rows(f_side, f_ref.shape[1])
        f_ref[...] = (
            f_keep_ref[:, rows, :].astype(F32) + f_came_ref[:, rows, :].astype(F32)
        ).astype(LOW)


def second_halves(where, u_keep, u_came, f_keep, f_came):
    planes, wide, slab, model = u_keep.shape
    rows = f_keep.shape[1]
    vmem = pl.BlockSpec(memory_space=pltpu.VMEM)
    return pl.pallas_call(
        second_halves_kernel,
        in_specs=[SMEM] + [vmem] * 4,
        out_specs=[vmem] * 4,
        out_shape=[
            shape_of((planes, wide, slab // 2, model), LOW),
            shape_of((planes, wide, slab // 2, model), LOW),
            shape_of((planes, rows // 2, model), LOW),
            shape_of((planes, rows // 2, model), LOW),
        ],
        compiler_params=params(),
        cost_estimate=cost(0, 7e6),
        name="second_halves",
    )(where, u_keep, u_came, f_keep, f_came)


def by_chip_kernel(where_ref, *refs):
    gate_refs, keep_ref, came_ref, out_refs = refs[:4], refs[4], refs[5], refs[6:]
    chip = where_ref[0]
    wide, depth, model = gate_refs[0].shape
    planes, slab, _ = keep_ref.shape
    rows, half, lanes = depth // 4, slab // 2, model // 2
    for away, out_ref in enumerate(out_refs):
        to_chip = jnp.bitwise_xor(chip, away)
        to_x, to_y = lax.rem(to_chip, 2), to_chip // 2
        at = block_rows(to_x * 2 + to_y, rows)
        for index in range(wide):
            total = gate_refs[0][index, at, :].astype(F32)
            for gate_ref in gate_refs[1:]:
                total = total + gate_ref[index, at, :].astype(F32)
            out_ref[index * rows : (index + 1) * rows, :] = total.astype(LOW)
        columns = block_rows(to_y, lanes)
        for plane in range(planes):
            low = wide * rows + (plane // 2) * half
            left = (plane % 2) * lanes
            out_ref[low : low + half, left : left + lanes] = (
                keep_ref[plane, block_rows(to_x, half), columns].astype(F32)
                + came_ref[plane, block_rows(to_x, half), columns].astype(F32)
            ).astype(LOW)


def by_chip(where, gates, keep, came):
    wide, depth, model = gates[0].shape
    planes, slab, _ = keep.shape
    vmem = pl.BlockSpec(memory_space=pltpu.VMEM)
    return pl.pallas_call(
        by_chip_kernel,
        in_specs=[SMEM] + [vmem] * 6,
        out_specs=[vmem] * 4,
        out_shape=[shape_of((wide * depth // 4 + planes * slab // 4, model), LOW)] * 4,
        compiler_params=params(),
        cost_estimate=cost(0, 3e6),
        name="by_chip",
    )(where, *gates, keep, came)


def by_plane_kernel(where_ref, *refs):
    u_ref, u_came_ref, f_ref, f_came_ref, w_ref, w_came_ref, line_ref, line_came_ref = refs[:8]
    part_refs, out_refs, gate_ref = refs[8:12], refs[12:16], refs[16]
    plane = where_ref[2]
    planes, wide, rows, model = u_ref.shape
    slab = w_ref.shape[1]
    half, lanes = slab // 2, model // 2

    def four(at, columns):
        total = part_refs[0][at, columns].astype(F32)
        for part_ref in part_refs[1:]:
            total = total + part_ref[at, columns].astype(F32)
        return total.astype(LOW)

    gate_ref[...] = four(slice(0, wide * rows), slice(0, model))
    for away, out_ref in enumerate(out_refs):
        at = lax.rem(plane + away, planes)

        def both(ref, came_ref):
            return (ref[at].astype(F32) + came_ref[at].astype(F32)).astype(LOW)

        for index in range(wide):
            out_ref[index * rows : (index + 1) * rows, :] = (
                u_ref[at, index].astype(F32) + u_came_ref[at, index].astype(F32)
            ).astype(LOW)
        low = wide * rows
        out_ref[low : low + f_ref.shape[1], :] = both(f_ref, f_came_ref)
        low = low + f_ref.shape[1]
        used = 3 * model // 4
        out_ref[low : low + slab, :used] = both(w_ref, w_came_ref)[:, :used]
        out_part = four(
            pl.ds(pl.multiple_of(wide * rows + at // 2 * half, half), half),
            pl.ds(pl.multiple_of(lax.rem(at, 2) * lanes, lanes), lanes),
        )
        out_ref[low : low + half, used:] = out_part[:, : model - used]
        out_ref[low + half : low + slab, used:] = out_part[:, model - used :]
        out_ref[low + slab :, :] = both(line_ref, line_came_ref)


def by_plane(where, u_mine, u_came, f_mine, f_came, w_keep, w_came, line_keep, line_came, parts):
    planes, wide, slab, model = u_mine.shape
    rows = wide * slab + f_mine.shape[1] + w_keep.shape[1] + line_keep.shape[1]
    vmem = pl.BlockSpec(memory_space=pltpu.VMEM)
    return pl.pallas_call(
        by_plane_kernel,
        in_specs=[SMEM] + [vmem] * 12,
        out_specs=[vmem] * (planes + 1),
        out_shape=[shape_of((rows, model), LOW)] * planes + [shape_of((wide * slab, model), LOW)],
        compiler_params=params(),
        cost_estimate=cost(0, 6e6),
        name="by_plane",
    )(
        where, u_mine, u_came, f_mine, f_came, w_keep, w_came, line_keep, line_came, *parts
    )


def unpack_kernel(where_ref, *refs):
    piece_refs = refs[:8]
    gate_ref, up_ref, down_ref, q_ref, k_ref, v_ref, out_ref, small_ref = refs[8:]
    chip, core = where_ref[0], where_ref[1]
    depth, units = gate_ref.shape
    model = down_ref.shape[1]
    part = down_ref.shape[0] // 2
    quarter, slab = depth // 4, depth // 2
    wide = units // 2 // model
    planes = units // 2 // part
    width, lanes, half = model // 4, model // 2, slab // 2
    small = jnp.zeros(small_ref.shape, F32)
    for far in range(8):
        away, other = far % 4, far // 4
        from_core = core if other == 0 else 1 - core
        from_chip = jnp.bitwise_xor(chip, away)
        from_x, from_y = lax.rem(from_chip, 2), from_chip // 2
        piece_ref = piece_refs[far]
        gate_rows = block_rows(from_x * 2 + from_y, quarter)
        for plane in range(planes):
            index, at = divmod(plane * part, model)
            columns = pl.ds(pl.multiple_of(plane * 2 * part + from_core * part, 128), part)
            rows = slice(index * quarter, (index + 1) * quarter)
            gate_ref[gate_rows, columns] = piece_ref[rows, at : at + part].astype(F32)
            rows = slice((wide + index) * quarter, (wide + index + 1) * quarter)
            up_ref[gate_rows, columns] = piece_ref[rows, at : at + part].astype(F32)
        low = 2 * wide * quarter
        rows = part // 4
        down_ref[block_rows(from_core * 4 + from_y * 2 + from_x, rows), :] = piece_ref[
            low : low + rows, :
        ].astype(F32)
        low = low + rows
        used = 3 * width
        out_ref[block_rows(from_core * 2 + from_x, half), block_rows(from_y, lanes)] = (
            jnp.concatenate(
                [piece_ref[low : low + half, used:], piece_ref[low + half : low + slab, used:]],
                axis=1,
            ).astype(F32)
        )
        for home in range(4):

            @pl.when(from_chip == home)
            def _(home=home, piece_ref=piece_ref, from_core=from_core, low=low):
                to_lanes = slice(home * width, (home + 1) * width)
                for kind, target_ref in enumerate((q_ref, k_ref, v_ref)):
                    target_ref[block_rows(from_core, slab), to_lanes] = piece_ref[
                        low : low + slab, kind * width : (kind + 1) * width
                    ].astype(F32)

        small = small + piece_ref[low + slab :, :].astype(F32)
    small_ref[...] = small


def unpack(where, pieces, depth, units):
    rows, model = pieces[0].shape
    planes = model // depth
    part = units // planes
    taken = units // 2 // model * depth // 2 + part // 8 + depth // 2
    vmem = pl.BlockSpec(memory_space=pltpu.VMEM)
    return pl.pallas_call(
        unpack_kernel,
        in_specs=[SMEM] + [vmem] * 8,
        out_specs=[vmem] * 8,
        out_shape=[
            shape_of((depth, units), F32),
            shape_of((depth, units), F32),
            shape_of((part, model), F32),
            shape_of((depth, model), F32),
            shape_of((depth, model), F32),
            shape_of((depth, model), F32),
            shape_of((depth, model), F32),
            shape_of((rows - taken, model), F32),
        ],
        compiler_params=params(),
        cost_estimate=cost(0, 24e6),
        name="unpack",
    )(where, *pieces)


def finish_out_kernel(order_ref, lens_ref, start_ref, res_ref, own_ref, recv_ref, out_ref):
    slot = pl.program_id(0)
    total = res_ref[...] + own_ref[...] + recv_ref[...].astype(F32)
    place_in = lax.broadcasted_iota(jnp.int32, total.shape, 0) + start_ref[0]
    out_ref[0] = jnp.where(place_in < lens_ref[slot], total, 0.0).astype(LOW)


def finish_out(order, lens, start, residual, own, recv, batch):
    rows, model = residual.shape[0] // batch, residual.shape[1]
    in_order = pl.BlockSpec((rows, model), lambda s, order, lens, start: (s, 0))
    return pl.pallas_call(
        finish_out_kernel,
        grid_spec=pltpu.PrefetchScalarGridSpec(
            num_scalar_prefetch=3,
            grid=(batch,),
            in_specs=[in_order, in_order, in_order],
            out_specs=pl.BlockSpec((1, rows, model), lambda s, order, lens, start: (order[s], 0, 0)),
        ),
        out_shape=shape_of((batch, rows, model), LOW),
        compiler_params=params(),
        cost_estimate=cost(0, 6e6),
        name="finish_out",
    )(order, lens, start, residual, own, recv)


def finish_tokens_kernel(order_ref, dn_ref, tok_ref, dres_ref, gain_ref, out_ref):
    grad = dn_ref[0, 0].astype(F32)
    for chip in range(1, dn_ref.shape[0]):
        grad = grad + dn_ref[chip, 0].astype(F32)
    rows_f = tok_ref[...].astype(F32)
    scale = rms_rows(rows_f)
    unit = rows_f * scale
    inner = grad * gain_ref[...]
    out_ref[0] = dres_ref[...] + scale * (
        inner - unit * jnp.mean(inner * unit, axis=-1, keepdims=True)
    )


def finish_tokens(order, dn, tokens, dres, gain):
    chips, batch, rows, model = dn.shape
    in_order = pl.BlockSpec((rows, model), lambda s, order: (s, 0))
    return pl.pallas_call(
        finish_tokens_kernel,
        grid_spec=pltpu.PrefetchScalarGridSpec(
            num_scalar_prefetch=1,
            grid=(batch,),
            in_specs=[
                pl.BlockSpec((chips, 1, rows, model), lambda s, order: (0, s, 0, 0)),
                in_order,
                in_order,
                pl.BlockSpec((1, model), lambda s, order: (0, 0)),
            ],
            out_specs=pl.BlockSpec((1, rows, model), lambda s, order: (order[s], 0, 0)),
        ),
        out_shape=shape_of((batch, rows, model), F32),
        compiler_params=params(),
        cost_estimate=cost(0, 10e6),
        name="finish_tokens",
    )(order, dn, tokens, dres, gain)


CORE, X, Y, XY = 1, 2, 4, 6


def swap(values, bits):
    count = lax.axis_size("ctx")
    return lax.ppermute(values, "ctx", [(i, i ^ bits) for i in range(count)])


def shift(values, places):
    count = lax.axis_size("fsdp")
    return lax.ppermute(values, "fsdp", [(i, (i + places) % count) for i in range(count)])


def column_ends(piece):
    return shift(piece, 1), shift(piece, 3)


def after(values, *others):
    return lax.optimization_barrier((values, *others))[0]


def pick(values, index, axis):
    return lax.dynamic_index_in_dim(values, index, axis, keepdims=False)


def add(*parts):
    total = parts[0].astype(F32)
    for part in parts[1:]:
        total = total + part.astype(F32)
    return total.astype(LOW)


def column_sum(picks):
    return [picks[0]] + [shift(picks[away], away) for away in range(1, len(picks))]


def plane_swaps(parts):
    return [parts[0], swap(parts[1], X), swap(parts[2], Y), swap(parts[3], XY)]


def per_device_plane(
    tokens, cotangent, lengths, bucket_table, gain_attn, w_query, w_key, w_value, w_out,
    bias_table, gain_ffn, w_gate, w_up, w_ffn_out,
):
    batch, rows, model = tokens.shape
    planes = lax.axis_size("fsdp")
    chips = lax.axis_size("ctx") // 2
    me = lax.axis_index("ctx")
    plane = lax.axis_index("fsdp")
    core, chip = me % 2, me // 2
    depth, units = w_gate.shape
    chip_heads = HEADS // chips
    width = chip_heads * HEAD_DIM
    where = jnp.stack([chip, core, plane]).astype(jnp.int32)
    start = (me * rows)[None].astype(jnp.int32)

    small = jnp.concatenate([gain_attn, gain_ffn, bias_table.reshape(-1)])
    small = jnp.pad(small[None], ((0, 15), (0, model - small.shape[0])))
    gate_mine, up_mine, x_piece, y_piece, qkv_mine, early_piece = pack_weights(
        where, w_gate, w_up, w_ffn_out, w_out, w_query, w_key, w_value, small
    )
    send, order, lens = prepare(lengths, after(tokens, early_piece), chips)
    gathered = lax.all_to_all(send.reshape(2 * chips, 2, rows, model), "ctx", 0, 0)

    near, far = column_ends(early_piece)
    early = [near, shift(near, 1), far]
    early_others = [swap(piece, CORE) for piece in early]
    x_piece, y_piece, *_ = lax.optimization_barrier((x_piece, y_piece, *early))
    x_near, x_far = column_ends(x_piece)
    y_near, y_far = column_ends(y_piece)

    by_distance = jnp.stack([piece[depth] for piece in [early_piece] + early])
    all_small = jnp.stack([pick(by_distance, (plane + planes - i) % planes, 0) for i in range(planes)])
    full_gain_attn = all_small[:, :depth].reshape(1, model).astype(F32)
    full_gain_ffn = all_small[:, depth : 2 * depth].reshape(1, model).astype(F32)
    small_end = 2 * depth + bias_table.size
    full_table = all_small[:, 2 * depth : small_end].reshape(BUCKETS, HEADS)

    hot = bucket_table[:, None] == jnp.arange(BUCKETS, dtype=jnp.int32)[None, :]
    hot = jnp.concatenate([hot, jnp.zeros((1, BUCKETS), bool)])
    my_table = lax.dynamic_slice_in_dim(full_table, chip * chip_heads, chip_heads, 1)
    offsets = jnp.einsum("tb,bh->ht", hot.astype(LOW), my_table, preferred_element_type=F32)

    first_out, *kept, w_qkv = attn_forward(
        0, lens, where, gathered, full_gain_attn, [qkv_mine, *early, *early_others], offsets
    )
    x_near, y_near, x_far, y_far, first_out = lax.optimization_barrier(
        (x_near, y_near, x_far, y_far, first_out)
    )
    x_found = [x_near, shift(x_near, 1), x_far]
    y_found = [y_near, shift(y_near, 1), y_far]
    x_swapped, y_swapped = [swap(t, X) for t in x_found], [swap(t, Y) for t in y_found]
    second_out, *kept = attn_forward(
        1, lens, where, gathered, full_gain_attn, [w_qkv], offsets, kept
    )
    attn = [lax.all_to_all(part, "ctx", 0, 0) for part in (first_out, second_out)]
    attn_full, query, key, value = kept
    flat, dy = sort_rows(order, lens, start, tokens, cotangent)
    residual, nf_own, full_out = out_project(
        where, flat, attn, w_out, early, early_others, full_gain_ffn
    )
    dy_other = swap(dy, CORE)
    nf_other = swap(nf_own, CORE)
    hidden, dup, dnf_own, dnf_send, full_down, *g_picks = ffn_first(
        where, nf_own, nf_other, dy, dy_other, (gate_mine, up_mine, w_ffn_out),
        x_found + y_found + x_swapped + y_swapped,
    )

    g_parts = column_sum(g_picks)
    dattn, dres, dgain_ffn, o_keep, o_send = out_back(
        where, dnf_own, swap(dnf_send, CORE), residual, dy, full_gain_ffn, full_out, attn, planes
    )
    dattn_all = lax.all_to_all(dattn, "ctx", 0, 0)
    o_came = swap(o_send, CORE)
    out_own, out_send, u_keep, u_send, f_keep, f_send = ffn_second(
        where, nf_own, nf_other, dy, dy_other, hidden, dup, full_down, planes
    )
    g_parts[1], g_parts[3], u_send, f_send, dattn_all = lax.optimization_barrier(
        (g_parts[1], g_parts[3], u_send, f_send, dattn_all)
    )
    u_came, f_came = swap(u_send, X), swap(f_send, Y)
    out_came = swap(out_send, CORE)
    dn, dw_keep, dw_send, dgain_attn, doffsets = attn_backward(
        lens, where, gathered, full_gain_attn, w_qkv, offsets,
        query, key, value, attn_full, dattn_all, planes,
    )

    u_came, f_came, dn, dw_send, dgain_attn, *g_parts = lax.optimization_barrier(
        (u_came, f_came, dn, dw_send, dgain_attn, *g_parts)
    )
    u_mine, u_send, f_mine, f_send = second_halves(where, u_keep, u_came, f_keep, f_came)
    u_came, f_came = swap(u_send, Y), swap(f_send, X)
    w_came = swap(dw_send, CORE)
    chip_parts = plane_swaps(by_chip(where, g_parts, o_keep, o_came))

    out_rows = finish_out(order, lens, start, residual, out_own, out_came, batch)
    mine_buckets = jnp.einsum(
        "ht,tb->bh", doffsets, hot.astype(F32), precision=lax.Precision.HIGHEST
    )
    buckets = lax.dynamic_update_slice_in_dim(
        jnp.zeros((BUCKETS, HEADS), F32), mine_buckets, chip * chip_heads, 1
    )
    line = jnp.concatenate(
        [
            dgain_attn.reshape(planes, depth),
            dgain_ffn.reshape(planes, depth),
            buckets.reshape(planes, -1),
        ],
        axis=1,
    ).astype(LOW)
    line = jnp.pad(line[:, None, :], ((0, 0), (0, 15), (0, model - line.shape[1])))
    nothing = jnp.zeros_like(line)
    line_came = swap(jnp.where(core == 1, line, nothing), CORE)
    line_kept = jnp.where(core == 0, line, nothing)
    *plane_parts, gate_part = by_plane(
        where, u_mine, u_came, f_mine, f_came, dw_keep, w_came, line_kept, line_came, chip_parts
    )
    dn, *plane_parts = lax.optimization_barrier((dn, *plane_parts))
    dn = lax.all_to_all(dn, "ctx", 0, 0).reshape(chips, batch, rows, model)
    dtok = finish_tokens(order, dn, flat, dres, full_gain_attn)
    pack = jnp.concatenate([gate_part, add(*column_sum(plane_parts))])

    packs = plane_swaps([after(pack, out_rows)] * 4)
    packs = packs + [swap(piece, CORE) for piece in packs]
    packs[-1] = after(packs[-1], dtok)
    grad_gate, grad_up, grad_down, grad_query, grad_key, grad_value, grad_out, sums = unpack(
        where, packs, depth, units
    )
    grad_gain_attn = sums[0, :depth]
    grad_gain_ffn = sums[0, depth : 2 * depth]
    grad_buckets = sums[0, 2 * depth : small_end].reshape(BUCKETS // planes, HEADS)

    return (
        out_rows, dtok, grad_gain_attn, grad_query, grad_key, grad_value, grad_out, grad_buckets,
        grad_gain_ffn, grad_gate, grad_up, grad_down,
    )


def gelu_tanh(values):
    return (
        0.5
        * values
        * (1.0 + jnp.tanh(0.7978845608028654 * (values + 0.044715 * values * values * values)))
    )


def normalize(values, gain_vec):
    return (
        values * lax.rsqrt(jnp.mean(values * values, axis=-1, keepdims=True) + norm_eps) * gain_vec
    )


def project(values, matrix):
    return jnp.einsum("msd,de->mse", values, matrix, preferred_element_type=jnp.float32)


def back_project(values, matrix):
    return jnp.einsum("mse,de->msd", values, matrix, preferred_element_type=jnp.float32)


def outer_sum(left_rows, right_rows):
    return jnp.einsum("msd,mse->de", left_rows, right_rows, preferred_element_type=jnp.float32)


def split_heads(values):
    return values.reshape(values.shape[0], values.shape[1], HEADS, HEAD_DIM)


def toeplitz_bias(offset_bias, start, query_rows, key_rows):
    span = query_rows + key_rows - 1
    window = lax.dynamic_slice_in_dim(offset_bias, start, span, 1)
    wrapped = jnp.concatenate(
        [
            window[:, query_rows - 1 :],
            jnp.zeros((window.shape[0], 1), jnp.float32),
            window[:, : query_rows - 1],
        ],
        axis=1,
    )
    tiled = jnp.tile(wrapped, (1, query_rows))
    shaped = tiled[:, : query_rows * span].reshape(window.shape[0], query_rows, span)
    return shaped[:, :, :key_rows]


def diagonal_sums(grad_bias, query_rows, key_rows):
    span = query_rows + key_rows - 1
    heads = grad_bias.shape[0]
    padded = jnp.pad(grad_bias, ((0, 0), (0, 0), (0, span - key_rows)))
    flat = jnp.pad(padded.reshape(heads, query_rows * span), ((0, 0), (0, query_rows)))
    slots = jnp.sum(flat.reshape(heads, query_rows, span + 1), axis=1)
    return jnp.concatenate([slots[:, key_rows + 1 :], slots[:, :key_rows]], axis=1)


def block_scores(query_heads, key_heads, pair_bias, key_ok):
    scores = jnp.einsum(
        "mihe,mjhe->mhij", query_heads, key_heads, preferred_element_type=jnp.float32
    )
    scores = scores + pair_bias[None]
    return jnp.where(key_ok[:, None, None, :], scores, -1e30)


def over_blocks(update, make_bias, carried, pieces):
    piece_rows = pieces[0].shape[1]
    block_rows = math.gcd(piece_rows, 256)
    block_count = piece_rows // block_rows

    def advance(block_index, running):
        block_start = block_index * block_rows
        sub_pieces = tuple(
            (
                lax.dynamic_slice_in_dim(member, block_index * block_rows, block_rows, 1)
                for member in pieces
            )
        )
        bias_info = make_bias(block_start, block_rows)
        return update(running, sub_pieces, block_start, slice(None), bias_info)

    return lax.fori_loop(0, block_count, advance, carried)


def per_device_general(
    tokens,
    cotangent,
    lengths,
    bucket_table,
    gain_attn,
    w_query,
    w_key,
    w_value,
    w_out,
    bias_table,
    gain_ffn,
    w_gate,
    w_up,
    w_ffn_out,
):
    shards = (
        gain_attn,
        w_query,
        w_key,
        w_value,
        w_out,
        bias_table,
        gain_ffn,
        w_gate,
        w_up,
        w_ffn_out,
    )
    gathered = (
        lax.all_gather(shards[0], "fsdp", axis=0, tiled=True),
        lax.all_gather(shards[1], "fsdp", axis=0, tiled=True),
        lax.all_gather(shards[2], "fsdp", axis=0, tiled=True),
        lax.all_gather(shards[3], "fsdp", axis=0, tiled=True),
        lax.all_gather(shards[4], "fsdp", axis=0, tiled=True),
        lax.all_gather(shards[5], "fsdp", axis=0, tiled=True),
        lax.all_gather(shards[6], "fsdp", axis=0, tiled=True),
        lax.all_gather(shards[7], "fsdp", axis=0, tiled=True),
        lax.all_gather(shards[8], "fsdp", axis=0, tiled=True),
        lax.all_gather(shards[9], "fsdp", axis=0, tiled=True),
    )
    (
        full_gain_attn,
        full_query,
        full_key,
        full_value,
        full_out,
        full_bias,
        full_gain_ffn,
        full_gate,
        full_up,
        full_ffn_out,
    ) = gathered
    batch_rows, local_rows, model_width = tokens.shape
    seq_len = local_rows * lax.axis_size("ctx")
    table_len = bucket_table.shape[0]
    first_pos = lax.axis_index("ctx") * local_rows
    positions = first_pos + jnp.arange(local_rows, dtype=jnp.int32)
    valid_mask = positions[None, :] < lengths[:, None]
    valid_rows = valid_mask.astype(jnp.float32)
    bucket_hot = bucket_table[:, None] == jnp.arange(BUCKETS, dtype=jnp.int32)[None, :]

    def offset_bias_of(bias_weights):
        return jnp.einsum(
            "tb,bh->ht",
            bucket_hot.astype(jnp.bfloat16),
            bias_weights,
            preferred_element_type=jnp.float32,
        )

    forward_offsets = offset_bias_of(full_bias)

    def keys_bias(offset_bias):

        def keys_make(block_start, block_rows):
            start = block_start - first_pos - (local_rows - 1) + (seq_len - 1)
            return (toeplitz_bias(offset_bias, start, local_rows, block_rows), start)

        return keys_make

    def queries_bias(offset_bias):

        def queries_make(block_start, block_rows):
            start = first_pos - block_start - (block_rows - 1) + (seq_len - 1)
            return (toeplitz_bias(offset_bias, start, block_rows, local_rows), start)

        return queries_make

    tokens_f = tokens.astype(jnp.float32)
    attn_gain = full_gain_attn.astype(jnp.float32)
    normed = normalize(tokens_f, attn_gain).astype(jnp.bfloat16)
    queries = project(normed, full_query).astype(jnp.bfloat16)
    keys_local = project(normed, full_key).astype(jnp.bfloat16)
    values_local = project(normed, full_value).astype(jnp.bfloat16)
    query_heads = split_heads(queries)

    def forward_block(running, sub_pieces, block_start, member_pick, bias_info):
        max_score, row_total, weighted = running
        key_part, value_part = sub_pieces
        key_pos = block_start + jnp.arange(key_part.shape[1], dtype=jnp.int32)
        key_ok = key_pos[None, :] < lengths[:, None]
        scores = block_scores(query_heads, split_heads(key_part), bias_info[0], key_ok)
        new_max = jnp.maximum(max_score, jnp.max(scores, axis=-1))
        shrink = jnp.exp(max_score - new_max)
        weights = jnp.exp(scores - new_max[..., None])
        row_total = row_total * shrink + jnp.sum(weights, axis=-1)
        weighted = weighted * jnp.transpose(shrink, (0, 2, 1))[..., None] + jnp.einsum(
            "mhij,mjhe->mihe",
            weights.astype(jnp.bfloat16),
            split_heads(value_part),
            preferred_element_type=jnp.float32,
        )
        return (new_max, row_total, weighted)

    start_state = (
        jnp.full((batch_rows, HEADS, local_rows), -1e30, jnp.float32),
        jnp.zeros((batch_rows, HEADS, local_rows), jnp.float32),
        jnp.zeros((batch_rows, local_rows, HEADS, HEAD_DIM), jnp.float32),
    )
    max_score, row_total, weighted = over_blocks(
        forward_block,
        keys_bias(forward_offsets),
        start_state,
        (
            lax.all_gather(keys_local, "ctx", axis=1, tiled=True),
            lax.all_gather(values_local, "ctx", axis=1, tiled=True),
        ),
    )
    log_total = max_score + jnp.log(row_total)
    attn_full = weighted / jnp.transpose(row_total, (0, 2, 1))[..., None]
    attn_low = attn_full.reshape(batch_rows, local_rows, model_width).astype(jnp.bfloat16)
    residual = tokens_f + project(attn_low, full_out)
    ffn_gain = full_gain_ffn.astype(jnp.float32)
    normed_ffn = normalize(residual, ffn_gain).astype(jnp.bfloat16)
    gate_proj = project(normed_ffn, full_gate)
    up_proj = project(normed_ffn, full_up)
    hidden = (gelu_tanh(gate_proj) * up_proj).astype(jnp.bfloat16)
    result = valid_rows[..., None] * (residual + project(hidden, full_ffn_out))
    output = result.astype(jnp.bfloat16)
    back_weights = (
        lax.all_gather(shards[0], "fsdp", axis=0, tiled=True),
        lax.all_gather(shards[1], "fsdp", axis=0, tiled=True),
        lax.all_gather(shards[2], "fsdp", axis=0, tiled=True),
        lax.all_gather(shards[3], "fsdp", axis=0, tiled=True),
        lax.all_gather(shards[4], "fsdp", axis=0, tiled=True),
        lax.all_gather(shards[5], "fsdp", axis=0, tiled=True),
        lax.all_gather(shards[6], "fsdp", axis=0, tiled=True),
        lax.all_gather(shards[7], "fsdp", axis=0, tiled=True),
        lax.all_gather(shards[8], "fsdp", axis=0, tiled=True),
        lax.all_gather(shards[9], "fsdp", axis=0, tiled=True),
    )
    (
        back_gain_attn,
        back_query,
        back_key,
        back_value,
        back_out,
        back_bias,
        back_gain_ffn,
        back_gate,
        back_up,
        back_ffn_out,
    ) = back_weights
    back_offsets = offset_bias_of(back_bias)
    grad_out = cotangent.astype(jnp.float32) * valid_rows[..., None]
    grad_low = grad_out.astype(jnp.bfloat16)
    grad_w_ffn_out = outer_sum(hidden, grad_low)
    grad_hidden = back_project(grad_low, back_ffn_out)

    def gated_product(gate_in, up_in):
        return gelu_tanh(gate_in) * up_in

    gated_value, gated_back = jax.vjp(gated_product, gate_proj, up_proj)
    grad_gate, grad_up = gated_back(grad_hidden)
    grad_gate = grad_gate.astype(jnp.bfloat16)
    grad_up = grad_up.astype(jnp.bfloat16)
    grad_w_gate = outer_sum(normed_ffn, grad_gate)
    grad_w_up = outer_sum(normed_ffn, grad_up)
    grad_normed_ffn = back_project(grad_gate, back_gate) + back_project(grad_up, back_up)
    norm_value, norm_back = jax.vjp(normalize, residual, back_gain_ffn.astype(jnp.float32))
    grad_resid_part, grad_gain_ffn = norm_back(grad_normed_ffn)
    grad_resid = grad_out + grad_resid_part
    grad_branch = grad_resid.astype(jnp.bfloat16)
    grad_w_out = outer_sum(attn_low, grad_branch)
    grad_attn = back_project(grad_branch, back_out).astype(jnp.bfloat16)
    grad_heads = split_heads(grad_attn)
    delta_row = jnp.einsum(
        "mihe,mihe->mhi", grad_heads, attn_full, preferred_element_type=jnp.float32
    )

    def query_grad_block(running, sub_pieces, block_start, member_pick, bias_info):
        grad_query, grad_offsets = running
        pair_bias, table_start = bias_info
        key_part, value_part = sub_pieces
        key_heads = split_heads(key_part)
        key_pos = block_start + jnp.arange(key_part.shape[1], dtype=jnp.int32)
        key_ok = key_pos[None, :] < lengths[:, None]
        scores = block_scores(query_heads, key_heads, pair_bias, key_ok)
        probabilities = jnp.exp(scores - log_total[..., None])
        grad_probs = jnp.einsum(
            "mihe,mjhe->mhij",
            grad_heads,
            split_heads(value_part),
            preferred_element_type=jnp.float32,
        )
        grad_scores = (probabilities * (grad_probs - delta_row[..., None])).astype(jnp.bfloat16)
        grad_query = grad_query + jnp.einsum(
            "mhij,mjhe->mihe", grad_scores, key_heads, preferred_element_type=jnp.float32
        )
        pair_grad = jnp.sum(grad_scores.astype(jnp.float32), axis=0)
        diag = diagonal_sums(pair_grad, pair_grad.shape[1], pair_grad.shape[2])
        current = lax.dynamic_slice_in_dim(grad_offsets, table_start, diag.shape[1], 1)
        grad_offsets = lax.dynamic_update_slice_in_dim(grad_offsets, current + diag, table_start, 1)
        return (grad_query, grad_offsets)

    query_state = (
        jnp.zeros((batch_rows, local_rows, HEADS, HEAD_DIM), jnp.float32),
        jnp.zeros((HEADS, table_len), jnp.float32),
    )
    grad_query, grad_offsets = over_blocks(
        query_grad_block,
        keys_bias(back_offsets),
        query_state,
        (
            lax.all_gather(keys_local, "ctx", axis=1, tiled=True),
            lax.all_gather(values_local, "ctx", axis=1, tiled=True),
        ),
    )
    grad_buckets = jnp.einsum(
        "ht,tb->bh", grad_offsets, bucket_hot.astype(jnp.float32), precision=lax.Precision.HIGHEST
    )
    stats_lse, stats_delta = (
        lax.all_gather(log_total, "ctx", axis=2, tiled=True),
        lax.all_gather(delta_row, "ctx", axis=2, tiled=True),
    )
    key_heads_local = split_heads(keys_local)
    value_heads_local = split_heads(values_local)

    def key_grad_block(running, sub_pieces, block_start, member_pick, bias_info):
        grad_key, grad_value = running
        query_part, grad_part = sub_pieces
        rows_here = query_part.shape[1]
        query_part_heads = split_heads(query_part)
        grad_part_heads = split_heads(grad_part)
        scores = block_scores(query_part_heads, key_heads_local, bias_info[0], valid_mask)
        lse_part = lax.dynamic_slice_in_dim(stats_lse, block_start, rows_here, 2)
        delta_part = lax.dynamic_slice_in_dim(stats_delta, block_start, rows_here, 2)
        probabilities = jnp.exp(scores - lse_part[..., None])
        grad_value = grad_value + jnp.einsum(
            "mhij,mihe->mjhe",
            probabilities.astype(jnp.bfloat16),
            grad_part_heads,
            preferred_element_type=jnp.float32,
        )
        grad_probs = jnp.einsum(
            "mihe,mjhe->mhij",
            grad_part_heads,
            value_heads_local,
            preferred_element_type=jnp.float32,
        )
        grad_scores = (probabilities * (grad_probs - delta_part[..., None])).astype(jnp.bfloat16)
        grad_key = grad_key + jnp.einsum(
            "mhij,mihe->mjhe", grad_scores, query_part_heads, preferred_element_type=jnp.float32
        )
        return (grad_key, grad_value)

    key_state = (
        jnp.zeros((batch_rows, local_rows, HEADS, HEAD_DIM), jnp.float32),
        jnp.zeros((batch_rows, local_rows, HEADS, HEAD_DIM), jnp.float32),
    )
    grad_key, grad_value = over_blocks(
        key_grad_block,
        queries_bias(back_offsets),
        key_state,
        (
            lax.all_gather(queries, "ctx", axis=1, tiled=True),
            lax.all_gather(grad_attn, "ctx", axis=1, tiled=True),
        ),
    )
    grad_q = grad_query.reshape(batch_rows, local_rows, model_width).astype(jnp.bfloat16)
    grad_k = grad_key.reshape(batch_rows, local_rows, model_width).astype(jnp.bfloat16)
    grad_v = grad_value.reshape(batch_rows, local_rows, model_width).astype(jnp.bfloat16)
    grad_w_query = outer_sum(normed, grad_q)
    grad_w_key = outer_sum(normed, grad_k)
    grad_w_value = outer_sum(normed, grad_v)
    grad_normed = (
        back_project(grad_q, back_query)
        + back_project(grad_k, back_key)
        + back_project(grad_v, back_value)
    )
    attn_norm_value, attn_norm_back = jax.vjp(
        normalize, tokens_f, back_gain_attn.astype(jnp.float32)
    )
    grad_tokens_part, grad_gain_attn = attn_norm_back(grad_normed)
    grad_tokens = grad_resid + grad_tokens_part
    grads = (
        grad_gain_attn,
        grad_w_query,
        grad_w_key,
        grad_w_value,
        grad_w_out,
        grad_buckets,
        grad_gain_ffn,
        grad_w_gate,
        grad_w_up,
        grad_w_ffn_out,
    )
    shard_sums = (
        lax.psum_scatter(grads[0], "fsdp", scatter_dimension=0, tiled=True),
        lax.psum_scatter(grads[1], "fsdp", scatter_dimension=0, tiled=True),
        lax.psum_scatter(grads[2], "fsdp", scatter_dimension=0, tiled=True),
        lax.psum_scatter(grads[3], "fsdp", scatter_dimension=0, tiled=True),
        lax.psum_scatter(grads[4], "fsdp", scatter_dimension=0, tiled=True),
        lax.psum_scatter(grads[5], "fsdp", scatter_dimension=0, tiled=True),
        lax.psum_scatter(grads[6], "fsdp", scatter_dimension=0, tiled=True),
        lax.psum_scatter(grads[7], "fsdp", scatter_dimension=0, tiled=True),
        lax.psum_scatter(grads[8], "fsdp", scatter_dimension=0, tiled=True),
        lax.psum_scatter(grads[9], "fsdp", scatter_dimension=0, tiled=True),
    )
    totals = lax.psum(
        (
            shard_sums[0],
            shard_sums[1],
            shard_sums[2],
            shard_sums[3],
            shard_sums[4],
            shard_sums[5],
            shard_sums[6],
            shard_sums[7],
            shard_sums[8],
            shard_sums[9],
        ),
        "ctx",
    )
    return (output, grad_tokens) + tuple(totals)


def solution(mesh):
    placed = (
        P("fsdp", "ctx", None),
        P("fsdp", "ctx", None),
        P("fsdp"),
        P(),
        P("fsdp"),
        P("fsdp", None),
        P("fsdp", None),
        P("fsdp", None),
        P("fsdp", None),
        P("fsdp", None),
        P("fsdp"),
        P("fsdp", None),
        P("fsdp", None),
        P("fsdp", None),
    )
    plane = mesh.shape["ctx"] == 8 and mesh.shape["fsdp"] == 4
    return jax.shard_map(
        per_device_plane if plane else per_device_general,
        mesh=mesh,
        in_specs=placed,
        out_specs=(
            P("fsdp", "ctx", None),
            P("fsdp", "ctx", None),
            P("fsdp"),
            P("fsdp", None),
            P("fsdp", None),
            P("fsdp", None),
            P("fsdp", None),
            P("fsdp", None),
            P("fsdp"),
            P("fsdp", None),
            P("fsdp", None),
            P("fsdp", None),
        ),
        check_vma=False,
    )
```

```python
import math

import jax
import jax.numpy as jnp
from jax import lax
from jax.experimental import pallas as pl
from jax.experimental.pallas import tpu as pltpu
from jax.sharding import PartitionSpec as P

HEADS = 12
HEAD_DIM = 64
BUCKETS = 32
BLOCK = 256
TILE = 256
VMEM_BYTES = 56 * 1024 * 1024
COST = 0.5

norm_eps = 1e-06
F32 = jnp.float32
LOW = jnp.bfloat16
NN = (((1,), (0,)), ((), ()))
NT = (((1,), (1,)), ((), ()))
TN = (((0,), (0,)), ((), ()))
SMEM = pl.BlockSpec(memory_space=pltpu.SMEM)
ANY = pl.BlockSpec(memory_space=pl.ANY)


def dot(left, right, dims=NN):
    return lax.dot_general(left, right, dims, preferred_element_type=F32)


def shape_of(dims, kind):
    return jax.ShapeDtypeStruct(dims, kind)


def params(limit=VMEM_BYTES):
    return pltpu.CompilerParams(vmem_limit_bytes=limit)


def cost(flops, moved, exps=0):
    return pl.CostEstimate(
        flops=int(flops * COST), bytes_accessed=int(moved * COST), transcendentals=int(exps)
    )


def block_rows(index, rows=BLOCK):
    return pl.ds(pl.multiple_of(index * rows, rows), rows)


def rms_rows(rows_f):
    return lax.rsqrt(jnp.mean(rows_f * rows_f, axis=-1, keepdims=True) + norm_eps)


def pack_kernel(
    where_ref, gate_ref, up_ref, down_ref, out_ref, q_ref, k_ref, v_ref, small_ref,
    gate_mine_ref, up_mine_ref, x_ref, y_ref, qkv_ref, early_ref,
):
    chip, core = where_ref[0], where_ref[1]
    x_side, y_side = chip % 2, chip // 2
    wide, depth, model = gate_mine_ref.shape
    planes = gate_ref.shape[1] // model
    part = gate_ref.shape[1] // planes // 2
    slab = depth // 2
    for plane in range(planes):
        columns = pl.ds(pl.multiple_of(plane * 2 * part + core * part, 128), part)
        half, at = divmod(plane * part, model)
        gate_mine_ref[half, :, at : at + part] = gate_ref[:, columns]
        up_mine_ref[half, :, at : at + part] = up_ref[:, columns]
    quarter = part // 4
    x_rows, y_rows = block_rows(x_side, slab), block_rows(y_side, slab)
    for half in range(wide):
        at = slice(half * slab, (half + 1) * slab)
        x_ref[at, :] = gate_mine_ref[half, x_rows, :]
        y_ref[at, :] = up_mine_ref[half, y_rows, :]
    x_down = pl.ds(pl.multiple_of(core * part + x_side * quarter, quarter), quarter)
    y_down = pl.ds(pl.multiple_of(core * part + 2 * quarter + y_side * quarter, quarter), quarter)
    x_ref[wide * slab :, :] = down_ref[x_down, :]
    y_ref[wide * slab :, :] = down_ref[y_down, :]
    early_ref[slab : 2 * slab, :] = out_ref[block_rows(core, slab), :]
    early_ref[2 * slab :, :] = small_ref[...]
    width = model // 4
    for owner in range(4):

        @pl.when(chip == owner)
        def _(owner=owner):
            lanes = slice(owner * width, (owner + 1) * width)
            qkv_ref[:, :width] = q_ref[:, lanes]
            qkv_ref[:, width : 2 * width] = k_ref[:, lanes]
            qkv_ref[:, 2 * width : 3 * width] = v_ref[:, lanes]
            qkv_ref[:, 3 * width :] = jnp.zeros((depth, width), LOW)

    early_ref[:slab, :] = qkv_ref[block_rows(core, slab), :]


def pack_weights(where, gate, up, down, out, query, key, value, small):
    depth, units = gate.shape
    model = query.shape[1]
    planes = model // depth
    wide = units // 2 // model
    part = units // planes // 2
    vmem = pl.BlockSpec(memory_space=pltpu.VMEM)
    return pl.pallas_call(
        pack_kernel,
        in_specs=[SMEM] + [vmem] * 8,
        out_specs=[vmem] * 6,
        out_shape=[
            shape_of((wide, depth, model), LOW),
            shape_of((wide, depth, model), LOW),
            shape_of((wide * depth // 2 + part // 4, model), LOW),
            shape_of((wide * depth // 2 + part // 4, model), LOW),
            shape_of((depth, model), LOW),
            shape_of((depth + small.shape[0], model), LOW),
        ],
        compiler_params=params(),
        cost_estimate=cost(0, 16e6),
        name="pack_weights",
    )(where, gate, up, down, out, query, key, value, small)


def prepare_kernel(lens_ref, tok_ref, send_ref, order_ref, sorted_ref):
    batch = tok_ref.shape[0]
    lens = [lens_ref[i] for i in range(batch)]
    for mine in range(batch):
        rank = 0
        for other in range(batch):
            if other != mine:
                ahead = lens[other] > lens[mine] if other > mine else lens[other] >= lens[mine]
                rank = rank + ahead.astype(jnp.int32)
        slot = jnp.where(rank == 0, 0, jnp.where(rank == batch - 1, 1, rank + 1))
        order_ref[slot] = mine
        sorted_ref[slot] = lens[mine]
    for slot in range(batch):
        rows = tok_ref[order_ref[slot]]
        for chip in range(send_ref.shape[0]):
            send_ref[chip, slot] = rows


def prepare(lengths, tokens, chips):
    batch, rows, model = tokens.shape
    vmem = pl.BlockSpec(memory_space=pltpu.VMEM)
    return pl.pallas_call(
        prepare_kernel,
        in_specs=[SMEM, vmem],
        out_specs=[vmem, SMEM, SMEM],
        out_shape=[
            shape_of((chips, batch, rows, model), LOW),
            shape_of((batch,), jnp.int32),
            shape_of((batch,), jnp.int32),
        ],
        compiler_params=params(),
        cost_estimate=cost(0, 4e6),
        name="prepare",
    )(lengths, tokens)


def sort_rows_kernel(order_ref, lens_ref, start_ref, tok_ref, cot_ref, local_ref, dy_ref):
    slot = pl.program_id(0)
    local_ref[...] = tok_ref[0]
    grads = cot_ref[0].astype(F32)
    place_in = lax.broadcasted_iota(jnp.int32, grads.shape, 0) + start_ref[0]
    dy_ref[...] = jnp.where(place_in < lens_ref[slot], grads, 0.0).astype(LOW)


def sort_rows(order, lens, start, tokens, cotangent):
    batch, rows, model = tokens.shape
    by_order = pl.BlockSpec((1, rows, model), lambda s, order, lens, start: (order[s], 0, 0))
    in_order = pl.BlockSpec((rows, model), lambda s, order, lens, start: (s, 0))
    return pl.pallas_call(
        sort_rows_kernel,
        grid_spec=pltpu.PrefetchScalarGridSpec(
            num_scalar_prefetch=3,
            grid=(batch,),
            in_specs=[by_order, by_order],
            out_specs=[in_order, in_order],
        ),
        out_shape=[
            shape_of((batch * rows, model), LOW),
            shape_of((batch * rows, model), LOW),
        ],
        compiler_params=params(),
        cost_estimate=cost(0, 3e6),
        name="sort_rows",
    )(order, lens, start, tokens, cotangent)


def build_bias(offsets_ref, bias_ref):
    heads, _, width = bias_ref.shape
    span = offsets_ref.shape[1]
    for head in range(heads):
        line = jnp.broadcast_to(offsets_ref[head : head + 1, :], (8, span))
        for group in range(BLOCK // 8):
            turned = pltpu.roll(
                line, (group * 8 - (BLOCK - 1)) % span, 1, stride=1, stride_axis=0
            )
            bias_ref[head, group * 8 : group * 8 + 8, :] = turned[:, :width]


def fold_diagonals(bias_grad_ref, offsets_grad_ref):
    heads, _, width = bias_grad_ref.shape
    span = offsets_grad_ref.shape[1]
    for head in range(heads):
        total = jnp.zeros((8, span), F32)
        for group in range(BLOCK // 8):
            rows = bias_grad_ref[head, group * 8 : group * 8 + 8, :]
            wide = jnp.concatenate([rows, jnp.zeros((8, span - width), F32)], axis=1)
            total = total + pltpu.roll(wide, (BLOCK - 8 - group * 8) % span, 1)
        line = jnp.zeros((1, span), F32)
        for row in range(8):
            line = line + pltpu.roll(total, (7 - row) % span, 1)[row : row + 1, :]
        offsets_grad_ref[head : head + 1, :] = line


def kept_scores(scores, column, length, count):
    wide = count * BLOCK
    tail = jnp.where(column < length - (wide - BLOCK), scores[:, wide - BLOCK :], -1e30)
    if count == 1:
        return tail
    return jnp.concatenate([scores[:, : wide - BLOCK], tail], axis=1)


def token_block(tok_ref, index):
    pieces, _, rows, model = tok_ref.shape
    parts = BLOCK // rows
    return tok_ref[pl.ds(index * parts, parts), 0].reshape(BLOCK, model)


def attn_forward_first_kernel(
    lens_ref, where_ref, tok_ref, gain_ref, w0_ref, w1_ref, w2_ref, w3_ref, v1_ref, v2_ref, v3_ref, off_ref,
    ot_ref, of_ref, q_ref, k_ref, v_ref, w_ref,
    bias_ref, vm_ref,
):
    depth, model = w0_ref.shape
    width = w_ref.shape[2]
    planes, slab = model // depth, depth // 2
    core, plane = where_ref[1], where_ref[2]
    for kind in range(3):
        lanes = slice(kind * width, (kind + 1) * width)
        w_ref[kind, block_rows(plane, depth), :] = w0_ref[:, lanes]
        for back, (piece_ref, other_ref) in enumerate(
            ((w1_ref, v1_ref), (w2_ref, v2_ref), (w3_ref, v3_ref))
        ):
            owner = lax.rem(plane + planes - 1 - back, planes)
            w_ref[kind, block_rows(owner * 2 + core, slab), :] = piece_ref[:slab, lanes]
            w_ref[kind, block_rows(owner * 2 + 1 - core, slab), :] = other_ref[:slab, lanes]
    attend_slot(
        lens_ref[2 * core], tok_ref, gain_ref, w_ref, off_ref,
        ot_ref, of_ref, q_ref, k_ref, v_ref, bias_ref, vm_ref,
    )


def attn_forward_second_kernel(
    lens_ref, where_ref, tok_ref, gain_ref, w_ref, off_ref, of_in, q_in, k_in, v_in,
    ot_ref, of_ref, q_ref, k_ref, v_ref,
    bias_ref, vm_ref,
):
    attend_slot(
        lens_ref[2 * where_ref[1] + 1], tok_ref, gain_ref, w_ref, off_ref,
        ot_ref, of_ref, q_ref, k_ref, v_ref, bias_ref, vm_ref,
    )


def attend_slot(
    length, tok_ref, gain_ref, w_ref, off_ref,
    ot_ref, of_ref, q_ref, k_ref, v_ref, bias_ref, vm_ref,
):
    pieces, _, piece_rows, model = tok_ref.shape
    blocks = pieces * piece_rows // BLOCK
    width = w_ref.shape[2]
    per_chip = width // HEAD_DIM
    used = (length + BLOCK - 1) // BLOCK
    parts = BLOCK // piece_rows
    build_bias(off_ref, bias_ref)
    owner = lax.broadcasted_iota(jnp.int32, (BLOCK, width), 1) // HEAD_DIM
    column = lax.broadcasted_iota(jnp.int32, (BLOCK, BLOCK), 1)
    spare = lax.broadcasted_iota(jnp.int32, (BLOCK, HEAD_DIM), 1)
    nothing = jnp.zeros((BLOCK, width), LOW)

    def project(index, carry):
        rows = block_rows(index)
        rows_f = token_block(tok_ref, index).astype(F32)
        normed = (rows_f * rms_rows(rows_f) * gain_ref[...]).astype(LOW)
        q_ref[0, rows, :] = dot(normed, w_ref[0]).astype(LOW)
        k_ref[0, rows, :] = dot(normed, w_ref[1]).astype(LOW)
        val = dot(normed, w_ref[2]).astype(LOW)
        v_ref[0, rows, :] = val
        for head in range(per_chip):
            vm_ref[head, rows, :] = jnp.where(owner == head, val, nothing)
        return carry

    lax.fori_loop(0, used, project, 0)

    def attend(index, carry):
        rows = block_rows(index)
        query = q_ref[0, rows, :]
        start = pl.multiple_of((blocks - 1 - index) * BLOCK, BLOCK)
        for count in range(1, blocks + 1):

            @pl.when(used == count)
            def _(count=count):
                wide = count * BLOCK
                total = jnp.zeros((BLOCK, width), F32)
                sums = jnp.zeros((BLOCK, HEAD_DIM), F32)
                for head in range(per_chip):
                    mine = jnp.where(owner == head, query, nothing)
                    scores = dot(mine, k_ref[0, :wide, :], NT)
                    scores = scores + bias_ref[head, :, pl.ds(start, wide)]
                    scores = kept_scores(scores, column, length, count)
                    top = jnp.max(scores, axis=-1, keepdims=True)
                    weights = jnp.exp(scores - top)
                    row_total = jnp.sum(weights, axis=-1, keepdims=True)
                    part = dot(weights.astype(LOW), vm_ref[head, :wide, :])
                    total = total + part * (1.0 / row_total)
                    sums = jnp.where(spare == head, top + jnp.log(row_total), sums)
                of_ref[0, rows, :width] = total
                of_ref[0, rows, width:] = sums
                turned = jnp.transpose(total.astype(LOW))
                for piece in range(parts):
                    lanes = slice(piece * piece_rows, (piece + 1) * piece_rows)
                    ot_ref[index * parts + piece, 0] = turned[:, lanes]

        return carry

    lax.fori_loop(0, used, attend, 0)

    def clear(index, carry):
        ot_ref[pl.ds(index * parts, parts), 0] = jnp.zeros((parts, width, piece_rows), LOW)
        return carry

    lax.fori_loop(used, blocks, clear, 0)


def attn_forward(slot, lens, where, tokens, gain, weights, offsets, kept=()):
    pieces, slots, rows, model = tokens.shape
    width = model // 4
    per_chip = width // HEAD_DIM
    seq = pieces * rows
    by_slot = lambda i: (slot, 0, 0)
    whole = lambda array: pl.BlockSpec(array.shape, lambda i: (0,) * array.ndim)
    lane_rows = pl.BlockSpec((1, seq, width), by_slot)
    results = [
        shape_of((slots, seq, width + HEAD_DIM), F32),
        shape_of((slots, seq, width), LOW),
        shape_of((slots, seq, width), LOW),
        shape_of((slots, seq, width), LOW),
    ]
    last = [shape_of((3, model, width), LOW)] if slot == 0 else []
    return pl.pallas_call(
        attn_forward_first_kernel if slot == 0 else attn_forward_second_kernel,
        grid=(1,),
        in_specs=[
            SMEM,
            SMEM,
            pl.BlockSpec((pieces, 1, rows, model), lambda i: (0, slot, 0, 0)),
            whole(gain),
        ]
        + [whole(array) for array in weights]
        + [whole(offsets)]
        + [ANY] * len(kept),
        out_specs=[
            pl.BlockSpec((pieces, 1, width, rows), lambda i: (0, 0, 0, 0)),
            pl.BlockSpec((1, seq, width + HEAD_DIM), by_slot),
            lane_rows,
            lane_rows,
            lane_rows,
        ]
        + [whole(array) for array in last],
        out_shape=[shape_of((pieces, 1, width, rows), LOW)] + results + last,
        scratch_shapes=[
            pltpu.VMEM((per_chip, BLOCK, 2 * seq - BLOCK), F32),
            pltpu.VMEM((per_chip, seq, width), LOW),
        ],
        input_output_aliases={5 + len(weights) + i: 1 + i for i in range(len(kept))},
        compiler_params=params(),
        cost_estimate=cost(
            2 * seq * (model * 3 * width + 2 * seq * 256 * per_chip),
            seq * 2 * (model + 8 * width),
        ),
        name="attn_forward",
    )(lens, where, tokens, gain, *weights, offsets, *kept)


def attn_backward_kernel(
    lens_ref, where_ref, tok_ref, gain_ref, w_ref, off_ref, q_ref, k_ref, v_ref, of_ref, dot_ref,
    dn_ref, dw_keep_ref, dw_send_ref, dgain_ref, doff_ref,
    bias_ref, dbias_ref, km_ref, dq_ref, dkt_ref, dvt_ref, dwt_ref, dw_ref,
):
    slot = pl.program_id(0)
    pieces, _, piece_rows, model = tok_ref.shape
    blocks = pieces * piece_rows // BLOCK
    width = w_ref.shape[2]
    per_chip = width // HEAD_DIM
    core = where_ref[1]
    length = lens_ref[2 * core + slot]
    used = (length + BLOCK - 1) // BLOCK
    parts = BLOCK // piece_rows

    @pl.when(slot == 0)
    def _():
        build_bias(off_ref, bias_ref)
        dbias_ref[...] = jnp.zeros_like(dbias_ref)
        dwt_ref[...] = jnp.zeros_like(dwt_ref)
        dgain_ref[...] = jnp.zeros_like(dgain_ref)

    dkt_ref[...] = jnp.zeros_like(dkt_ref)
    dvt_ref[...] = jnp.zeros_like(dvt_ref)
    owner = lax.broadcasted_iota(jnp.int32, (BLOCK, width), 1) // HEAD_DIM
    column = lax.broadcasted_iota(jnp.int32, (BLOCK, BLOCK), 1)
    nothing = jnp.zeros((BLOCK, width), LOW)

    def split_keys(index, carry):
        rows = block_rows(index)
        key = k_ref[0, rows, :]
        for head in range(per_chip):
            km_ref[head, rows, :] = jnp.where(owner == head, key, nothing)
        return carry

    lax.fori_loop(0, used, split_keys, 0)

    def attend(index, carry):
        rows = block_rows(index)
        query = q_ref[0, rows, :]
        query_t = jnp.transpose(query)
        grad_t = jnp.concatenate(
            [dot_ref[index * parts + piece, 0] for piece in range(parts)], axis=1
        )
        grad = jnp.transpose(grad_t)
        product = grad.astype(F32) * of_ref[0, rows, :width]
        start = pl.multiple_of((blocks - 1 - index) * BLOCK, BLOCK)
        for count in range(1, blocks + 1):

            @pl.when(used == count)
            def _(count=count):
                wide = count * BLOCK
                grad_query = jnp.zeros((BLOCK, width), F32)
                for head in range(per_chip):
                    lanes = slice(head * HEAD_DIM, (head + 1) * HEAD_DIM)
                    mine = jnp.where(owner == head, query, nothing)
                    scores = dot(mine, k_ref[0, :wide, :], NT)
                    scores = scores + bias_ref[head, :, pl.ds(start, wide)]
                    scores = kept_scores(scores, column, length, count)
                    lse = of_ref[0, rows, width + head : width + head + 1]
                    probs = jnp.exp(scores - lse)
                    delta = jnp.sum(
                        jnp.where(owner == head, product, 0.0), axis=-1, keepdims=True
                    )
                    grad_mine = jnp.where(owner == head, grad, nothing)
                    grad_probs = dot(grad_mine, v_ref[0, :wide, :], NT)
                    grad_scores = probs * (grad_probs - delta)
                    dbias_ref[head, :, pl.ds(start, wide)] += grad_scores
                    grad_scores = grad_scores.astype(LOW)
                    grad_query = grad_query + dot(grad_scores, km_ref[head, :wide, :])
                    dkt_ref[lanes, :wide] += dot(query_t[lanes, :], grad_scores)
                    dvt_ref[lanes, :wide] += dot(grad_t[lanes, :], probs.astype(LOW))
                dq_ref[rows, :] = grad_query.astype(LOW)

        return carry

    lax.fori_loop(0, used, attend, 0)

    def finish(index, carry):
        rows = block_rows(index)
        grad_query = dq_ref[rows, :]
        key_t = dkt_ref[:, rows].astype(LOW)
        value_t = dvt_ref[:, rows].astype(LOW)
        rows_f = token_block(tok_ref, index).astype(F32)
        unit = rows_f * rms_rows(rows_f)
        normed = (unit * gain_ref[...]).astype(LOW)
        grad_normed = (
            dot(grad_query, w_ref[0], NT)
            + dot(jnp.transpose(key_t), w_ref[1], NT)
            + dot(jnp.transpose(value_t), w_ref[2], NT)
        )
        dgain_ref[...] += jnp.sum(grad_normed * unit, axis=0, keepdims=True)
        dn_ref[pl.ds(index * parts, parts), 0] = grad_normed.astype(LOW).reshape(
            parts, piece_rows, model
        )
        dwt_ref[0:width, :] += dot(jnp.transpose(grad_query), normed)
        dwt_ref[width : 2 * width, :] += dot(key_t, normed)
        dwt_ref[2 * width :, :] += dot(value_t, normed)
        return carry

    lax.fori_loop(0, used, finish, 0)

    def clear(index, carry):
        dn_ref[pl.ds(index * parts, parts), 0] = jnp.zeros((parts, piece_rows, model), LOW)
        return carry

    lax.fori_loop(used, blocks, clear, 0)

    @pl.when(slot == pl.num_programs(0) - 1)
    def _():
        fold_diagonals(dbias_ref, doff_ref)
        dw_ref[...] = jnp.transpose(dwt_ref[...].astype(LOW))
        planes, slab, _ = dw_keep_ref.shape
        for plane in range(planes):
            lanes = slice(0, 3 * width)
            dw_keep_ref[plane, :, lanes] = dw_ref[block_rows(2 * plane + core, slab), :]
            dw_send_ref[plane, :, lanes] = dw_ref[block_rows(2 * plane + 1 - core, slab), :]
            rest = jnp.zeros((slab, model - 3 * width), LOW)
            dw_keep_ref[plane, :, 3 * width :] = rest
            dw_send_ref[plane, :, 3 * width :] = rest


def attn_backward(
    lens, where, tokens, gain, w_qkv, offsets, query, key, value, attn_full, grad, planes
):
    pieces, slots, rows, model = tokens.shape
    width = w_qkv.shape[2]
    per_chip = width // HEAD_DIM
    seq = pieces * rows
    lane_rows = pl.BlockSpec((1, seq, width), lambda s: (s, 0, 0))
    by_slot = lambda s: (0, s, 0, 0)
    once = lambda s: (0, 0)
    return pl.pallas_call(
        attn_backward_kernel,
        grid=(slots,),
        in_specs=[
            SMEM,
            SMEM,
            pl.BlockSpec((pieces, 1, rows, model), by_slot),
            pl.BlockSpec((1, model), once),
            pl.BlockSpec((3, model, width), lambda s: (0, 0, 0)),
            pl.BlockSpec(offsets.shape, once),
            lane_rows,
            lane_rows,
            lane_rows,
            pl.BlockSpec((1, seq, width + HEAD_DIM), lambda s: (s, 0, 0)),
            pl.BlockSpec((pieces, 1, width, rows), by_slot),
        ],
        out_specs=[
            pl.BlockSpec((pieces, 1, rows, model), by_slot),
            pl.BlockSpec((planes, model // planes // 2, model), lambda s: (0, 0, 0)),
            pl.BlockSpec((planes, model // planes // 2, model), lambda s: (0, 0, 0)),
            pl.BlockSpec((1, model), once),
            pl.BlockSpec((per_chip, 2 * seq), once),
        ],
        out_shape=[
            shape_of((pieces, slots, rows, model), LOW),
            shape_of((planes, model // planes // 2, model), LOW),
            shape_of((planes, model // planes // 2, model), LOW),
            shape_of((1, model), F32),
            shape_of((per_chip, 2 * seq), F32),
        ],
        scratch_shapes=[
            pltpu.VMEM((per_chip, BLOCK, 2 * seq - BLOCK), F32),
            pltpu.VMEM((per_chip, BLOCK, 2 * seq - BLOCK), F32),
            pltpu.VMEM((per_chip, seq, width), LOW),
            pltpu.VMEM((seq, width), LOW),
            pltpu.VMEM((width, seq), F32),
            pltpu.VMEM((width, seq), F32),
            pltpu.VMEM((3 * width, model), F32),
            pltpu.VMEM((model, 3 * width), LOW),
        ],
        compiler_params=params(),
        cost_estimate=cost(
            4 * slots * seq * (model * 6 * width + 5 * seq * 256 * per_chip),
            slots * seq * 2 * (2 * model + 12 * width),
        ),
        name="attn_backward",
    )(lens, where, tokens, gain, w_qkv, offsets, query, key, value, attn_full, grad)


def side_by_side(attn_refs, chip):
    return jnp.concatenate(
        [ref[2 * chip + core, 0] for core in range(2) for ref in attn_refs], axis=1
    )


def out_project_kernel(
    where_ref, tok_ref, attn0_ref, attn1_ref, own_ref, a1_ref, a2_ref, a3_ref, b1_ref, b2_ref, b3_ref, gain_ref,
    res_ref, nf_ref, w_ref,
):
    core, plane = where_ref[1], where_ref[2]
    depth = own_ref.shape[0]
    slab = depth // 2
    planes = w_ref.shape[0] // depth
    w_ref[block_rows(plane, depth), :] = own_ref[...]
    for back, (piece_ref, other_ref) in enumerate(
        ((a1_ref, b1_ref), (a2_ref, b2_ref), (a3_ref, b3_ref))
    ):
        owner = lax.rem(plane + planes - 1 - back, planes)
        w_ref[block_rows(owner * 2 + core, slab), :] = piece_ref[slab : 2 * slab, :]
        w_ref[block_rows(owner * 2 + 1 - core, slab), :] = other_ref[slab : 2 * slab, :]
    chips, width = attn0_ref.shape[0] // 2, attn0_ref.shape[2]
    total = tok_ref[...].astype(F32)
    for chip in range(chips):
        total = total + dot(
            side_by_side((attn0_ref, attn1_ref), chip), w_ref[chip * width : (chip + 1) * width, :], TN
        )
    res_ref[...] = total
    nf_ref[...] = (total * rms_rows(total) * gain_ref[...]).astype(LOW)


def out_project(where, tokens, attn, own, pieces, others, gain):
    rows, model = tokens.shape
    vmem = pl.BlockSpec(memory_space=pltpu.VMEM)
    return pl.pallas_call(
        out_project_kernel,
        in_specs=[SMEM] + [vmem] * 11,
        out_specs=[vmem] * 3,
        out_shape=[
            shape_of((rows, model), F32),
            shape_of((rows, model), LOW),
            shape_of((model, model), LOW),
        ],
        compiler_params=params(),
        cost_estimate=cost(4 * rows * model * model, rows * model * 12),
        name="out_project",
    )(where, tokens, *attn, own, *pieces, *others, gain)


def out_back_kernel(
    where_ref, own_ref, recv_ref, res_ref, dy_ref, gain_ref, w_ref, attn0_ref, attn1_ref,
    dattn_ref, dres_ref, dgain_ref, keep_ref, send_ref,
    gout_ref,
):
    chips, width, rows = dattn_ref.shape[0] // 2, dattn_ref.shape[2], dattn_ref.shape[3]
    grad = own_ref[...] + recv_ref[...].astype(F32)
    residual = res_ref[...]
    scale = rms_rows(residual)
    unit = residual * scale
    dgain_ref[...] = jnp.sum(grad * unit, axis=0, keepdims=True)
    inner = grad * gain_ref[...]
    dres = dy_ref[...].astype(F32) + scale * (
        inner - unit * jnp.mean(inner * unit, axis=-1, keepdims=True)
    )
    dres_ref[...] = dres
    branch = dres.astype(LOW)
    for chip in range(chips):
        heads = slice(chip * width, (chip + 1) * width)
        part = dot(w_ref[heads, :], branch, NT).astype(LOW)
        for slot in range(4):
            dattn_ref[2 * chip + slot // 2, slot % 2] = part[:, slot * rows : (slot + 1) * rows]
        gout_ref[heads, :] = dot(side_by_side((attn0_ref, attn1_ref), chip), branch).astype(LOW)
    core = where_ref[1]
    planes, slab, _ = keep_ref.shape
    for plane in range(planes):
        keep_ref[plane] = gout_ref[block_rows(2 * plane + core, slab), :]
        send_ref[plane] = gout_ref[block_rows(2 * plane + 1 - core, slab), :]


def out_back(where, own, recv, residual, dy, gain, w_out, attn, planes):
    rows, model = own.shape
    vmem = pl.BlockSpec(memory_space=pltpu.VMEM)
    half = shape_of((planes, model // planes // 2, model), LOW)
    return pl.pallas_call(
        out_back_kernel,
        in_specs=[SMEM] + [vmem] * 8,
        out_specs=[vmem] * 5,
        out_shape=[
            shape_of((attn[0].shape[0], 2, *attn[0].shape[2:]), LOW),
            shape_of((rows, model), F32),
            shape_of((1, model), F32),
            half,
            half,
        ],
        scratch_shapes=[pltpu.VMEM((model, model), LOW)],
        compiler_params=params(),
        cost_estimate=cost(8 * rows * model * model, rows * model * 20),
        name="out_back",
    )(where, own, recv, residual, dy, gain, w_out, *attn)


def gate_and_slope(gate):
    square = gate * gate
    half = 0.5 + 0.5 * jnp.tanh(gate * (0.7978845608028654 + 0.035677408136300125 * square))
    turn = gate * (1.5957691216057308 + 0.21406444881780075 * square)
    return gate * half, half * (1.0 + (1.0 - half) * turn)


def ffn_first_kernel(
    where_ref, nf_own_ref, nf_other_ref, dy_own_ref, dy_other_ref,
    gate_own, up_own, down_own, x1, x2, x3, y1, y2, y3, sx1, sx2, sx3, sy1, sy2, sy3,
    hidden_ref, dup_ref, own_ref, other_ref, down_ref, g0_ref, g1_ref, g2_ref, g3_ref,
    gate_ref, up_ref, nf_ref, nft_ref, dy_ref, total_ref, dgate_ref, grad_ref, sems,
):
    step = pl.program_id(0)
    half = nf_own_ref.shape[0]
    chip, core, plane = where_ref[0], where_ref[1], where_ref[2]
    wide, model, _ = gate_ref.shape
    units = down_ref.shape[0]
    tile = hidden_ref.shape[1]
    depth = gate_own.shape[1]
    planes = model // depth
    slab = depth // 2
    part = units // planes
    quarter = part // 4

    def all_copies():
        copies = []

        def copy(source, target, late=False):
            copies.append(((source, target, sems.at[len(copies)]), late))

        own_rows = pl.ds(pl.multiple_of(plane * depth, depth), depth)
        for index in range(wide):
            copy(gate_own.at[index], gate_ref.at[index, own_rows, :], index > 0)
            copy(up_own.at[index], up_ref.at[index, own_rows, :], index > 0)
        copy(
            down_own.at[pl.ds(pl.multiple_of(core * part, part), part), :],
            down_ref.at[pl.ds(pl.multiple_of(plane * part, part), part), :],
        )
        for back in range(planes - 1):
            owner = lax.rem(plane + planes - 1 - back, planes)
            for along, straight, swapped, weight_ref, side in (
                (0, (x1, x2, x3)[back], (sx1, sx2, sx3)[back], gate_ref, lax.rem(chip, 2)),
                (1, (y1, y2, y3)[back], (sy1, sy2, sy3)[back], up_ref, chip // 2),
            ):
                for piece, here in ((straight, side), (swapped, 1 - side)):
                    at = pl.ds(pl.multiple_of(owner * depth + here * slab, slab), slab)
                    for index in range(wide):
                        copy(
                            piece.at[pl.ds(index * slab, slab), :],
                            weight_ref.at[index, at, :],
                            index > 0,
                        )
                    copy(
                        piece.at[pl.ds(wide * slab, quarter), :],
                        down_ref.at[
                            pl.ds(
                                pl.multiple_of(
                                    owner * part + (2 * along + here) * quarter, quarter
                                ),
                                quarter,
                            ),
                            :,
                        ],
                    )
        return copies

    @pl.when(step == 0)
    def _():
        copies = all_copies()
        for late_turn in (False, True):
            for copied, late in copies:
                if late == late_turn:
                    pltpu.make_async_copy(*copied).start()
        nf_ref[:half, :] = nf_own_ref[...]
        nf_ref[half:, :] = nf_other_ref[...]
        nft_ref[:, :half] = jnp.transpose(nf_own_ref[...])
        nft_ref[:, half:] = jnp.transpose(nf_other_ref[...])
        dy_ref[:half, :] = dy_own_ref[...]
        dy_ref[half:, :] = dy_other_ref[...]
        total_ref[...] = jnp.zeros_like(total_ref)
        for copied, late in copies:
            if not late:
                pltpu.make_async_copy(*copied).wait()

    per = model // tile

    @pl.when(step == per)
    def _():
        for copied, late in all_copies():
            if late:
                pltpu.make_async_copy(*copied).wait()

    index = step // per
    lanes = pl.ds(pl.multiple_of(lax.rem(step, per) * tile, tile), tile)
    gate_w = gate_ref[index, :, lanes]
    up_w = up_ref[index, :, lanes]
    down_w = down_ref[block_rows(step, tile), :]
    count = 4
    size = 2 * half // count

    def products(part):
        rows = slice(part * size, (part + 1) * size)
        nf = nf_ref[rows, :]
        return dot(nf, gate_w), dot(nf, up_w), dot(dy_ref[rows, :], down_w, NT)

    ahead = products(0)
    for part in range(count):
        rows = slice(part * size, (part + 1) * size)
        gate, up, dhidden = ahead
        if part + 1 < count:
            ahead = products(part + 1)
        bent, slope = gate_and_slope(gate)
        hidden_ref[rows, :] = (bent * up).astype(LOW)
        dgate = (dhidden * up * slope).astype(LOW)
        dup = (dhidden * bent).astype(LOW)
        dgate_ref[rows, :] = dgate
        dup_ref[rows, :] = dup
        total_ref[rows, :] += dot(dgate, gate_w, NT) + dot(dup, up_w, NT)

    grad_ref[...] = dot(nft_ref[...], dgate_ref[...]).astype(LOW)
    for away, out_ref in enumerate((g0_ref, g1_ref, g2_ref, g3_ref)):
        out_ref[0] = grad_ref[block_rows(lax.rem(plane + away, planes), depth), :]

    @pl.when(step == pl.num_programs(0) - 1)
    def _():
        own_ref[...] = total_ref[:half, :]
        other_ref[...] = total_ref[half:, :].astype(LOW)


def ffn_first(where, nf_own, nf_other, dy_own, dy_other, own_weights, pieces, tile=TILE):
    half, model = nf_own.shape
    wide, depth, _ = own_weights[0].shape
    units = wide * model
    per = model // tile
    whole = pl.BlockSpec((half, model), lambda t: (0, 0))
    lane_tile = pl.BlockSpec((2 * half, tile), lambda t: (0, t))
    grad_tile = pl.BlockSpec((1, depth, tile), lambda t: (t // per, 0, t % per))
    copies = 2 * wide + 1 + 3 * 4 * (wide + 1)
    return pl.pallas_call(
        ffn_first_kernel,
        grid=(units // tile,),
        in_specs=[SMEM, whole, whole, whole, whole] + [ANY] * 15,
        out_specs=[
            lane_tile, lane_tile, whole, whole,
            pl.BlockSpec((units, model), lambda t: (0, 0)),
        ]
        + [grad_tile] * 4,
        out_shape=[
            shape_of((2 * half, units), LOW),
            shape_of((2 * half, units), LOW),
            shape_of((half, model), F32),
            shape_of((half, model), LOW),
            shape_of((units, model), LOW),
        ]
        + [shape_of((wide, depth, model), LOW)] * 4,
        scratch_shapes=[
            pltpu.VMEM((wide, model, model), LOW),
            pltpu.VMEM((wide, model, model), LOW),
            pltpu.VMEM((2 * half, model), LOW),
            pltpu.VMEM((model, 2 * half), LOW),
            pltpu.VMEM((2 * half, model), LOW),
            pltpu.VMEM((2 * half, model), F32),
            pltpu.VMEM((2 * half, tile), LOW),
            pltpu.VMEM((model, tile), LOW),
            pltpu.SemaphoreType.DMA((copies,)),
        ],
        compiler_params=params(),
        cost_estimate=cost(
            2 * 2 * 6 * 2 * half * model * units,
            6 * model * units + 12 * half * units + 20 * half * model,
        ),
        name="ffn_first",
    )(where, nf_own, nf_other, dy_own, dy_other, *own_weights, *pieces)


def ffn_second_kernel(
    where_ref, nf_own_ref, nf_other_ref, dy_own_ref, dy_other_ref, hidden_ref, dup_ref, down_ref,
    own_ref, other_ref, u_keep_ref, u_send_ref, f_keep_ref, f_send_ref,
    nft_ref, dy_ref, total_ref, grad_ref, gdown_ref,
):
    step = pl.program_id(0)
    half = nf_own_ref.shape[0]
    chip = where_ref[0]
    x_side, y_side = lax.rem(chip, 2), chip // 2
    planes, _, slab, tile = u_keep_ref.shape

    @pl.when(step == 0)
    def _():
        nft_ref[:, :half] = jnp.transpose(nf_own_ref[...])
        nft_ref[:, half:] = jnp.transpose(nf_other_ref[...])
        dy_ref[:half, :] = dy_own_ref[...]
        dy_ref[half:, :] = dy_other_ref[...]
        total_ref[...] = jnp.zeros_like(total_ref)

    hidden = hidden_ref[...]
    grad_ref[...] = dot(nft_ref[...], dup_ref[...]).astype(LOW)
    for plane in range(planes):
        u_keep_ref[plane, 0] = grad_ref[block_rows(2 * plane + x_side, slab), :]
        u_send_ref[plane, 0] = grad_ref[block_rows(2 * plane + 1 - x_side, slab), :]
    gdown_ref[block_rows(step, tile), :] = dot(jnp.transpose(hidden), dy_ref[...]).astype(LOW)
    total_ref[...] += dot(hidden, down_ref[...])

    @pl.when(step == pl.num_programs(0) - 1)
    def _():
        own_ref[...] = total_ref[:half, :]
        other_ref[...] = total_ref[half:, :].astype(LOW)
        rows = f_keep_ref.shape[1]
        for plane in range(planes):
            f_keep_ref[plane] = gdown_ref[block_rows(2 * plane + y_side, rows), :]
            f_send_ref[plane] = gdown_ref[block_rows(2 * plane + 1 - y_side, rows), :]


def ffn_second(
    where, nf_own, nf_other, dy_own, dy_other, hidden, dup, w_down, planes, tile=TILE
):
    half, model = nf_own.shape
    units = hidden.shape[1]
    wide, slab, rows = units // model, model // planes // 2, units // planes // 2
    per = model // tile
    whole = pl.BlockSpec((half, model), lambda t: (0, 0))
    lane_tile = pl.BlockSpec((2 * half, tile), lambda t: (0, t))
    row_tile = pl.BlockSpec((tile, model), lambda t: (t, 0))
    up_tile = pl.BlockSpec((planes, 1, slab, tile), lambda t: (0, t // per, 0, t % per))
    down_whole = pl.BlockSpec((planes, rows, model), lambda t: (0, 0, 0))
    return pl.pallas_call(
        ffn_second_kernel,
        grid=(units // tile,),
        in_specs=[SMEM, whole, whole, whole, whole, lane_tile, lane_tile, row_tile],
        out_specs=[whole, whole, up_tile, up_tile, down_whole, down_whole],
        out_shape=[
            shape_of((half, model), F32),
            shape_of((half, model), LOW),
            shape_of((planes, wide, slab, model), LOW),
            shape_of((planes, wide, slab, model), LOW),
            shape_of((planes, rows, model), LOW),
            shape_of((planes, rows, model), LOW),
        ],
        scratch_shapes=[
            pltpu.VMEM((model, 2 * half), LOW),
            pltpu.VMEM((2 * half, model), LOW),
            pltpu.VMEM((2 * half, model), F32),
            pltpu.VMEM((model, tile), LOW),
            pltpu.VMEM((units, model), LOW),
        ],
        compiler_params=params(),
        cost_estimate=cost(
            2 * 2 * 3 * 2 * half * model * units,
            8 * model * units + 12 * half * units + 20 * half * model,
        ),
        name="ffn_second",
    )(where, nf_own, nf_other, dy_own, dy_other, hidden, dup, w_down)


def second_halves_kernel(
    where_ref, u_keep_ref, u_came_ref, f_keep_ref, f_came_ref,
    u_mine_ref, u_send_ref, f_mine_ref, f_send_ref,
):
    chip = where_ref[0]
    x_side, y_side = lax.rem(chip, 2), chip // 2
    for wanted, u_ref, f_ref in ((0, u_mine_ref, f_mine_ref), (1, u_send_ref, f_send_ref)):
        u_side = jnp.bitwise_xor(y_side, wanted)
        rows = block_rows(u_side, u_ref.shape[2])
        u_ref[...] = (
            u_keep_ref[:, :, rows, :].astype(F32) + u_came_ref[:, :, rows, :].astype(F32)
        ).astype(LOW)
        f_side = jnp.bitwise_xor(x_side, wanted)
        rows = block_rows(f_side, f_ref.shape[1])
        f_ref[...] = (
            f_keep_ref[:, rows, :].astype(F32) + f_came_ref[:, rows, :].astype(F32)
        ).astype(LOW)


def second_halves(where, u_keep, u_came, f_keep, f_came):
    planes, wide, slab, model = u_keep.shape
    rows = f_keep.shape[1]
    vmem = pl.BlockSpec(memory_space=pltpu.VMEM)
    return pl.pallas_call(
        second_halves_kernel,
        in_specs=[SMEM] + [vmem] * 4,
        out_specs=[vmem] * 4,
        out_shape=[
            shape_of((planes, wide, slab // 2, model), LOW),
            shape_of((planes, wide, slab // 2, model), LOW),
            shape_of((planes, rows // 2, model), LOW),
            shape_of((planes, rows // 2, model), LOW),
        ],
        compiler_params=params(),
        cost_estimate=cost(0, 7e6),
        name="second_halves",
    )(where, u_keep, u_came, f_keep, f_came)


def by_chip_kernel(where_ref, *refs):
    gate_refs, keep_ref, came_ref, out_refs = refs[:4], refs[4], refs[5], refs[6:]
    chip = where_ref[0]
    wide, depth, model = gate_refs[0].shape
    planes, slab, _ = keep_ref.shape
    rows, half, lanes = depth // 4, slab // 2, model // 2
    for away, out_ref in enumerate(out_refs):
        to_chip = jnp.bitwise_xor(chip, away)
        to_x, to_y = lax.rem(to_chip, 2), to_chip // 2
        at = block_rows(to_x * 2 + to_y, rows)
        for index in range(wide):
            total = gate_refs[0][index, at, :].astype(F32)
            for gate_ref in gate_refs[1:]:
                total = total + gate_ref[index, at, :].astype(F32)
            out_ref[index * rows : (index + 1) * rows, :] = total.astype(LOW)
        columns = block_rows(to_y, lanes)
        for plane in range(planes):
            low = wide * rows + (plane // 2) * half
            left = (plane % 2) * lanes
            out_ref[low : low + half, left : left + lanes] = (
                keep_ref[plane, block_rows(to_x, half), columns].astype(F32)
                + came_ref[plane, block_rows(to_x, half), columns].astype(F32)
            ).astype(LOW)


def by_chip(where, gates, keep, came):
    wide, depth, model = gates[0].shape
    planes, slab, _ = keep.shape
    vmem = pl.BlockSpec(memory_space=pltpu.VMEM)
    return pl.pallas_call(
        by_chip_kernel,
        in_specs=[SMEM] + [vmem] * 6,
        out_specs=[vmem] * 4,
        out_shape=[shape_of((wide * depth // 4 + planes * slab // 4, model), LOW)] * 4,
        compiler_params=params(),
        cost_estimate=cost(0, 3e6),
        name="by_chip",
    )(where, *gates, keep, came)


def by_plane_kernel(where_ref, *refs):
    u_ref, u_came_ref, f_ref, f_came_ref, w_ref, w_came_ref, line_ref, line_came_ref = refs[:8]
    part_refs, out_refs, gate_ref = refs[8:12], refs[12:16], refs[16]
    plane = where_ref[2]
    planes, wide, rows, model = u_ref.shape
    slab = w_ref.shape[1]
    half, lanes = slab // 2, model // 2

    def four(at, columns):
        total = part_refs[0][at, columns].astype(F32)
        for part_ref in part_refs[1:]:
            total = total + part_ref[at, columns].astype(F32)
        return total.astype(LOW)

    gate_ref[...] = four(slice(0, wide * rows), slice(0, model))
    for away, out_ref in enumerate(out_refs):
        at = lax.rem(plane + away, planes)

        def both(ref, came_ref):
            return (ref[at].astype(F32) + came_ref[at].astype(F32)).astype(LOW)

        for index in range(wide):
            out_ref[index * rows : (index + 1) * rows, :] = (
                u_ref[at, index].astype(F32) + u_came_ref[at, index].astype(F32)
            ).astype(LOW)
        low = wide * rows
        out_ref[low : low + f_ref.shape[1], :] = both(f_ref, f_came_ref)
        low = low + f_ref.shape[1]
        used = 3 * model // 4
        out_ref[low : low + slab, :used] = both(w_ref, w_came_ref)[:, :used]
        out_part = four(
            pl.ds(pl.multiple_of(wide * rows + at // 2 * half, half), half),
            pl.ds(pl.multiple_of(lax.rem(at, 2) * lanes, lanes), lanes),
        )
        out_ref[low : low + half, used:] = out_part[:, : model - used]
        out_ref[low + half : low + slab, used:] = out_part[:, model - used :]
        out_ref[low + slab :, :] = both(line_ref, line_came_ref)


def by_plane(where, u_mine, u_came, f_mine, f_came, w_keep, w_came, line_keep, line_came, parts):
    planes, wide, slab, model = u_mine.shape
    rows = wide * slab + f_mine.shape[1] + w_keep.shape[1] + line_keep.shape[1]
    vmem = pl.BlockSpec(memory_space=pltpu.VMEM)
    return pl.pallas_call(
        by_plane_kernel,
        in_specs=[SMEM] + [vmem] * 12,
        out_specs=[vmem] * (planes + 1),
        out_shape=[shape_of((rows, model), LOW)] * planes + [shape_of((wide * slab, model), LOW)],
        compiler_params=params(),
        cost_estimate=cost(0, 6e6),
        name="by_plane",
    )(
        where, u_mine, u_came, f_mine, f_came, w_keep, w_came, line_keep, line_came, *parts
    )


def unpack_kernel(where_ref, *refs):
    piece_refs = refs[:8]
    gate_ref, up_ref, down_ref, q_ref, k_ref, v_ref, out_ref, small_ref = refs[8:]
    chip, core = where_ref[0], where_ref[1]
    depth, units = gate_ref.shape
    model = down_ref.shape[1]
    part = down_ref.shape[0] // 2
    quarter, slab = depth // 4, depth // 2
    wide = units // 2 // model
    planes = units // 2 // part
    width, lanes, half = model // 4, model // 2, slab // 2
    small = jnp.zeros(small_ref.shape, F32)
    for far in range(8):
        away, other = far % 4, far // 4
        from_core = core if other == 0 else 1 - core
        from_chip = jnp.bitwise_xor(chip, away)
        from_x, from_y = lax.rem(from_chip, 2), from_chip // 2
        piece_ref = piece_refs[far]
        gate_rows = block_rows(from_x * 2 + from_y, quarter)
        for plane in range(planes):
            index, at = divmod(plane * part, model)
            columns = pl.ds(pl.multiple_of(plane * 2 * part + from_core * part, 128), part)
            rows = slice(index * quarter, (index + 1) * quarter)
            gate_ref[gate_rows, columns] = piece_ref[rows, at : at + part].astype(F32)
            rows = slice((wide + index) * quarter, (wide + index + 1) * quarter)
            up_ref[gate_rows, columns] = piece_ref[rows, at : at + part].astype(F32)
        low = 2 * wide * quarter
        rows = part // 4
        down_ref[block_rows(from_core * 4 + from_y * 2 + from_x, rows), :] = piece_ref[
            low : low + rows, :
        ].astype(F32)
        low = low + rows
        used = 3 * width
        out_ref[block_rows(from_core * 2 + from_x, half), block_rows(from_y, lanes)] = (
            jnp.concatenate(
                [piece_ref[low : low + half, used:], piece_ref[low + half : low + slab, used:]],
                axis=1,
            ).astype(F32)
        )
        for home in range(4):

            @pl.when(from_chip == home)
            def _(home=home, piece_ref=piece_ref, from_core=from_core, low=low):
                to_lanes = slice(home * width, (home + 1) * width)
                for kind, target_ref in enumerate((q_ref, k_ref, v_ref)):
                    target_ref[block_rows(from_core, slab), to_lanes] = piece_ref[
                        low : low + slab, kind * width : (kind + 1) * width
                    ].astype(F32)

        small = small + piece_ref[low + slab :, :].astype(F32)
    small_ref[...] = small


def unpack(where, pieces, depth, units):
    rows, model = pieces[0].shape
    planes = model // depth
    part = units // planes
    taken = units // 2 // model * depth // 2 + part // 8 + depth // 2
    vmem = pl.BlockSpec(memory_space=pltpu.VMEM)
    return pl.pallas_call(
        unpack_kernel,
        in_specs=[SMEM] + [vmem] * 8,
        out_specs=[vmem] * 8,
        out_shape=[
            shape_of((depth, units), F32),
            shape_of((depth, units), F32),
            shape_of((part, model), F32),
            shape_of((depth, model), F32),
            shape_of((depth, model), F32),
            shape_of((depth, model), F32),
            shape_of((depth, model), F32),
            shape_of((rows - taken, model), F32),
        ],
        compiler_params=params(),
        cost_estimate=cost(0, 24e6),
        name="unpack",
    )(where, *pieces)


def finish_out_kernel(order_ref, lens_ref, start_ref, res_ref, own_ref, recv_ref, out_ref):
    slot = pl.program_id(0)
    total = res_ref[...] + own_ref[...] + recv_ref[...].astype(F32)
    place_in = lax.broadcasted_iota(jnp.int32, total.shape, 0) + start_ref[0]
    out_ref[0] = jnp.where(place_in < lens_ref[slot], total, 0.0).astype(LOW)


def finish_out(order, lens, start, residual, own, recv, batch):
    rows, model = residual.shape[0] // batch, residual.shape[1]
    in_order = pl.BlockSpec((rows, model), lambda s, order, lens, start: (s, 0))
    return pl.pallas_call(
        finish_out_kernel,
        grid_spec=pltpu.PrefetchScalarGridSpec(
            num_scalar_prefetch=3,
            grid=(batch,),
            in_specs=[in_order, in_order, in_order],
            out_specs=pl.BlockSpec((1, rows, model), lambda s, order, lens, start: (order[s], 0, 0)),
        ),
        out_shape=shape_of((batch, rows, model), LOW),
        compiler_params=params(),
        cost_estimate=cost(0, 6e6),
        name="finish_out",
    )(order, lens, start, residual, own, recv)


def finish_tokens_kernel(order_ref, dn_ref, tok_ref, dres_ref, gain_ref, out_ref):
    grad = dn_ref[0, 0].astype(F32)
    for chip in range(1, dn_ref.shape[0]):
        grad = grad + dn_ref[chip, 0].astype(F32)
    rows_f = tok_ref[...].astype(F32)
    scale = rms_rows(rows_f)
    unit = rows_f * scale
    inner = grad * gain_ref[...]
    out_ref[0] = dres_ref[...] + scale * (
        inner - unit * jnp.mean(inner * unit, axis=-1, keepdims=True)
    )


def finish_tokens(order, dn, tokens, dres, gain):
    chips, batch, rows, model = dn.shape
    in_order = pl.BlockSpec((rows, model), lambda s, order: (s, 0))
    return pl.pallas_call(
        finish_tokens_kernel,
        grid_spec=pltpu.PrefetchScalarGridSpec(
            num_scalar_prefetch=1,
            grid=(batch,),
            in_specs=[
                pl.BlockSpec((chips, 1, rows, model), lambda s, order: (0, s, 0, 0)),
                in_order,
                in_order,
                pl.BlockSpec((1, model), lambda s, order: (0, 0)),
            ],
            out_specs=pl.BlockSpec((1, rows, model), lambda s, order: (order[s], 0, 0)),
        ),
        out_shape=shape_of((batch, rows, model), F32),
        compiler_params=params(),
        cost_estimate=cost(0, 10e6),
        name="finish_tokens",
    )(order, dn, tokens, dres, gain)


CORE, X, Y, XY = 1, 2, 4, 6


def swap(values, bits):
    count = lax.axis_size("ctx")
    return lax.ppermute(values, "ctx", [(i, i ^ bits) for i in range(count)])


def shift(values, places):
    count = lax.axis_size("fsdp")
    return lax.ppermute(values, "fsdp", [(i, (i + places) % count) for i in range(count)])


def column_ends(piece):
    return shift(piece, 1), shift(piece, 3)


def after(values, *others):
    return lax.optimization_barrier((values, *others))[0]


def pick(values, index, axis):
    return lax.dynamic_index_in_dim(values, index, axis, keepdims=False)


def add(*parts):
    total = parts[0].astype(F32)
    for part in parts[1:]:
        total = total + part.astype(F32)
    return total.astype(LOW)


def column_sum(picks):
    return [picks[0]] + [shift(picks[away], away) for away in range(1, len(picks))]


def plane_swaps(parts):
    return [parts[0], swap(parts[1], X), swap(parts[2], Y), swap(parts[3], XY)]


def per_device_plane(
    tokens, cotangent, lengths, bucket_table, gain_attn, w_query, w_key, w_value, w_out,
    bias_table, gain_ffn, w_gate, w_up, w_ffn_out,
):
    batch, rows, model = tokens.shape
    planes = lax.axis_size("fsdp")
    chips = lax.axis_size("ctx") // 2
    me = lax.axis_index("ctx")
    plane = lax.axis_index("fsdp")
    core, chip = me % 2, me // 2
    depth, units = w_gate.shape
    chip_heads = HEADS // chips
    width = chip_heads * HEAD_DIM
    where = jnp.stack([chip, core, plane]).astype(jnp.int32)
    start = (me * rows)[None].astype(jnp.int32)

    small = jnp.concatenate([gain_attn, gain_ffn, bias_table.reshape(-1)])
    small = jnp.pad(small[None], ((0, 15), (0, model - small.shape[0])))
    gate_mine, up_mine, x_piece, y_piece, qkv_mine, early_piece = pack_weights(
        where, w_gate, w_up, w_ffn_out, w_out, w_query, w_key, w_value, small
    )
    send, order, lens = prepare(lengths, after(tokens, early_piece), chips)
    gathered = lax.all_to_all(send.reshape(2 * chips, 2, rows, model), "ctx", 0, 0)

    near, far = column_ends(early_piece)
    early = [near, shift(near, 1), far]
    early_others = [swap(piece, CORE) for piece in early]
    x_near, x_far = column_ends(after(x_piece, near, far))
    y_near, y_far = column_ends(after(y_piece, *early))

    by_distance = jnp.stack([piece[depth] for piece in [early_piece] + early])
    all_small = jnp.stack([pick(by_distance, (plane + planes - i) % planes, 0) for i in range(planes)])
    full_gain_attn = all_small[:, :depth].reshape(1, model).astype(F32)
    full_gain_ffn = all_small[:, depth : 2 * depth].reshape(1, model).astype(F32)
    small_end = 2 * depth + bias_table.size
    full_table = all_small[:, 2 * depth : small_end].reshape(BUCKETS, HEADS)

    hot = bucket_table[:, None] == jnp.arange(BUCKETS, dtype=jnp.int32)[None, :]
    hot = jnp.concatenate([hot, jnp.zeros((1, BUCKETS), bool)])
    my_table = lax.dynamic_slice_in_dim(full_table, chip * chip_heads, chip_heads, 1)
    offsets = jnp.einsum("tb,bh->ht", hot.astype(LOW), my_table, preferred_element_type=F32)

    first_out, *kept, w_qkv = attn_forward(
        0, lens, where, gathered, full_gain_attn, [qkv_mine, *early, *early_others], offsets
    )
    x_near, y_near, first_out = lax.optimization_barrier((x_near, y_near, first_out))
    x_found = [x_near, shift(x_near, 1), x_far]
    y_found = [y_near, shift(y_near, 1), y_far]
    second_out, *kept = attn_forward(
        1, lens, where, gathered, full_gain_attn, [w_qkv], offsets, kept
    )
    attn_first = lax.all_to_all(first_out, "ctx", 0, 0)
    second_out, attn_first, x_found[2], y_found[2], *_ = lax.optimization_barrier(
        (second_out, attn_first, x_found[2], y_found[2], x_near, y_near)
    )
    attn = [attn_first, lax.all_to_all(second_out, "ctx", 0, 0)]
    x_swapped, y_swapped = [swap(t, X) for t in x_found], [swap(t, Y) for t in y_found]
    attn[1] = after(attn[1], *x_swapped, *y_swapped)
    attn_full, query, key, value = kept
    flat, dy = sort_rows(order, lens, start, tokens, cotangent)
    residual, nf_own, full_out = out_project(
        where, flat, attn, w_out, early, early_others, full_gain_ffn
    )
    dy_other = swap(after(dy, nf_own), CORE)
    nf_other = swap(nf_own, CORE)
    hidden, dup, dnf_own, dnf_send, full_down, *g_picks = ffn_first(
        where, nf_own, nf_other, dy, dy_other, (gate_mine, up_mine, w_ffn_out),
        x_found + y_found + x_swapped + y_swapped,
    )

    g_parts = column_sum(g_picks)
    dattn, dres, dgain_ffn, o_keep, o_send = out_back(
        where, dnf_own, swap(dnf_send, CORE), residual, dy, full_gain_ffn, full_out, attn, planes
    )
    dattn_all = lax.all_to_all(dattn, "ctx", 0, 0)
    o_came = swap(o_send, CORE)
    out_own, out_send, u_keep, u_send, f_keep, f_send = ffn_second(
        where, nf_own, nf_other, dy, dy_other, hidden, dup, full_down, planes
    )
    g_parts[1], g_parts[3], u_send, f_send, dattn_all = lax.optimization_barrier(
        (g_parts[1], g_parts[3], u_send, f_send, dattn_all)
    )
    u_came, f_came = swap(u_send, X), swap(f_send, Y)
    out_came = swap(out_send, CORE)
    dn, dw_keep, dw_send, dgain_attn, doffsets = attn_backward(
        lens, where, gathered, full_gain_attn, w_qkv, offsets,
        query, key, value, attn_full, dattn_all, planes,
    )

    u_came, f_came, dn, dw_send, dgain_attn, *g_parts = lax.optimization_barrier(
        (u_came, f_came, dn, dw_send, dgain_attn, *g_parts)
    )
    u_mine, u_send, f_mine, f_send = second_halves(where, u_keep, u_came, f_keep, f_came)
    u_came, f_came = swap(u_send, Y), swap(f_send, X)
    w_came = swap(dw_send, CORE)
    chip_parts = plane_swaps(by_chip(where, g_parts, o_keep, o_came))

    out_rows = finish_out(order, lens, start, residual, out_own, out_came, batch)
    mine_buckets = jnp.einsum(
        "ht,tb->bh", doffsets, hot.astype(F32), precision=lax.Precision.HIGHEST
    )
    buckets = lax.dynamic_update_slice_in_dim(
        jnp.zeros((BUCKETS, HEADS), F32), mine_buckets, chip * chip_heads, 1
    )
    line = jnp.concatenate(
        [
            dgain_attn.reshape(planes, depth),
            dgain_ffn.reshape(planes, depth),
            buckets.reshape(planes, -1),
        ],
        axis=1,
    ).astype(LOW)
    line = jnp.pad(line[:, None, :], ((0, 0), (0, 15), (0, model - line.shape[1])))
    nothing = jnp.zeros_like(line)
    line_came = swap(jnp.where(core == 1, line, nothing), CORE)
    line_kept = jnp.where(core == 0, line, nothing)
    *plane_parts, gate_part = by_plane(
        where, u_mine, u_came, f_mine, f_came, dw_keep, w_came, line_kept, line_came, chip_parts
    )
    dn, *plane_parts = lax.optimization_barrier((dn, *plane_parts))
    dn = lax.all_to_all(dn, "ctx", 0, 0).reshape(chips, batch, rows, model)
    dtok = finish_tokens(order, dn, flat, dres, full_gain_attn)
    pack = jnp.concatenate([gate_part, add(*column_sum(plane_parts))])

    packs = plane_swaps([after(pack, out_rows)] * 4)
    packs = packs + [swap(piece, CORE) for piece in packs]
    packs[-1] = after(packs[-1], dtok)
    grad_gate, grad_up, grad_down, grad_query, grad_key, grad_value, grad_out, sums = unpack(
        where, packs, depth, units
    )
    grad_gain_attn = sums[0, :depth]
    grad_gain_ffn = sums[0, depth : 2 * depth]
    grad_buckets = sums[0, 2 * depth : small_end].reshape(BUCKETS // planes, HEADS)

    return (
        out_rows, dtok, grad_gain_attn, grad_query, grad_key, grad_value, grad_out, grad_buckets,
        grad_gain_ffn, grad_gate, grad_up, grad_down,
    )


def gelu_tanh(values):
    return (
        0.5
        * values
        * (1.0 + jnp.tanh(0.7978845608028654 * (values + 0.044715 * values * values * values)))
    )


def normalize(values, gain_vec):
    return (
        values * lax.rsqrt(jnp.mean(values * values, axis=-1, keepdims=True) + norm_eps) * gain_vec
    )


def project(values, matrix):
    return jnp.einsum("msd,de->mse", values, matrix, preferred_element_type=jnp.float32)


def back_project(values, matrix):
    return jnp.einsum("mse,de->msd", values, matrix, preferred_element_type=jnp.float32)


def outer_sum(left_rows, right_rows):
    return jnp.einsum("msd,mse->de", left_rows, right_rows, preferred_element_type=jnp.float32)


def split_heads(values):
    return values.reshape(values.shape[0], values.shape[1], HEADS, HEAD_DIM)


def toeplitz_bias(offset_bias, start, query_rows, key_rows):
    span = query_rows + key_rows - 1
    window = lax.dynamic_slice_in_dim(offset_bias, start, span, 1)
    wrapped = jnp.concatenate(
        [
            window[:, query_rows - 1 :],
            jnp.zeros((window.shape[0], 1), jnp.float32),
            window[:, : query_rows - 1],
        ],
        axis=1,
    )
    tiled = jnp.tile(wrapped, (1, query_rows))
    shaped = tiled[:, : query_rows * span].reshape(window.shape[0], query_rows, span)
    return shaped[:, :, :key_rows]


def diagonal_sums(grad_bias, query_rows, key_rows):
    span = query_rows + key_rows - 1
    heads = grad_bias.shape[0]
    padded = jnp.pad(grad_bias, ((0, 0), (0, 0), (0, span - key_rows)))
    flat = jnp.pad(padded.reshape(heads, query_rows * span), ((0, 0), (0, query_rows)))
    slots = jnp.sum(flat.reshape(heads, query_rows, span + 1), axis=1)
    return jnp.concatenate([slots[:, key_rows + 1 :], slots[:, :key_rows]], axis=1)


def block_scores(query_heads, key_heads, pair_bias, key_ok):
    scores = jnp.einsum(
        "mihe,mjhe->mhij", query_heads, key_heads, preferred_element_type=jnp.float32
    )
    scores = scores + pair_bias[None]
    return jnp.where(key_ok[:, None, None, :], scores, -1e30)


def over_blocks(update, make_bias, carried, pieces):
    piece_rows = pieces[0].shape[1]
    block_rows = math.gcd(piece_rows, 256)
    block_count = piece_rows // block_rows

    def advance(block_index, running):
        block_start = block_index * block_rows
        sub_pieces = tuple(
            (
                lax.dynamic_slice_in_dim(member, block_index * block_rows, block_rows, 1)
                for member in pieces
            )
        )
        bias_info = make_bias(block_start, block_rows)
        return update(running, sub_pieces, block_start, slice(None), bias_info)

    return lax.fori_loop(0, block_count, advance, carried)


def per_device_general(
    tokens,
    cotangent,
    lengths,
    bucket_table,
    gain_attn,
    w_query,
    w_key,
    w_value,
    w_out,
    bias_table,
    gain_ffn,
    w_gate,
    w_up,
    w_ffn_out,
):
    shards = (
        gain_attn,
        w_query,
        w_key,
        w_value,
        w_out,
        bias_table,
        gain_ffn,
        w_gate,
        w_up,
        w_ffn_out,
    )
    gathered = (
        lax.all_gather(shards[0], "fsdp", axis=0, tiled=True),
        lax.all_gather(shards[1], "fsdp", axis=0, tiled=True),
        lax.all_gather(shards[2], "fsdp", axis=0, tiled=True),
        lax.all_gather(shards[3], "fsdp", axis=0, tiled=True),
        lax.all_gather(shards[4], "fsdp", axis=0, tiled=True),
        lax.all_gather(shards[5], "fsdp", axis=0, tiled=True),
        lax.all_gather(shards[6], "fsdp", axis=0, tiled=True),
        lax.all_gather(shards[7], "fsdp", axis=0, tiled=True),
        lax.all_gather(shards[8], "fsdp", axis=0, tiled=True),
        lax.all_gather(shards[9], "fsdp", axis=0, tiled=True),
    )
    (
        full_gain_attn,
        full_query,
        full_key,
        full_value,
        full_out,
        full_bias,
        full_gain_ffn,
        full_gate,
        full_up,
        full_ffn_out,
    ) = gathered
    batch_rows, local_rows, model_width = tokens.shape
    seq_len = local_rows * lax.axis_size("ctx")
    table_len = bucket_table.shape[0]
    first_pos = lax.axis_index("ctx") * local_rows
    positions = first_pos + jnp.arange(local_rows, dtype=jnp.int32)
    valid_mask = positions[None, :] < lengths[:, None]
    valid_rows = valid_mask.astype(jnp.float32)
    bucket_hot = bucket_table[:, None] == jnp.arange(BUCKETS, dtype=jnp.int32)[None, :]

    def offset_bias_of(bias_weights):
        return jnp.einsum(
            "tb,bh->ht",
            bucket_hot.astype(jnp.bfloat16),
            bias_weights,
            preferred_element_type=jnp.float32,
        )

    forward_offsets = offset_bias_of(full_bias)

    def keys_bias(offset_bias):

        def keys_make(block_start, block_rows):
            start = block_start - first_pos - (local_rows - 1) + (seq_len - 1)
            return (toeplitz_bias(offset_bias, start, local_rows, block_rows), start)

        return keys_make

    def queries_bias(offset_bias):

        def queries_make(block_start, block_rows):
            start = first_pos - block_start - (block_rows - 1) + (seq_len - 1)
            return (toeplitz_bias(offset_bias, start, block_rows, local_rows), start)

        return queries_make

    tokens_f = tokens.astype(jnp.float32)
    attn_gain = full_gain_attn.astype(jnp.float32)
    normed = normalize(tokens_f, attn_gain).astype(jnp.bfloat16)
    queries = project(normed, full_query).astype(jnp.bfloat16)
    keys_local = project(normed, full_key).astype(jnp.bfloat16)
    values_local = project(normed, full_value).astype(jnp.bfloat16)
    query_heads = split_heads(queries)

    def forward_block(running, sub_pieces, block_start, member_pick, bias_info):
        max_score, row_total, weighted = running
        key_part, value_part = sub_pieces
        key_pos = block_start + jnp.arange(key_part.shape[1], dtype=jnp.int32)
        key_ok = key_pos[None, :] < lengths[:, None]
        scores = block_scores(query_heads, split_heads(key_part), bias_info[0], key_ok)
        new_max = jnp.maximum(max_score, jnp.max(scores, axis=-1))
        shrink = jnp.exp(max_score - new_max)
        weights = jnp.exp(scores - new_max[..., None])
        row_total = row_total * shrink + jnp.sum(weights, axis=-1)
        weighted = weighted * jnp.transpose(shrink, (0, 2, 1))[..., None] + jnp.einsum(
            "mhij,mjhe->mihe",
            weights.astype(jnp.bfloat16),
            split_heads(value_part),
            preferred_element_type=jnp.float32,
        )
        return (new_max, row_total, weighted)

    start_state = (
        jnp.full((batch_rows, HEADS, local_rows), -1e30, jnp.float32),
        jnp.zeros((batch_rows, HEADS, local_rows), jnp.float32),
        jnp.zeros((batch_rows, local_rows, HEADS, HEAD_DIM), jnp.float32),
    )
    max_score, row_total, weighted = over_blocks(
        forward_block,
        keys_bias(forward_offsets),
        start_state,
        (
            lax.all_gather(keys_local, "ctx", axis=1, tiled=True),
            lax.all_gather(values_local, "ctx", axis=1, tiled=True),
        ),
    )
    log_total = max_score + jnp.log(row_total)
    attn_full = weighted / jnp.transpose(row_total, (0, 2, 1))[..., None]
    attn_low = attn_full.reshape(batch_rows, local_rows, model_width).astype(jnp.bfloat16)
    residual = tokens_f + project(attn_low, full_out)
    ffn_gain = full_gain_ffn.astype(jnp.float32)
    normed_ffn = normalize(residual, ffn_gain).astype(jnp.bfloat16)
    gate_proj = project(normed_ffn, full_gate)
    up_proj = project(normed_ffn, full_up)
    hidden = (gelu_tanh(gate_proj) * up_proj).astype(jnp.bfloat16)
    result = valid_rows[..., None] * (residual + project(hidden, full_ffn_out))
    output = result.astype(jnp.bfloat16)
    back_weights = (
        lax.all_gather(shards[0], "fsdp", axis=0, tiled=True),
        lax.all_gather(shards[1], "fsdp", axis=0, tiled=True),
        lax.all_gather(shards[2], "fsdp", axis=0, tiled=True),
        lax.all_gather(shards[3], "fsdp", axis=0, tiled=True),
        lax.all_gather(shards[4], "fsdp", axis=0, tiled=True),
        lax.all_gather(shards[5], "fsdp", axis=0, tiled=True),
        lax.all_gather(shards[6], "fsdp", axis=0, tiled=True),
        lax.all_gather(shards[7], "fsdp", axis=0, tiled=True),
        lax.all_gather(shards[8], "fsdp", axis=0, tiled=True),
        lax.all_gather(shards[9], "fsdp", axis=0, tiled=True),
    )
    (
        back_gain_attn,
        back_query,
        back_key,
        back_value,
        back_out,
        back_bias,
        back_gain_ffn,
        back_gate,
        back_up,
        back_ffn_out,
    ) = back_weights
    back_offsets = offset_bias_of(back_bias)
    grad_out = cotangent.astype(jnp.float32) * valid_rows[..., None]
    grad_low = grad_out.astype(jnp.bfloat16)
    grad_w_ffn_out = outer_sum(hidden, grad_low)
    grad_hidden = back_project(grad_low, back_ffn_out)

    def gated_product(gate_in, up_in):
        return gelu_tanh(gate_in) * up_in

    gated_value, gated_back = jax.vjp(gated_product, gate_proj, up_proj)
    grad_gate, grad_up = gated_back(grad_hidden)
    grad_gate = grad_gate.astype(jnp.bfloat16)
    grad_up = grad_up.astype(jnp.bfloat16)
    grad_w_gate = outer_sum(normed_ffn, grad_gate)
    grad_w_up = outer_sum(normed_ffn, grad_up)
    grad_normed_ffn = back_project(grad_gate, back_gate) + back_project(grad_up, back_up)
    norm_value, norm_back = jax.vjp(normalize, residual, back_gain_ffn.astype(jnp.float32))
    grad_resid_part, grad_gain_ffn = norm_back(grad_normed_ffn)
    grad_resid = grad_out + grad_resid_part
    grad_branch = grad_resid.astype(jnp.bfloat16)
    grad_w_out = outer_sum(attn_low, grad_branch)
    grad_attn = back_project(grad_branch, back_out).astype(jnp.bfloat16)
    grad_heads = split_heads(grad_attn)
    delta_row = jnp.einsum(
        "mihe,mihe->mhi", grad_heads, attn_full, preferred_element_type=jnp.float32
    )

    def query_grad_block(running, sub_pieces, block_start, member_pick, bias_info):
        grad_query, grad_offsets = running
        pair_bias, table_start = bias_info
        key_part, value_part = sub_pieces
        key_heads = split_heads(key_part)
        key_pos = block_start + jnp.arange(key_part.shape[1], dtype=jnp.int32)
        key_ok = key_pos[None, :] < lengths[:, None]
        scores = block_scores(query_heads, key_heads, pair_bias, key_ok)
        probabilities = jnp.exp(scores - log_total[..., None])
        grad_probs = jnp.einsum(
            "mihe,mjhe->mhij",
            grad_heads,
            split_heads(value_part),
            preferred_element_type=jnp.float32,
        )
        grad_scores = (probabilities * (grad_probs - delta_row[..., None])).astype(jnp.bfloat16)
        grad_query = grad_query + jnp.einsum(
            "mhij,mjhe->mihe", grad_scores, key_heads, preferred_element_type=jnp.float32
        )
        pair_grad = jnp.sum(grad_scores.astype(jnp.float32), axis=0)
        diag = diagonal_sums(pair_grad, pair_grad.shape[1], pair_grad.shape[2])
        current = lax.dynamic_slice_in_dim(grad_offsets, table_start, diag.shape[1], 1)
        grad_offsets = lax.dynamic_update_slice_in_dim(grad_offsets, current + diag, table_start, 1)
        return (grad_query, grad_offsets)

    query_state = (
        jnp.zeros((batch_rows, local_rows, HEADS, HEAD_DIM), jnp.float32),
        jnp.zeros((HEADS, table_len), jnp.float32),
    )
    grad_query, grad_offsets = over_blocks(
        query_grad_block,
        keys_bias(back_offsets),
        query_state,
        (
            lax.all_gather(keys_local, "ctx", axis=1, tiled=True),
            lax.all_gather(values_local, "ctx", axis=1, tiled=True),
        ),
    )
    grad_buckets = jnp.einsum(
        "ht,tb->bh", grad_offsets, bucket_hot.astype(jnp.float32), precision=lax.Precision.HIGHEST
    )
    stats_lse, stats_delta = (
        lax.all_gather(log_total, "ctx", axis=2, tiled=True),
        lax.all_gather(delta_row, "ctx", axis=2, tiled=True),
    )
    key_heads_local = split_heads(keys_local)
    value_heads_local = split_heads(values_local)

    def key_grad_block(running, sub_pieces, block_start, member_pick, bias_info):
        grad_key, grad_value = running
        query_part, grad_part = sub_pieces
        rows_here = query_part.shape[1]
        query_part_heads = split_heads(query_part)
        grad_part_heads = split_heads(grad_part)
        scores = block_scores(query_part_heads, key_heads_local, bias_info[0], valid_mask)
        lse_part = lax.dynamic_slice_in_dim(stats_lse, block_start, rows_here, 2)
        delta_part = lax.dynamic_slice_in_dim(stats_delta, block_start, rows_here, 2)
        probabilities = jnp.exp(scores - lse_part[..., None])
        grad_value = grad_value + jnp.einsum(
            "mhij,mihe->mjhe",
            probabilities.astype(jnp.bfloat16),
            grad_part_heads,
            preferred_element_type=jnp.float32,
        )
        grad_probs = jnp.einsum(
            "mihe,mjhe->mhij",
            grad_part_heads,
            value_heads_local,
            preferred_element_type=jnp.float32,
        )
        grad_scores = (probabilities * (grad_probs - delta_part[..., None])).astype(jnp.bfloat16)
        grad_key = grad_key + jnp.einsum(
            "mhij,mihe->mjhe", grad_scores, query_part_heads, preferred_element_type=jnp.float32
        )
        return (grad_key, grad_value)

    key_state = (
        jnp.zeros((batch_rows, local_rows, HEADS, HEAD_DIM), jnp.float32),
        jnp.zeros((batch_rows, local_rows, HEADS, HEAD_DIM), jnp.float32),
    )
    grad_key, grad_value = over_blocks(
        key_grad_block,
        queries_bias(back_offsets),
        key_state,
        (
            lax.all_gather(queries, "ctx", axis=1, tiled=True),
            lax.all_gather(grad_attn, "ctx", axis=1, tiled=True),
        ),
    )
    grad_q = grad_query.reshape(batch_rows, local_rows, model_width).astype(jnp.bfloat16)
    grad_k = grad_key.reshape(batch_rows, local_rows, model_width).astype(jnp.bfloat16)
    grad_v = grad_value.reshape(batch_rows, local_rows, model_width).astype(jnp.bfloat16)
    grad_w_query = outer_sum(normed, grad_q)
    grad_w_key = outer_sum(normed, grad_k)
    grad_w_value = outer_sum(normed, grad_v)
    grad_normed = (
        back_project(grad_q, back_query)
        + back_project(grad_k, back_key)
        + back_project(grad_v, back_value)
    )
    attn_norm_value, attn_norm_back = jax.vjp(
        normalize, tokens_f, back_gain_attn.astype(jnp.float32)
    )
    grad_tokens_part, grad_gain_attn = attn_norm_back(grad_normed)
    grad_tokens = grad_resid + grad_tokens_part
    grads = (
        grad_gain_attn,
        grad_w_query,
        grad_w_key,
        grad_w_value,
        grad_w_out,
        grad_buckets,
        grad_gain_ffn,
        grad_w_gate,
        grad_w_up,
        grad_w_ffn_out,
    )
    shard_sums = (
        lax.psum_scatter(grads[0], "fsdp", scatter_dimension=0, tiled=True),
        lax.psum_scatter(grads[1], "fsdp", scatter_dimension=0, tiled=True),
        lax.psum_scatter(grads[2], "fsdp", scatter_dimension=0, tiled=True),
        lax.psum_scatter(grads[3], "fsdp", scatter_dimension=0, tiled=True),
        lax.psum_scatter(grads[4], "fsdp", scatter_dimension=0, tiled=True),
        lax.psum_scatter(grads[5], "fsdp", scatter_dimension=0, tiled=True),
        lax.psum_scatter(grads[6], "fsdp", scatter_dimension=0, tiled=True),
        lax.psum_scatter(grads[7], "fsdp", scatter_dimension=0, tiled=True),
        lax.psum_scatter(grads[8], "fsdp", scatter_dimension=0, tiled=True),
        lax.psum_scatter(grads[9], "fsdp", scatter_dimension=0, tiled=True),
    )
    totals = lax.psum(
        (
            shard_sums[0],
            shard_sums[1],
            shard_sums[2],
            shard_sums[3],
            shard_sums[4],
            shard_sums[5],
            shard_sums[6],
            shard_sums[7],
            shard_sums[8],
            shard_sums[9],
        ),
        "ctx",
    )
    return (output, grad_tokens) + tuple(totals)


def solution(mesh):
    placed = (
        P("fsdp", "ctx", None),
        P("fsdp", "ctx", None),
        P("fsdp"),
        P(),
        P("fsdp"),
        P("fsdp", None),
        P("fsdp", None),
        P("fsdp", None),
        P("fsdp", None),
        P("fsdp", None),
        P("fsdp"),
        P("fsdp", None),
        P("fsdp", None),
        P("fsdp", None),
    )
    plane = mesh.shape["ctx"] == 8 and mesh.shape["fsdp"] == 4
    return jax.shard_map(
        per_device_plane if plane else per_device_general,
        mesh=mesh,
        in_specs=placed,
        out_specs=(
            P("fsdp", "ctx", None),
            P("fsdp", "ctx", None),
            P("fsdp"),
            P("fsdp", None),
            P("fsdp", None),
            P("fsdp", None),
            P("fsdp", None),
            P("fsdp", None),
            P("fsdp"),
            P("fsdp", None),
            P("fsdp", None),
            P("fsdp", None),
        ),
        check_vma=False,
    )
```

```python
import math

import jax
import jax.numpy as jnp
from jax import lax
from jax.experimental import pallas as pl
from jax.experimental.pallas import tpu as pltpu
from jax.sharding import PartitionSpec as P

HEADS = 12
HEAD_DIM = 64
BUCKETS = 32
BLOCK = 256
TILE = 256
VMEM_BYTES = 56 * 1024 * 1024
COST = 4

norm_eps = 1e-06
F32 = jnp.float32
LOW = jnp.bfloat16
NN = (((1,), (0,)), ((), ()))
NT = (((1,), (1,)), ((), ()))
TN = (((0,), (0,)), ((), ()))
SMEM = pl.BlockSpec(memory_space=pltpu.SMEM)
ANY = pl.BlockSpec(memory_space=pl.ANY)


def dot(left, right, dims=NN):
    return lax.dot_general(left, right, dims, preferred_element_type=F32)


def shape_of(dims, kind):
    return jax.ShapeDtypeStruct(dims, kind)


def params(limit=VMEM_BYTES):
    return pltpu.CompilerParams(vmem_limit_bytes=limit)


def cost(flops, moved, exps=0):
    return pl.CostEstimate(
        flops=int(flops * COST), bytes_accessed=int(moved * COST), transcendentals=int(exps)
    )


def block_rows(index, rows=BLOCK):
    return pl.ds(pl.multiple_of(index * rows, rows), rows)


def rms_rows(rows_f):
    return lax.rsqrt(jnp.mean(rows_f * rows_f, axis=-1, keepdims=True) + norm_eps)


def pack_kernel(
    where_ref, gate_ref, up_ref, down_ref, out_ref, q_ref, k_ref, v_ref, small_ref,
    gate_mine_ref, up_mine_ref, x_ref, y_ref, qkv_ref, early_ref,
):
    chip, core = where_ref[0], where_ref[1]
    x_side, y_side = chip % 2, chip // 2
    wide, depth, model = gate_mine_ref.shape
    planes = gate_ref.shape[1] // model
    part = gate_ref.shape[1] // planes // 2
    slab = depth // 2
    for plane in range(planes):
        columns = pl.ds(pl.multiple_of(plane * 2 * part + core * part, 128), part)
        half, at = divmod(plane * part, model)
        gate_mine_ref[half, :, at : at + part] = gate_ref[:, columns]
        up_mine_ref[half, :, at : at + part] = up_ref[:, columns]
    quarter = part // 4
    x_rows, y_rows = block_rows(x_side, slab), block_rows(y_side, slab)
    for half in range(wide):
        at = slice(half * slab, (half + 1) * slab)
        x_ref[at, :] = gate_mine_ref[half, x_rows, :]
        y_ref[at, :] = up_mine_ref[half, y_rows, :]
    x_down = pl.ds(pl.multiple_of(core * part + x_side * quarter, quarter), quarter)
    y_down = pl.ds(pl.multiple_of(core * part + 2 * quarter + y_side * quarter, quarter), quarter)
    x_ref[wide * slab :, :] = down_ref[x_down, :]
    y_ref[wide * slab :, :] = down_ref[y_down, :]
    early_ref[slab : 2 * slab, :] = out_ref[block_rows(core, slab), :]
    early_ref[2 * slab :, :] = small_ref[...]
    width = model // 4
    for owner in range(4):

        @pl.when(chip == owner)
        def _(owner=owner):
            lanes = slice(owner * width, (owner + 1) * width)
            qkv_ref[:, :width] = q_ref[:, lanes]
            qkv_ref[:, width : 2 * width] = k_ref[:, lanes]
            qkv_ref[:, 2 * width : 3 * width] = v_ref[:, lanes]
            qkv_ref[:, 3 * width :] = jnp.zeros((depth, width), LOW)

    early_ref[:slab, :] = qkv_ref[block_rows(core, slab), :]


def pack_weights(where, gate, up, down, out, query, key, value, small):
    depth, units = gate.shape
    model = query.shape[1]
    planes = model // depth
    wide = units // 2 // model
    part = units // planes // 2
    vmem = pl.BlockSpec(memory_space=pltpu.VMEM)
    return pl.pallas_call(
        pack_kernel,
        in_specs=[SMEM] + [vmem] * 8,
        out_specs=[vmem] * 6,
        out_shape=[
            shape_of((wide, depth, model), LOW),
            shape_of((wide, depth, model), LOW),
            shape_of((wide * depth // 2 + part // 4, model), LOW),
            shape_of((wide * depth // 2 + part // 4, model), LOW),
            shape_of((depth, model), LOW),
            shape_of((depth + small.shape[0], model), LOW),
        ],
        compiler_params=params(),
        cost_estimate=cost(0, 16e6),
        name="pack_weights",
    )(where, gate, up, down, out, query, key, value, small)


def prepare_kernel(lens_ref, tok_ref, send_ref, order_ref, sorted_ref):
    batch = tok_ref.shape[0]
    lens = [lens_ref[i] for i in range(batch)]
    for mine in range(batch):
        rank = 0
        for other in range(batch):
            if other != mine:
                ahead = lens[other] > lens[mine] if other > mine else lens[other] >= lens[mine]
                rank = rank + ahead.astype(jnp.int32)
        slot = jnp.where(rank == 0, 0, jnp.where(rank == batch - 1, 1, rank + 1))
        order_ref[slot] = mine
        sorted_ref[slot] = lens[mine]
    for slot in range(batch):
        rows = tok_ref[order_ref[slot]]
        for chip in range(send_ref.shape[0]):
            send_ref[chip, slot] = rows


def prepare(lengths, tokens, chips):
    batch, rows, model = tokens.shape
    vmem = pl.BlockSpec(memory_space=pltpu.VMEM)
    return pl.pallas_call(
        prepare_kernel,
        in_specs=[SMEM, vmem],
        out_specs=[vmem, SMEM, SMEM],
        out_shape=[
            shape_of((chips, batch, rows, model), LOW),
            shape_of((batch,), jnp.int32),
            shape_of((batch,), jnp.int32),
        ],
        compiler_params=params(),
        cost_estimate=cost(0, 4e6),
        name="prepare",
    )(lengths, tokens)


def sort_rows_kernel(order_ref, lens_ref, start_ref, tok_ref, cot_ref, local_ref, dy_ref):
    slot = pl.program_id(0)
    local_ref[...] = tok_ref[0]
    grads = cot_ref[0].astype(F32)
    place_in = lax.broadcasted_iota(jnp.int32, grads.shape, 0) + start_ref[0]
    dy_ref[...] = jnp.where(place_in < lens_ref[slot], grads, 0.0).astype(LOW)


def sort_rows(order, lens, start, tokens, cotangent):
    batch, rows, model = tokens.shape
    by_order = pl.BlockSpec((1, rows, model), lambda s, order, lens, start: (order[s], 0, 0))
    in_order = pl.BlockSpec((rows, model), lambda s, order, lens, start: (s, 0))
    return pl.pallas_call(
        sort_rows_kernel,
        grid_spec=pltpu.PrefetchScalarGridSpec(
            num_scalar_prefetch=3,
            grid=(batch,),
            in_specs=[by_order, by_order],
            out_specs=[in_order, in_order],
        ),
        out_shape=[
            shape_of((batch * rows, model), LOW),
            shape_of((batch * rows, model), LOW),
        ],
        compiler_params=params(),
        cost_estimate=cost(0, 3e6),
        name="sort_rows",
    )(order, lens, start, tokens, cotangent)


def build_bias(offsets_ref, bias_ref):
    heads, _, width = bias_ref.shape
    span = offsets_ref.shape[1]
    for head in range(heads):
        line = jnp.broadcast_to(offsets_ref[head : head + 1, :], (8, span))
        for group in range(128 // 8):
            turned = pltpu.roll(
                line, (group * 8 - (BLOCK - 1)) % span, 1, stride=1, stride_axis=0
            )
            for first in range(0, BLOCK, 128):
                rows = slice(first + group * 8, first + group * 8 + 8)
                if first == 0:
                    bias_ref[head, rows, :] = turned[:, :width]
                else:
                    bias_ref[head, rows, :first] = turned[:, span - first :]
                    bias_ref[head, rows, first:] = turned[:, : width - first]


def fold_diagonals(bias_grad_ref, offsets_grad_ref):
    heads, _, width = bias_grad_ref.shape
    span = offsets_grad_ref.shape[1]
    for head in range(heads):
        total = jnp.zeros((8, span), F32)
        for group in range(128 // 8):
            part = jnp.zeros((8, span), F32)
            for first in range(0, BLOCK, 128):
                rows = bias_grad_ref[head, first + group * 8 : first + group * 8 + 8, :]
                turned = [rows[:, first:], jnp.zeros((8, span - width), F32)]
                if first > 0:
                    turned.append(rows[:, :first])
                part = part + jnp.concatenate(turned, axis=1)
            total = total + pltpu.roll(part, (BLOCK - 8 - group * 8) % span, 1)
        line = jnp.zeros((1, span), F32)
        for row in range(8):
            line = line + pltpu.roll(total, (7 - row) % span, 1)[row : row + 1, :]
        offsets_grad_ref[head : head + 1, :] = line


def kept_scores(scores, column, length, count):
    wide = count * BLOCK
    tail = jnp.where(column < length - (wide - BLOCK), scores[:, wide - BLOCK :], -1e30)
    if count == 1:
        return tail
    return jnp.concatenate([scores[:, : wide - BLOCK], tail], axis=1)


def token_block(tok_ref, index):
    pieces, _, rows, model = tok_ref.shape
    parts = BLOCK // rows
    return tok_ref[pl.ds(index * parts, parts), 0].reshape(BLOCK, model)


def attn_forward_first_kernel(
    lens_ref, where_ref, tok_ref, gain_ref, w0_ref, w1_ref, w2_ref, w3_ref, v1_ref, v2_ref, v3_ref, off_ref,
    ot_ref, of_ref, q_ref, k_ref, v_ref, w_ref,
    bias_ref, vm_ref,
):
    depth, model = w0_ref.shape
    width = w_ref.shape[2]
    planes, slab = model // depth, depth // 2
    core, plane = where_ref[1], where_ref[2]
    for kind in range(3):
        lanes = slice(kind * width, (kind + 1) * width)
        w_ref[kind, block_rows(plane, depth), :] = w0_ref[:, lanes]
        for back, (piece_ref, other_ref) in enumerate(
            ((w1_ref, v1_ref), (w2_ref, v2_ref), (w3_ref, v3_ref))
        ):
            owner = lax.rem(plane + planes - 1 - back, planes)
            w_ref[kind, block_rows(owner * 2 + core, slab), :] = piece_ref[:slab, lanes]
            w_ref[kind, block_rows(owner * 2 + 1 - core, slab), :] = other_ref[:slab, lanes]
    attend_slot(
        lens_ref[2 * core], tok_ref, gain_ref, w_ref, off_ref,
        ot_ref, of_ref, q_ref, k_ref, v_ref, bias_ref, vm_ref,
    )


def attn_forward_second_kernel(
    lens_ref, where_ref, tok_ref, gain_ref, w_ref, off_ref, of_in, q_in, k_in, v_in,
    ot_ref, of_ref, q_ref, k_ref, v_ref,
    bias_ref, vm_ref,
):
    attend_slot(
        lens_ref[2 * where_ref[1] + 1], tok_ref, gain_ref, w_ref, off_ref,
        ot_ref, of_ref, q_ref, k_ref, v_ref, bias_ref, vm_ref,
    )


def attend_slot(
    length, tok_ref, gain_ref, w_ref, off_ref,
    ot_ref, of_ref, q_ref, k_ref, v_ref, bias_ref, vm_ref,
):
    pieces, _, piece_rows, model = tok_ref.shape
    blocks = pieces * piece_rows // BLOCK
    width = w_ref.shape[2]
    per_chip = width // HEAD_DIM
    used = (length + BLOCK - 1) // BLOCK
    parts = BLOCK // piece_rows
    build_bias(off_ref, bias_ref)
    owner = lax.broadcasted_iota(jnp.int32, (BLOCK, width), 1) // HEAD_DIM
    column = lax.broadcasted_iota(jnp.int32, (BLOCK, BLOCK), 1)
    spare = lax.broadcasted_iota(jnp.int32, (BLOCK, HEAD_DIM), 1)
    nothing = jnp.zeros((BLOCK, width), LOW)

    def project(index, carry):
        rows = block_rows(index)
        rows_f = token_block(tok_ref, index).astype(F32)
        normed = (rows_f * rms_rows(rows_f) * gain_ref[...]).astype(LOW)
        q_ref[0, rows, :] = dot(normed, w_ref[0]).astype(LOW)
        k_ref[0, rows, :] = dot(normed, w_ref[1]).astype(LOW)
        val = dot(normed, w_ref[2]).astype(LOW)
        v_ref[0, rows, :] = val
        for head in range(per_chip):
            vm_ref[head, rows, :] = jnp.where(owner == head, val, nothing)
        return carry

    lax.fori_loop(0, used, project, 0)

    def attend(index, carry):
        rows = block_rows(index)
        query = q_ref[0, rows, :]
        start = pl.multiple_of((blocks - 1 - index) * BLOCK, BLOCK)
        for count in range(1, blocks + 1):

            @pl.when(used == count)
            def _(count=count):
                wide = count * BLOCK
                total = jnp.zeros((BLOCK, width), F32)
                sums = jnp.zeros((BLOCK, HEAD_DIM), F32)
                for head in range(per_chip):
                    mine = jnp.where(owner == head, query, nothing)
                    scores = dot(mine, k_ref[0, :wide, :], NT)
                    scores = scores + bias_ref[head, :, pl.ds(start, wide)]
                    scores = kept_scores(scores, column, length, count)
                    top = jnp.max(scores, axis=-1, keepdims=True)
                    weights = jnp.exp(scores - top)
                    row_total = jnp.sum(weights, axis=-1, keepdims=True)
                    part = dot(weights.astype(LOW), vm_ref[head, :wide, :])
                    total = total + part * (1.0 / row_total)
                    sums = jnp.where(spare == head, top + jnp.log(row_total), sums)
                of_ref[0, rows, :width] = total
                of_ref[0, rows, width:] = sums
                turned = jnp.transpose(total.astype(LOW))
                for piece in range(parts):
                    lanes = slice(piece * piece_rows, (piece + 1) * piece_rows)
                    ot_ref[index * parts + piece, 0] = turned[:, lanes]

        return carry

    lax.fori_loop(0, used, attend, 0)

    def clear(index, carry):
        ot_ref[pl.ds(index * parts, parts), 0] = jnp.zeros((parts, width, piece_rows), LOW)
        return carry

    lax.fori_loop(used, blocks, clear, 0)


def attn_forward(slot, lens, where, tokens, gain, weights, offsets, kept=()):
    pieces, slots, rows, model = tokens.shape
    width = model // 4
    per_chip = width // HEAD_DIM
    seq = pieces * rows
    by_slot = lambda i: (slot, 0, 0)
    whole = lambda array: pl.BlockSpec(array.shape, lambda i: (0,) * array.ndim)
    lane_rows = pl.BlockSpec((1, seq, width), by_slot)
    results = [
        shape_of((slots, seq, width + HEAD_DIM), F32),
        shape_of((slots, seq, width), LOW),
        shape_of((slots, seq, width), LOW),
        shape_of((slots, seq, width), LOW),
    ]
    last = [shape_of((3, model, width), LOW)] if slot == 0 else []
    return pl.pallas_call(
        attn_forward_first_kernel if slot == 0 else attn_forward_second_kernel,
        grid=(1,),
        in_specs=[
            SMEM,
            SMEM,
            pl.BlockSpec((pieces, 1, rows, model), lambda i: (0, slot, 0, 0)),
            whole(gain),
        ]
        + [whole(array) for array in weights]
        + [whole(offsets)]
        + [ANY] * len(kept),
        out_specs=[
            pl.BlockSpec((pieces, 1, width, rows), lambda i: (0, 0, 0, 0)),
            pl.BlockSpec((1, seq, width + HEAD_DIM), by_slot),
            lane_rows,
            lane_rows,
            lane_rows,
        ]
        + [whole(array) for array in last],
        out_shape=[shape_of((pieces, 1, width, rows), LOW)] + results + last,
        scratch_shapes=[
            pltpu.VMEM((per_chip, BLOCK, 2 * seq - BLOCK), F32),
            pltpu.VMEM((per_chip, seq, width), LOW),
        ],
        input_output_aliases={5 + len(weights) + i: 1 + i for i in range(len(kept))},
        compiler_params=params(),
        cost_estimate=cost(
            2 * seq * (model * 3 * width + 2 * seq * 256 * per_chip),
            seq * 2 * (model + 8 * width),
        ),
        name="attn_forward",
    )(lens, where, tokens, gain, *weights, offsets, *kept)


def attn_backward_kernel(
    lens_ref, where_ref, tok_ref, gain_ref, w_ref, off_ref, q_ref, k_ref, v_ref, of_ref, dot_ref,
    dn_ref, dw_keep_ref, dw_send_ref, dgain_ref, doff_ref,
    bias_ref, dbias_ref, km_ref, dq_ref, dkt_ref, dvt_ref, dwt_ref, dw_ref,
):
    slot = pl.program_id(0)
    pieces, _, piece_rows, model = tok_ref.shape
    blocks = pieces * piece_rows // BLOCK
    width = w_ref.shape[2]
    per_chip = width // HEAD_DIM
    core = where_ref[1]
    length = lens_ref[2 * core + slot]
    used = (length + BLOCK - 1) // BLOCK
    parts = BLOCK // piece_rows

    @pl.when(slot == 0)
    def _():
        build_bias(off_ref, bias_ref)
        dbias_ref[...] = jnp.zeros_like(dbias_ref)
        dwt_ref[...] = jnp.zeros_like(dwt_ref)
        dgain_ref[...] = jnp.zeros_like(dgain_ref)

    dkt_ref[...] = jnp.zeros_like(dkt_ref)
    dvt_ref[...] = jnp.zeros_like(dvt_ref)
    owner = lax.broadcasted_iota(jnp.int32, (BLOCK, width), 1) // HEAD_DIM
    column = lax.broadcasted_iota(jnp.int32, (BLOCK, BLOCK), 1)
    nothing = jnp.zeros((BLOCK, width), LOW)

    def split_keys(index, carry):
        rows = block_rows(index)
        key = k_ref[0, rows, :]
        for head in range(per_chip):
            km_ref[head, rows, :] = jnp.where(owner == head, key, nothing)
        return carry

    lax.fori_loop(0, used, split_keys, 0)

    def attend(index, carry):
        rows = block_rows(index)
        query = q_ref[0, rows, :]
        query_t = jnp.transpose(query)
        grad_t = jnp.concatenate(
            [dot_ref[index * parts + piece, 0] for piece in range(parts)], axis=1
        )
        grad = jnp.transpose(grad_t)
        product = grad.astype(F32) * of_ref[0, rows, :width]
        start = pl.multiple_of((blocks - 1 - index) * BLOCK, BLOCK)
        for count in range(1, blocks + 1):

            @pl.when(used == count)
            def _(count=count):
                wide = count * BLOCK
                grad_query = jnp.zeros((BLOCK, width), F32)
                for head in range(per_chip):
                    lanes = slice(head * HEAD_DIM, (head + 1) * HEAD_DIM)
                    mine = jnp.where(owner == head, query, nothing)
                    scores = dot(mine, k_ref[0, :wide, :], NT)
                    scores = scores + bias_ref[head, :, pl.ds(start, wide)]
                    scores = kept_scores(scores, column, length, count)
                    lse = of_ref[0, rows, width + head : width + head + 1]
                    probs = jnp.exp(scores - lse)
                    delta = jnp.sum(
                        jnp.where(owner == head, product, 0.0), axis=-1, keepdims=True
                    )
                    grad_mine = jnp.where(owner == head, grad, nothing)
                    grad_probs = dot(grad_mine, v_ref[0, :wide, :], NT)
                    grad_scores = probs * (grad_probs - delta)
                    dbias_ref[head, :, pl.ds(start, wide)] += grad_scores
                    grad_scores = grad_scores.astype(LOW)
                    grad_query = grad_query + dot(grad_scores, km_ref[head, :wide, :])
                    dkt_ref[lanes, :wide] += dot(query_t[lanes, :], grad_scores)
                    dvt_ref[lanes, :wide] += dot(grad_t[lanes, :], probs.astype(LOW))
                dq_ref[rows, :] = grad_query.astype(LOW)

        return carry

    lax.fori_loop(0, used, attend, 0)

    def finish(index, carry):
        rows = block_rows(index)
        grad_query = dq_ref[rows, :]
        key_t = dkt_ref[:, rows].astype(LOW)
        value_t = dvt_ref[:, rows].astype(LOW)
        rows_f = token_block(tok_ref, index).astype(F32)
        unit = rows_f * rms_rows(rows_f)
        normed = (unit * gain_ref[...]).astype(LOW)
        grad_normed = (
            dot(grad_query, w_ref[0], NT)
            + dot(jnp.transpose(key_t), w_ref[1], NT)
            + dot(jnp.transpose(value_t), w_ref[2], NT)
        )
        dgain_ref[...] += jnp.sum(grad_normed * unit, axis=0, keepdims=True)
        dn_ref[pl.ds(index * parts, parts), 0] = grad_normed.astype(LOW).reshape(
            parts, piece_rows, model
        )
        dwt_ref[0:width, :] += dot(jnp.transpose(grad_query), normed)
        dwt_ref[width : 2 * width, :] += dot(key_t, normed)
        dwt_ref[2 * width :, :] += dot(value_t, normed)
        return carry

    lax.fori_loop(0, used, finish, 0)

    def clear(index, carry):
        dn_ref[pl.ds(index * parts, parts), 0] = jnp.zeros((parts, piece_rows, model), LOW)
        return carry

    lax.fori_loop(used, blocks, clear, 0)

    @pl.when(slot == pl.num_programs(0) - 1)
    def _():
        fold_diagonals(dbias_ref, doff_ref)
        dw_ref[...] = jnp.transpose(dwt_ref[...].astype(LOW))
        planes, slab, _ = dw_keep_ref.shape
        for plane in range(planes):
            lanes = slice(0, 3 * width)
            dw_keep_ref[plane, :, lanes] = dw_ref[block_rows(2 * plane + core, slab), :]
            dw_send_ref[plane, :, lanes] = dw_ref[block_rows(2 * plane + 1 - core, slab), :]
            rest = jnp.zeros((slab, model - 3 * width), LOW)
            dw_keep_ref[plane, :, 3 * width :] = rest
            dw_send_ref[plane, :, 3 * width :] = rest


def attn_backward(
    lens, where, tokens, gain, w_qkv, offsets, query, key, value, attn_full, grad, planes
):
    pieces, slots, rows, model = tokens.shape
    width = w_qkv.shape[2]
    per_chip = width // HEAD_DIM
    seq = pieces * rows
    lane_rows = pl.BlockSpec((1, seq, width), lambda s: (s, 0, 0))
    by_slot = lambda s: (0, s, 0, 0)
    once = lambda s: (0, 0)
    return pl.pallas_call(
        attn_backward_kernel,
        grid=(slots,),
        in_specs=[
            SMEM,
            SMEM,
            pl.BlockSpec((pieces, 1, rows, model), by_slot),
            pl.BlockSpec((1, model), once),
            pl.BlockSpec((3, model, width), lambda s: (0, 0, 0)),
            pl.BlockSpec(offsets.shape, once),
            lane_rows,
            lane_rows,
            lane_rows,
            pl.BlockSpec((1, seq, width + HEAD_DIM), lambda s: (s, 0, 0)),
            pl.BlockSpec((pieces, 1, width, rows), by_slot),
        ],
        out_specs=[
            pl.BlockSpec((pieces, 1, rows, model), by_slot),
            pl.BlockSpec((planes, model // planes // 2, model), lambda s: (0, 0, 0)),
            pl.BlockSpec((planes, model // planes // 2, model), lambda s: (0, 0, 0)),
            pl.BlockSpec((1, model), once),
            pl.BlockSpec((per_chip, 2 * seq), once),
        ],
        out_shape=[
            shape_of((pieces, slots, rows, model), LOW),
            shape_of((planes, model // planes // 2, model), LOW),
            shape_of((planes, model // planes // 2, model), LOW),
            shape_of((1, model), F32),
            shape_of((per_chip, 2 * seq), F32),
        ],
        scratch_shapes=[
            pltpu.VMEM((per_chip, BLOCK, 2 * seq - BLOCK), F32),
            pltpu.VMEM((per_chip, BLOCK, 2 * seq - BLOCK), F32),
            pltpu.VMEM((per_chip, seq, width), LOW),
            pltpu.VMEM((seq, width), LOW),
            pltpu.VMEM((width, seq), F32),
            pltpu.VMEM((width, seq), F32),
            pltpu.VMEM((3 * width, model), F32),
            pltpu.VMEM((model, 3 * width), LOW),
        ],
        compiler_params=params(),
        cost_estimate=cost(
            4 * slots * seq * (model * 6 * width + 5 * seq * 256 * per_chip),
            slots * seq * 2 * (2 * model + 12 * width),
        ),
        name="attn_backward",
    )(lens, where, tokens, gain, w_qkv, offsets, query, key, value, attn_full, grad)


def side_by_side(attn_refs, chip):
    return jnp.concatenate(
        [ref[2 * chip + core, 0] for core in range(2) for ref in attn_refs], axis=1
    )


def out_project_kernel(
    where_ref, tok_ref, attn0_ref, attn1_ref, own_ref, a1_ref, a2_ref, a3_ref, b1_ref, b2_ref, b3_ref, gain_ref,
    res_ref, nf_ref, w_ref,
):
    core, plane = where_ref[1], where_ref[2]
    depth = own_ref.shape[0]
    slab = depth // 2
    planes = w_ref.shape[0] // depth
    w_ref[block_rows(plane, depth), :] = own_ref[...]
    for back, (piece_ref, other_ref) in enumerate(
        ((a1_ref, b1_ref), (a2_ref, b2_ref), (a3_ref, b3_ref))
    ):
        owner = lax.rem(plane + planes - 1 - back, planes)
        w_ref[block_rows(owner * 2 + core, slab), :] = piece_ref[slab : 2 * slab, :]
        w_ref[block_rows(owner * 2 + 1 - core, slab), :] = other_ref[slab : 2 * slab, :]
    chips, width = attn0_ref.shape[0] // 2, attn0_ref.shape[2]
    total = tok_ref[...].astype(F32)
    for chip in range(chips):
        total = total + dot(
            side_by_side((attn0_ref, attn1_ref), chip), w_ref[chip * width : (chip + 1) * width, :], TN
        )
    res_ref[...] = total
    nf_ref[...] = (total * rms_rows(total) * gain_ref[...]).astype(LOW)


def out_project(where, tokens, attn, own, pieces, others, gain):
    rows, model = tokens.shape
    vmem = pl.BlockSpec(memory_space=pltpu.VMEM)
    return pl.pallas_call(
        out_project_kernel,
        in_specs=[SMEM] + [vmem] * 11,
        out_specs=[vmem] * 3,
        out_shape=[
            shape_of((rows, model), F32),
            shape_of((rows, model), LOW),
            shape_of((model, model), LOW),
        ],
        compiler_params=params(),
        cost_estimate=cost(4 * rows * model * model, rows * model * 12),
        name="out_project",
    )(where, tokens, *attn, own, *pieces, *others, gain)


def out_back_kernel(
    where_ref, own_ref, recv_ref, res_ref, dy_ref, gain_ref, w_ref, attn0_ref, attn1_ref,
    dattn_ref, dres_ref, dgain_ref, keep_ref, send_ref,
    gout_ref,
):
    chips, width, rows = dattn_ref.shape[0] // 2, dattn_ref.shape[2], dattn_ref.shape[3]
    grad = own_ref[...] + recv_ref[...].astype(F32)
    residual = res_ref[...]
    scale = rms_rows(residual)
    unit = residual * scale
    dgain_ref[...] = jnp.sum(grad * unit, axis=0, keepdims=True)
    inner = grad * gain_ref[...]
    dres = dy_ref[...].astype(F32) + scale * (
        inner - unit * jnp.mean(inner * unit, axis=-1, keepdims=True)
    )
    dres_ref[...] = dres
    branch = dres.astype(LOW)
    for chip in range(chips):
        heads = slice(chip * width, (chip + 1) * width)
        part = dot(w_ref[heads, :], branch, NT).astype(LOW)
        for slot in range(4):
            dattn_ref[2 * chip + slot // 2, slot % 2] = part[:, slot * rows : (slot + 1) * rows]
        gout_ref[heads, :] = dot(side_by_side((attn0_ref, attn1_ref), chip), branch).astype(LOW)
    core = where_ref[1]
    planes, slab, _ = keep_ref.shape
    for plane in range(planes):
        keep_ref[plane] = gout_ref[block_rows(2 * plane + core, slab), :]
        send_ref[plane] = gout_ref[block_rows(2 * plane + 1 - core, slab), :]


def out_back(where, own, recv, residual, dy, gain, w_out, attn, planes):
    rows, model = own.shape
    vmem = pl.BlockSpec(memory_space=pltpu.VMEM)
    half = shape_of((planes, model // planes // 2, model), LOW)
    return pl.pallas_call(
        out_back_kernel,
        in_specs=[SMEM] + [vmem] * 8,
        out_specs=[vmem] * 5,
        out_shape=[
            shape_of((attn[0].shape[0], 2, *attn[0].shape[2:]), LOW),
            shape_of((rows, model), F32),
            shape_of((1, model), F32),
            half,
            half,
        ],
        scratch_shapes=[pltpu.VMEM((model, model), LOW)],
        compiler_params=params(),
        cost_estimate=cost(8 * rows * model * model, rows * model * 20),
        name="out_back",
    )(where, own, recv, residual, dy, gain, w_out, *attn)


def gate_and_slope(gate):
    square = gate * gate
    half = 0.5 + 0.5 * jnp.tanh(gate * (0.7978845608028654 + 0.035677408136300125 * square))
    turn = gate * (1.5957691216057308 + 0.21406444881780075 * square)
    return gate * half, half * (1.0 + (1.0 - half) * turn)


def ffn_first_kernel(
    where_ref, nf_own_ref, nf_other_ref, dy_own_ref, dy_other_ref,
    gate_own, up_own, down_own, x1, x2, x3, y1, y2, y3, sx1, sx2, sx3, sy1, sy2, sy3,
    hidden_ref, dup_ref, own_ref, other_ref, down_ref, g0_ref, g1_ref, g2_ref, g3_ref,
    gate_ref, up_ref, nf_ref, nft_ref, dy_ref, total_ref, dgate_ref, grad_ref, sems,
):
    step = pl.program_id(0)
    half = nf_own_ref.shape[0]
    chip, core, plane = where_ref[0], where_ref[1], where_ref[2]
    wide, model, _ = gate_ref.shape
    units = down_ref.shape[0]
    tile = hidden_ref.shape[1]
    depth = gate_own.shape[1]
    planes = model // depth
    slab = depth // 2
    part = units // planes
    quarter = part // 4

    def all_copies():
        copies = []

        def copy(source, target, late=False):
            copies.append(((source, target, sems.at[len(copies)]), late))

        own_rows = pl.ds(pl.multiple_of(plane * depth, depth), depth)
        for index in range(wide):
            copy(gate_own.at[index], gate_ref.at[index, own_rows, :], index > 0)
            copy(up_own.at[index], up_ref.at[index, own_rows, :], index > 0)
        copy(
            down_own.at[pl.ds(pl.multiple_of(core * part, part), part), :],
            down_ref.at[pl.ds(pl.multiple_of(plane * part, part), part), :],
        )
        for back in range(planes - 1):
            owner = lax.rem(plane + planes - 1 - back, planes)
            for along, straight, swapped, weight_ref, side in (
                (0, (x1, x2, x3)[back], (sx1, sx2, sx3)[back], gate_ref, lax.rem(chip, 2)),
                (1, (y1, y2, y3)[back], (sy1, sy2, sy3)[back], up_ref, chip // 2),
            ):
                for piece, here in ((straight, side), (swapped, 1 - side)):
                    at = pl.ds(pl.multiple_of(owner * depth + here * slab, slab), slab)
                    for index in range(wide):
                        copy(
                            piece.at[pl.ds(index * slab, slab), :],
                            weight_ref.at[index, at, :],
                            index > 0,
                        )
                    copy(
                        piece.at[pl.ds(wide * slab, quarter), :],
                        down_ref.at[
                            pl.ds(
                                pl.multiple_of(
                                    owner * part + (2 * along + here) * quarter, quarter
                                ),
                                quarter,
                            ),
                            :,
                        ],
                    )
        return copies

    @pl.when(step == 0)
    def _():
        copies = all_copies()
        for late_turn in (False, True):
            for copied, late in copies:
                if late == late_turn:
                    pltpu.make_async_copy(*copied).start()
        nf_ref[:half, :] = nf_own_ref[...]
        nf_ref[half:, :] = nf_other_ref[...]
        nft_ref[:, :half] = jnp.transpose(nf_own_ref[...])
        nft_ref[:, half:] = jnp.transpose(nf_other_ref[...])
        dy_ref[:half, :] = dy_own_ref[...]
        dy_ref[half:, :] = dy_other_ref[...]
        total_ref[...] = jnp.zeros_like(total_ref)
        for copied, late in copies:
            if not late:
                pltpu.make_async_copy(*copied).wait()

    per = model // tile

    @pl.when(step == per)
    def _():
        for copied, late in all_copies():
            if late:
                pltpu.make_async_copy(*copied).wait()

    index = step // per
    lanes = pl.ds(pl.multiple_of(lax.rem(step, per) * tile, tile), tile)
    gate_w = gate_ref[index, :, lanes]
    up_w = up_ref[index, :, lanes]
    down_w = down_ref[block_rows(step, tile), :]
    count = 4
    size = 2 * half // count

    def products(part):
        rows = slice(part * size, (part + 1) * size)
        nf = nf_ref[rows, :]
        return dot(nf, gate_w), dot(nf, up_w), dot(dy_ref[rows, :], down_w, NT)

    ahead = products(0)
    for part in range(count):
        rows = slice(part * size, (part + 1) * size)
        gate, up, dhidden = ahead
        if part + 1 < count:
            ahead = products(part + 1)
        bent, slope = gate_and_slope(gate)
        hidden_ref[rows, :] = (bent * up).astype(LOW)
        dgate = (dhidden * up * slope).astype(LOW)
        dup = (dhidden * bent).astype(LOW)
        dgate_ref[rows, :] = dgate
        dup_ref[rows, :] = dup
        total_ref[rows, :] += dot(dgate, gate_w, NT) + dot(dup, up_w, NT)

    grad_ref[...] = dot(nft_ref[...], dgate_ref[...]).astype(LOW)
    for away, out_ref in enumerate((g0_ref, g1_ref, g2_ref, g3_ref)):
        out_ref[0] = grad_ref[block_rows(lax.rem(plane + away, planes), depth), :]

    @pl.when(step == pl.num_programs(0) - 1)
    def _():
        own_ref[...] = total_ref[:half, :]
        other_ref[...] = total_ref[half:, :].astype(LOW)


def ffn_first(where, nf_own, nf_other, dy_own, dy_other, own_weights, pieces, tile=TILE):
    half, model = nf_own.shape
    wide, depth, _ = own_weights[0].shape
    units = wide * model
    per = model // tile
    whole = pl.BlockSpec((half, model), lambda t: (0, 0))
    lane_tile = pl.BlockSpec((2 * half, tile), lambda t: (0, t))
    grad_tile = pl.BlockSpec((1, depth, tile), lambda t: (t // per, 0, t % per))
    copies = 2 * wide + 1 + 3 * 4 * (wide + 1)
    return pl.pallas_call(
        ffn_first_kernel,
        grid=(units // tile,),
        in_specs=[SMEM, whole, whole, whole, whole] + [ANY] * 15,
        out_specs=[
            lane_tile, lane_tile, whole, whole,
            pl.BlockSpec((units, model), lambda t: (0, 0)),
        ]
        + [grad_tile] * 4,
        out_shape=[
            shape_of((2 * half, units), LOW),
            shape_of((2 * half, units), LOW),
            shape_of((half, model), F32),
            shape_of((half, model), LOW),
            shape_of((units, model), LOW),
        ]
        + [shape_of((wide, depth, model), LOW)] * 4,
        scratch_shapes=[
            pltpu.VMEM((wide, model, model), LOW),
            pltpu.VMEM((wide, model, model), LOW),
            pltpu.VMEM((2 * half, model), LOW),
            pltpu.VMEM((model, 2 * half), LOW),
            pltpu.VMEM((2 * half, model), LOW),
            pltpu.VMEM((2 * half, model), F32),
            pltpu.VMEM((2 * half, tile), LOW),
            pltpu.VMEM((model, tile), LOW),
            pltpu.SemaphoreType.DMA((copies,)),
        ],
        compiler_params=params(),
        cost_estimate=cost(
            2 * 2 * 6 * 2 * half * model * units,
            6 * model * units + 12 * half * units + 20 * half * model,
        ),
        name="ffn_first",
    )(where, nf_own, nf_other, dy_own, dy_other, *own_weights, *pieces)


def ffn_second_kernel(
    where_ref, nf_own_ref, nf_other_ref, dy_own_ref, dy_other_ref, hidden_ref, dup_ref, down_ref,
    own_ref, other_ref, u_keep_ref, u_send_ref, f_keep_ref, f_send_ref,
    nft_ref, dy_ref, total_ref, grad_ref, gdown_ref,
):
    step = pl.program_id(0)
    half = nf_own_ref.shape[0]
    chip = where_ref[0]
    x_side, y_side = lax.rem(chip, 2), chip // 2
    planes, _, slab, tile = u_keep_ref.shape

    @pl.when(step == 0)
    def _():
        nft_ref[:, :half] = jnp.transpose(nf_own_ref[...])
        nft_ref[:, half:] = jnp.transpose(nf_other_ref[...])
        dy_ref[:half, :] = dy_own_ref[...]
        dy_ref[half:, :] = dy_other_ref[...]
        total_ref[...] = jnp.zeros_like(total_ref)

    hidden = hidden_ref[...]
    grad_ref[...] = dot(nft_ref[...], dup_ref[...]).astype(LOW)
    for plane in range(planes):
        u_keep_ref[plane, 0] = grad_ref[block_rows(2 * plane + x_side, slab), :]
        u_send_ref[plane, 0] = grad_ref[block_rows(2 * plane + 1 - x_side, slab), :]
    gdown_ref[block_rows(step, tile), :] = dot(jnp.transpose(hidden), dy_ref[...]).astype(LOW)
    total_ref[...] += dot(hidden, down_ref[...])

    @pl.when(step == pl.num_programs(0) - 1)
    def _():
        own_ref[...] = total_ref[:half, :]
        other_ref[...] = total_ref[half:, :].astype(LOW)
        rows = f_keep_ref.shape[1]
        for plane in range(planes):
            f_keep_ref[plane] = gdown_ref[block_rows(2 * plane + y_side, rows), :]
            f_send_ref[plane] = gdown_ref[block_rows(2 * plane + 1 - y_side, rows), :]


def ffn_second(
    where, nf_own, nf_other, dy_own, dy_other, hidden, dup, w_down, planes, tile=TILE
):
    half, model = nf_own.shape
    units = hidden.shape[1]
    wide, slab, rows = units // model, model // planes // 2, units // planes // 2
    per = model // tile
    whole = pl.BlockSpec((half, model), lambda t: (0, 0))
    lane_tile = pl.BlockSpec((2 * half, tile), lambda t: (0, t))
    row_tile = pl.BlockSpec((tile, model), lambda t: (t, 0))
    up_tile = pl.BlockSpec((planes, 1, slab, tile), lambda t: (0, t // per, 0, t % per))
    down_whole = pl.BlockSpec((planes, rows, model), lambda t: (0, 0, 0))
    return pl.pallas_call(
        ffn_second_kernel,
        grid=(units // tile,),
        in_specs=[SMEM, whole, whole, whole, whole, lane_tile, lane_tile, row_tile],
        out_specs=[whole, whole, up_tile, up_tile, down_whole, down_whole],
        out_shape=[
            shape_of((half, model), F32),
            shape_of((half, model), LOW),
            shape_of((planes, wide, slab, model), LOW),
            shape_of((planes, wide, slab, model), LOW),
            shape_of((planes, rows, model), LOW),
            shape_of((planes, rows, model), LOW),
        ],
        scratch_shapes=[
            pltpu.VMEM((model, 2 * half), LOW),
            pltpu.VMEM((2 * half, model), LOW),
            pltpu.VMEM((2 * half, model), F32),
            pltpu.VMEM((model, tile), LOW),
            pltpu.VMEM((units, model), LOW),
        ],
        compiler_params=params(),
        cost_estimate=cost(
            2 * 2 * 3 * 2 * half * model * units,
            8 * model * units + 12 * half * units + 20 * half * model,
        ),
        name="ffn_second",
    )(where, nf_own, nf_other, dy_own, dy_other, hidden, dup, w_down)


def second_halves_kernel(
    where_ref, u_keep_ref, u_came_ref, f_keep_ref, f_came_ref,
    u_mine_ref, u_send_ref, f_mine_ref, f_send_ref,
):
    chip = where_ref[0]
    x_side, y_side = lax.rem(chip, 2), chip // 2
    for wanted, u_ref, f_ref in ((0, u_mine_ref, f_mine_ref), (1, u_send_ref, f_send_ref)):
        u_side = jnp.bitwise_xor(y_side, wanted)
        rows = block_rows(u_side, u_ref.shape[2])
        u_ref[...] = (
            u_keep_ref[:, :, rows, :].astype(F32) + u_came_ref[:, :, rows, :].astype(F32)
        ).astype(LOW)
        f_side = jnp.bitwise_xor(x_side, wanted)
        rows = block_rows(f_side, f_ref.shape[1])
        f_ref[...] = (
            f_keep_ref[:, rows, :].astype(F32) + f_came_ref[:, rows, :].astype(F32)
        ).astype(LOW)


def second_halves(where, u_keep, u_came, f_keep, f_came):
    planes, wide, slab, model = u_keep.shape
    rows = f_keep.shape[1]
    vmem = pl.BlockSpec(memory_space=pltpu.VMEM)
    return pl.pallas_call(
        second_halves_kernel,
        in_specs=[SMEM] + [vmem] * 4,
        out_specs=[vmem] * 4,
        out_shape=[
            shape_of((planes, wide, slab // 2, model), LOW),
            shape_of((planes, wide, slab // 2, model), LOW),
            shape_of((planes, rows // 2, model), LOW),
            shape_of((planes, rows // 2, model), LOW),
        ],
        compiler_params=params(),
        cost_estimate=cost(0, 7e6),
        name="second_halves",
    )(where, u_keep, u_came, f_keep, f_came)


def by_chip_kernel(where_ref, *refs):
    gate_refs, keep_ref, came_ref, out_refs = refs[:4], refs[4], refs[5], refs[6:]
    chip = where_ref[0]
    wide, depth, model = gate_refs[0].shape
    planes, slab, _ = keep_ref.shape
    rows, half, lanes = depth // 4, slab // 2, model // 2
    for away, out_ref in enumerate(out_refs):
        to_chip = jnp.bitwise_xor(chip, away)
        to_x, to_y = lax.rem(to_chip, 2), to_chip // 2
        at = block_rows(to_x * 2 + to_y, rows)
        for index in range(wide):
            total = gate_refs[0][index, at, :].astype(F32)
            for gate_ref in gate_refs[1:]:
                total = total + gate_ref[index, at, :].astype(F32)
            out_ref[index * rows : (index + 1) * rows, :] = total.astype(LOW)
        columns = block_rows(to_y, lanes)
        for plane in range(planes):
            low = wide * rows + (plane // 2) * half
            left = (plane % 2) * lanes
            out_ref[low : low + half, left : left + lanes] = (
                keep_ref[plane, block_rows(to_x, half), columns].astype(F32)
                + came_ref[plane, block_rows(to_x, half), columns].astype(F32)
            ).astype(LOW)


def by_chip(where, gates, keep, came):
    wide, depth, model = gates[0].shape
    planes, slab, _ = keep.shape
    vmem = pl.BlockSpec(memory_space=pltpu.VMEM)
    return pl.pallas_call(
        by_chip_kernel,
        in_specs=[SMEM] + [vmem] * 6,
        out_specs=[vmem] * 4,
        out_shape=[shape_of((wide * depth // 4 + planes * slab // 4, model), LOW)] * 4,
        compiler_params=params(),
        cost_estimate=cost(0, 3e6),
        name="by_chip",
    )(where, *gates, keep, came)


def by_plane_kernel(where_ref, *refs):
    u_ref, u_came_ref, f_ref, f_came_ref, w_ref, w_came_ref, line_ref, line_came_ref = refs[:8]
    part_refs, out_refs, gate_ref = refs[8:12], refs[12:16], refs[16]
    plane = where_ref[2]
    planes, wide, rows, model = u_ref.shape
    slab = w_ref.shape[1]
    half, lanes = slab // 2, model // 2

    def four(at, columns):
        total = part_refs[0][at, columns].astype(F32)
        for part_ref in part_refs[1:]:
            total = total + part_ref[at, columns].astype(F32)
        return total.astype(LOW)

    gate_ref[...] = four(slice(0, wide * rows), slice(0, model))
    for away, out_ref in enumerate(out_refs):
        at = lax.rem(plane + away, planes)

        def both(ref, came_ref):
            return (ref[at].astype(F32) + came_ref[at].astype(F32)).astype(LOW)

        for index in range(wide):
            out_ref[index * rows : (index + 1) * rows, :] = (
                u_ref[at, index].astype(F32) + u_came_ref[at, index].astype(F32)
            ).astype(LOW)
        low = wide * rows
        out_ref[low : low + f_ref.shape[1], :] = both(f_ref, f_came_ref)
        low = low + f_ref.shape[1]
        used = 3 * model // 4
        out_ref[low : low + slab, :used] = both(w_ref, w_came_ref)[:, :used]
        out_part = four(
            pl.ds(pl.multiple_of(wide * rows + at // 2 * half, half), half),
            pl.ds(pl.multiple_of(lax.rem(at, 2) * lanes, lanes), lanes),
        )
        out_ref[low : low + half, used:] = out_part[:, : model - used]
        out_ref[low + half : low + slab, used:] = out_part[:, model - used :]
        out_ref[low + slab :, :] = both(line_ref, line_came_ref)


def by_plane(where, u_mine, u_came, f_mine, f_came, w_keep, w_came, line_keep, line_came, parts):
    planes, wide, slab, model = u_mine.shape
    rows = wide * slab + f_mine.shape[1] + w_keep.shape[1] + line_keep.shape[1]
    vmem = pl.BlockSpec(memory_space=pltpu.VMEM)
    return pl.pallas_call(
        by_plane_kernel,
        in_specs=[SMEM] + [vmem] * 12,
        out_specs=[vmem] * (planes + 1),
        out_shape=[shape_of((rows, model), LOW)] * planes + [shape_of((wide * slab, model), LOW)],
        compiler_params=params(),
        cost_estimate=cost(0, 6e6),
        name="by_plane",
    )(
        where, u_mine, u_came, f_mine, f_came, w_keep, w_came, line_keep, line_came, *parts
    )


def unpack_kernel(where_ref, *refs):
    piece_refs = refs[:8]
    gate_ref, up_ref, down_ref, q_ref, k_ref, v_ref, out_ref, small_ref = refs[8:]
    step = pl.program_id(0)
    chip, core = where_ref[0], where_ref[1]
    rows_here, units = gate_ref.shape
    _, _, rows, model = down_ref.shape
    quarter, slab = rows_here // 2, rows_here
    part = rows * 4
    wide = units // 2 // model
    planes = units // 2 // part
    width, lanes, half = model // 4, model // 2, slab // 2
    used = 3 * width
    low = 2 * wide * quarter
    last = low + rows
    for far in range(8):
        away, other = far % 4, far // 4
        from_core = core if other == 0 else 1 - core
        from_chip = jnp.bitwise_xor(chip, away)
        from_x, from_y = lax.rem(from_chip, 2), from_chip // 2
        piece_ref = piece_refs[far]

        @pl.when(from_x == step)
        def _(piece_ref=piece_ref, from_core=from_core, from_y=from_y):
            to_rows = block_rows(from_y, quarter)
            for plane in range(planes):
                index, at = divmod(plane * part, model)
                columns = pl.ds(pl.multiple_of(plane * 2 * part + from_core * part, 128), part)
                own = slice(index * quarter, (index + 1) * quarter)
                gate_ref[to_rows, columns] = piece_ref[own, at : at + part].astype(F32)
                own = slice((wide + index) * quarter, (wide + index + 1) * quarter)
                up_ref[to_rows, columns] = piece_ref[own, at : at + part].astype(F32)
            down_ref[from_core * 2 + from_y, 0] = piece_ref[low:last, :].astype(F32)
            out_ref[from_core, 0, :, block_rows(from_y, lanes)] = jnp.concatenate(
                [piece_ref[last : last + half, used:], piece_ref[last + half : last + slab, used:]],
                axis=1,
            ).astype(F32)

        for home in range(4):

            @pl.when((from_chip == home) & (from_x == step))
            def _(home=home, piece_ref=piece_ref, from_core=from_core):
                to_lanes = slice(home * width, (home + 1) * width)
                for kind, target_ref in enumerate((q_ref, k_ref, v_ref)):
                    target_ref[block_rows(from_core, slab), to_lanes] = piece_ref[
                        last : last + slab, kind * width : (kind + 1) * width
                    ].astype(F32)

    @pl.when(step == 0)
    def _():
        small = piece_refs[0][last + slab :, :].astype(F32)
        for piece_ref in piece_refs[1:]:
            small = small + piece_ref[last + slab :, :].astype(F32)
        small_ref[...] = small


def unpack(where, pieces, depth, units):
    rows, model = pieces[0].shape
    planes = model // depth
    part = units // planes
    wide, slab = units // 2 // model, depth // 2
    taken = wide * slab + part // 8 + slab
    whole = lambda dims: pl.BlockSpec(dims, lambda s: (0,) * len(dims))
    by_rows = pl.BlockSpec((slab, units), lambda s: (s, 0))
    square = (depth, model)
    gate, up, down, query, key, value, out, small = pl.pallas_call(
        unpack_kernel,
        grid=(2,),
        in_specs=[SMEM] + [whole((rows, model))] * 8,
        out_specs=[
            by_rows,
            by_rows,
            pl.BlockSpec((4, 1, part // 8, model), lambda s: (0, s, 0, 0)),
            whole(square),
            whole(square),
            whole(square),
            pl.BlockSpec((2, 1, slab // 2, model), lambda s: (0, s, 0, 0)),
            whole((rows - taken, model)),
        ],
        out_shape=[
            shape_of((depth, units), F32),
            shape_of((depth, units), F32),
            shape_of((4, 2, part // 8, model), F32),
            shape_of(square, F32),
            shape_of(square, F32),
            shape_of(square, F32),
            shape_of((2, 2, slab // 2, model), F32),
            shape_of((rows - taken, model), F32),
        ],
        compiler_params=params(),
        cost_estimate=cost(0, 24e6),
        name="unpack",
    )(where, *pieces)
    return gate, up, down.reshape(part, model), query, key, value, out.reshape(square), small


def finish_out_kernel(order_ref, lens_ref, start_ref, res_ref, own_ref, recv_ref, out_ref):
    slot = pl.program_id(0)
    total = res_ref[...] + own_ref[...] + recv_ref[...].astype(F32)
    place_in = lax.broadcasted_iota(jnp.int32, total.shape, 0) + start_ref[0]
    out_ref[0] = jnp.where(place_in < lens_ref[slot], total, 0.0).astype(LOW)


def finish_out(order, lens, start, residual, own, recv, batch):
    rows, model = residual.shape[0] // batch, residual.shape[1]
    in_order = pl.BlockSpec((rows, model), lambda s, order, lens, start: (s, 0))
    return pl.pallas_call(
        finish_out_kernel,
        grid_spec=pltpu.PrefetchScalarGridSpec(
            num_scalar_prefetch=3,
            grid=(batch,),
            in_specs=[in_order, in_order, in_order],
            out_specs=pl.BlockSpec((1, rows, model), lambda s, order, lens, start: (order[s], 0, 0)),
        ),
        out_shape=shape_of((batch, rows, model), LOW),
        compiler_params=params(),
        cost_estimate=cost(0, 6e6),
        name="finish_out",
    )(order, lens, start, residual, own, recv)


def finish_tokens_kernel(order_ref, dn_ref, tok_ref, dres_ref, gain_ref, out_ref):
    grad = dn_ref[0, 0].astype(F32)
    for chip in range(1, dn_ref.shape[0]):
        grad = grad + dn_ref[chip, 0].astype(F32)
    rows_f = tok_ref[...].astype(F32)
    scale = rms_rows(rows_f)
    unit = rows_f * scale
    inner = grad * gain_ref[...]
    out_ref[0] = dres_ref[...] + scale * (
        inner - unit * jnp.mean(inner * unit, axis=-1, keepdims=True)
    )


def finish_tokens(order, dn, tokens, dres, gain):
    chips, batch, rows, model = dn.shape
    in_order = pl.BlockSpec((rows, model), lambda s, order: (s, 0))
    return pl.pallas_call(
        finish_tokens_kernel,
        grid_spec=pltpu.PrefetchScalarGridSpec(
            num_scalar_prefetch=1,
            grid=(batch,),
            in_specs=[
                pl.BlockSpec((chips, 1, rows, model), lambda s, order: (0, s, 0, 0)),
                in_order,
                in_order,
                pl.BlockSpec((1, model), lambda s, order: (0, 0)),
            ],
            out_specs=pl.BlockSpec((1, rows, model), lambda s, order: (order[s], 0, 0)),
        ),
        out_shape=shape_of((batch, rows, model), F32),
        compiler_params=params(),
        cost_estimate=cost(0, 10e6),
        name="finish_tokens",
    )(order, dn, tokens, dres, gain)


CORE, X, Y, XY = 1, 2, 4, 6


def swap(values, bits):
    count = lax.axis_size("ctx")
    return lax.ppermute(values, "ctx", [(i, i ^ bits) for i in range(count)])


def shift(values, places):
    count = lax.axis_size("fsdp")
    return lax.ppermute(values, "fsdp", [(i, (i + places) % count) for i in range(count)])


def column_ends(piece):
    return shift(piece, 1), shift(piece, 3)


def after(values, *others):
    return lax.optimization_barrier((values, *others))[0]


def pick(values, index, axis):
    return lax.dynamic_index_in_dim(values, index, axis, keepdims=False)


def add(*parts):
    total = parts[0].astype(F32)
    for part in parts[1:]:
        total = total + part.astype(F32)
    return total.astype(LOW)


def column_sum(picks):
    return [picks[0]] + [shift(picks[away], away) for away in range(1, len(picks))]


def plane_swaps(parts):
    return [parts[0], swap(parts[1], X), swap(parts[2], Y), swap(parts[3], XY)]


def per_device_plane(
    tokens, cotangent, lengths, bucket_table, gain_attn, w_query, w_key, w_value, w_out,
    bias_table, gain_ffn, w_gate, w_up, w_ffn_out,
):
    batch, rows, model = tokens.shape
    planes = lax.axis_size("fsdp")
    chips = lax.axis_size("ctx") // 2
    me = lax.axis_index("ctx")
    plane = lax.axis_index("fsdp")
    core, chip = me % 2, me // 2
    depth, units = w_gate.shape
    chip_heads = HEADS // chips
    width = chip_heads * HEAD_DIM
    where = jnp.stack([chip, core, plane]).astype(jnp.int32)
    start = (me * rows)[None].astype(jnp.int32)

    small = jnp.concatenate([gain_attn, gain_ffn, bias_table.reshape(-1)])
    small = jnp.pad(small[None], ((0, 15), (0, model - small.shape[0])))
    gate_mine, up_mine, x_piece, y_piece, qkv_mine, early_piece = pack_weights(
        where, w_gate, w_up, w_ffn_out, w_out, w_query, w_key, w_value, small
    )
    send, order, lens = prepare(lengths, after(tokens, early_piece), chips)
    gathered = lax.all_to_all(send.reshape(2 * chips, 2, rows, model), "ctx", 0, 0)

    near, far = column_ends(early_piece)
    early = [near, shift(near, 1), far]
    early_others = [swap(piece, CORE) for piece in early]
    x_near, x_far = column_ends(after(x_piece, near, far))
    y_near, y_far = column_ends(after(y_piece, *early))

    by_distance = jnp.stack([piece[depth] for piece in [early_piece] + early])
    all_small = jnp.stack([pick(by_distance, (plane + planes - i) % planes, 0) for i in range(planes)])
    full_gain_attn = all_small[:, :depth].reshape(1, model).astype(F32)
    full_gain_ffn = all_small[:, depth : 2 * depth].reshape(1, model).astype(F32)
    small_end = 2 * depth + bias_table.size
    full_table = all_small[:, 2 * depth : small_end].reshape(BUCKETS, HEADS)

    hot = bucket_table[:, None] == jnp.arange(BUCKETS, dtype=jnp.int32)[None, :]
    hot = jnp.concatenate([hot, jnp.zeros((1, BUCKETS), bool)])
    my_table = lax.dynamic_slice_in_dim(full_table, chip * chip_heads, chip_heads, 1)
    offsets = jnp.einsum("tb,bh->ht", hot.astype(LOW), my_table, preferred_element_type=F32)

    first_out, *kept, w_qkv = attn_forward(
        0, lens, where, gathered, full_gain_attn, [qkv_mine, *early, *early_others], offsets
    )
    x_near, y_near, first_out = lax.optimization_barrier((x_near, y_near, first_out))
    x_found = [x_near, shift(x_near, 1), x_far]
    y_found = [y_near, shift(y_near, 1), y_far]
    second_out, *kept = attn_forward(
        1, lens, where, gathered, full_gain_attn, [w_qkv], offsets, kept
    )
    attn_first = lax.all_to_all(first_out, "ctx", 0, 0)
    second_out, attn_first, x_found[2], y_found[2], *_ = lax.optimization_barrier(
        (second_out, attn_first, x_found[2], y_found[2], x_near, y_near)
    )
    attn = [attn_first, lax.all_to_all(second_out, "ctx", 0, 0)]
    x_swapped, y_swapped = [swap(t, X) for t in x_found], [swap(t, Y) for t in y_found]
    attn[1] = after(attn[1], *x_swapped, *y_swapped)
    attn_full, query, key, value = kept
    flat, dy = sort_rows(order, lens, start, tokens, cotangent)
    residual, nf_own, full_out = out_project(
        where, flat, attn, w_out, early, early_others, full_gain_ffn
    )
    dy_other = swap(after(dy, nf_own), CORE)
    nf_other = swap(nf_own, CORE)
    hidden, dup, dnf_own, dnf_send, full_down, *g_picks = ffn_first(
        where, nf_own, nf_other, dy, dy_other, (gate_mine, up_mine, w_ffn_out),
        x_found + y_found + x_swapped + y_swapped,
    )

    g_parts = column_sum(g_picks)
    dattn, dres, dgain_ffn, o_keep, o_send = out_back(
        where, dnf_own, swap(dnf_send, CORE), residual, dy, full_gain_ffn, full_out, attn, planes
    )
    dattn_all = lax.all_to_all(dattn, "ctx", 0, 0)
    o_came = swap(o_send, CORE)
    out_own, out_send, u_keep, u_send, f_keep, f_send = ffn_second(
        where, nf_own, nf_other, dy, dy_other, hidden, dup, full_down, planes
    )
    g_parts[1], g_parts[3], u_send, f_send, dattn_all = lax.optimization_barrier(
        (g_parts[1], g_parts[3], u_send, f_send, dattn_all)
    )
    u_came, f_came = swap(u_send, X), swap(f_send, Y)
    out_came = swap(out_send, CORE)
    dn, dw_keep, dw_send, dgain_attn, doffsets = attn_backward(
        lens, where, gathered, full_gain_attn, w_qkv, offsets,
        query, key, value, attn_full, dattn_all, planes,
    )

    u_came, f_came, dn, dw_send, dgain_attn, *g_parts = lax.optimization_barrier(
        (u_came, f_came, dn, dw_send, dgain_attn, *g_parts)
    )
    u_mine, u_send, f_mine, f_send = second_halves(where, u_keep, u_came, f_keep, f_came)
    u_came, f_came = swap(u_send, Y), swap(f_send, X)
    w_came = swap(dw_send, CORE)
    chip_parts = plane_swaps(by_chip(where, g_parts, o_keep, o_came))

    out_rows = finish_out(order, lens, start, residual, out_own, out_came, batch)
    mine_buckets = jnp.einsum(
        "ht,tb->bh", doffsets, hot.astype(F32), precision=lax.Precision.HIGHEST
    )
    buckets = lax.dynamic_update_slice_in_dim(
        jnp.zeros((BUCKETS, HEADS), F32), mine_buckets, chip * chip_heads, 1
    )
    line = jnp.concatenate(
        [
            dgain_attn.reshape(planes, depth),
            dgain_ffn.reshape(planes, depth),
            buckets.reshape(planes, -1),
        ],
        axis=1,
    ).astype(LOW)
    line = jnp.pad(line[:, None, :], ((0, 0), (0, 15), (0, model - line.shape[1])))
    nothing = jnp.zeros_like(line)
    line_came = swap(jnp.where(core == 1, line, nothing), CORE)
    line_kept = jnp.where(core == 0, line, nothing)
    *plane_parts, gate_part = by_plane(
        where, u_mine, u_came, f_mine, f_came, dw_keep, w_came, line_kept, line_came, chip_parts
    )
    dn, *plane_parts = lax.optimization_barrier((dn, *plane_parts))
    dn = lax.all_to_all(dn, "ctx", 0, 0).reshape(chips, batch, rows, model)
    dtok = finish_tokens(order, dn, flat, dres, full_gain_attn)
    pack = jnp.concatenate([gate_part, add(*column_sum(plane_parts))])

    packs = plane_swaps([after(pack, out_rows)] * 4)
    packs = packs + [swap(piece, CORE) for piece in packs]
    packs[-1] = after(packs[-1], dtok)
    grad_gate, grad_up, grad_down, grad_query, grad_key, grad_value, grad_out, sums = unpack(
        where, packs, depth, units
    )
    grad_gain_attn = sums[0, :depth]
    grad_gain_ffn = sums[0, depth : 2 * depth]
    grad_buckets = sums[0, 2 * depth : small_end].reshape(BUCKETS // planes, HEADS)

    return (
        out_rows, dtok, grad_gain_attn, grad_query, grad_key, grad_value, grad_out, grad_buckets,
        grad_gain_ffn, grad_gate, grad_up, grad_down,
    )


def gelu_tanh(values):
    return (
        0.5
        * values
        * (1.0 + jnp.tanh(0.7978845608028654 * (values + 0.044715 * values * values * values)))
    )


def normalize(values, gain_vec):
    return (
        values * lax.rsqrt(jnp.mean(values * values, axis=-1, keepdims=True) + norm_eps) * gain_vec
    )


def project(values, matrix):
    return jnp.einsum("msd,de->mse", values, matrix, preferred_element_type=jnp.float32)


def back_project(values, matrix):
    return jnp.einsum("mse,de->msd", values, matrix, preferred_element_type=jnp.float32)


def outer_sum(left_rows, right_rows):
    return jnp.einsum("msd,mse->de", left_rows, right_rows, preferred_element_type=jnp.float32)


def split_heads(values):
    return values.reshape(values.shape[0], values.shape[1], HEADS, HEAD_DIM)


def toeplitz_bias(offset_bias, start, query_rows, key_rows):
    span = query_rows + key_rows - 1
    window = lax.dynamic_slice_in_dim(offset_bias, start, span, 1)
    wrapped = jnp.concatenate(
        [
            window[:, query_rows - 1 :],
            jnp.zeros((window.shape[0], 1), jnp.float32),
            window[:, : query_rows - 1],
        ],
        axis=1,
    )
    tiled = jnp.tile(wrapped, (1, query_rows))
    shaped = tiled[:, : query_rows * span].reshape(window.shape[0], query_rows, span)
    return shaped[:, :, :key_rows]


def diagonal_sums(grad_bias, query_rows, key_rows):
    span = query_rows + key_rows - 1
    heads = grad_bias.shape[0]
    padded = jnp.pad(grad_bias, ((0, 0), (0, 0), (0, span - key_rows)))
    flat = jnp.pad(padded.reshape(heads, query_rows * span), ((0, 0), (0, query_rows)))
    slots = jnp.sum(flat.reshape(heads, query_rows, span + 1), axis=1)
    return jnp.concatenate([slots[:, key_rows + 1 :], slots[:, :key_rows]], axis=1)


def block_scores(query_heads, key_heads, pair_bias, key_ok):
    scores = jnp.einsum(
        "mihe,mjhe->mhij", query_heads, key_heads, preferred_element_type=jnp.float32
    )
    scores = scores + pair_bias[None]
    return jnp.where(key_ok[:, None, None, :], scores, -1e30)


def over_blocks(update, make_bias, carried, pieces):
    piece_rows = pieces[0].shape[1]
    block_rows = math.gcd(piece_rows, 256)
    block_count = piece_rows // block_rows

    def advance(block_index, running):
        block_start = block_index * block_rows
        sub_pieces = tuple(
            (
                lax.dynamic_slice_in_dim(member, block_index * block_rows, block_rows, 1)
                for member in pieces
            )
        )
        bias_info = make_bias(block_start, block_rows)
        return update(running, sub_pieces, block_start, slice(None), bias_info)

    return lax.fori_loop(0, block_count, advance, carried)


def per_device_general(
    tokens,
    cotangent,
    lengths,
    bucket_table,
    gain_attn,
    w_query,
    w_key,
    w_value,
    w_out,
    bias_table,
    gain_ffn,
    w_gate,
    w_up,
    w_ffn_out,
):
    shards = (
        gain_attn,
        w_query,
        w_key,
        w_value,
        w_out,
        bias_table,
        gain_ffn,
        w_gate,
        w_up,
        w_ffn_out,
    )
    gathered = (
        lax.all_gather(shards[0], "fsdp", axis=0, tiled=True),
        lax.all_gather(shards[1], "fsdp", axis=0, tiled=True),
        lax.all_gather(shards[2], "fsdp", axis=0, tiled=True),
        lax.all_gather(shards[3], "fsdp", axis=0, tiled=True),
        lax.all_gather(shards[4], "fsdp", axis=0, tiled=True),
        lax.all_gather(shards[5], "fsdp", axis=0, tiled=True),
        lax.all_gather(shards[6], "fsdp", axis=0, tiled=True),
        lax.all_gather(shards[7], "fsdp", axis=0, tiled=True),
        lax.all_gather(shards[8], "fsdp", axis=0, tiled=True),
        lax.all_gather(shards[9], "fsdp", axis=0, tiled=True),
    )
    (
        full_gain_attn,
        full_query,
        full_key,
        full_value,
        full_out,
        full_bias,
        full_gain_ffn,
        full_gate,
        full_up,
        full_ffn_out,
    ) = gathered
    batch_rows, local_rows, model_width = tokens.shape
    seq_len = local_rows * lax.axis_size("ctx")
    table_len = bucket_table.shape[0]
    first_pos = lax.axis_index("ctx") * local_rows
    positions = first_pos + jnp.arange(local_rows, dtype=jnp.int32)
    valid_mask = positions[None, :] < lengths[:, None]
    valid_rows = valid_mask.astype(jnp.float32)
    bucket_hot = bucket_table[:, None] == jnp.arange(BUCKETS, dtype=jnp.int32)[None, :]

    def offset_bias_of(bias_weights):
        return jnp.einsum(
            "tb,bh->ht",
            bucket_hot.astype(jnp.bfloat16),
            bias_weights,
            preferred_element_type=jnp.float32,
        )

    forward_offsets = offset_bias_of(full_bias)

    def keys_bias(offset_bias):

        def keys_make(block_start, block_rows):
            start = block_start - first_pos - (local_rows - 1) + (seq_len - 1)
            return (toeplitz_bias(offset_bias, start, local_rows, block_rows), start)

        return keys_make

    def queries_bias(offset_bias):

        def queries_make(block_start, block_rows):
            start = first_pos - block_start - (block_rows - 1) + (seq_len - 1)
            return (toeplitz_bias(offset_bias, start, block_rows, local_rows), start)

        return queries_make

    tokens_f = tokens.astype(jnp.float32)
    attn_gain = full_gain_attn.astype(jnp.float32)
    normed = normalize(tokens_f, attn_gain).astype(jnp.bfloat16)
    queries = project(normed, full_query).astype(jnp.bfloat16)
    keys_local = project(normed, full_key).astype(jnp.bfloat16)
    values_local = project(normed, full_value).astype(jnp.bfloat16)
    query_heads = split_heads(queries)

    def forward_block(running, sub_pieces, block_start, member_pick, bias_info):
        max_score, row_total, weighted = running
        key_part, value_part = sub_pieces
        key_pos = block_start + jnp.arange(key_part.shape[1], dtype=jnp.int32)
        key_ok = key_pos[None, :] < lengths[:, None]
        scores = block_scores(query_heads, split_heads(key_part), bias_info[0], key_ok)
        new_max = jnp.maximum(max_score, jnp.max(scores, axis=-1))
        shrink = jnp.exp(max_score - new_max)
        weights = jnp.exp(scores - new_max[..., None])
        row_total = row_total * shrink + jnp.sum(weights, axis=-1)
        weighted = weighted * jnp.transpose(shrink, (0, 2, 1))[..., None] + jnp.einsum(
            "mhij,mjhe->mihe",
            weights.astype(jnp.bfloat16),
            split_heads(value_part),
            preferred_element_type=jnp.float32,
        )
        return (new_max, row_total, weighted)

    start_state = (
        jnp.full((batch_rows, HEADS, local_rows), -1e30, jnp.float32),
        jnp.zeros((batch_rows, HEADS, local_rows), jnp.float32),
        jnp.zeros((batch_rows, local_rows, HEADS, HEAD_DIM), jnp.float32),
    )
    max_score, row_total, weighted = over_blocks(
        forward_block,
        keys_bias(forward_offsets),
        start_state,
        (
            lax.all_gather(keys_local, "ctx", axis=1, tiled=True),
            lax.all_gather(values_local, "ctx", axis=1, tiled=True),
        ),
    )
    log_total = max_score + jnp.log(row_total)
    attn_full = weighted / jnp.transpose(row_total, (0, 2, 1))[..., None]
    attn_low = attn_full.reshape(batch_rows, local_rows, model_width).astype(jnp.bfloat16)
    residual = tokens_f + project(attn_low, full_out)
    ffn_gain = full_gain_ffn.astype(jnp.float32)
    normed_ffn = normalize(residual, ffn_gain).astype(jnp.bfloat16)
    gate_proj = project(normed_ffn, full_gate)
    up_proj = project(normed_ffn, full_up)
    hidden = (gelu_tanh(gate_proj) * up_proj).astype(jnp.bfloat16)
    result = valid_rows[..., None] * (residual + project(hidden, full_ffn_out))
    output = result.astype(jnp.bfloat16)
    back_weights = (
        lax.all_gather(shards[0], "fsdp", axis=0, tiled=True),
        lax.all_gather(shards[1], "fsdp", axis=0, tiled=True),
        lax.all_gather(shards[2], "fsdp", axis=0, tiled=True),
        lax.all_gather(shards[3], "fsdp", axis=0, tiled=True),
        lax.all_gather(shards[4], "fsdp", axis=0, tiled=True),
        lax.all_gather(shards[5], "fsdp", axis=0, tiled=True),
        lax.all_gather(shards[6], "fsdp", axis=0, tiled=True),
        lax.all_gather(shards[7], "fsdp", axis=0, tiled=True),
        lax.all_gather(shards[8], "fsdp", axis=0, tiled=True),
        lax.all_gather(shards[9], "fsdp", axis=0, tiled=True),
    )
    (
        back_gain_attn,
        back_query,
        back_key,
        back_value,
        back_out,
        back_bias,
        back_gain_ffn,
        back_gate,
        back_up,
        back_ffn_out,
    ) = back_weights
    back_offsets = offset_bias_of(back_bias)
    grad_out = cotangent.astype(jnp.float32) * valid_rows[..., None]
    grad_low = grad_out.astype(jnp.bfloat16)
    grad_w_ffn_out = outer_sum(hidden, grad_low)
    grad_hidden = back_project(grad_low, back_ffn_out)

    def gated_product(gate_in, up_in):
        return gelu_tanh(gate_in) * up_in

    gated_value, gated_back = jax.vjp(gated_product, gate_proj, up_proj)
    grad_gate, grad_up = gated_back(grad_hidden)
    grad_gate = grad_gate.astype(jnp.bfloat16)
    grad_up = grad_up.astype(jnp.bfloat16)
    grad_w_gate = outer_sum(normed_ffn, grad_gate)
    grad_w_up = outer_sum(normed_ffn, grad_up)
    grad_normed_ffn = back_project(grad_gate, back_gate) + back_project(grad_up, back_up)
    norm_value, norm_back = jax.vjp(normalize, residual, back_gain_ffn.astype(jnp.float32))
    grad_resid_part, grad_gain_ffn = norm_back(grad_normed_ffn)
    grad_resid = grad_out + grad_resid_part
    grad_branch = grad_resid.astype(jnp.bfloat16)
    grad_w_out = outer_sum(attn_low, grad_branch)
    grad_attn = back_project(grad_branch, back_out).astype(jnp.bfloat16)
    grad_heads = split_heads(grad_attn)
    delta_row = jnp.einsum(
        "mihe,mihe->mhi", grad_heads, attn_full, preferred_element_type=jnp.float32
    )

    def query_grad_block(running, sub_pieces, block_start, member_pick, bias_info):
        grad_query, grad_offsets = running
        pair_bias, table_start = bias_info
        key_part, value_part = sub_pieces
        key_heads = split_heads(key_part)
        key_pos = block_start + jnp.arange(key_part.shape[1], dtype=jnp.int32)
        key_ok = key_pos[None, :] < lengths[:, None]
        scores = block_scores(query_heads, key_heads, pair_bias, key_ok)
        probabilities = jnp.exp(scores - log_total[..., None])
        grad_probs = jnp.einsum(
            "mihe,mjhe->mhij",
            grad_heads,
            split_heads(value_part),
            preferred_element_type=jnp.float32,
        )
        grad_scores = (probabilities * (grad_probs - delta_row[..., None])).astype(jnp.bfloat16)
        grad_query = grad_query + jnp.einsum(
            "mhij,mjhe->mihe", grad_scores, key_heads, preferred_element_type=jnp.float32
        )
        pair_grad = jnp.sum(grad_scores.astype(jnp.float32), axis=0)
        diag = diagonal_sums(pair_grad, pair_grad.shape[1], pair_grad.shape[2])
        current = lax.dynamic_slice_in_dim(grad_offsets, table_start, diag.shape[1], 1)
        grad_offsets = lax.dynamic_update_slice_in_dim(grad_offsets, current + diag, table_start, 1)
        return (grad_query, grad_offsets)

    query_state = (
        jnp.zeros((batch_rows, local_rows, HEADS, HEAD_DIM), jnp.float32),
        jnp.zeros((HEADS, table_len), jnp.float32),
    )
    grad_query, grad_offsets = over_blocks(
        query_grad_block,
        keys_bias(back_offsets),
        query_state,
        (
            lax.all_gather(keys_local, "ctx", axis=1, tiled=True),
            lax.all_gather(values_local, "ctx", axis=1, tiled=True),
        ),
    )
    grad_buckets = jnp.einsum(
        "ht,tb->bh", grad_offsets, bucket_hot.astype(jnp.float32), precision=lax.Precision.HIGHEST
    )
    stats_lse, stats_delta = (
        lax.all_gather(log_total, "ctx", axis=2, tiled=True),
        lax.all_gather(delta_row, "ctx", axis=2, tiled=True),
    )
    key_heads_local = split_heads(keys_local)
    value_heads_local = split_heads(values_local)

    def key_grad_block(running, sub_pieces, block_start, member_pick, bias_info):
        grad_key, grad_value = running
        query_part, grad_part = sub_pieces
        rows_here = query_part.shape[1]
        query_part_heads = split_heads(query_part)
        grad_part_heads = split_heads(grad_part)
        scores = block_scores(query_part_heads, key_heads_local, bias_info[0], valid_mask)
        lse_part = lax.dynamic_slice_in_dim(stats_lse, block_start, rows_here, 2)
        delta_part = lax.dynamic_slice_in_dim(stats_delta, block_start, rows_here, 2)
        probabilities = jnp.exp(scores - lse_part[..., None])
        grad_value = grad_value + jnp.einsum(
            "mhij,mihe->mjhe",
            probabilities.astype(jnp.bfloat16),
            grad_part_heads,
            preferred_element_type=jnp.float32,
        )
        grad_probs = jnp.einsum(
            "mihe,mjhe->mhij",
            grad_part_heads,
            value_heads_local,
            preferred_element_type=jnp.float32,
        )
        grad_scores = (probabilities * (grad_probs - delta_part[..., None])).astype(jnp.bfloat16)
        grad_key = grad_key + jnp.einsum(
            "mhij,mihe->mjhe", grad_scores, query_part_heads, preferred_element_type=jnp.float32
        )
        return (grad_key, grad_value)

    key_state = (
        jnp.zeros((batch_rows, local_rows, HEADS, HEAD_DIM), jnp.float32),
        jnp.zeros((batch_rows, local_rows, HEADS, HEAD_DIM), jnp.float32),
    )
    grad_key, grad_value = over_blocks(
        key_grad_block,
        queries_bias(back_offsets),
        key_state,
        (
            lax.all_gather(queries, "ctx", axis=1, tiled=True),
            lax.all_gather(grad_attn, "ctx", axis=1, tiled=True),
        ),
    )
    grad_q = grad_query.reshape(batch_rows, local_rows, model_width).astype(jnp.bfloat16)
    grad_k = grad_key.reshape(batch_rows, local_rows, model_width).astype(jnp.bfloat16)
    grad_v = grad_value.reshape(batch_rows, local_rows, model_width).astype(jnp.bfloat16)
    grad_w_query = outer_sum(normed, grad_q)
    grad_w_key = outer_sum(normed, grad_k)
    grad_w_value = outer_sum(normed, grad_v)
    grad_normed = (
        back_project(grad_q, back_query)
        + back_project(grad_k, back_key)
        + back_project(grad_v, back_value)
    )
    attn_norm_value, attn_norm_back = jax.vjp(
        normalize, tokens_f, back_gain_attn.astype(jnp.float32)
    )
    grad_tokens_part, grad_gain_attn = attn_norm_back(grad_normed)
    grad_tokens = grad_resid + grad_tokens_part
    grads = (
        grad_gain_attn,
        grad_w_query,
        grad_w_key,
        grad_w_value,
        grad_w_out,
        grad_buckets,
        grad_gain_ffn,
        grad_w_gate,
        grad_w_up,
        grad_w_ffn_out,
    )
    shard_sums = (
        lax.psum_scatter(grads[0], "fsdp", scatter_dimension=0, tiled=True),
        lax.psum_scatter(grads[1], "fsdp", scatter_dimension=0, tiled=True),
        lax.psum_scatter(grads[2], "fsdp", scatter_dimension=0, tiled=True),
        lax.psum_scatter(grads[3], "fsdp", scatter_dimension=0, tiled=True),
        lax.psum_scatter(grads[4], "fsdp", scatter_dimension=0, tiled=True),
        lax.psum_scatter(grads[5], "fsdp", scatter_dimension=0, tiled=True),
        lax.psum_scatter(grads[6], "fsdp", scatter_dimension=0, tiled=True),
        lax.psum_scatter(grads[7], "fsdp", scatter_dimension=0, tiled=True),
        lax.psum_scatter(grads[8], "fsdp", scatter_dimension=0, tiled=True),
        lax.psum_scatter(grads[9], "fsdp", scatter_dimension=0, tiled=True),
    )
    totals = lax.psum(
        (
            shard_sums[0],
            shard_sums[1],
            shard_sums[2],
            shard_sums[3],
            shard_sums[4],
            shard_sums[5],
            shard_sums[6],
            shard_sums[7],
            shard_sums[8],
            shard_sums[9],
        ),
        "ctx",
    )
    return (output, grad_tokens) + tuple(totals)


def solution(mesh):
    placed = (
        P("fsdp", "ctx", None),
        P("fsdp", "ctx", None),
        P("fsdp"),
        P(),
        P("fsdp"),
        P("fsdp", None),
        P("fsdp", None),
        P("fsdp", None),
        P("fsdp", None),
        P("fsdp", None),
        P("fsdp"),
        P("fsdp", None),
        P("fsdp", None),
        P("fsdp", None),
    )
    plane = mesh.shape["ctx"] == 8 and mesh.shape["fsdp"] == 4
    return jax.shard_map(
        per_device_plane if plane else per_device_general,
        mesh=mesh,
        in_specs=placed,
        out_specs=(
            P("fsdp", "ctx", None),
            P("fsdp", "ctx", None),
            P("fsdp"),
            P("fsdp", None),
            P("fsdp", None),
            P("fsdp", None),
            P("fsdp", None),
            P("fsdp", None),
            P("fsdp"),
            P("fsdp", None),
            P("fsdp", None),
            P("fsdp", None),
        ),
        check_vma=False,
    )
```

```python
import math

import jax
import jax.numpy as jnp
from jax import lax
from jax.experimental import pallas as pl
from jax.experimental.pallas import tpu as pltpu
from jax.sharding import PartitionSpec as P

HEADS = 12
HEAD_DIM = 64
BUCKETS = 32
BLOCK = 256
TILE = 256
VMEM_BYTES = 56 * 1024 * 1024
COST = 12

norm_eps = 1e-06
F32 = jnp.float32
LOW = jnp.bfloat16
NN = (((1,), (0,)), ((), ()))
NT = (((1,), (1,)), ((), ()))
TN = (((0,), (0,)), ((), ()))
SMEM = pl.BlockSpec(memory_space=pltpu.SMEM)
ANY = pl.BlockSpec(memory_space=pl.ANY)


def dot(left, right, dims=NN):
    return lax.dot_general(left, right, dims, preferred_element_type=F32)


def shape_of(dims, kind):
    return jax.ShapeDtypeStruct(dims, kind)


def params(limit=VMEM_BYTES):
    return pltpu.CompilerParams(vmem_limit_bytes=limit)


def cost(flops, moved, exps=0):
    return pl.CostEstimate(
        flops=int(flops * COST), bytes_accessed=int(moved * COST), transcendentals=int(exps)
    )


def block_rows(index, rows=BLOCK):
    return pl.ds(pl.multiple_of(index * rows, rows), rows)


def rms_rows(rows_f):
    return lax.rsqrt(jnp.mean(rows_f * rows_f, axis=-1, keepdims=True) + norm_eps)


def pack_kernel(
    where_ref, gate_ref, up_ref, down_ref, out_ref, q_ref, k_ref, v_ref, small_ref,
    gate_mine_ref, up_mine_ref, x_ref, y_ref, qkv_ref, early_ref,
):
    chip, core = where_ref[0], where_ref[1]
    x_side, y_side = chip % 2, chip // 2
    wide, depth, model = gate_mine_ref.shape
    planes = gate_ref.shape[1] // model
    part = gate_ref.shape[1] // planes // 2
    slab = depth // 2
    for plane in range(planes):
        columns = pl.ds(pl.multiple_of(plane * 2 * part + core * part, 128), part)
        half, at = divmod(plane * part, model)
        gate_mine_ref[half, :, at : at + part] = gate_ref[:, columns]
        up_mine_ref[half, :, at : at + part] = up_ref[:, columns]
    quarter = part // 4
    x_rows, y_rows = block_rows(x_side, slab), block_rows(y_side, slab)
    for half in range(wide):
        at = slice(half * slab, (half + 1) * slab)
        x_ref[at, :] = gate_mine_ref[half, x_rows, :]
        y_ref[at, :] = up_mine_ref[half, y_rows, :]
    x_down = pl.ds(pl.multiple_of(core * part + x_side * quarter, quarter), quarter)
    y_down = pl.ds(pl.multiple_of(core * part + 2 * quarter + y_side * quarter, quarter), quarter)
    x_ref[wide * slab :, :] = down_ref[x_down, :]
    y_ref[wide * slab :, :] = down_ref[y_down, :]
    early_ref[slab : 2 * slab, :] = out_ref[block_rows(core, slab), :]
    early_ref[2 * slab :, :] = small_ref[...]
    width = model // 4
    for owner in range(4):

        @pl.when(chip == owner)
        def _(owner=owner):
            lanes = slice(owner * width, (owner + 1) * width)
            qkv_ref[:, :width] = q_ref[:, lanes]
            qkv_ref[:, width : 2 * width] = k_ref[:, lanes]
            qkv_ref[:, 2 * width : 3 * width] = v_ref[:, lanes]
            qkv_ref[:, 3 * width :] = jnp.zeros((depth, width), LOW)

    early_ref[:slab, :] = qkv_ref[block_rows(core, slab), :]


def pack_weights(where, gate, up, down, out, query, key, value, small):
    depth, units = gate.shape
    model = query.shape[1]
    planes = model // depth
    wide = units // 2 // model
    part = units // planes // 2
    vmem = pl.BlockSpec(memory_space=pltpu.VMEM)
    return pl.pallas_call(
        pack_kernel,
        in_specs=[SMEM] + [vmem] * 8,
        out_specs=[vmem] * 6,
        out_shape=[
            shape_of((wide, depth, model), LOW),
            shape_of((wide, depth, model), LOW),
            shape_of((wide * depth // 2 + part // 4, model), LOW),
            shape_of((wide * depth // 2 + part // 4, model), LOW),
            shape_of((depth, model), LOW),
            shape_of((depth + small.shape[0], model), LOW),
        ],
        compiler_params=params(),
        cost_estimate=cost(0, 16e6),
        name="pack_weights",
    )(where, gate, up, down, out, query, key, value, small)


def prepare_kernel(lens_ref, tok_ref, send_ref, order_ref, sorted_ref):
    batch = tok_ref.shape[0]
    lens = [lens_ref[i] for i in range(batch)]
    for mine in range(batch):
        rank = 0
        for other in range(batch):
            if other != mine:
                ahead = lens[other] > lens[mine] if other > mine else lens[other] >= lens[mine]
                rank = rank + ahead.astype(jnp.int32)
        slot = jnp.where(rank == 0, 0, jnp.where(rank == batch - 1, 1, rank + 1))
        order_ref[slot] = mine
        sorted_ref[slot] = lens[mine]
    for slot in range(batch):
        rows = tok_ref[order_ref[slot]]
        for chip in range(send_ref.shape[0]):
            send_ref[chip, slot] = rows


def prepare(lengths, tokens, chips):
    batch, rows, model = tokens.shape
    vmem = pl.BlockSpec(memory_space=pltpu.VMEM)
    return pl.pallas_call(
        prepare_kernel,
        in_specs=[SMEM, vmem],
        out_specs=[vmem, SMEM, SMEM],
        out_shape=[
            shape_of((chips, batch, rows, model), LOW),
            shape_of((batch,), jnp.int32),
            shape_of((batch,), jnp.int32),
        ],
        compiler_params=params(),
        cost_estimate=cost(0, 4e6),
        name="prepare",
    )(lengths, tokens)


def sort_rows_kernel(order_ref, lens_ref, start_ref, tok_ref, cot_ref, local_ref, dy_ref):
    slot = pl.program_id(0)
    local_ref[...] = tok_ref[0]
    grads = cot_ref[0].astype(F32)
    place_in = lax.broadcasted_iota(jnp.int32, grads.shape, 0) + start_ref[0]
    dy_ref[...] = jnp.where(place_in < lens_ref[slot], grads, 0.0).astype(LOW)


def sort_rows(order, lens, start, tokens, cotangent):
    batch, rows, model = tokens.shape
    by_order = pl.BlockSpec((1, rows, model), lambda s, order, lens, start: (order[s], 0, 0))
    in_order = pl.BlockSpec((rows, model), lambda s, order, lens, start: (s, 0))
    return pl.pallas_call(
        sort_rows_kernel,
        grid_spec=pltpu.PrefetchScalarGridSpec(
            num_scalar_prefetch=3,
            grid=(batch,),
            in_specs=[by_order, by_order],
            out_specs=[in_order, in_order],
        ),
        out_shape=[
            shape_of((batch * rows, model), LOW),
            shape_of((batch * rows, model), LOW),
        ],
        compiler_params=params(),
        cost_estimate=cost(0, 3e6),
        name="sort_rows",
    )(order, lens, start, tokens, cotangent)


def build_bias(offsets_ref, bias_ref):
    heads, _, width = bias_ref.shape
    span = offsets_ref.shape[1]
    for head in range(heads):
        line = jnp.broadcast_to(offsets_ref[head : head + 1, :], (8, span))
        for group in range(128 // 8):
            turned = pltpu.roll(
                line, (group * 8 - (BLOCK - 1)) % span, 1, stride=1, stride_axis=0
            )
            for first in range(0, BLOCK, 128):
                rows = slice(first + group * 8, first + group * 8 + 8)
                if first == 0:
                    bias_ref[head, rows, :] = turned[:, :width]
                else:
                    bias_ref[head, rows, :first] = turned[:, span - first :]
                    bias_ref[head, rows, first:] = turned[:, : width - first]


def fold_diagonals(bias_grad_ref, offsets_grad_ref):
    heads, _, width = bias_grad_ref.shape
    span = offsets_grad_ref.shape[1]
    for head in range(heads):
        total = jnp.zeros((8, span), F32)
        for group in range(128 // 8):
            part = jnp.zeros((8, span), F32)
            for first in range(0, BLOCK, 128):
                rows = bias_grad_ref[head, first + group * 8 : first + group * 8 + 8, :]
                turned = [rows[:, first:], jnp.zeros((8, span - width), F32)]
                if first > 0:
                    turned.append(rows[:, :first])
                part = part + jnp.concatenate(turned, axis=1)
            total = total + pltpu.roll(part, (BLOCK - 8 - group * 8) % span, 1)
        line = jnp.zeros((1, span), F32)
        for row in range(8):
            line = line + pltpu.roll(total, (7 - row) % span, 1)[row : row + 1, :]
        offsets_grad_ref[head : head + 1, :] = line


def kept_scores(scores, column, length, count):
    wide = count * BLOCK
    tail = jnp.where(column < length - (wide - BLOCK), scores[:, wide - BLOCK :], -1e30)
    if count == 1:
        return tail
    return jnp.concatenate([scores[:, : wide - BLOCK], tail], axis=1)


def token_block(tok_ref, index):
    pieces, _, rows, model = tok_ref.shape
    parts = BLOCK // rows
    return tok_ref[pl.ds(index * parts, parts), 0].reshape(BLOCK, model)


def attn_forward_first_kernel(
    lens_ref, where_ref, tok_ref, gain_ref, w0_ref, w1_ref, w2_ref, w3_ref, v1_ref, v2_ref, v3_ref, off_ref,
    ot_ref, of_ref, q_ref, k_ref, v_ref, w_ref,
    bias_ref, vm_ref,
):
    depth, model = w0_ref.shape
    width = w_ref.shape[2]
    planes, slab = model // depth, depth // 2
    core, plane = where_ref[1], where_ref[2]
    for kind in range(3):
        lanes = slice(kind * width, (kind + 1) * width)
        w_ref[kind, block_rows(plane, depth), :] = w0_ref[:, lanes]
        for back, (piece_ref, other_ref) in enumerate(
            ((w1_ref, v1_ref), (w2_ref, v2_ref), (w3_ref, v3_ref))
        ):
            owner = lax.rem(plane + planes - 1 - back, planes)
            w_ref[kind, block_rows(owner * 2 + core, slab), :] = piece_ref[:slab, lanes]
            w_ref[kind, block_rows(owner * 2 + 1 - core, slab), :] = other_ref[:slab, lanes]
    attend_slot(
        lens_ref[2 * core], tok_ref, gain_ref, w_ref, off_ref,
        ot_ref, of_ref, q_ref, k_ref, v_ref, bias_ref, vm_ref,
    )


def attn_forward_second_kernel(
    lens_ref, where_ref, tok_ref, gain_ref, w_ref, off_ref, of_in, q_in, k_in, v_in,
    ot_ref, of_ref, q_ref, k_ref, v_ref,
    bias_ref, vm_ref,
):
    attend_slot(
        lens_ref[2 * where_ref[1] + 1], tok_ref, gain_ref, w_ref, off_ref,
        ot_ref, of_ref, q_ref, k_ref, v_ref, bias_ref, vm_ref,
    )


def attend_slot(
    length, tok_ref, gain_ref, w_ref, off_ref,
    ot_ref, of_ref, q_ref, k_ref, v_ref, bias_ref, vm_ref,
):
    pieces, _, piece_rows, model = tok_ref.shape
    blocks = pieces * piece_rows // BLOCK
    width = w_ref.shape[2]
    per_chip = width // HEAD_DIM
    used = (length + BLOCK - 1) // BLOCK
    parts = BLOCK // piece_rows
    build_bias(off_ref, bias_ref)
    owner = lax.broadcasted_iota(jnp.int32, (BLOCK, width), 1) // HEAD_DIM
    column = lax.broadcasted_iota(jnp.int32, (BLOCK, BLOCK), 1)
    spare = lax.broadcasted_iota(jnp.int32, (BLOCK, HEAD_DIM), 1)
    nothing = jnp.zeros((BLOCK, width), LOW)

    def project(index, carry):
        rows = block_rows(index)
        rows_f = token_block(tok_ref, index).astype(F32)
        normed = (rows_f * rms_rows(rows_f) * gain_ref[...]).astype(LOW)
        q_ref[0, rows, :] = dot(normed, w_ref[0]).astype(LOW)
        k_ref[0, rows, :] = dot(normed, w_ref[1]).astype(LOW)
        val = dot(normed, w_ref[2]).astype(LOW)
        v_ref[0, rows, :] = val
        for head in range(per_chip):
            vm_ref[head, rows, :] = jnp.where(owner == head, val, nothing)
        return carry

    lax.fori_loop(0, used, project, 0)

    def attend(index, carry):
        rows = block_rows(index)
        query = q_ref[0, rows, :]
        start = pl.multiple_of((blocks - 1 - index) * BLOCK, BLOCK)
        for count in range(1, blocks + 1):

            @pl.when(used == count)
            def _(count=count):
                wide = count * BLOCK
                total = jnp.zeros((BLOCK, width), F32)
                sums = jnp.zeros((BLOCK, HEAD_DIM), F32)
                for head in range(per_chip):
                    mine = jnp.where(owner == head, query, nothing)
                    scores = dot(mine, k_ref[0, :wide, :], NT)
                    scores = scores + bias_ref[head, :, pl.ds(start, wide)]
                    scores = kept_scores(scores, column, length, count)
                    top = jnp.max(scores, axis=-1, keepdims=True)
                    weights = jnp.exp(scores - top)
                    row_total = jnp.sum(weights, axis=-1, keepdims=True)
                    part = dot(weights.astype(LOW), vm_ref[head, :wide, :])
                    total = total + part * (1.0 / row_total)
                    sums = jnp.where(spare == head, top + jnp.log(row_total), sums)
                of_ref[0, rows, :width] = total
                of_ref[0, rows, width:] = sums
                turned = jnp.transpose(total.astype(LOW))
                for piece in range(parts):
                    lanes = slice(piece * piece_rows, (piece + 1) * piece_rows)
                    ot_ref[index * parts + piece, 0] = turned[:, lanes]

        return carry

    lax.fori_loop(0, used, attend, 0)

    def clear(index, carry):
        ot_ref[pl.ds(index * parts, parts), 0] = jnp.zeros((parts, width, piece_rows), LOW)
        return carry

    lax.fori_loop(used, blocks, clear, 0)


def attn_forward(slot, lens, where, tokens, gain, weights, offsets, kept=()):
    pieces, slots, rows, model = tokens.shape
    width = model // 4
    per_chip = width // HEAD_DIM
    seq = pieces * rows
    by_slot = lambda i: (slot, 0, 0)
    whole = lambda array: pl.BlockSpec(array.shape, lambda i: (0,) * array.ndim)
    lane_rows = pl.BlockSpec((1, seq, width), by_slot)
    results = [
        shape_of((slots, seq, width + HEAD_DIM), F32),
        shape_of((slots, seq, width), LOW),
        shape_of((slots, seq, width), LOW),
        shape_of((slots, seq, width), LOW),
    ]
    last = [shape_of((3, model, width), LOW)] if slot == 0 else []
    return pl.pallas_call(
        attn_forward_first_kernel if slot == 0 else attn_forward_second_kernel,
        grid=(1,),
        in_specs=[
            SMEM,
            SMEM,
            pl.BlockSpec((pieces, 1, rows, model), lambda i: (0, slot, 0, 0)),
            whole(gain),
        ]
        + [whole(array) for array in weights]
        + [whole(offsets)]
        + [ANY] * len(kept),
        out_specs=[
            pl.BlockSpec((pieces, 1, width, rows), lambda i: (0, 0, 0, 0)),
            pl.BlockSpec((1, seq, width + HEAD_DIM), by_slot),
            lane_rows,
            lane_rows,
            lane_rows,
        ]
        + [whole(array) for array in last],
        out_shape=[shape_of((pieces, 1, width, rows), LOW)] + results + last,
        scratch_shapes=[
            pltpu.VMEM((per_chip, BLOCK, 2 * seq - BLOCK), F32),
            pltpu.VMEM((per_chip, seq, width), LOW),
        ],
        input_output_aliases={5 + len(weights) + i: 1 + i for i in range(len(kept))},
        compiler_params=params(),
        cost_estimate=cost(
            2 * seq * (model * 3 * width + 2 * seq * 256 * per_chip),
            seq * 2 * (model + 8 * width),
        ),
        name="attn_forward",
    )(lens, where, tokens, gain, *weights, offsets, *kept)


def attn_backward_kernel(
    lens_ref, where_ref, tok_ref, gain_ref, w_ref, off_ref, q_ref, k_ref, v_ref, of_ref, dot_ref,
    dn_ref, dw_keep_ref, dw_send_ref, dgain_ref, doff_ref,
    bias_ref, dbias_ref, km_ref, dq_ref, dkt_ref, dvt_ref, dwt_ref, dw_ref,
):
    slot = pl.program_id(0)
    pieces, _, piece_rows, model = tok_ref.shape
    blocks = pieces * piece_rows // BLOCK
    width = w_ref.shape[2]
    per_chip = width // HEAD_DIM
    core = where_ref[1]
    length = lens_ref[2 * core + slot]
    used = (length + BLOCK - 1) // BLOCK
    parts = BLOCK // piece_rows

    @pl.when(slot == 0)
    def _():
        build_bias(off_ref, bias_ref)
        dbias_ref[...] = jnp.zeros_like(dbias_ref)
        dwt_ref[...] = jnp.zeros_like(dwt_ref)
        dgain_ref[...] = jnp.zeros_like(dgain_ref)

    dkt_ref[...] = jnp.zeros_like(dkt_ref)
    dvt_ref[...] = jnp.zeros_like(dvt_ref)
    owner = lax.broadcasted_iota(jnp.int32, (BLOCK, width), 1) // HEAD_DIM
    column = lax.broadcasted_iota(jnp.int32, (BLOCK, BLOCK), 1)
    nothing = jnp.zeros((BLOCK, width), LOW)

    def split_keys(index, carry):
        rows = block_rows(index)
        key = k_ref[0, rows, :]
        for head in range(per_chip):
            km_ref[head, rows, :] = jnp.where(owner == head, key, nothing)
        return carry

    lax.fori_loop(0, used, split_keys, 0)

    def attend(index, carry):
        rows = block_rows(index)
        query = q_ref[0, rows, :]
        query_t = jnp.transpose(query)
        grad_t = jnp.concatenate(
            [dot_ref[index * parts + piece, 0] for piece in range(parts)], axis=1
        )
        grad = jnp.transpose(grad_t)
        product = grad.astype(F32) * of_ref[0, rows, :width]
        start = pl.multiple_of((blocks - 1 - index) * BLOCK, BLOCK)
        for count in range(1, blocks + 1):

            @pl.when(used == count)
            def _(count=count):
                wide = count * BLOCK
                grad_query = jnp.zeros((BLOCK, width), F32)
                for head in range(per_chip):
                    lanes = slice(head * HEAD_DIM, (head + 1) * HEAD_DIM)
                    mine = jnp.where(owner == head, query, nothing)
                    scores = dot(mine, k_ref[0, :wide, :], NT)
                    scores = scores + bias_ref[head, :, pl.ds(start, wide)]
                    scores = kept_scores(scores, column, length, count)
                    lse = of_ref[0, rows, width + head : width + head + 1]
                    probs = jnp.exp(scores - lse)
                    delta = jnp.sum(
                        jnp.where(owner == head, product, 0.0), axis=-1, keepdims=True
                    )
                    grad_mine = jnp.where(owner == head, grad, nothing)
                    grad_probs = dot(grad_mine, v_ref[0, :wide, :], NT)
                    grad_scores = probs * (grad_probs - delta)
                    dbias_ref[head, :, pl.ds(start, wide)] += grad_scores
                    grad_scores = grad_scores.astype(LOW)
                    grad_query = grad_query + dot(grad_scores, km_ref[head, :wide, :])
                    dkt_ref[lanes, :wide] += dot(query_t[lanes, :], grad_scores)
                    dvt_ref[lanes, :wide] += dot(grad_t[lanes, :], probs.astype(LOW))
                dq_ref[rows, :] = grad_query.astype(LOW)

        return carry

    lax.fori_loop(0, used, attend, 0)

    def finish(index, carry):
        rows = block_rows(index)
        grad_query = dq_ref[rows, :]
        key_t = dkt_ref[:, rows].astype(LOW)
        value_t = dvt_ref[:, rows].astype(LOW)
        rows_f = token_block(tok_ref, index).astype(F32)
        unit = rows_f * rms_rows(rows_f)
        normed = (unit * gain_ref[...]).astype(LOW)
        grad_normed = (
            dot(grad_query, w_ref[0], NT)
            + dot(jnp.transpose(key_t), w_ref[1], NT)
            + dot(jnp.transpose(value_t), w_ref[2], NT)
        )
        dgain_ref[...] += jnp.sum(grad_normed * unit, axis=0, keepdims=True)
        dn_ref[pl.ds(index * parts, parts), 0] = grad_normed.astype(LOW).reshape(
            parts, piece_rows, model
        )
        dwt_ref[0:width, :] += dot(jnp.transpose(grad_query), normed)
        dwt_ref[width : 2 * width, :] += dot(key_t, normed)
        dwt_ref[2 * width :, :] += dot(value_t, normed)
        return carry

    lax.fori_loop(0, used, finish, 0)

    def clear(index, carry):
        dn_ref[pl.ds(index * parts, parts), 0] = jnp.zeros((parts, piece_rows, model), LOW)
        return carry

    lax.fori_loop(used, blocks, clear, 0)

    @pl.when(slot == pl.num_programs(0) - 1)
    def _():
        fold_diagonals(dbias_ref, doff_ref)
        dw_ref[...] = jnp.transpose(dwt_ref[...].astype(LOW))
        planes, slab, _ = dw_keep_ref.shape
        for plane in range(planes):
            lanes = slice(0, 3 * width)
            dw_keep_ref[plane, :, lanes] = dw_ref[block_rows(2 * plane + core, slab), :]
            dw_send_ref[plane, :, lanes] = dw_ref[block_rows(2 * plane + 1 - core, slab), :]
            rest = jnp.zeros((slab, model - 3 * width), LOW)
            dw_keep_ref[plane, :, 3 * width :] = rest
            dw_send_ref[plane, :, 3 * width :] = rest


def attn_backward(
    lens, where, tokens, gain, w_qkv, offsets, query, key, value, attn_full, grad, planes
):
    pieces, slots, rows, model = tokens.shape
    width = w_qkv.shape[2]
    per_chip = width // HEAD_DIM
    seq = pieces * rows
    lane_rows = pl.BlockSpec((1, seq, width), lambda s: (s, 0, 0))
    by_slot = lambda s: (0, s, 0, 0)
    once = lambda s: (0, 0)
    return pl.pallas_call(
        attn_backward_kernel,
        grid=(slots,),
        in_specs=[
            SMEM,
            SMEM,
            pl.BlockSpec((pieces, 1, rows, model), by_slot),
            pl.BlockSpec((1, model), once),
            pl.BlockSpec((3, model, width), lambda s: (0, 0, 0)),
            pl.BlockSpec(offsets.shape, once),
            lane_rows,
            lane_rows,
            lane_rows,
            pl.BlockSpec((1, seq, width + HEAD_DIM), lambda s: (s, 0, 0)),
            pl.BlockSpec((pieces, 1, width, rows), by_slot),
        ],
        out_specs=[
            pl.BlockSpec((pieces, 1, rows, model), by_slot),
            pl.BlockSpec((planes, model // planes // 2, model), lambda s: (0, 0, 0)),
            pl.BlockSpec((planes, model // planes // 2, model), lambda s: (0, 0, 0)),
            pl.BlockSpec((1, model), once),
            pl.BlockSpec((per_chip, 2 * seq), once),
        ],
        out_shape=[
            shape_of((pieces, slots, rows, model), LOW),
            shape_of((planes, model // planes // 2, model), LOW),
            shape_of((planes, model // planes // 2, model), LOW),
            shape_of((1, model), F32),
            shape_of((per_chip, 2 * seq), F32),
        ],
        scratch_shapes=[
            pltpu.VMEM((per_chip, BLOCK, 2 * seq - BLOCK), F32),
            pltpu.VMEM((per_chip, BLOCK, 2 * seq - BLOCK), F32),
            pltpu.VMEM((per_chip, seq, width), LOW),
            pltpu.VMEM((seq, width), LOW),
            pltpu.VMEM((width, seq), F32),
            pltpu.VMEM((width, seq), F32),
            pltpu.VMEM((3 * width, model), F32),
            pltpu.VMEM((model, 3 * width), LOW),
        ],
        compiler_params=params(),
        cost_estimate=cost(
            4 * slots * seq * (model * 6 * width + 5 * seq * 256 * per_chip),
            slots * seq * 2 * (2 * model + 12 * width),
        ),
        name="attn_backward",
    )(lens, where, tokens, gain, w_qkv, offsets, query, key, value, attn_full, grad)


def side_by_side(attn_refs, chip):
    return jnp.concatenate(
        [ref[2 * chip + core, 0] for core in range(2) for ref in attn_refs], axis=1
    )


def out_project_kernel(
    where_ref, tok_ref, attn0_ref, attn1_ref, own_ref, a1_ref, a2_ref, a3_ref, b1_ref, b2_ref, b3_ref, gain_ref,
    res_ref, nf_ref, w_ref,
):
    core, plane = where_ref[1], where_ref[2]
    depth = own_ref.shape[0]
    slab = depth // 2
    planes = w_ref.shape[0] // depth
    w_ref[block_rows(plane, depth), :] = own_ref[...]
    for back, (piece_ref, other_ref) in enumerate(
        ((a1_ref, b1_ref), (a2_ref, b2_ref), (a3_ref, b3_ref))
    ):
        owner = lax.rem(plane + planes - 1 - back, planes)
        w_ref[block_rows(owner * 2 + core, slab), :] = piece_ref[slab : 2 * slab, :]
        w_ref[block_rows(owner * 2 + 1 - core, slab), :] = other_ref[slab : 2 * slab, :]
    chips, width = attn0_ref.shape[0] // 2, attn0_ref.shape[2]
    total = tok_ref[...].astype(F32)
    for chip in range(chips):
        total = total + dot(
            side_by_side((attn0_ref, attn1_ref), chip), w_ref[chip * width : (chip + 1) * width, :], TN
        )
    res_ref[...] = total
    nf_ref[...] = (total * rms_rows(total) * gain_ref[...]).astype(LOW)


def out_project(where, tokens, attn, own, pieces, others, gain):
    rows, model = tokens.shape
    vmem = pl.BlockSpec(memory_space=pltpu.VMEM)
    return pl.pallas_call(
        out_project_kernel,
        in_specs=[SMEM] + [vmem] * 11,
        out_specs=[vmem] * 3,
        out_shape=[
            shape_of((rows, model), F32),
            shape_of((rows, model), LOW),
            shape_of((model, model), LOW),
        ],
        compiler_params=params(),
        cost_estimate=cost(4 * rows * model * model, rows * model * 12),
        name="out_project",
    )(where, tokens, *attn, own, *pieces, *others, gain)


def out_back_kernel(
    where_ref, own_ref, recv_ref, res_ref, dy_ref, gain_ref, w_ref, attn0_ref, attn1_ref,
    dattn_ref, dres_ref, dgain_ref, keep_ref, send_ref,
    gout_ref,
):
    chips, width, rows = dattn_ref.shape[0] // 2, dattn_ref.shape[2], dattn_ref.shape[3]
    grad = own_ref[...] + recv_ref[...].astype(F32)
    residual = res_ref[...]
    scale = rms_rows(residual)
    unit = residual * scale
    dgain_ref[...] = jnp.sum(grad * unit, axis=0, keepdims=True)
    inner = grad * gain_ref[...]
    dres = dy_ref[...].astype(F32) + scale * (
        inner - unit * jnp.mean(inner * unit, axis=-1, keepdims=True)
    )
    dres_ref[...] = dres
    branch = dres.astype(LOW)
    for chip in range(chips):
        heads = slice(chip * width, (chip + 1) * width)
        part = dot(w_ref[heads, :], branch, NT).astype(LOW)
        for slot in range(4):
            dattn_ref[2 * chip + slot // 2, slot % 2] = part[:, slot * rows : (slot + 1) * rows]
        gout_ref[heads, :] = dot(side_by_side((attn0_ref, attn1_ref), chip), branch).astype(LOW)
    core = where_ref[1]
    planes, slab, _ = keep_ref.shape
    for plane in range(planes):
        keep_ref[plane] = gout_ref[block_rows(2 * plane + core, slab), :]
        send_ref[plane] = gout_ref[block_rows(2 * plane + 1 - core, slab), :]


def out_back(where, own, recv, residual, dy, gain, w_out, attn, planes):
    rows, model = own.shape
    vmem = pl.BlockSpec(memory_space=pltpu.VMEM)
    half = shape_of((planes, model // planes // 2, model), LOW)
    return pl.pallas_call(
        out_back_kernel,
        in_specs=[SMEM] + [vmem] * 8,
        out_specs=[vmem] * 5,
        out_shape=[
            shape_of((attn[0].shape[0], 2, *attn[0].shape[2:]), LOW),
            shape_of((rows, model), F32),
            shape_of((1, model), F32),
            half,
            half,
        ],
        scratch_shapes=[pltpu.VMEM((model, model), LOW)],
        compiler_params=params(),
        cost_estimate=cost(8 * rows * model * model, rows * model * 20),
        name="out_back",
    )(where, own, recv, residual, dy, gain, w_out, *attn)


def gate_and_slope(gate):
    square = gate * gate
    half = 0.5 + 0.5 * jnp.tanh(gate * (0.7978845608028654 + 0.035677408136300125 * square))
    turn = gate * (1.5957691216057308 + 0.21406444881780075 * square)
    return gate * half, half * (1.0 + (1.0 - half) * turn)


def ffn_first_kernel(
    where_ref, nf_own_ref, nf_other_ref, dy_own_ref, dy_other_ref,
    gate_own, up_own, down_own, x1, x2, x3, y1, y2, y3, sx1, sx2, sx3, sy1, sy2, sy3,
    hidden_ref, dup_ref, own_ref, other_ref, down_ref, g0_ref, g1_ref, g2_ref, g3_ref,
    gate_ref, up_ref, nf_ref, nft_ref, dy_ref, total_ref, dgate_ref, grad_ref, sems,
):
    step = pl.program_id(0)
    half = nf_own_ref.shape[0]
    chip, core, plane = where_ref[0], where_ref[1], where_ref[2]
    wide, model, _ = gate_ref.shape
    units = down_ref.shape[0]
    tile = hidden_ref.shape[1]
    depth = gate_own.shape[1]
    planes = model // depth
    slab = depth // 2
    part = units // planes
    quarter = part // 4

    def all_copies():
        copies = []

        def copy(source, target, late=False):
            copies.append(((source, target, sems.at[len(copies)]), late))

        own_rows = pl.ds(pl.multiple_of(plane * depth, depth), depth)
        for index in range(wide):
            copy(gate_own.at[index], gate_ref.at[index, own_rows, :], index > 0)
            copy(up_own.at[index], up_ref.at[index, own_rows, :], index > 0)
        copy(
            down_own.at[pl.ds(pl.multiple_of(core * part, part), part), :],
            down_ref.at[pl.ds(pl.multiple_of(plane * part, part), part), :],
        )
        for back in range(planes - 1):
            owner = lax.rem(plane + planes - 1 - back, planes)
            for along, straight, swapped, weight_ref, side in (
                (0, (x1, x2, x3)[back], (sx1, sx2, sx3)[back], gate_ref, lax.rem(chip, 2)),
                (1, (y1, y2, y3)[back], (sy1, sy2, sy3)[back], up_ref, chip // 2),
            ):
                for piece, here in ((straight, side), (swapped, 1 - side)):
                    at = pl.ds(pl.multiple_of(owner * depth + here * slab, slab), slab)
                    for index in range(wide):
                        copy(
                            piece.at[pl.ds(index * slab, slab), :],
                            weight_ref.at[index, at, :],
                            index > 0,
                        )
                    copy(
                        piece.at[pl.ds(wide * slab, quarter), :],
                        down_ref.at[
                            pl.ds(
                                pl.multiple_of(
                                    owner * part + (2 * along + here) * quarter, quarter
                                ),
                                quarter,
                            ),
                            :,
                        ],
                    )
        return copies

    @pl.when(step == 0)
    def _():
        copies = all_copies()
        for late_turn in (False, True):
            for copied, late in copies:
                if late == late_turn:
                    pltpu.make_async_copy(*copied).start()
        nf_ref[:half, :] = nf_own_ref[...]
        nf_ref[half:, :] = nf_other_ref[...]
        nft_ref[:, :half] = jnp.transpose(nf_own_ref[...])
        nft_ref[:, half:] = jnp.transpose(nf_other_ref[...])
        dy_ref[:half, :] = dy_own_ref[...]
        dy_ref[half:, :] = dy_other_ref[...]
        total_ref[...] = jnp.zeros_like(total_ref)
        for copied, late in copies:
            if not late:
                pltpu.make_async_copy(*copied).wait()

    per = model // tile

    @pl.when(step == per)
    def _():
        for copied, late in all_copies():
            if late:
                pltpu.make_async_copy(*copied).wait()

    index = step // per
    lanes = pl.ds(pl.multiple_of(lax.rem(step, per) * tile, tile), tile)
    gate_w = gate_ref[index, :, lanes]
    up_w = up_ref[index, :, lanes]
    down_w = down_ref[block_rows(step, tile), :]
    count = 4
    size = 2 * half // count

    def products(part):
        rows = slice(part * size, (part + 1) * size)
        nf = nf_ref[rows, :]
        return dot(nf, gate_w), dot(nf, up_w), dot(dy_ref[rows, :], down_w, NT)

    ahead = products(0)
    for part in range(count):
        rows = slice(part * size, (part + 1) * size)
        gate, up, dhidden = ahead
        if part + 1 < count:
            ahead = products(part + 1)
        bent, slope = gate_and_slope(gate)
        hidden_ref[rows, :] = (bent * up).astype(LOW)
        dgate = (dhidden * up * slope).astype(LOW)
        dup = (dhidden * bent).astype(LOW)
        dgate_ref[rows, :] = dgate
        dup_ref[rows, :] = dup
        total_ref[rows, :] += dot(dgate, gate_w, NT) + dot(dup, up_w, NT)

    grad_ref[...] = dot(nft_ref[...], dgate_ref[...]).astype(LOW)
    for away, out_ref in enumerate((g0_ref, g1_ref, g2_ref, g3_ref)):
        out_ref[0] = grad_ref[block_rows(lax.rem(plane + away, planes), depth), :]

    @pl.when(step == pl.num_programs(0) - 1)
    def _():
        own_ref[...] = total_ref[:half, :]
        other_ref[...] = total_ref[half:, :].astype(LOW)


def ffn_first(where, nf_own, nf_other, dy_own, dy_other, own_weights, pieces, tile=TILE):
    half, model = nf_own.shape
    wide, depth, _ = own_weights[0].shape
    units = wide * model
    per = model // tile
    whole = pl.BlockSpec((half, model), lambda t: (0, 0))
    lane_tile = pl.BlockSpec((2 * half, tile), lambda t: (0, t))
    grad_tile = pl.BlockSpec((1, depth, tile), lambda t: (t // per, 0, t % per))
    copies = 2 * wide + 1 + 3 * 4 * (wide + 1)
    return pl.pallas_call(
        ffn_first_kernel,
        grid=(units // tile,),
        in_specs=[SMEM, whole, whole, whole, whole] + [ANY] * 15,
        out_specs=[
            lane_tile, lane_tile, whole, whole,
            pl.BlockSpec((units, model), lambda t: (0, 0)),
        ]
        + [grad_tile] * 4,
        out_shape=[
            shape_of((2 * half, units), LOW),
            shape_of((2 * half, units), LOW),
            shape_of((half, model), F32),
            shape_of((half, model), LOW),
            shape_of((units, model), LOW),
        ]
        + [shape_of((wide, depth, model), LOW)] * 4,
        scratch_shapes=[
            pltpu.VMEM((wide, model, model), LOW),
            pltpu.VMEM((wide, model, model), LOW),
            pltpu.VMEM((2 * half, model), LOW),
            pltpu.VMEM((model, 2 * half), LOW),
            pltpu.VMEM((2 * half, model), LOW),
            pltpu.VMEM((2 * half, model), F32),
            pltpu.VMEM((2 * half, tile), LOW),
            pltpu.VMEM((model, tile), LOW),
            pltpu.SemaphoreType.DMA((copies,)),
        ],
        compiler_params=params(),
        cost_estimate=cost(
            2 * 2 * 6 * 2 * half * model * units,
            6 * model * units + 12 * half * units + 20 * half * model,
        ),
        name="ffn_first",
    )(where, nf_own, nf_other, dy_own, dy_other, *own_weights, *pieces)


def ffn_second_kernel(
    where_ref, nf_own_ref, nf_other_ref, dy_own_ref, dy_other_ref, hidden_ref, dup_ref, down_ref,
    own_ref, other_ref, u_keep_ref, u_send_ref, f_keep_ref, f_send_ref,
    nft_ref, dy_ref, total_ref, grad_ref, gdown_ref,
):
    step = pl.program_id(0)
    half = nf_own_ref.shape[0]
    chip = where_ref[0]
    x_side, y_side = lax.rem(chip, 2), chip // 2
    planes, _, slab, tile = u_keep_ref.shape

    @pl.when(step == 0)
    def _():
        nft_ref[:, :half] = jnp.transpose(nf_own_ref[...])
        nft_ref[:, half:] = jnp.transpose(nf_other_ref[...])
        dy_ref[:half, :] = dy_own_ref[...]
        dy_ref[half:, :] = dy_other_ref[...]
        total_ref[...] = jnp.zeros_like(total_ref)

    hidden = hidden_ref[...]
    grad_ref[...] = dot(nft_ref[...], dup_ref[...]).astype(LOW)
    for plane in range(planes):
        u_keep_ref[plane, 0] = grad_ref[block_rows(2 * plane + x_side, slab), :]
        u_send_ref[plane, 0] = grad_ref[block_rows(2 * plane + 1 - x_side, slab), :]
    gdown_ref[block_rows(step, tile), :] = dot(jnp.transpose(hidden), dy_ref[...]).astype(LOW)
    total_ref[...] += dot(hidden, down_ref[...])

    @pl.when(step == pl.num_programs(0) - 1)
    def _():
        own_ref[...] = total_ref[:half, :]
        other_ref[...] = total_ref[half:, :].astype(LOW)
        rows = f_keep_ref.shape[1]
        for plane in range(planes):
            f_keep_ref[plane] = gdown_ref[block_rows(2 * plane + y_side, rows), :]
            f_send_ref[plane] = gdown_ref[block_rows(2 * plane + 1 - y_side, rows), :]


def ffn_second(
    where, nf_own, nf_other, dy_own, dy_other, hidden, dup, w_down, planes, tile=TILE
):
    half, model = nf_own.shape
    units = hidden.shape[1]
    wide, slab, rows = units // model, model // planes // 2, units // planes // 2
    per = model // tile
    whole = pl.BlockSpec((half, model), lambda t: (0, 0))
    lane_tile = pl.BlockSpec((2 * half, tile), lambda t: (0, t))
    row_tile = pl.BlockSpec((tile, model), lambda t: (t, 0))
    up_tile = pl.BlockSpec((planes, 1, slab, tile), lambda t: (0, t // per, 0, t % per))
    down_whole = pl.BlockSpec((planes, rows, model), lambda t: (0, 0, 0))
    return pl.pallas_call(
        ffn_second_kernel,
        grid=(units // tile,),
        in_specs=[SMEM, whole, whole, whole, whole, lane_tile, lane_tile, row_tile],
        out_specs=[whole, whole, up_tile, up_tile, down_whole, down_whole],
        out_shape=[
            shape_of((half, model), F32),
            shape_of((half, model), LOW),
            shape_of((planes, wide, slab, model), LOW),
            shape_of((planes, wide, slab, model), LOW),
            shape_of((planes, rows, model), LOW),
            shape_of((planes, rows, model), LOW),
        ],
        scratch_shapes=[
            pltpu.VMEM((model, 2 * half), LOW),
            pltpu.VMEM((2 * half, model), LOW),
            pltpu.VMEM((2 * half, model), F32),
            pltpu.VMEM((model, tile), LOW),
            pltpu.VMEM((units, model), LOW),
        ],
        compiler_params=params(),
        cost_estimate=cost(
            2 * 2 * 3 * 2 * half * model * units,
            8 * model * units + 12 * half * units + 20 * half * model,
        ),
        name="ffn_second",
    )(where, nf_own, nf_other, dy_own, dy_other, hidden, dup, w_down)


def second_halves_kernel(
    where_ref, u_keep_ref, u_came_ref, f_keep_ref, f_came_ref,
    u_mine_ref, u_send_ref, f_mine_ref, f_send_ref,
):
    chip = where_ref[0]
    x_side, y_side = lax.rem(chip, 2), chip // 2
    for wanted, u_ref, f_ref in ((0, u_mine_ref, f_mine_ref), (1, u_send_ref, f_send_ref)):
        u_side = jnp.bitwise_xor(y_side, wanted)
        rows = block_rows(u_side, u_ref.shape[2])
        u_ref[...] = (
            u_keep_ref[:, :, rows, :].astype(F32) + u_came_ref[:, :, rows, :].astype(F32)
        ).astype(LOW)
        f_side = jnp.bitwise_xor(x_side, wanted)
        rows = block_rows(f_side, f_ref.shape[1])
        f_ref[...] = (
            f_keep_ref[:, rows, :].astype(F32) + f_came_ref[:, rows, :].astype(F32)
        ).astype(LOW)


def second_halves(where, u_keep, u_came, f_keep, f_came):
    planes, wide, slab, model = u_keep.shape
    rows = f_keep.shape[1]
    vmem = pl.BlockSpec(memory_space=pltpu.VMEM)
    return pl.pallas_call(
        second_halves_kernel,
        in_specs=[SMEM] + [vmem] * 4,
        out_specs=[vmem] * 4,
        out_shape=[
            shape_of((planes, wide, slab // 2, model), LOW),
            shape_of((planes, wide, slab // 2, model), LOW),
            shape_of((planes, rows // 2, model), LOW),
            shape_of((planes, rows // 2, model), LOW),
        ],
        compiler_params=params(),
        cost_estimate=cost(0, 7e6),
        name="second_halves",
    )(where, u_keep, u_came, f_keep, f_came)


def by_chip_kernel(where_ref, *refs):
    gate_refs, keep_ref, came_ref, out_refs = refs[:4], refs[4], refs[5], refs[6:]
    chip = where_ref[0]
    wide, depth, model = gate_refs[0].shape
    planes, slab, _ = keep_ref.shape
    rows, half, lanes = depth // 4, slab // 2, model // 2
    for away, out_ref in enumerate(out_refs):
        to_chip = jnp.bitwise_xor(chip, away)
        to_x, to_y = lax.rem(to_chip, 2), to_chip // 2
        at = block_rows(to_x * 2 + to_y, rows)
        for index in range(wide):
            total = gate_refs[0][index, at, :].astype(F32)
            for gate_ref in gate_refs[1:]:
                total = total + gate_ref[index, at, :].astype(F32)
            out_ref[index * rows : (index + 1) * rows, :] = total.astype(LOW)
        columns = block_rows(to_y, lanes)
        for plane in range(planes):
            low = wide * rows + (plane // 2) * half
            left = (plane % 2) * lanes
            out_ref[low : low + half, left : left + lanes] = (
                keep_ref[plane, block_rows(to_x, half), columns].astype(F32)
                + came_ref[plane, block_rows(to_x, half), columns].astype(F32)
            ).astype(LOW)


def by_chip(where, gates, keep, came):
    wide, depth, model = gates[0].shape
    planes, slab, _ = keep.shape
    vmem = pl.BlockSpec(memory_space=pltpu.VMEM)
    return pl.pallas_call(
        by_chip_kernel,
        in_specs=[SMEM] + [vmem] * 6,
        out_specs=[vmem] * 4,
        out_shape=[shape_of((wide * depth // 4 + planes * slab // 4, model), LOW)] * 4,
        compiler_params=params(),
        cost_estimate=cost(0, 3e6),
        name="by_chip",
    )(where, *gates, keep, came)


def by_plane_kernel(where_ref, *refs):
    u_ref, u_came_ref, f_ref, f_came_ref, w_ref, w_came_ref, line_ref, line_came_ref = refs[:8]
    part_refs, out_refs, gate_ref = refs[8:12], refs[12:16], refs[16]
    plane = where_ref[2]
    planes, wide, rows, model = u_ref.shape
    slab = w_ref.shape[1]
    half, lanes = slab // 2, model // 2

    def four(at, columns):
        total = part_refs[0][at, columns].astype(F32)
        for part_ref in part_refs[1:]:
            total = total + part_ref[at, columns].astype(F32)
        return total.astype(LOW)

    gate_ref[...] = four(slice(0, wide * rows), slice(0, model))
    for away, out_ref in enumerate(out_refs):
        at = lax.rem(plane + away, planes)

        def both(ref, came_ref):
            return (ref[at].astype(F32) + came_ref[at].astype(F32)).astype(LOW)

        for index in range(wide):
            out_ref[index * rows : (index + 1) * rows, :] = (
                u_ref[at, index].astype(F32) + u_came_ref[at, index].astype(F32)
            ).astype(LOW)
        low = wide * rows
        out_ref[low : low + f_ref.shape[1], :] = both(f_ref, f_came_ref)
        low = low + f_ref.shape[1]
        used = 3 * model // 4
        out_ref[low : low + slab, :used] = both(w_ref, w_came_ref)[:, :used]
        out_part = four(
            pl.ds(pl.multiple_of(wide * rows + at // 2 * half, half), half),
            pl.ds(pl.multiple_of(lax.rem(at, 2) * lanes, lanes), lanes),
        )
        out_ref[low : low + half, used:] = out_part[:, : model - used]
        out_ref[low + half : low + slab, used:] = out_part[:, model - used :]
        out_ref[low + slab :, :] = both(line_ref, line_came_ref)


def by_plane(where, u_mine, u_came, f_mine, f_came, w_keep, w_came, line_keep, line_came, parts):
    planes, wide, slab, model = u_mine.shape
    rows = wide * slab + f_mine.shape[1] + w_keep.shape[1] + line_keep.shape[1]
    vmem = pl.BlockSpec(memory_space=pltpu.VMEM)
    return pl.pallas_call(
        by_plane_kernel,
        in_specs=[SMEM] + [vmem] * 12,
        out_specs=[vmem] * (planes + 1),
        out_shape=[shape_of((rows, model), LOW)] * planes + [shape_of((wide * slab, model), LOW)],
        compiler_params=params(),
        cost_estimate=cost(0, 6e6),
        name="by_plane",
    )(
        where, u_mine, u_came, f_mine, f_came, w_keep, w_came, line_keep, line_came, *parts
    )


def unpack_kernel(where_ref, *refs):
    piece_refs = refs[:8]
    gate_ref, up_ref, down_ref, q_ref, k_ref, v_ref, out_ref, small_ref = refs[8:]
    step = pl.program_id(0)
    chip, core = where_ref[0], where_ref[1]
    rows_here, units = gate_ref.shape
    _, _, rows, model = down_ref.shape
    quarter, slab = rows_here // 2, rows_here
    part = rows * 4
    wide = units // 2 // model
    planes = units // 2 // part
    width, lanes, half = model // 4, model // 2, slab // 2
    used = 3 * width
    low = 2 * wide * quarter
    last = low + rows
    for far in range(8):
        away, other = far % 4, far // 4
        from_core = core if other == 0 else 1 - core
        from_chip = jnp.bitwise_xor(chip, away)
        from_x, from_y = lax.rem(from_chip, 2), from_chip // 2
        piece_ref = piece_refs[far]

        @pl.when(from_x == step)
        def _(piece_ref=piece_ref, from_core=from_core, from_y=from_y):
            to_rows = block_rows(from_y, quarter)
            for plane in range(planes):
                index, at = divmod(plane * part, model)
                columns = pl.ds(pl.multiple_of(plane * 2 * part + from_core * part, 128), part)
                own = slice(index * quarter, (index + 1) * quarter)
                gate_ref[to_rows, columns] = piece_ref[own, at : at + part].astype(F32)
                own = slice((wide + index) * quarter, (wide + index + 1) * quarter)
                up_ref[to_rows, columns] = piece_ref[own, at : at + part].astype(F32)
            down_ref[from_core * 2 + from_y, 0] = piece_ref[low:last, :].astype(F32)
            out_ref[from_core, 0, :, block_rows(from_y, lanes)] = jnp.concatenate(
                [piece_ref[last : last + half, used:], piece_ref[last + half : last + slab, used:]],
                axis=1,
            ).astype(F32)

        for home in range(4):

            @pl.when((from_chip == home) & (from_x == step))
            def _(home=home, piece_ref=piece_ref, from_core=from_core):
                to_lanes = slice(home * width, (home + 1) * width)
                for kind, target_ref in enumerate((q_ref, k_ref, v_ref)):
                    target_ref[block_rows(from_core, slab), to_lanes] = piece_ref[
                        last : last + slab, kind * width : (kind + 1) * width
                    ].astype(F32)

    @pl.when(step == 0)
    def _():
        small = piece_refs[0][last + slab :, :].astype(F32)
        for piece_ref in piece_refs[1:]:
            small = small + piece_ref[last + slab :, :].astype(F32)
        small_ref[...] = small


def unpack(where, pieces, depth, units):
    rows, model = pieces[0].shape
    planes = model // depth
    part = units // planes
    wide, slab = units // 2 // model, depth // 2
    taken = wide * slab + part // 8 + slab
    whole = lambda dims: pl.BlockSpec(dims, lambda s: (0,) * len(dims))
    by_rows = pl.BlockSpec((slab, units), lambda s: (s, 0))
    square = (depth, model)
    gate, up, down, query, key, value, out, small = pl.pallas_call(
        unpack_kernel,
        grid=(2,),
        in_specs=[SMEM] + [whole((rows, model))] * 8,
        out_specs=[
            by_rows,
            by_rows,
            pl.BlockSpec((4, 1, part // 8, model), lambda s: (0, s, 0, 0)),
            whole(square),
            whole(square),
            whole(square),
            pl.BlockSpec((2, 1, slab // 2, model), lambda s: (0, s, 0, 0)),
            whole((rows - taken, model)),
        ],
        out_shape=[
            shape_of((depth, units), F32),
            shape_of((depth, units), F32),
            shape_of((4, 2, part // 8, model), F32),
            shape_of(square, F32),
            shape_of(square, F32),
            shape_of(square, F32),
            shape_of((2, 2, slab // 2, model), F32),
            shape_of((rows - taken, model), F32),
        ],
        compiler_params=params(),
        cost_estimate=cost(0, 24e6),
        name="unpack",
    )(where, *pieces)
    return gate, up, down.reshape(part, model), query, key, value, out.reshape(square), small


def finish_out_kernel(order_ref, lens_ref, start_ref, res_ref, own_ref, recv_ref, out_ref):
    slot = pl.program_id(0)
    total = res_ref[...] + own_ref[...] + recv_ref[...].astype(F32)
    place_in = lax.broadcasted_iota(jnp.int32, total.shape, 0) + start_ref[0]
    out_ref[0] = jnp.where(place_in < lens_ref[slot], total, 0.0).astype(LOW)


def finish_out(order, lens, start, residual, own, recv, batch):
    rows, model = residual.shape[0] // batch, residual.shape[1]
    in_order = pl.BlockSpec((rows, model), lambda s, order, lens, start: (s, 0))
    return pl.pallas_call(
        finish_out_kernel,
        grid_spec=pltpu.PrefetchScalarGridSpec(
            num_scalar_prefetch=3,
            grid=(batch,),
            in_specs=[in_order, in_order, in_order],
            out_specs=pl.BlockSpec((1, rows, model), lambda s, order, lens, start: (order[s], 0, 0)),
        ),
        out_shape=shape_of((batch, rows, model), LOW),
        compiler_params=params(),
        cost_estimate=cost(0, 6e6),
        name="finish_out",
    )(order, lens, start, residual, own, recv)


def finish_tokens_kernel(order_ref, dn_ref, tok_ref, dres_ref, gain_ref, out_ref):
    grad = dn_ref[0, 0].astype(F32)
    for chip in range(1, dn_ref.shape[0]):
        grad = grad + dn_ref[chip, 0].astype(F32)
    rows_f = tok_ref[...].astype(F32)
    scale = rms_rows(rows_f)
    unit = rows_f * scale
    inner = grad * gain_ref[...]
    out_ref[0] = dres_ref[...] + scale * (
        inner - unit * jnp.mean(inner * unit, axis=-1, keepdims=True)
    )


def finish_tokens(order, dn, tokens, dres, gain):
    chips, batch, rows, model = dn.shape
    in_order = pl.BlockSpec((rows, model), lambda s, order: (s, 0))
    return pl.pallas_call(
        finish_tokens_kernel,
        grid_spec=pltpu.PrefetchScalarGridSpec(
            num_scalar_prefetch=1,
            grid=(batch,),
            in_specs=[
                pl.BlockSpec((chips, 1, rows, model), lambda s, order: (0, s, 0, 0)),
                in_order,
                in_order,
                pl.BlockSpec((1, model), lambda s, order: (0, 0)),
            ],
            out_specs=pl.BlockSpec((1, rows, model), lambda s, order: (order[s], 0, 0)),
        ),
        out_shape=shape_of((batch, rows, model), F32),
        compiler_params=params(),
        cost_estimate=cost(0, 10e6),
        name="finish_tokens",
    )(order, dn, tokens, dres, gain)


CORE, X, Y, XY = 1, 2, 4, 6


def swap(values, bits):
    count = lax.axis_size("ctx")
    return lax.ppermute(values, "ctx", [(i, i ^ bits) for i in range(count)])


def shift(values, places):
    count = lax.axis_size("fsdp")
    return lax.ppermute(values, "fsdp", [(i, (i + places) % count) for i in range(count)])


def column_ends(piece):
    return shift(piece, 1), shift(piece, 3)


def after(values, *others):
    return lax.optimization_barrier((values, *others))[0]


def pick(values, index, axis):
    return lax.dynamic_index_in_dim(values, index, axis, keepdims=False)


def add(*parts):
    total = parts[0].astype(F32)
    for part in parts[1:]:
        total = total + part.astype(F32)
    return total.astype(LOW)


def column_sum(picks):
    return [picks[0]] + [shift(picks[away], away) for away in range(1, len(picks))]


def plane_swaps(parts):
    return [parts[0], swap(parts[1], X), swap(parts[2], Y), swap(parts[3], XY)]


def per_device_plane(
    tokens, cotangent, lengths, bucket_table, gain_attn, w_query, w_key, w_value, w_out,
    bias_table, gain_ffn, w_gate, w_up, w_ffn_out,
):
    batch, rows, model = tokens.shape
    planes = lax.axis_size("fsdp")
    chips = lax.axis_size("ctx") // 2
    me = lax.axis_index("ctx")
    plane = lax.axis_index("fsdp")
    core, chip = me % 2, me // 2
    depth, units = w_gate.shape
    chip_heads = HEADS // chips
    width = chip_heads * HEAD_DIM
    where = jnp.stack([chip, core, plane]).astype(jnp.int32)
    start = (me * rows)[None].astype(jnp.int32)

    small = jnp.concatenate([gain_attn, gain_ffn, bias_table.reshape(-1)])
    small = jnp.pad(small[None], ((0, 15), (0, model - small.shape[0])))
    gate_mine, up_mine, x_piece, y_piece, qkv_mine, early_piece = pack_weights(
        where, w_gate, w_up, w_ffn_out, w_out, w_query, w_key, w_value, small
    )
    send, order, lens = prepare(lengths, after(tokens, early_piece), chips)
    gathered = lax.all_to_all(send.reshape(2 * chips, 2, rows, model), "ctx", 0, 0)

    near, far = column_ends(early_piece)
    early = [near, shift(near, 1), far]
    early_others = [swap(piece, CORE) for piece in early]
    x_near, x_far = column_ends(after(x_piece, near, far))
    y_near, y_far = column_ends(after(y_piece, *early))

    by_distance = jnp.stack([piece[depth] for piece in [early_piece] + early])
    all_small = jnp.stack([pick(by_distance, (plane + planes - i) % planes, 0) for i in range(planes)])
    full_gain_attn = all_small[:, :depth].reshape(1, model).astype(F32)
    full_gain_ffn = all_small[:, depth : 2 * depth].reshape(1, model).astype(F32)
    small_end = 2 * depth + bias_table.size
    full_table = all_small[:, 2 * depth : small_end].reshape(BUCKETS, HEADS)

    hot = bucket_table[:, None] == jnp.arange(BUCKETS, dtype=jnp.int32)[None, :]
    hot = jnp.concatenate([hot, jnp.zeros((1, BUCKETS), bool)])
    my_table = lax.dynamic_slice_in_dim(full_table, chip * chip_heads, chip_heads, 1)
    offsets = jnp.einsum("tb,bh->ht", hot.astype(LOW), my_table, preferred_element_type=F32)

    first_out, *kept, w_qkv = attn_forward(
        0, lens, where, gathered, full_gain_attn, [qkv_mine, *early, *early_others], offsets
    )
    x_near, y_near, first_out = lax.optimization_barrier((x_near, y_near, first_out))
    x_found = [x_near, shift(x_near, 1), x_far]
    y_found = [y_near, shift(y_near, 1), y_far]
    second_out, *kept = attn_forward(
        1, lens, where, gathered, full_gain_attn, [w_qkv], offsets, kept
    )
    attn_first = lax.all_to_all(first_out, "ctx", 0, 0)
    second_out, attn_first, x_found[2], y_found[2], *_ = lax.optimization_barrier(
        (second_out, attn_first, x_found[2], y_found[2], x_near, y_near)
    )
    attn = [attn_first, lax.all_to_all(second_out, "ctx", 0, 0)]
    x_swapped, y_swapped = [swap(t, X) for t in x_found], [swap(t, Y) for t in y_found]
    attn[1] = after(attn[1], *x_swapped, *y_swapped)
    attn_full, query, key, value = kept
    flat, dy = sort_rows(order, lens, start, tokens, cotangent)
    residual, nf_own, full_out = out_project(
        where, flat, attn, w_out, early, early_others, full_gain_ffn
    )
    dy_other = swap(after(dy, nf_own), CORE)
    nf_other = swap(nf_own, CORE)
    hidden, dup, dnf_own, dnf_send, full_down, *g_picks = ffn_first(
        where, nf_own, nf_other, dy, dy_other, (gate_mine, up_mine, w_ffn_out),
        x_found + y_found + x_swapped + y_swapped,
    )

    g_parts = column_sum(g_picks)
    dattn, dres, dgain_ffn, o_keep, o_send = out_back(
        where, dnf_own, swap(dnf_send, CORE), residual, dy, full_gain_ffn, full_out, attn, planes
    )
    dattn_all = lax.all_to_all(dattn, "ctx", 0, 0)
    o_came = swap(o_send, CORE)
    out_own, out_send, u_keep, u_send, f_keep, f_send = ffn_second(
        where, nf_own, nf_other, dy, dy_other, hidden, dup, full_down, planes
    )
    g_parts[1], g_parts[3], u_send, f_send, dattn_all = lax.optimization_barrier(
        (g_parts[1], g_parts[3], u_send, f_send, dattn_all)
    )
    u_came, f_came = swap(u_send, X), swap(f_send, Y)
    out_came = swap(out_send, CORE)
    dn, dw_keep, dw_send, dgain_attn, doffsets = attn_backward(
        lens, where, gathered, full_gain_attn, w_qkv, offsets,
        query, key, value, attn_full, dattn_all, planes,
    )

    u_came, f_came, dn, dw_send, dgain_attn, *g_parts = lax.optimization_barrier(
        (u_came, f_came, dn, dw_send, dgain_attn, *g_parts)
    )
    u_mine, u_send, f_mine, f_send = second_halves(where, u_keep, u_came, f_keep, f_came)
    u_came, f_came = swap(u_send, Y), swap(f_send, X)
    w_came = swap(dw_send, CORE)
    chip_parts = plane_swaps(by_chip(where, g_parts, o_keep, o_came))

    out_rows = finish_out(order, lens, start, residual, out_own, out_came, batch)
    mine_buckets = jnp.einsum(
        "ht,tb->bh", doffsets, hot.astype(F32), precision=lax.Precision.HIGHEST
    )
    buckets = lax.dynamic_update_slice_in_dim(
        jnp.zeros((BUCKETS, HEADS), F32), mine_buckets, chip * chip_heads, 1
    )
    line = jnp.concatenate(
        [
            dgain_attn.reshape(planes, depth),
            dgain_ffn.reshape(planes, depth),
            buckets.reshape(planes, -1),
        ],
        axis=1,
    ).astype(LOW)
    line = jnp.pad(line[:, None, :], ((0, 0), (0, 15), (0, model - line.shape[1])))
    nothing = jnp.zeros_like(line)
    line_came = swap(jnp.where(core == 1, line, nothing), CORE)
    line_kept = jnp.where(core == 0, line, nothing)
    *plane_parts, gate_part = by_plane(
        where, u_mine, u_came, f_mine, f_came, dw_keep, w_came, line_kept, line_came, chip_parts
    )
    dn, *plane_parts = lax.optimization_barrier((dn, *plane_parts))
    dn = lax.all_to_all(dn, "ctx", 0, 0).reshape(chips, batch, rows, model)
    dtok = finish_tokens(order, dn, flat, dres, full_gain_attn)
    pack = jnp.concatenate([gate_part, add(*column_sum(plane_parts))])

    packs = plane_swaps([after(pack, out_rows)] * 4)
    packs = packs + [swap(piece, CORE) for piece in packs]
    packs[-1] = after(packs[-1], dtok)
    grad_gate, grad_up, grad_down, grad_query, grad_key, grad_value, grad_out, sums = unpack(
        where, packs, depth, units
    )
    grad_gain_attn = sums[0, :depth]
    grad_gain_ffn = sums[0, depth : 2 * depth]
    grad_buckets = sums[0, 2 * depth : small_end].reshape(BUCKETS // planes, HEADS)

    return (
        out_rows, dtok, grad_gain_attn, grad_query, grad_key, grad_value, grad_out, grad_buckets,
        grad_gain_ffn, grad_gate, grad_up, grad_down,
    )


def gelu_tanh(values):
    return (
        0.5
        * values
        * (1.0 + jnp.tanh(0.7978845608028654 * (values + 0.044715 * values * values * values)))
    )


def normalize(values, gain_vec):
    return (
        values * lax.rsqrt(jnp.mean(values * values, axis=-1, keepdims=True) + norm_eps) * gain_vec
    )


def project(values, matrix):
    return jnp.einsum("msd,de->mse", values, matrix, preferred_element_type=jnp.float32)


def back_project(values, matrix):
    return jnp.einsum("mse,de->msd", values, matrix, preferred_element_type=jnp.float32)


def outer_sum(left_rows, right_rows):
    return jnp.einsum("msd,mse->de", left_rows, right_rows, preferred_element_type=jnp.float32)


def split_heads(values):
    return values.reshape(values.shape[0], values.shape[1], HEADS, HEAD_DIM)


def toeplitz_bias(offset_bias, start, query_rows, key_rows):
    span = query_rows + key_rows - 1
    window = lax.dynamic_slice_in_dim(offset_bias, start, span, 1)
    wrapped = jnp.concatenate(
        [
            window[:, query_rows - 1 :],
            jnp.zeros((window.shape[0], 1), jnp.float32),
            window[:, : query_rows - 1],
        ],
        axis=1,
    )
    tiled = jnp.tile(wrapped, (1, query_rows))
    shaped = tiled[:, : query_rows * span].reshape(window.shape[0], query_rows, span)
    return shaped[:, :, :key_rows]


def diagonal_sums(grad_bias, query_rows, key_rows):
    span = query_rows + key_rows - 1
    heads = grad_bias.shape[0]
    padded = jnp.pad(grad_bias, ((0, 0), (0, 0), (0, span - key_rows)))
    flat = jnp.pad(padded.reshape(heads, query_rows * span), ((0, 0), (0, query_rows)))
    slots = jnp.sum(flat.reshape(heads, query_rows, span + 1), axis=1)
    return jnp.concatenate([slots[:, key_rows + 1 :], slots[:, :key_rows]], axis=1)


def block_scores(query_heads, key_heads, pair_bias, key_ok):
    scores = jnp.einsum(
        "mihe,mjhe->mhij", query_heads, key_heads, preferred_element_type=jnp.float32
    )
    scores = scores + pair_bias[None]
    return jnp.where(key_ok[:, None, None, :], scores, -1e30)


def over_blocks(update, make_bias, carried, pieces):
    piece_rows = pieces[0].shape[1]
    block_rows = math.gcd(piece_rows, 256)
    block_count = piece_rows // block_rows

    def advance(block_index, running):
        block_start = block_index * block_rows
        sub_pieces = tuple(
            (
                lax.dynamic_slice_in_dim(member, block_index * block_rows, block_rows, 1)
                for member in pieces
            )
        )
        bias_info = make_bias(block_start, block_rows)
        return update(running, sub_pieces, block_start, slice(None), bias_info)

    return lax.fori_loop(0, block_count, advance, carried)


def per_device_general(
    tokens,
    cotangent,
    lengths,
    bucket_table,
    gain_attn,
    w_query,
    w_key,
    w_value,
    w_out,
    bias_table,
    gain_ffn,
    w_gate,
    w_up,
    w_ffn_out,
):
    shards = (
        gain_attn,
        w_query,
        w_key,
        w_value,
        w_out,
        bias_table,
        gain_ffn,
        w_gate,
        w_up,
        w_ffn_out,
    )
    gathered = (
        lax.all_gather(shards[0], "fsdp", axis=0, tiled=True),
        lax.all_gather(shards[1], "fsdp", axis=0, tiled=True),
        lax.all_gather(shards[2], "fsdp", axis=0, tiled=True),
        lax.all_gather(shards[3], "fsdp", axis=0, tiled=True),
        lax.all_gather(shards[4], "fsdp", axis=0, tiled=True),
        lax.all_gather(shards[5], "fsdp", axis=0, tiled=True),
        lax.all_gather(shards[6], "fsdp", axis=0, tiled=True),
        lax.all_gather(shards[7], "fsdp", axis=0, tiled=True),
        lax.all_gather(shards[8], "fsdp", axis=0, tiled=True),
        lax.all_gather(shards[9], "fsdp", axis=0, tiled=True),
    )
    (
        full_gain_attn,
        full_query,
        full_key,
        full_value,
        full_out,
        full_bias,
        full_gain_ffn,
        full_gate,
        full_up,
        full_ffn_out,
    ) = gathered
    batch_rows, local_rows, model_width = tokens.shape
    seq_len = local_rows * lax.axis_size("ctx")
    table_len = bucket_table.shape[0]
    first_pos = lax.axis_index("ctx") * local_rows
    positions = first_pos + jnp.arange(local_rows, dtype=jnp.int32)
    valid_mask = positions[None, :] < lengths[:, None]
    valid_rows = valid_mask.astype(jnp.float32)
    bucket_hot = bucket_table[:, None] == jnp.arange(BUCKETS, dtype=jnp.int32)[None, :]

    def offset_bias_of(bias_weights):
        return jnp.einsum(
            "tb,bh->ht",
            bucket_hot.astype(jnp.bfloat16),
            bias_weights,
            preferred_element_type=jnp.float32,
        )

    forward_offsets = offset_bias_of(full_bias)

    def keys_bias(offset_bias):

        def keys_make(block_start, block_rows):
            start = block_start - first_pos - (local_rows - 1) + (seq_len - 1)
            return (toeplitz_bias(offset_bias, start, local_rows, block_rows), start)

        return keys_make

    def queries_bias(offset_bias):

        def queries_make(block_start, block_rows):
            start = first_pos - block_start - (block_rows - 1) + (seq_len - 1)
            return (toeplitz_bias(offset_bias, start, block_rows, local_rows), start)

        return queries_make

    tokens_f = tokens.astype(jnp.float32)
    attn_gain = full_gain_attn.astype(jnp.float32)
    normed = normalize(tokens_f, attn_gain).astype(jnp.bfloat16)
    queries = project(normed, full_query).astype(jnp.bfloat16)
    keys_local = project(normed, full_key).astype(jnp.bfloat16)
    values_local = project(normed, full_value).astype(jnp.bfloat16)
    query_heads = split_heads(queries)

    def forward_block(running, sub_pieces, block_start, member_pick, bias_info):
        max_score, row_total, weighted = running
        key_part, value_part = sub_pieces
        key_pos = block_start + jnp.arange(key_part.shape[1], dtype=jnp.int32)
        key_ok = key_pos[None, :] < lengths[:, None]
        scores = block_scores(query_heads, split_heads(key_part), bias_info[0], key_ok)
        new_max = jnp.maximum(max_score, jnp.max(scores, axis=-1))
        shrink = jnp.exp(max_score - new_max)
        weights = jnp.exp(scores - new_max[..., None])
        row_total = row_total * shrink + jnp.sum(weights, axis=-1)
        weighted = weighted * jnp.transpose(shrink, (0, 2, 1))[..., None] + jnp.einsum(
            "mhij,mjhe->mihe",
            weights.astype(jnp.bfloat16),
            split_heads(value_part),
            preferred_element_type=jnp.float32,
        )
        return (new_max, row_total, weighted)

    start_state = (
        jnp.full((batch_rows, HEADS, local_rows), -1e30, jnp.float32),
        jnp.zeros((batch_rows, HEADS, local_rows), jnp.float32),
        jnp.zeros((batch_rows, local_rows, HEADS, HEAD_DIM), jnp.float32),
    )
    max_score, row_total, weighted = over_blocks(
        forward_block,
        keys_bias(forward_offsets),
        start_state,
        (
            lax.all_gather(keys_local, "ctx", axis=1, tiled=True),
            lax.all_gather(values_local, "ctx", axis=1, tiled=True),
        ),
    )
    log_total = max_score + jnp.log(row_total)
    attn_full = weighted / jnp.transpose(row_total, (0, 2, 1))[..., None]
    attn_low = attn_full.reshape(batch_rows, local_rows, model_width).astype(jnp.bfloat16)
    residual = tokens_f + project(attn_low, full_out)
    ffn_gain = full_gain_ffn.astype(jnp.float32)
    normed_ffn = normalize(residual, ffn_gain).astype(jnp.bfloat16)
    gate_proj = project(normed_ffn, full_gate)
    up_proj = project(normed_ffn, full_up)
    hidden = (gelu_tanh(gate_proj) * up_proj).astype(jnp.bfloat16)
    result = valid_rows[..., None] * (residual + project(hidden, full_ffn_out))
    output = result.astype(jnp.bfloat16)
    back_weights = (
        lax.all_gather(shards[0], "fsdp", axis=0, tiled=True),
        lax.all_gather(shards[1], "fsdp", axis=0, tiled=True),
        lax.all_gather(shards[2], "fsdp", axis=0, tiled=True),
        lax.all_gather(shards[3], "fsdp", axis=0, tiled=True),
        lax.all_gather(shards[4], "fsdp", axis=0, tiled=True),
        lax.all_gather(shards[5], "fsdp", axis=0, tiled=True),
        lax.all_gather(shards[6], "fsdp", axis=0, tiled=True),
        lax.all_gather(shards[7], "fsdp", axis=0, tiled=True),
        lax.all_gather(shards[8], "fsdp", axis=0, tiled=True),
        lax.all_gather(shards[9], "fsdp", axis=0, tiled=True),
    )
    (
        back_gain_attn,
        back_query,
        back_key,
        back_value,
        back_out,
        back_bias,
        back_gain_ffn,
        back_gate,
        back_up,
        back_ffn_out,
    ) = back_weights
    back_offsets = offset_bias_of(back_bias)
    grad_out = cotangent.astype(jnp.float32) * valid_rows[..., None]
    grad_low = grad_out.astype(jnp.bfloat16)
    grad_w_ffn_out = outer_sum(hidden, grad_low)
    grad_hidden = back_project(grad_low, back_ffn_out)

    def gated_product(gate_in, up_in):
        return gelu_tanh(gate_in) * up_in

    gated_value, gated_back = jax.vjp(gated_product, gate_proj, up_proj)
    grad_gate, grad_up = gated_back(grad_hidden)
    grad_gate = grad_gate.astype(jnp.bfloat16)
    grad_up = grad_up.astype(jnp.bfloat16)
    grad_w_gate = outer_sum(normed_ffn, grad_gate)
    grad_w_up = outer_sum(normed_ffn, grad_up)
    grad_normed_ffn = back_project(grad_gate, back_gate) + back_project(grad_up, back_up)
    norm_value, norm_back = jax.vjp(normalize, residual, back_gain_ffn.astype(jnp.float32))
    grad_resid_part, grad_gain_ffn = norm_back(grad_normed_ffn)
    grad_resid = grad_out + grad_resid_part
    grad_branch = grad_resid.astype(jnp.bfloat16)
    grad_w_out = outer_sum(attn_low, grad_branch)
    grad_attn = back_project(grad_branch, back_out).astype(jnp.bfloat16)
    grad_heads = split_heads(grad_attn)
    delta_row = jnp.einsum(
        "mihe,mihe->mhi", grad_heads, attn_full, preferred_element_type=jnp.float32
    )

    def query_grad_block(running, sub_pieces, block_start, member_pick, bias_info):
        grad_query, grad_offsets = running
        pair_bias, table_start = bias_info
        key_part, value_part = sub_pieces
        key_heads = split_heads(key_part)
        key_pos = block_start + jnp.arange(key_part.shape[1], dtype=jnp.int32)
        key_ok = key_pos[None, :] < lengths[:, None]
        scores = block_scores(query_heads, key_heads, pair_bias, key_ok)
        probabilities = jnp.exp(scores - log_total[..., None])
        grad_probs = jnp.einsum(
            "mihe,mjhe->mhij",
            grad_heads,
            split_heads(value_part),
            preferred_element_type=jnp.float32,
        )
        grad_scores = (probabilities * (grad_probs - delta_row[..., None])).astype(jnp.bfloat16)
        grad_query = grad_query + jnp.einsum(
            "mhij,mjhe->mihe", grad_scores, key_heads, preferred_element_type=jnp.float32
        )
        pair_grad = jnp.sum(grad_scores.astype(jnp.float32), axis=0)
        diag = diagonal_sums(pair_grad, pair_grad.shape[1], pair_grad.shape[2])
        current = lax.dynamic_slice_in_dim(grad_offsets, table_start, diag.shape[1], 1)
        grad_offsets = lax.dynamic_update_slice_in_dim(grad_offsets, current + diag, table_start, 1)
        return (grad_query, grad_offsets)

    query_state = (
        jnp.zeros((batch_rows, local_rows, HEADS, HEAD_DIM), jnp.float32),
        jnp.zeros((HEADS, table_len), jnp.float32),
    )
    grad_query, grad_offsets = over_blocks(
        query_grad_block,
        keys_bias(back_offsets),
        query_state,
        (
            lax.all_gather(keys_local, "ctx", axis=1, tiled=True),
            lax.all_gather(values_local, "ctx", axis=1, tiled=True),
        ),
    )
    grad_buckets = jnp.einsum(
        "ht,tb->bh", grad_offsets, bucket_hot.astype(jnp.float32), precision=lax.Precision.HIGHEST
    )
    stats_lse, stats_delta = (
        lax.all_gather(log_total, "ctx", axis=2, tiled=True),
        lax.all_gather(delta_row, "ctx", axis=2, tiled=True),
    )
    key_heads_local = split_heads(keys_local)
    value_heads_local = split_heads(values_local)

    def key_grad_block(running, sub_pieces, block_start, member_pick, bias_info):
        grad_key, grad_value = running
        query_part, grad_part = sub_pieces
        rows_here = query_part.shape[1]
        query_part_heads = split_heads(query_part)
        grad_part_heads = split_heads(grad_part)
        scores = block_scores(query_part_heads, key_heads_local, bias_info[0], valid_mask)
        lse_part = lax.dynamic_slice_in_dim(stats_lse, block_start, rows_here, 2)
        delta_part = lax.dynamic_slice_in_dim(stats_delta, block_start, rows_here, 2)
        probabilities = jnp.exp(scores - lse_part[..., None])
        grad_value = grad_value + jnp.einsum(
            "mhij,mihe->mjhe",
            probabilities.astype(jnp.bfloat16),
            grad_part_heads,
            preferred_element_type=jnp.float32,
        )
        grad_probs = jnp.einsum(
            "mihe,mjhe->mhij",
            grad_part_heads,
            value_heads_local,
            preferred_element_type=jnp.float32,
        )
        grad_scores = (probabilities * (grad_probs - delta_part[..., None])).astype(jnp.bfloat16)
        grad_key = grad_key + jnp.einsum(
            "mhij,mihe->mjhe", grad_scores, query_part_heads, preferred_element_type=jnp.float32
        )
        return (grad_key, grad_value)

    key_state = (
        jnp.zeros((batch_rows, local_rows, HEADS, HEAD_DIM), jnp.float32),
        jnp.zeros((batch_rows, local_rows, HEADS, HEAD_DIM), jnp.float32),
    )
    grad_key, grad_value = over_blocks(
        key_grad_block,
        queries_bias(back_offsets),
        key_state,
        (
            lax.all_gather(queries, "ctx", axis=1, tiled=True),
            lax.all_gather(grad_attn, "ctx", axis=1, tiled=True),
        ),
    )
    grad_q = grad_query.reshape(batch_rows, local_rows, model_width).astype(jnp.bfloat16)
    grad_k = grad_key.reshape(batch_rows, local_rows, model_width).astype(jnp.bfloat16)
    grad_v = grad_value.reshape(batch_rows, local_rows, model_width).astype(jnp.bfloat16)
    grad_w_query = outer_sum(normed, grad_q)
    grad_w_key = outer_sum(normed, grad_k)
    grad_w_value = outer_sum(normed, grad_v)
    grad_normed = (
        back_project(grad_q, back_query)
        + back_project(grad_k, back_key)
        + back_project(grad_v, back_value)
    )
    attn_norm_value, attn_norm_back = jax.vjp(
        normalize, tokens_f, back_gain_attn.astype(jnp.float32)
    )
    grad_tokens_part, grad_gain_attn = attn_norm_back(grad_normed)
    grad_tokens = grad_resid + grad_tokens_part
    grads = (
        grad_gain_attn,
        grad_w_query,
        grad_w_key,
        grad_w_value,
        grad_w_out,
        grad_buckets,
        grad_gain_ffn,
        grad_w_gate,
        grad_w_up,
        grad_w_ffn_out,
    )
    shard_sums = (
        lax.psum_scatter(grads[0], "fsdp", scatter_dimension=0, tiled=True),
        lax.psum_scatter(grads[1], "fsdp", scatter_dimension=0, tiled=True),
        lax.psum_scatter(grads[2], "fsdp", scatter_dimension=0, tiled=True),
        lax.psum_scatter(grads[3], "fsdp", scatter_dimension=0, tiled=True),
        lax.psum_scatter(grads[4], "fsdp", scatter_dimension=0, tiled=True),
        lax.psum_scatter(grads[5], "fsdp", scatter_dimension=0, tiled=True),
        lax.psum_scatter(grads[6], "fsdp", scatter_dimension=0, tiled=True),
        lax.psum_scatter(grads[7], "fsdp", scatter_dimension=0, tiled=True),
        lax.psum_scatter(grads[8], "fsdp", scatter_dimension=0, tiled=True),
        lax.psum_scatter(grads[9], "fsdp", scatter_dimension=0, tiled=True),
    )
    totals = lax.psum(
        (
            shard_sums[0],
            shard_sums[1],
            shard_sums[2],
            shard_sums[3],
            shard_sums[4],
            shard_sums[5],
            shard_sums[6],
            shard_sums[7],
            shard_sums[8],
            shard_sums[9],
        ),
        "ctx",
    )
    return (output, grad_tokens) + tuple(totals)


def solution(mesh):
    placed = (
        P("fsdp", "ctx", None),
        P("fsdp", "ctx", None),
        P("fsdp"),
        P(),
        P("fsdp"),
        P("fsdp", None),
        P("fsdp", None),
        P("fsdp", None),
        P("fsdp", None),
        P("fsdp", None),
        P("fsdp"),
        P("fsdp", None),
        P("fsdp", None),
        P("fsdp", None),
    )
    plane = mesh.shape["ctx"] == 8 and mesh.shape["fsdp"] == 4
    return jax.shard_map(
        per_device_plane if plane else per_device_general,
        mesh=mesh,
        in_specs=placed,
        out_specs=(
            P("fsdp", "ctx", None),
            P("fsdp", "ctx", None),
            P("fsdp"),
            P("fsdp", None),
            P("fsdp", None),
            P("fsdp", None),
            P("fsdp", None),
            P("fsdp", None),
            P("fsdp"),
            P("fsdp", None),
            P("fsdp", None),
            P("fsdp", None),
        ),
        check_vma=False,
    )
```
